32 devices in a mesh: items: 8 (over y, x, core), frames: 4 (over z).
Axes of the slice: x: 2, y: 2, z: 4, core: 2. Of those that a mesh axis runs over, the one named last changes fastest.
Arguments:
- tokens: bfloat16 [8, 16, 196, 768], P('items', 'frames'), may hold values from -6 to 6
- cotangent: bfloat16 [8, 16, 196, 768], P('items', 'frames'), may hold values from -6 to 6
- date_year: int32 [8, 16], P('items', 'frames'), may hold values from 2015 to 2024
- date_day: int32 [8, 16], P('items', 'frames'), may hold values from 1 to 366
- item_dates: int32 [8, 3], P('items'), may hold values from 1 to 6, 16 in all within a row
- slot_frame: int32 [8, 16], P('items'), may hold values from 0 to 15, as said below
- frame_mask: int32 [8, 16], P('items'), may hold values 0 or 1
- qkv_weight: float32 [768, 2304], P('frames'), may hold values from -0.21875 to 0.21875
- qkv_first: float32 [768, 2304], P('frames'), may hold values from -112 to 112
- qkv_second: float32 [768, 2304], P('frames'), may hold values from 25.088 to 100.352
- out_weight: float32 [768, 768], P('frames'), may hold values from -2.5 to 2.5
- out_first: float32 [768, 768], P('frames'), may hold values from -6 to 6
- out_second: float32 [768, 768], P('frames'), may hold values from 0.25088 to 1.00352
- up_weight: float32 [768, 3072], P('frames'), may hold values from -0.21875 to 0.21875
- up_first: float32 [768, 3072], P('frames'), may hold values from -32 to 32
- up_second: float32 [768, 3072], P('frames'), may hold values from 2.25792 to 9.03168
- down_weight: float32 [3072, 768], P('frames'), may hold values from -0.109375 to 0.109375
- down_first: float32 [3072, 768], P('frames'), may hold values from -64 to 64
- down_second: float32 [3072, 768], P('frames'), may hold values from 9.03168 to 36.12672
- vectors: float32 [9216], P('frames')
- vector_first: float32 [9216], P('frames'), may hold values from -160 to 160
- vector_second: float32 [9216], P('frames'), may hold values from 56.448 to 225.792
Outputs:
- block_out: bfloat16 [8, 16, 196, 768], P('items', 'frames')
- token_grad: float32 [8, 16, 196, 768], P('items', 'frames')
- qkv_moment: float32 [768, 2304], P('frames')
- qkv_square: float32 [768, 2304], P('frames')
- qkv_master: float32 [768, 2304], P('frames')
- out_moment: float32 [768, 768], P('frames')
- out_square: float32 [768, 768], P('frames')
- out_master: float32 [768, 768], P('frames')
- up_moment: float32 [768, 3072], P('frames')
- up_square: float32 [768, 3072], P('frames')
- up_master: float32 [768, 3072], P('frames')
- down_moment: float32 [3072, 768], P('frames')
- down_square: float32 [3072, 768], P('frames')
- down_master: float32 [3072, 768], P('frames')
- vector_moment: float32 [9216], P('frames')
- vector_square: float32 [9216], P('frames')
- vector_master: float32 [9216], P('frames')
The draws below stay inside these ranges and needn't reach their ends.
Inputs may be any that keep to these rules, and one draw needn't show every extreme that they name: `item_dates`: in each group the 3 items' dates add up to 16; the longest item has exactly 6. `slot_frame`: in each group a permutation of the frame numbers 0 to 15; frame numbers that follow each other stand on devices of frames that follow each other, cyclically.
All inputs are finite; a program needn't handle non-finite values. No bound on the sum of `frame_mask` on one device may be relied on, other than what follows from the above.
Results may differ from the reference program's by a relative error of at most 0.012.
Values may be sent and summed in bfloat16 or wider, within the bound.
A program may use at most 576 MiB of HBM per device.

```python
import math
import jax
import jax.numpy as jnp
import numpy as np
from jax import lax

D = 768
HEADS = 12
HEAD = 64
FF = 3072
GRID = 14
STEP = 10
FR_DEV = 4
FRAME_TOK = 196
SLOTS = 16
ITEMS_G = 3
GROUPS = 8
ROWS = 784
KEYS = 3136
ALL_TOK = 25088
VEC = 9216
N_FRAMES = 4


def draw_slot_frame(key, part):
    key = jax.random.fold_in(key, 11)
    first_key, second_key = jax.random.split(key)
    frames_each = SLOTS // FR_DEV
    rotation = jax.random.randint(first_key, (GROUPS, 1), 0, frames_each)
    inner_turn = jax.random.randint(second_key, (GROUPS, frames_each), 0, FR_DEV)
    slot_index = jnp.arange(SLOTS, dtype=jnp.int32)
    device = slot_index // FR_DEV
    position = slot_index % FR_DEV
    turned = (position[None, :] + inner_turn[:, device]) % FR_DEV
    return (turned * frames_each + (device[None, :] + rotation) % frames_each).astype(jnp.int32)


def draw_vectors(key, part):
    key = jax.random.fold_in(key, 7)
    total = 8 * D + FF
    random_part = jax.random.normal(key, (total,), jnp.float32)
    scales = jnp.concatenate([jnp.full((D,), 0.2, jnp.float32), jnp.full((D,), 0.3, jnp.float32), jnp.full((3 * D,), 0.5, jnp.float32), jnp.full((D,), 0.2, jnp.float32), jnp.full((D,), 0.3, jnp.float32), jnp.full((D,), 0.5, jnp.float32), jnp.full((FF,), 0.5, jnp.float32)])
    offsets = jnp.concatenate([jnp.ones((D,), jnp.float32), jnp.zeros((4 * D,), jnp.float32), jnp.ones((D,), jnp.float32), jnp.zeros((2 * D + FF,), jnp.float32)])
    return offsets + scales * random_part


def set_ends(values, rng, low, top_value):
    extent = values.shape
    index_at = [jax.random.randint(jax.random.fold_in(rng, axis), (), 0, extent[axis]) for axis in range(len(extent))]
    values = values.at[tuple(index_at)].set(low)
    longest = extent.index(max(extent))
    index_at[longest] = (index_at[longest] + 1) % extent[longest]
    return values.at[tuple(index_at)].set(top_value)


def shard_levels(key, dims, cuts, smallest, high):
    factor_of, own = 1.0, jax.random.fold_in(key, 6)
    for dim, shards_of in cuts:
        draws = jnp.exp(jax.random.uniform(jax.random.fold_in(own, dim), (shards_of,), jnp.float32, smallest / len(cuts), high / len(cuts)))
        factor_of = factor_of * jnp.repeat(draws, dims[dim] // shards_of).reshape([-1 if axis == dim else 1 for axis in range(len(dims))])
    return factor_of


def split_up(amount, total, limit, skew):
    loads = [(1 << 20) // math.isqrt(standing ** skew) + 1 for standing in range(2, amount + 1)]
    surplus, counts = total - limit - (amount - 1), [1] * (amount - 1)
    while surplus > 0:
        movable = [i for i in range(amount - 1) if counts[i] < limit]
        pool, remaining = sum([loads[i] for i in movable]), surplus
        for i in movable:
            addition = min(limit - counts[i], max(1, remaining * loads[i] // pool), surplus)
            counts[i] = counts[i] + addition
            surplus = surplus - addition
    return np.array([limit] + counts)


def uneven(key, count, total, reach, slope):
    if count == 2:
        one = jax.random.randint(key, (), max(1, total - reach), min(reach, total - 1) + 1)
        return jnp.stack([one, total - one])
    lengths = jnp.asarray(split_up(count, total, reach, slope), jnp.int32)
    couples = (count - 1) // 2
    source_of, taker = lengths[1:1 + 2 * couples:2], lengths[2:2 + 2 * couples:2]
    room = jnp.minimum(source_of - 1, reach - taker)
    shifted = jax.random.randint(jax.random.fold_in(key, 1), (couples,), 0, 1 << 20) % (room + 1)
    lengths = lengths.at[1:1 + 2 * couples:2].set(source_of - shifted).at[2:2 + 2 * couples:2].set(taker + shifted)
    return lengths[jax.random.permutation(jax.random.fold_in(key, 2), count)]


def bell_draw(rng, extent, scale, limit, cuts=(), held_as=jnp.bfloat16):
    drawn = jax.random.normal(rng, extent, jnp.float32) * scale
    if len(cuts) > 0:
        drawn = shard_levels(rng, extent, cuts, -0.22, 0.18) * drawn
    return jnp.clip(drawn, min=-limit, max=limit).astype(held_as)


def setup_inputs(seed: int = 0) -> dict:
    key_list = jax.random.split(jax.random.key(seed), 23)
    return {
        "tokens": bell_draw(key_list[0], (GROUPS, SLOTS, FRAME_TOK, D), 1.0, 6.0, ((0, 8), (1, 4))),
        "cotangent": bell_draw(key_list[1], (GROUPS, SLOTS, FRAME_TOK, D), 1.0, 6.0, ((0, 8), (1, 4))),
        "date_year": set_ends(jax.random.randint(key_list[2], (GROUPS, SLOTS), 2015, 2025), jax.random.fold_in(key_list[2], 1), 2015, 2024).astype(jnp.int32),
        "date_day": set_ends(jax.random.randint(key_list[3], (GROUPS, SLOTS), 1, 367), jax.random.fold_in(key_list[3], 1), 1, 366).astype(jnp.int32),
        "item_dates": jax.vmap(lambda own: uneven(own, ITEMS_G, SLOTS, 6, 1))(jax.random.split(key_list[4], GROUPS)).reshape((GROUPS, ITEMS_G)).astype(jnp.int32),
        "slot_frame": draw_slot_frame(jax.random.fold_in(key_list[22], 71), 0),
        "frame_mask": set_ends((jax.random.randint(key_list[6], (GROUPS, SLOTS), 0, 4) < 3).astype(jnp.int32), jax.random.fold_in(key_list[6], 1), 0, 1),
        "qkv_weight": bell_draw(key_list[7], (D, 3 * D), D ** -0.5, 0.21875, ((0, 4),), jnp.float32),
        "qkv_first": bell_draw(key_list[8], (D, 3 * D), (0.11 * ALL_TOK ** 0.5), 112.0, ((0, 4),), jnp.float32),
        "qkv_second": jnp.clip(jnp.exp(math.log(100.352) - 1.3862944 * jax.random.uniform(key_list[9], (D, 3 * D), jnp.float32) ** shard_levels(key_list[9], (D, 3 * D), ((0, 4),), -0.2, 0.2)), 25.088, 100.352),
        "out_weight": bell_draw(key_list[10], (D, D), (max(1, 3 * D // (2 * FRAME_TOK))) ** -0.5, 2.5, ((0, 4),), jnp.float32),
        "out_first": bell_draw(key_list[11], (D, D), (0.011 * ALL_TOK ** 0.5), 6.0, ((0, 4),), jnp.float32),
        "out_second": jnp.clip(jnp.exp(math.log(1.00352) - 1.3862944 * jax.random.uniform(key_list[12], (D, D), jnp.float32) ** shard_levels(key_list[12], (D, D), ((0, 4),), -0.2, 0.2)), 0.25088, 1.00352),
        "up_weight": bell_draw(key_list[13], (D, FF), D ** -0.5, 0.21875, ((0, 4),), jnp.float32),
        "up_first": bell_draw(key_list[14], (D, FF), (0.033 * ALL_TOK ** 0.5), 32.0, ((0, 4),), jnp.float32),
        "up_second": jnp.clip(jnp.exp(math.log(9.03168) - 1.3862944 * jax.random.uniform(key_list[15], (D, FF), jnp.float32) ** shard_levels(key_list[15], (D, FF), ((0, 4),), -0.2, 0.2)), 2.25792, 9.03168),
        "down_weight": bell_draw(key_list[16], (FF, D), FF ** -0.5, 0.109375, ((0, 4),), jnp.float32),
        "down_first": bell_draw(key_list[17], (FF, D), (0.066 * ALL_TOK ** 0.5), 64.0, ((0, 4),), jnp.float32),
        "down_second": jnp.clip(jnp.exp(math.log(36.12672) - 1.3862944 * jax.random.uniform(key_list[18], (FF, D), jnp.float32) ** shard_levels(key_list[18], (FF, D), ((0, 4),), -0.2, 0.2)), 9.03168, 36.12672),
        "vectors": draw_vectors(jax.random.fold_in(key_list[22], 71), 0),
        "vector_first": bell_draw(key_list[20], (VEC,), (0.165 * ALL_TOK ** 0.5), 160.0, ((0, 4),), jnp.float32),
        "vector_second": jnp.clip(jnp.exp(math.log(225.792) - 1.3862944 * jax.random.uniform(key_list[21], (VEC,), jnp.float32) ** shard_levels(key_list[21], (VEC,), ((0, 4),), -0.2, 0.2)), 56.448, 225.792),
    }


@jax.custom_vjp
def low(v):
    return lax.optimization_barrier(v.astype(jnp.bfloat16)).astype(jnp.float32)

@jax.custom_vjp
def low_back(v):
    return v

def low_keep(v):
    return (low(v), None)

def low_pass(kept, grad):
    return (grad,)

def back_keep(v):
    return (v, None)

def back_low(kept, grad):
    return (low(grad),)
low.defvjp(low_keep, low_pass)
low_back.defvjp(back_keep, back_low)
precise = lax.Precision.HIGHEST
beta_one = 0.9
beta_two = 0.999

def sincos(values, length_out):
    half_width = length_out // 2
    frequency = 1.0 / 10000.0 ** (jnp.arange(half_width, dtype=jnp.float32) / half_width)
    angles = values[..., None] * frequency
    return jnp.concatenate([jnp.sin(angles), jnp.cos(angles)], axis=-1)

def positions(year_values, day_values):
    cell_index = jnp.arange(FRAME_TOK, dtype=jnp.int32)
    spatial = jnp.concatenate([sincos((cell_index // GRID).astype(jnp.float32), 3 * D // 8), sincos((cell_index % GRID).astype(jnp.float32), 3 * D // 8)], axis=-1)
    temporal = jnp.concatenate([sincos((year_values - 2000).astype(jnp.float32), D // 8), sincos(day_values.astype(jnp.float32), D // 8)], axis=-1)
    slot_count = year_values.shape[0]
    return jnp.concatenate([jnp.broadcast_to(spatial[None], (slot_count, FRAME_TOK, 3 * D // 4)), jnp.broadcast_to(temporal[:, None], (slot_count, FRAME_TOK, D // 4))], axis=-1)

def slot_items(dates_group, frames_group, mask_group):
    item_ends = jnp.cumsum(dates_group).astype(jnp.int32)
    starts = (item_ends - dates_group).astype(jnp.int32)
    item_index = lax.optimization_barrier(jnp.sum((frames_group[:, None] >= item_ends[None, :]).astype(jnp.int32), axis=1)).astype(jnp.int32)
    is_first = jnp.any(frames_group[:, None] == starts[None, :], axis=1)
    is_valid = jnp.logical_or(mask_group > 0, is_first)
    return (item_index, is_valid)

def layer_norm(values, gain_vec, shift_vec):
    average = lax.optimization_barrier(jnp.mean(values, axis=-1, keepdims=True))
    centred = values - average
    spread = lax.optimization_barrier(jnp.mean(centred * centred, axis=-1, keepdims=True))
    return centred * lax.rsqrt(spread + 1e-06) * gain_vec + shift_vec

def unpack(vector_all):
    pieces = [vector_all[index * D:(index + 1) * D] for index in range(8)]
    return tuple(pieces) + (vector_all[8 * D:],)

def attend(query_block, key_rows, value_rows, allowed_block):
    scores = jnp.einsum('qhe,khe->hqk', query_block, key_rows, precision=precise) * 0.125
    scores = low_back(scores)
    scores = jnp.where(allowed_block[None], scores, -1000000000.0)
    row_max = lax.optimization_barrier(jnp.max(scores, axis=-1, keepdims=True))
    weights = jnp.exp(scores - row_max)
    probs = low(weights / lax.optimization_barrier(jnp.sum(weights, axis=-1, keepdims=True)))
    return jnp.einsum('hqk,khe->qhe', probs, value_rows, precision=precise)

def forward(inputs, qkv_w, out_w, up_w, down_w, vector_all, pos_table, item_ids, key_valid):
    gain_one, shift_one, bias_query, bias_value, bias_output, gain_two, shift_two, bias_down, bias_up = unpack(vector_all)
    residual_in = inputs + pos_table
    normed = low(layer_norm(residual_in, gain_one, shift_one))
    projected = jnp.dot(normed, qkv_w, precision=precise)
    queries = low_back(low(projected[:, :D] + bias_query))
    key_rows = low_back(low(projected[:, D:2 * D]))
    value_rows = low_back(low(projected[:, 2 * D:] + bias_value))
    allowed = (item_ids[:, None] == item_ids[None, :]) & key_valid[None, :]
    query_blocks = queries.reshape(N_FRAMES, ROWS, HEADS, HEAD)
    allowed_blocks = allowed.reshape(N_FRAMES, ROWS, KEYS)
    key_heads = key_rows.reshape(KEYS, HEADS, HEAD)
    value_heads = value_rows.reshape(KEYS, HEADS, HEAD)

    def one_block(block):
        return attend(block[0], key_heads, value_heads, block[1])
    mixed = lax.map(jax.checkpoint(one_block), (query_blocks, allowed_blocks))
    attended = low_back(low(mixed.reshape(KEYS, D)))
    branch = low_back(jnp.dot(attended, out_w, precision=precise) + bias_output)
    hidden = residual_in + branch
    normed_two = low(layer_norm(hidden, gain_two, shift_two))
    inner = low_back(jnp.dot(normed_two, up_w, precision=precise) + bias_up)
    active = low(jax.nn.gelu(inner, approximate=False))
    mlp_out = low_back(jnp.dot(active, down_w, precision=precise) + bias_down)
    return hidden + mlp_out

def adamw(weight, first_moment, second, gradient, step_rate, decay):
    first_new = beta_one * first_moment + (1.0 - beta_one) * gradient
    second_new = beta_two * second + (1.0 - beta_two) * gradient * gradient
    first_hat = first_new / (1.0 - beta_one ** STEP)
    second_hat = second_new / (1.0 - beta_two ** STEP)
    weight_new = weight - step_rate * (first_hat / (jnp.sqrt(second_hat) + 1e-08) + decay * weight)
    return (first_new, second_new, weight_new)

def reference(tokens, cotangent, date_year, date_day, item_dates, slot_frame, frame_mask, qkv_weight, qkv_first, qkv_second, out_weight, out_first, out_second, up_weight, up_first, up_second, down_weight, down_first, down_second, vectors, vector_first, vector_second):
    params = (low(qkv_weight), low(out_weight), low(up_weight), low(down_weight), low(vectors))

    def group_step(totals, per_group):
        group_tokens, group_cot, years_group, days_group, dates_group, frames_group, mask_group = per_group
        pos_table = positions(years_group, days_group).reshape(KEYS, D)
        item_index, is_valid = slot_items(dates_group, frames_group, mask_group)
        item_ids = jnp.repeat(item_index, FRAME_TOK)
        key_valid = jnp.repeat(is_valid, FRAME_TOK)

        def apply_layer(inputs, qkv_w, out_w, up_w, down_w, vector_all):
            return forward(inputs, qkv_w, out_w, up_w, down_w, vector_all, pos_table, item_ids, key_valid)
        result, pullback = jax.vjp(apply_layer, group_tokens.reshape(KEYS, D).astype(jnp.float32), *params)
        gradients = pullback(group_cot.reshape(KEYS, D).astype(jnp.float32))
        totals = tuple((total + added for total, added in zip(totals, gradients[1:])))
        return (totals, (result.astype(jnp.bfloat16).reshape(SLOTS, FRAME_TOK, D), gradients[0].reshape(SLOTS, FRAME_TOK, D)))
    zero_sums = tuple((jnp.zeros(param.shape, jnp.float32) for param in params))
    totals, (block_out, token_grad) = lax.scan(group_step, zero_sums, (tokens, cotangent, date_year, date_day, item_dates, slot_frame, frame_mask))
    qkv_new = adamw(qkv_weight, qkv_first, qkv_second, totals[0], 0.05, 0.05)
    out_new = adamw(out_weight, out_first, out_second, totals[1], 0.5, 0.05)
    up_new = adamw(up_weight, up_first, up_second, totals[2], 0.05, 0.05)
    down_new = adamw(down_weight, down_first, down_second, totals[3], 0.03, 0.05)
    vector_new = adamw(vectors, vector_first, vector_second, totals[4], 0.3, 0.0)
    return (block_out, token_grad, qkv_new[0], qkv_new[1], qkv_new[2], out_new[0], out_new[1], out_new[2], up_new[0], up_new[1], up_new[2], down_new[0], down_new[1], down_new[2], vector_new[0], vector_new[1], vector_new[2])
```

```python
import jax
import jax.numpy as jnp
from jax import lax
from jax.experimental import pallas as pl
from jax.experimental.pallas import tpu as pltpu
from jax.sharding import PartitionSpec as P

D = 768
HEADS = 12
HEAD = 64
GRID = 14
STEP = 10
FRAME_TOK = 196


beta_one = 0.9
beta_two = 0.999


def sincos(values, length_out):
    half_width = length_out // 2
    frequency = 1.0 / 10000.0 ** (jnp.arange(half_width, dtype=jnp.float32) / half_width)
    angles = values[..., None] * frequency
    return jnp.concatenate([jnp.sin(angles), jnp.cos(angles)], axis=-1)


def positions(year_values, day_values):
    cell_index = jnp.arange(FRAME_TOK, dtype=jnp.int32)
    spatial = jnp.concatenate(
        [
            sincos((cell_index // GRID).astype(jnp.float32), 3 * D // 8),
            sincos((cell_index % GRID).astype(jnp.float32), 3 * D // 8),
        ],
        axis=-1,
    )
    temporal = jnp.concatenate(
        [
            sincos((year_values - 2000).astype(jnp.float32), D // 8),
            sincos(day_values.astype(jnp.float32), D // 8),
        ],
        axis=-1,
    )
    slot_count = year_values.shape[0]
    return jnp.concatenate(
        [
            jnp.broadcast_to(spatial[None], (slot_count, FRAME_TOK, 3 * D // 4)),
            jnp.broadcast_to(temporal[:, None], (slot_count, FRAME_TOK, D // 4)),
        ],
        axis=-1,
    )


def slot_items(dates_group, frames_group, mask_group):
    item_ends = jnp.cumsum(dates_group)
    starts = item_ends - dates_group
    item_index = jnp.sum((frames_group[:, None] >= item_ends[None, :]).astype(jnp.int32), axis=1)
    is_first = jnp.any(frames_group[:, None] == starts[None, :], axis=1)
    is_valid = jnp.logical_or(mask_group > 0, is_first)
    return (item_index, is_valid)


def layer_norm(values, gain_vec, shift_vec):
    average = jnp.mean(values, axis=-1, keepdims=True)
    centred = values - average
    spread = jnp.mean(centred * centred, axis=-1, keepdims=True)
    return centred * lax.rsqrt(spread + 1e-06) * gain_vec + shift_vec


def unpack(vector_all):
    pieces = [vector_all[index * D : (index + 1) * D] for index in range(8)]
    return tuple(pieces) + (vector_all[8 * D :],)


def exact_gelu(values):
    return jax.nn.gelu(values, approximate=False)


SP = 208
NK = 6
NEG = -1e30
NT = (((1,), (1,)), ((), ()))
NN = (((1,), (0,)), ((), ()))


def mm(a, b, dims=NN):
    return lax.dot_general(a, b, dims, preferred_element_type=jnp.float32)


def augmented_keys(parts, valid, bias_lane, mine):
    row = lax.broadcasted_iota(jnp.int32, (SP, 128), 0)
    lane = lax.broadcasted_iota(jnp.int32, (SP, 128), 1)
    blocks = []
    for part, live in zip(parts, valid):
        bias = jnp.where(row >= FRAME_TOK, NEG, live).astype(jnp.bfloat16)
        blocks.append(jnp.where(mine, part, jnp.where(lane == bias_lane, bias, jnp.zeros_like(part))))
    return jnp.concatenate(blocks, axis=0)


def attn_fwd_kernel(idx_ref, val_ref, q_ref, k_ref, v_ref, o_ref, lse_ref):
    lane = lax.broadcasted_iota(jnp.int32, (SP, 128), 1)

    def one(step, _):
        j, b = step // 6, step % 6
        cols = pl.ds(pl.multiple_of(b * 128, 128), 128)
        parts = [k_ref[idx_ref[j * NK + t], :, cols] for t in range(NK)]
        valid = [jnp.where(val_ref[j * NK + t] > 0, 0.0, NEG) for t in range(NK)]
        vg = jnp.concatenate([v_ref[idx_ref[j * NK + t], :, cols] for t in range(NK)], axis=0)
        q = q_ref[j, :, cols]
        scores = []
        for h in range(2):
            mine = (lane < 64) if h == 0 else (lane >= 64)
            spare = 64 if h == 0 else 0
            ka = augmented_keys(parts, valid, spare, mine)
            qa = jnp.where(mine, q, jnp.where(lane == spare, jnp.ones_like(q), jnp.zeros_like(q)))
            scores.append(mm(qa, ka, NT))
        peaks = [jnp.max(s, axis=1, keepdims=True) for s in scores]
        probs = [jnp.exp(s - m) for s, m in zip(scores, peaks)]
        sums = [jnp.sum(p, axis=1, keepdims=True) for p in probs]
        outs = [mm(p.astype(jnp.bfloat16), vg) / total for p, total in zip(probs, sums)]
        o_ref[j, :, cols] = jnp.where(lane < 64, outs[0], outs[1]).astype(jnp.bfloat16)
        logs = [m + jnp.log(total) for m, total in zip(peaks, sums)]
        lse_ref[j, b] = jnp.transpose(jnp.where(lane == 0, logs[0], logs[1]))[:8]
        return 0

    lax.fori_loop(0, 24, one, 0)


def attn_bwd_kernel(
    idx_ref, val_ref, q_ref, k_ref, v_ref, o_ref, do_ref, lse_ref, dq_ref, dk_ref, dv_ref
):
    lane = lax.broadcasted_iota(jnp.int32, (SP, 128), 1)
    row = lax.broadcasted_iota(jnp.int32, (SP, 128), 0)
    dk_ref[...] = jnp.zeros_like(dk_ref)
    dv_ref[...] = jnp.zeros_like(dv_ref)

    def one(step, _):
        j, b = step // 6, step % 6
        cols = pl.ds(pl.multiple_of(b * 128, 128), 128)
        parts = [k_ref[idx_ref[j * NK + t], :, cols] for t in range(NK)]
        valid = [jnp.where(val_ref[j * NK + t] > 0, 0.0, NEG) for t in range(NK)]
        kg = jnp.concatenate(parts, axis=0)
        vg = jnp.concatenate([v_ref[idx_ref[j * NK + t], :, cols] for t in range(NK)], axis=0)
        kg_t = jnp.transpose(kg)
        q, do, o = q_ref[j, :, cols], do_ref[j, :, cols], o_ref[j, :, cols]
        prod_t = jnp.transpose(do.astype(jnp.float32) * o.astype(jnp.float32))
        logs = lse_ref[j, b]
        dk = jnp.zeros((NK * SP, 128), jnp.float32)
        dv = jnp.zeros((NK * SP, 128), jnp.float32)
        dq_t = []
        for h in range(2):
            mine = (lane < 64) if h == 0 else (lane >= 64)
            spare = 64 if h == 0 else 0
            ka = augmented_keys(parts, valid, spare, mine)
            qm = jnp.where(mine, q, jnp.zeros_like(q))
            qa = jnp.where(lane == spare, jnp.ones_like(q), qm)
            dom = jnp.where(mine, do, jnp.zeros_like(do))
            centre = jnp.sum(prod_t[h * 64 : (h + 1) * 64], axis=0, keepdims=True)
            s_t = mm(ka, qa, NT)
            da_t = mm(vg, dom, NT)
            p = jnp.exp(s_t - logs[h : h + 1])
            ds = (p * (da_t - centre)).astype(jnp.bfloat16)
            dv = dv + mm(p.astype(jnp.bfloat16), dom)
            dk = dk + mm(ds, qm)
            dq_t.append(mm(kg_t, ds))
        dq = jnp.transpose(jnp.concatenate([dq_t[0][:64], dq_t[1][64:]], axis=0))
        dq_ref[j, :, cols] = (dq * 0.125).astype(jnp.bfloat16)
        for t in range(NK):
            slot = idx_ref[j * NK + t]
            keep = jnp.logical_and(row < FRAME_TOK, val_ref[j * NK + t] > 0)
            dk_ref[slot, :, cols] += jnp.where(keep, dk[t * SP : (t + 1) * SP], 0.0)
            dv_ref[slot, :, cols] += jnp.where(keep, dv[t * SP : (t + 1) * SP], 0.0)
        return 0

    lax.fori_loop(0, 24, one, 0)


VM = pl.BlockSpec(memory_space=pltpu.VMEM)
SM = pl.BlockSpec(memory_space=pltpu.SMEM)


def attn_fwd(idx, val, q, k, v):
    return pl.pallas_call(
        attn_fwd_kernel,
        out_shape=(
            jax.ShapeDtypeStruct((4, SP, D), jnp.bfloat16),
            jax.ShapeDtypeStruct((4, 6, 8, SP), jnp.float32),
        ),
        in_specs=[SM, SM, VM, VM, VM],
        out_specs=(VM, VM),
        compiler_params=pltpu.CompilerParams(vmem_limit_bytes=60 * 2**20),
        cost_estimate=pl.CostEstimate(
            flops=2 * 2 * 24 * 12 * SP * SP * 256,
            bytes_accessed=14 * 2**20,
            transcendentals=24 * 12 * SP * SP,
        ),
        name="attn_fwd",
    )(idx, val, q, k, v)


def attn_bwd(idx, val, q, k, v, o, do, lse):
    return pl.pallas_call(
        attn_bwd_kernel,
        out_shape=(
            jax.ShapeDtypeStruct((4, SP, D), jnp.bfloat16),
            jax.ShapeDtypeStruct((16, SP, D), jnp.float32),
            jax.ShapeDtypeStruct((16, SP, D), jnp.float32),
        ),
        in_specs=[SM, SM] + [VM] * 6,
        out_specs=(VM, VM, VM),
        compiler_params=pltpu.CompilerParams(vmem_limit_bytes=62 * 2**20),
        cost_estimate=pl.CostEstimate(
            flops=2 * 5 * 24 * 12 * SP * SP * 256,
            bytes_accessed=40 * 2**20,
            transcendentals=24 * 12 * SP * SP,
        ),
        name="attn_bwd",
    )(idx, val, q, k, v, o, do, lse)


def key_tables(item_index, is_valid, q_items):
    match = (q_items[:, None] == item_index[None, :]) & is_valid[None, :]
    rank = jnp.cumsum(match.astype(jnp.int32), axis=1) - 1
    count = jnp.sum(match.astype(jnp.int32), axis=1)
    place = jnp.arange(NK, dtype=jnp.int32)
    hit = match[:, None, :] & (rank[:, None, :] == place[None, :, None])
    slots = jnp.arange(item_index.shape[0], dtype=jnp.int32)
    idx = jnp.sum(jnp.where(hit, slots[None, None, :], 0), axis=2)
    val = (place[None, :] < count[:, None]).astype(jnp.int32)
    return idx.reshape(-1), val.reshape(-1)


def adamw(weight, first_moment, second, gradient, step_rate, decay):
    first_new = beta_one * first_moment + (1.0 - beta_one) * gradient
    second_new = beta_two * second + (1.0 - beta_two) * gradient * gradient
    first_hat = first_new / (1.0 - beta_one**STEP)
    second_hat = second_new / (1.0 - beta_two**STEP)
    weight_new = weight - step_rate * (first_hat / (jnp.sqrt(second_hat) + 1e-08) + decay * weight)
    return (first_new, second_new, weight_new)


def on_device(
    tokens,
    cotangent,
    date_year,
    date_day,
    item_dates,
    slot_frame,
    frame_mask,
    qkv_weight,
    qkv_first,
    qkv_second,
    out_weight,
    out_first,
    out_second,
    up_weight,
    up_first,
    up_second,
    down_weight,
    down_first,
    down_second,
    vectors,
    vector_first,
    vector_second,
):
    frame_rank = lax.axis_index("frames")
    bf, f32 = jnp.bfloat16, jnp.float32
    gather = lambda w: lax.all_gather(w.astype(bf), "frames", axis=0, tiled=True)
    qkv_full, vector_full, out_full, up_full, down_full = (
        gather(qkv_weight), gather(vectors), gather(out_weight), gather(up_weight), gather(down_weight))
    (gain_one, shift_one, bias_query, bias_value, bias_output, gain_two, shift_two, bias_down, bias_up,
    ) = unpack(vector_full.astype(f32))
    pad = lambda a: jnp.pad(a[0], ((0, 0), (0, SP - FRAME_TOK), (0, 0))).reshape(4 * SP, D)
    pos = jnp.pad(positions(date_year[0], date_day[0]), ((0, 0), (0, SP - FRAME_TOK), (0, 0))).reshape(4 * SP, D)
    residual_in = pad(tokens).astype(f32) + pos
    item_index, is_valid = slot_items(item_dates[0], slot_frame[0], frame_mask[0])
    own_items = lax.dynamic_slice_in_dim(item_index, frame_rank * 4, 4)
    idx, val = key_tables(item_index, is_valid, own_items)
    normed, norm_one_back = jax.vjp(layer_norm, residual_in, gain_one, shift_one)
    normed_low = normed.astype(bf)
    normed_all = lax.all_gather(normed_low, "frames", axis=0, tiled=True)
    query_low = (mm(normed_low, qkv_full[:, :D]) + bias_query).astype(bf)
    key_value = mm(normed_all, qkv_full[:, D:]) + jnp.concatenate([jnp.zeros_like(bias_value), bias_value])
    key_all = key_value[:, :D].astype(bf)
    value_all = key_value[:, D:].astype(bf)
    q3 = (query_low * jnp.asarray(0.125, bf)).reshape(4, SP, D)
    k3 = key_all.reshape(16, SP, D)
    v3 = value_all.reshape(16, SP, D)
    o3, lse = attn_fwd(idx, val, q3, k3, v3)
    attended_low = o3.reshape(4 * SP, D)
    branch = mm(attended_low, out_full) + bias_output
    hidden = residual_in + branch
    normed_two, norm_two_back = jax.vjp(layer_norm, hidden, gain_two, shift_two)
    normed_two_low = normed_two.astype(bf)
    inner = mm(normed_two_low, up_full) + bias_up
    active, gelu_back = jax.vjp(exact_gelu, inner)
    active_low = active.astype(bf)
    mlp_out = mm(active_low, down_full) + bias_down
    block_out = (hidden + mlp_out).astype(bf)
    grad_out_low = pad(cotangent)
    grad_out = grad_out_low.astype(f32)
    TN = (((0,), (0,)), ((), ()))
    down_grad = mm(active_low, grad_out_low, TN)
    bias_down_grad = jnp.sum(grad_out, axis=0)
    (inner_grad,) = gelu_back(mm(grad_out_low, down_full, NT))
    inner_grad_low = inner_grad.astype(bf)
    up_grad = mm(normed_two_low, inner_grad_low, TN)
    bias_up_grad = jnp.sum(inner_grad_low.astype(f32), axis=0)
    hidden_from_norm, gain_two_grad, shift_two_grad = norm_two_back(mm(inner_grad_low, up_full, NT))
    hidden_grad = grad_out + hidden_from_norm
    branch_grad_low = hidden_grad.astype(bf)
    out_grad = mm(attended_low, branch_grad_low, TN)
    bias_output_grad = jnp.sum(branch_grad_low.astype(f32), axis=0)
    attended_grad_low = mm(branch_grad_low, out_full, NT).astype(bf)
    dq3, dk3, dv3 = attn_bwd(idx, val, q3, k3, v3, o3, attended_grad_low.reshape(4, SP, D), lse)
    dq = dq3.reshape(4 * SP, D)
    dk = dk3.reshape(16 * SP, D).astype(bf)
    dv = dv3.reshape(16 * SP, D).astype(bf)
    bias_query_grad = jnp.sum(dq.astype(f32), axis=0)
    bias_value_grad = jnp.sum(dv3, axis=(0, 1))
    qkv_grad = jnp.concatenate([mm(normed_low, dq, TN), mm(normed_all, dk, TN), mm(normed_all, dv, TN)], axis=1)
    part = (mm(dk, qkv_full[:, D : 2 * D], NT) + mm(dv, qkv_full[:, 2 * D :], NT)).astype(bf)
    normed_grad = lax.psum_scatter(part, "frames", scatter_dimension=0, tiled=True).astype(f32)
    normed_grad = normed_grad + mm(dq, qkv_full[:, :D], NT)
    input_from_norm, gain_one_grad, shift_one_grad = norm_one_back(normed_grad)
    token_grad = hidden_grad + input_from_norm
    vector_grad = jnp.concatenate([gain_one_grad, shift_one_grad, bias_query_grad, bias_value_grad,
        bias_output_grad, gain_two_grad, shift_two_grad, bias_down_grad, bias_up_grad])
    scatter = lambda g: lax.psum_scatter(g.astype(bf), "frames", scatter_dimension=0, tiled=True)
    vec_sum = lax.psum(lax.psum_scatter(vector_grad, "frames", scatter_dimension=0, tiled=True), "items")
    sums = [lax.psum(scatter(g), "items").astype(f32) for g in (down_grad, up_grad, out_grad, qkv_grad)]
    qkv_new = adamw(qkv_weight, qkv_first, qkv_second, sums[3], 0.05, 0.05)
    out_new = adamw(out_weight, out_first, out_second, sums[2], 0.5, 0.05)
    up_new = adamw(up_weight, up_first, up_second, sums[1], 0.05, 0.05)
    down_new = adamw(down_weight, down_first, down_second, sums[0], 0.03, 0.05)
    vector_new = adamw(vectors, vector_first, vector_second, vec_sum, 0.3, 0.0)
    cut = lambda a: a.reshape(1, 4, SP, D)[:, :, :FRAME_TOK]
    return (cut(block_out), cut(token_grad)) + qkv_new + out_new + up_new + down_new + vector_new


def solution(mesh):
    placed = (
        P("items", "frames", None, None),
        P("items", "frames", None, None),
        P("items", "frames"),
        P("items", "frames"),
        P("items", None),
        P("items", None),
        P("items", None),
        P("frames", None),
        P("frames", None),
        P("frames", None),
        P("frames", None),
        P("frames", None),
        P("frames", None),
        P("frames", None),
        P("frames", None),
        P("frames", None),
        P("frames", None),
        P("frames", None),
        P("frames", None),
        P("frames"),
        P("frames"),
        P("frames"),
    )
    return jax.shard_map(
        on_device,
        mesh=mesh,
        in_specs=placed,
        out_specs=(
            P("items", "frames", None, None),
            P("items", "frames", None, None),
            P("frames", None),
            P("frames", None),
            P("frames", None),
            P("frames", None),
            P("frames", None),
            P("frames", None),
            P("frames", None),
            P("frames", None),
            P("frames", None),
            P("frames", None),
            P("frames", None),
            P("frames", None),
            P("frames"),
            P("frames"),
            P("frames"),
        ),
        check_vma=False,
    )
```

```python
import functools

import jax
import jax.numpy as jnp
import numpy as np
from jax import lax
from jax.experimental import pallas as pl
from jax.experimental.pallas import tpu as pltpu
from jax.sharding import PartitionSpec as P

D = 768
HEADS = 12
HEAD = 64
GRID = 14
STEP = 10
FRAME_TOK = 196


beta_one = 0.9
beta_two = 0.999


def sincos(values, length_out):
    half_width = length_out // 2
    frequency = 1.0 / 10000.0 ** (jnp.arange(half_width, dtype=jnp.float32) / half_width)
    angles = values[..., None] * frequency
    return jnp.concatenate([jnp.sin(angles), jnp.cos(angles)], axis=-1)


def temporal_rows(year_values, day_values):
    dates = jnp.concatenate(
        [
            sincos((year_values - 2000).astype(jnp.float32), D // 8),
            sincos(day_values.astype(jnp.float32), D // 8),
        ],
        axis=-1,
    )
    return jnp.pad(dates, ((0, 0), (3 * D // 4, 0)))


def spatial_rows():
    half = 3 * D // 16
    frequency = (1.0 / np.float32(10000.0) ** (np.arange(half, dtype=np.float32) / np.float32(half))).astype(np.float32)
    cells = np.arange(FRAME_TOK)
    parts = []
    for values in (cells // GRID, cells % GRID):
        angles = values.astype(np.float32)[:, None] * frequency
        parts += [np.sin(angles), np.cos(angles)]
    rows = np.zeros((SP, D), np.float32)
    rows[:FRAME_TOK, : 3 * D // 4] = np.concatenate(parts, axis=-1)
    return rows


def slot_items(dates_group, frames_group, mask_group):
    item_ends = jnp.cumsum(dates_group)
    starts = item_ends - dates_group
    item_index = jnp.sum((frames_group[:, None] >= item_ends[None, :]).astype(jnp.int32), axis=1)
    is_first = jnp.any(frames_group[:, None] == starts[None, :], axis=1)
    is_valid = jnp.logical_or(mask_group > 0, is_first)
    return (item_index, is_valid)


def layer_norm(values, gain_vec, shift_vec):
    average = jnp.mean(values, axis=-1, keepdims=True)
    centred = values - average
    spread = jnp.mean(centred * centred, axis=-1, keepdims=True)
    return centred * lax.rsqrt(spread + 1e-06) * gain_vec + shift_vec


def unpack(vector_all):
    pieces = [vector_all[index * D : (index + 1) * D] for index in range(8)]
    return tuple(pieces) + (vector_all[8 * D :],)


def exact_gelu(values):
    return jax.nn.gelu(values, approximate=False)


SP = 208
NK = 6
NEG = -1e30
NT = (((1,), (1,)), ((), ()))
NN = (((1,), (0,)), ((), ()))


def mm(a, b, dims=NN):
    return lax.dot_general(a, b, dims, preferred_element_type=jnp.float32)


def augmented_keys(parts, valid, bias_lane, mine):
    row = lax.broadcasted_iota(jnp.int32, (SP, 128), 0)
    lane = lax.broadcasted_iota(jnp.int32, (SP, 128), 1)
    blocks = []
    for part, live in zip(parts, valid):
        bias = jnp.where(row >= FRAME_TOK, NEG, live).astype(jnp.bfloat16)
        blocks.append(jnp.where(mine, part, jnp.where(lane == bias_lane, bias, jnp.zeros_like(part))))
    return jnp.concatenate(blocks, axis=0)


def attn_fwd_kernel(idx_ref, val_ref, q_ref, k_ref, v_ref, o_ref, lse_ref):
    lane = lax.broadcasted_iota(jnp.int32, (SP, 128), 1)

    def one(step, _):
        j, b = step // 6, step % 6
        cols = pl.ds(pl.multiple_of(b * 128, 128), 128)
        parts = [k_ref[idx_ref[j * NK + t], :, cols] for t in range(NK)]
        valid = [jnp.where(val_ref[j * NK + t] > 0, 0.0, NEG) for t in range(NK)]
        vg = jnp.concatenate([v_ref[idx_ref[j * NK + t], :, cols] for t in range(NK)], axis=0)
        q = q_ref[j, :, cols]
        scores = []
        for h in range(2):
            mine = (lane < 64) if h == 0 else (lane >= 64)
            spare = 64 if h == 0 else 0
            ka = augmented_keys(parts, valid, spare, mine)
            qa = jnp.where(mine, q, jnp.where(lane == spare, jnp.ones_like(q), jnp.zeros_like(q)))
            scores.append(mm(qa, ka, NT))
        peaks = [jnp.max(s, axis=1, keepdims=True) for s in scores]
        probs = [jnp.exp(s - m) for s, m in zip(scores, peaks)]
        sums = [jnp.sum(p, axis=1, keepdims=True) for p in probs]
        outs = [mm(p.astype(jnp.bfloat16), vg) / total for p, total in zip(probs, sums)]
        o_ref[j, :, cols] = jnp.where(lane < 64, outs[0], outs[1]).astype(jnp.bfloat16)
        logs = [m + jnp.log(total) for m, total in zip(peaks, sums)]
        lse_ref[j, b] = jnp.transpose(jnp.where(lane == 0, logs[0], logs[1]))[:8]
        return 0

    lax.fori_loop(0, 24, one, 0)


def attn_bwd_kernel(
    idx_ref, val_ref, q_ref, k_ref, v_ref, o_ref, do_ref, lse_ref, dq_ref, dk_out, dv_out, dk_ref, dv_ref
):
    lane = lax.broadcasted_iota(jnp.int32, (SP, 128), 1)
    row = lax.broadcasted_iota(jnp.int32, (SP, 128), 0)
    dk_ref[...] = jnp.zeros_like(dk_ref)
    dv_ref[...] = jnp.zeros_like(dv_ref)

    def one(step, _):
        j, b = step // 6, step % 6
        cols = pl.ds(pl.multiple_of(b * 128, 128), 128)
        parts = [k_ref[idx_ref[j * NK + t], :, cols] for t in range(NK)]
        valid = [jnp.where(val_ref[j * NK + t] > 0, 0.0, NEG) for t in range(NK)]
        kg = jnp.concatenate(parts, axis=0)
        vg = jnp.concatenate([v_ref[idx_ref[j * NK + t], :, cols] for t in range(NK)], axis=0)
        kg_t = jnp.transpose(kg)
        q, do, o = q_ref[j, :, cols], do_ref[j, :, cols], o_ref[j, :, cols]
        prod_t = jnp.transpose(do.astype(jnp.float32) * o.astype(jnp.float32))
        logs = lse_ref[j, b]
        dk = jnp.zeros((NK * SP, 128), jnp.float32)
        dv = jnp.zeros((NK * SP, 128), jnp.float32)
        dq_t = []
        for h in range(2):
            mine = (lane < 64) if h == 0 else (lane >= 64)
            spare = 64 if h == 0 else 0
            ka = augmented_keys(parts, valid, spare, mine)
            qm = jnp.where(mine, q, jnp.zeros_like(q))
            qa = jnp.where(lane == spare, jnp.ones_like(q), qm)
            dom = jnp.where(mine, do, jnp.zeros_like(do))
            centre = jnp.sum(prod_t[h * 64 : (h + 1) * 64], axis=0, keepdims=True)
            s_t = mm(ka, qa, NT)
            da_t = mm(vg, dom, NT)
            p = jnp.exp(s_t - logs[h : h + 1])
            ds = (p * (da_t - centre)).astype(jnp.bfloat16)
            dv = dv + mm(p.astype(jnp.bfloat16), dom)
            dk = dk + mm(ds, qm)
            dq_t.append(mm(kg_t, ds))
        dq = jnp.transpose(jnp.concatenate([dq_t[0][:64], dq_t[1][64:]], axis=0))
        dq_ref[j, :, cols] = (dq * 0.125).astype(jnp.bfloat16)
        for t in range(NK):
            slot = idx_ref[j * NK + t]
            keep = jnp.logical_and(row < FRAME_TOK, val_ref[j * NK + t] > 0)
            dk_ref[slot, :, cols] += jnp.where(keep, dk[t * SP : (t + 1) * SP], 0.0)
            dv_ref[slot, :, cols] += jnp.where(keep, dv[t * SP : (t + 1) * SP], 0.0)
        return 0

    lax.fori_loop(0, 24, one, 0)

    def narrow(slot, _):
        dk_out[slot] = dk_ref[slot].astype(jnp.bfloat16)
        dv_out[slot] = dv_ref[slot].astype(jnp.bfloat16)
        return 0

    lax.fori_loop(0, 16, narrow, 0)


VM = pl.BlockSpec(memory_space=pltpu.VMEM)
SM = pl.BlockSpec(memory_space=pltpu.SMEM)


def attn_fwd(idx, val, q, k, v):
    return pl.pallas_call(
        attn_fwd_kernel,
        out_shape=(
            jax.ShapeDtypeStruct((4, SP, D), jnp.bfloat16),
            jax.ShapeDtypeStruct((4, 6, 8, SP), jnp.float32),
        ),
        in_specs=[SM, SM, VM, VM, VM],
        out_specs=(VM, VM),
        compiler_params=pltpu.CompilerParams(vmem_limit_bytes=60 * 2**20),
        cost_estimate=pl.CostEstimate(
            flops=2 * 2 * 24 * 12 * SP * SP * 256,
            bytes_accessed=14 * 2**20,
            transcendentals=24 * 12 * SP * SP,
        ),
        name="attn_fwd",
    )(idx, val, q, k, v)


def attn_bwd(idx, val, q, k, v, o, do, lse):
    return pl.pallas_call(
        attn_bwd_kernel,
        out_shape=(
            jax.ShapeDtypeStruct((4, SP, D), jnp.bfloat16),
            jax.ShapeDtypeStruct((16, SP, D), jnp.bfloat16),
            jax.ShapeDtypeStruct((16, SP, D), jnp.bfloat16),
        ),
        in_specs=[SM, SM] + [VM] * 6,
        out_specs=(VM, VM, VM),
        scratch_shapes=[pltpu.VMEM((16, SP, D), jnp.float32)] * 2,
        compiler_params=pltpu.CompilerParams(vmem_limit_bytes=62 * 2**20),
        cost_estimate=pl.CostEstimate(
            flops=2 * 5 * 24 * 12 * SP * SP * 256,
            bytes_accessed=40 * 2**20,
            transcendentals=24 * 12 * SP * SP,
        ),
        name="attn_bwd",
    )(idx, val, q, k, v, o, do, lse)


def key_tables(item_index, is_valid, q_items):
    match = (q_items[:, None] == item_index[None, :]) & is_valid[None, :]
    rank = jnp.cumsum(match.astype(jnp.int32), axis=1) - 1
    count = jnp.sum(match.astype(jnp.int32), axis=1)
    place = jnp.arange(NK, dtype=jnp.int32)
    hit = match[:, None, :] & (rank[:, None, :] == place[None, :, None])
    slots = jnp.arange(item_index.shape[0], dtype=jnp.int32)
    idx = jnp.sum(jnp.where(hit, slots[None, None, :], 0), axis=2)
    val = (place[None, :] < count[:, None]).astype(jnp.int32)
    return idx.reshape(-1), val.reshape(-1)


def adamw(weight, first_moment, second, gradient, step_rate, decay):
    first_new = beta_one * first_moment + (1.0 - beta_one) * gradient
    second_new = beta_two * second + (1.0 - beta_two) * gradient * gradient
    first_hat = first_new / (1.0 - beta_one**STEP)
    second_hat = second_new / (1.0 - beta_two**STEP)
    weight_new = weight - step_rate * (first_hat / (jnp.sqrt(second_hat) + 1e-08) + decay * weight)
    return (first_new, second_new, weight_new)


VEC_ROWS = 16
MESH = pl.DeviceIdType.MESH
Z, X, Y, DA, DB, C0, C1, C2, C3 = range(9)


def norm_rows(x):
    mean = jnp.mean(x, axis=-1, keepdims=True)
    centred = x - mean
    spread = jnp.mean(centred * centred, axis=-1, keepdims=True)
    return centred * lax.rsqrt(spread + 1e-06)


def place():
    i, f = lax.axis_index("items"), lax.axis_index("frames")
    core = i % 2
    upper = f // 2
    stay = core == upper
    mine = jnp.where(stay, f, 3 - f)
    other = f + 1 - 2 * (f % 2)
    far = jnp.where(stay, other, 3 - other)
    flip = lambda v, bit: v + bit - 2 * bit * ((v // bit) % 2)
    return i, f, core, stay, mine, other, far, flip


def halves(core, a, b):
    return jnp.where(core == 0, a, b)


def front_kernel(
    tok, tmp, vec, spatial, wq, wo, wu, wd,
    q_out, k_out, v_out, n_out, x_out, vec_out, tmp_out, wq_out, wo_out, wu_out, wd_out,
    t_s, tmp_s, vec_s, n_s, q_s, k_s, v_s, x_s, wq_s,
    rq32, ro32, ru32, rd32, rq, ro, ru, rd, sq32, so32, su32, sd32, sq, so, su, sd,
    t_send, t_recv, m_send, m_recv, v_send, v_recv, w_send, w_recv, reg_sem, own_sem, put_sem, loc_sem, out_sem,
):
    bf, f32 = jnp.bfloat16, jnp.float32
    i, f, core, stay, mine, other, far, flip = place()
    c_dev = (flip(i, 1), f)
    x_dev = (halves(core, flip(i, 2), flip(i, 4)), f)
    y_dev = (halves(core, flip(i, 4), flip(i, 2)), f)
    e_dev = (i, other)
    m_dev = (flip(i, 1), 3 - f)
    xy = (i // 2) % 4
    xy_x, xy_y = halves(core, flip(xy, 1), flip(xy, 2)), halves(core, flip(xy, 2), flip(xy, 1))
    diag = flip(flip(xy, 1), 2)
    zs = [flip(f, 1), flip(f, 2), flip(flip(f, 1), 2)]

    barrier = pltpu.get_barrier_semaphore()
    partners = [c_dev, x_dev, y_dev, m_dev] + [(i, z) for z in zs]
    for dev in partners:
        pl.semaphore_signal(barrier, inc=1, device_id=dev, device_id_type=MESH)

    weights = [(wq, wq_out, rq32, rq, sq32, sq), (wo, wo_out, ro32, ro, so32, so),
               (wu, wu_out, ru32, ru, su32, su), (wd, wd_out, rd32, rd, sd32, sd)]

    def region_load(w):
        src, _, r32, _, _, _ = weights[w]
        rows, cols = r32.shape
        return pltpu.make_async_copy(
            src.at[pl.ds(pl.multiple_of(xy * rows, rows), rows), pl.ds(pl.multiple_of(core * cols, 128), cols)],
            r32, reg_sem.at[w])

    def own_load(w):
        return pltpu.make_async_copy(weights[w][0], weights[w][4], own_sem.at[w])

    def own_put(w):
        out, small = weights[w][1], weights[w][5]
        rows = small.shape[0]
        return pltpu.make_async_copy(small, out.at[pl.ds(pl.multiple_of(f * rows, rows), rows), :], put_sem.at[w])

    for w in range(4):
        region_load(w).start()
    for w in range(4):
        own_load(w).start()
    tok_load = pltpu.make_async_copy(tok, t_s.at[mine], loc_sem.at[0])
    tmp_load = pltpu.make_async_copy(tmp, tmp_s.at[mine], loc_sem.at[1])
    vec_load = pltpu.make_async_copy(vec, vec_s.at[f], loc_sem.at[2])

    @pl.when(stay)
    def _():
        tok_load.start()
        tmp_load.start()

    vec_load.start()
    pl.semaphore_wait(barrier, len(partners))

    def remote(src, dst, ssem, rsem, dev):
        return pltpu.make_async_remote_copy(
            src_ref=src, dst_ref=dst, send_sem=ssem, recv_sem=rsem, device_id=dev, device_id_type=MESH)

    def tok_copy(kind, j):
        if kind == 0:
            return remote(tok.at[j], t_s.at[f, j], t_send.at[0, j], t_recv.at[0, j], m_dev)
        if kind == 3:
            return remote(t_s.at[far, j], t_s.at[far, j], t_send.at[3, j], t_recv.at[3, j], c_dev)
        return remote(t_s.at[mine, j], t_s.at[mine, j], t_send.at[kind, j], t_recv.at[kind, j],
                      c_dev if kind == 1 else e_dev)

    def tok_arrival(kind, j):
        shard = (mine, 3 - mine, far, 3 - far)[kind]
        return remote(t_s.at[shard, j], t_s.at[shard, j], t_send.at[kind, j], t_recv.at[kind, j], c_dev)

    def tmp_copy(kind):
        if kind == 0:
            return remote(tmp, tmp_s.at[f], m_send.at[0], m_recv.at[0], m_dev)
        if kind == 3:
            return remote(tmp_s.at[far], tmp_s.at[far], m_send.at[3], m_recv.at[3], c_dev)
        return remote(tmp_s.at[mine], tmp_s.at[mine], m_send.at[kind], m_recv.at[kind], c_dev if kind == 1 else e_dev)

    def tmp_arrival(kind):
        shard = (mine, 3 - mine, far, 3 - far)[kind]
        return remote(tmp_s.at[shard], tmp_s.at[shard], m_send.at[kind], m_recv.at[kind], c_dev)

    def part(w, z, at, half, piece):
        out, r = weights[w][1], weights[w][3]
        rows, cols = r.shape
        unit = rows // 3
        start = z * 4 * rows + at * rows
        if piece == 0:
            return out.at[pl.ds(pl.multiple_of(start, 16), rows), pl.ds(pl.multiple_of(half * cols, 128), cols)]
        if piece == 1:
            return out.at[pl.ds(pl.multiple_of(start, 16), 2 * unit), pl.ds(pl.multiple_of(half * cols, 128), cols)]
        return out.at[pl.ds(pl.multiple_of(start + 2 * unit, 16), unit), pl.ds(pl.multiple_of(half * cols, 128), cols)]

    def w_copy(w, d, kind):
        sems = (w_send.at[w, d, kind], w_recv.at[w, d, kind])
        z = zs[d]
        if kind == Z:
            return remote(weights[w][3], part(w, f, xy, core, 0), *sems, (i, z))
        at = {X: xy, Y: xy, DA: xy_x, DB: xy_y, C0: xy, C1: xy_x, C2: xy_y, C3: diag}[kind]
        piece = {DA: 1, DB: 2}.get(kind, 0)
        dev = {X: x_dev, Y: y_dev, DA: y_dev, DB: x_dev}.get(kind, c_dev)
        ref = part(w, z, at, core, piece)
        return remote(ref, ref, *sems, dev)

    def w_arrival(w, d, kind):
        sems = (w_send.at[w, d, kind], w_recv.at[w, d, kind])
        z = zs[d]
        at = {Z: xy, X: xy_x, Y: xy_y, DA: diag, DB: diag, C0: xy, C1: xy_y, C2: xy_x, C3: diag}[kind]
        piece = {DA: 1, DB: 2}.get(kind, 0)
        half = (1 - core) if kind >= C0 else core
        ref = part(w, z, at, half, piece)
        return remote(ref, ref, *sems, c_dev)

    def w_send_region(w):
        region_load(w).wait()
        weights[w][3][...] = weights[w][2][...].astype(bf)
        for d in range(3):
            w_copy(w, d, Z).start()

    def w_stage_one(w):
        for d in range(3):
            w_arrival(w, d, Z).wait_recv()
            for kind in (X, Y, C0):
                w_copy(w, d, kind).start()

    def w_stage_two(w):
        for d in range(3):
            w_arrival(w, d, X).wait_recv()
            w_copy(w, d, DA).start()
            w_copy(w, d, C1).start()
            w_arrival(w, d, Y).wait_recv()
            w_copy(w, d, DB).start()
            w_copy(w, d, C2).start()

    def w_stage_three(w):
        for d in range(3):
            w_arrival(w, d, DA).wait_recv()
            w_arrival(w, d, DB).wait_recv()
            w_copy(w, d, C3).start()

    def w_stage_four(w):
        for d in range(3):
            for kind in (C0, C1, C2, C3):
                w_arrival(w, d, kind).wait_recv()

    def w_own(w):
        own_load(w).wait()
        weights[w][5][...] = weights[w][4][...].astype(bf)
        own_put(w).start()

    w_send_region(0)

    @pl.when(jnp.logical_not(stay))
    def _():
        tmp_copy(0).start()
        for j in range(4):
            tok_copy(0, j).start()

    @pl.when(stay)
    def _():
        tok_load.wait()
        tmp_load.wait()
        for kind in (2, 1):
            tmp_copy(kind).start()
            for j in range(4):
                tok_copy(kind, j).start()

    vec_load.wait()
    def v_copy(d):
        return remote(vec_s.at[f], vec_s.at[f], v_send.at[d], v_recv.at[d], (i, zs[d]))
    def v_arrival(d):
        return remote(vec_s.at[zs[d]], vec_s.at[zs[d]], v_send.at[d], v_recv.at[d], (i, zs[d]))
    for d in range(3):
        v_copy(d).start()
    for w in range(4):
        w_own(w)
    w_stage_one(0)
    w_stage_two(0)
    w_stage_three(0)

    @pl.when(jnp.logical_not(stay))
    def _():
        tmp_arrival(0).wait_recv()
        for kind in (2, 1):
            tmp_copy(kind).start()
        for j in range(4):
            tok_arrival(0, j).wait_recv()
            for kind in (2, 1):
                tok_copy(kind, j).start()

    for w in (1, 2, 3):
        w_send_region(w)
    w_stage_four(0)
    own_put(0).wait()
    wq_load = pltpu.make_async_copy(wq_out, wq_s, loc_sem.at[3])
    wq_load.start()
    for d in range(3):
        v_arrival(d).wait_recv()
    vec_put = pltpu.make_async_copy(vec_s, vec_out, loc_sem.at[4])
    vec_put.start()
    tmp_put = pltpu.make_async_copy(tmp_s.at[mine], tmp_out, loc_sem.at[5])
    tmp_put.start()
    gain = vec_s[0, 0:1, :].astype(f32)
    shift = vec_s[0, 1:2, :].astype(f32)
    bias_q = vec_s[0, 2:3, :].astype(f32)
    bias_v = vec_s[1, 0:1, :].astype(f32)
    wq_load.wait()

    def normalise(shard, keep_x):
        def slot(j, _):
            x = t_s[shard, j].astype(f32) + (spatial[...] + tmp_s[shard, pl.ds(j, 1), :])
            if keep_x:
                x_s[j] = x
            n_s[shard, j] = (norm_rows(x) * gain + shift).astype(bf)
            return 0
        lax.fori_loop(0, 4, slot, 0)

    def project(shard):
        rows = n_s[shard].reshape(4 * SP, D)
        def keys(t, _):
            cols = pl.ds(pl.multiple_of(t * 256, 256), 256)
            k_s[shard, :, :, cols] = mm(rows, wq_s[:, pl.ds(pl.multiple_of(D + t * 256, 256), 256)]).astype(bf).reshape(4, SP, 256)
            v_s[shard, :, :, cols] = (mm(rows, wq_s[:, pl.ds(pl.multiple_of(2 * D + t * 256, 256), 256)])
                                      + vec_s[1, 0:1, cols].astype(f32)).astype(bf).reshape(4, SP, 256)
            return 0
        lax.fori_loop(0, 3, keys, 0)

    def project_q(shard):
        rows = n_s[shard].reshape(4 * SP, D)
        def queries(t, _):
            cols = pl.ds(pl.multiple_of(t * 256, 256), 256)
            q = (mm(rows, wq_s[:, cols]) + vec_s[0, 2:3, cols].astype(f32)).astype(bf)
            q_s[:, :, cols] = (q.astype(f32) * 0.125).astype(bf).reshape(4, SP, 256)
            return 0
        lax.fori_loop(0, 3, queries, 0)

    outs = []
    def put(src, dst):
        copy = pltpu.make_async_copy(src, dst, out_sem.at[len(outs)])
        copy.start()
        outs.append(copy)

    def put_shard(shard):
        put(n_s.at[shard], n_out.at[shard])
        put(k_s.at[shard], k_out.at[shard])
        put(v_s.at[shard], v_out.at[shard])

    normalise(mine, True)
    put(x_s, x_out)
    project_q(mine)
    put(q_s, q_out)
    project(mine)
    put_shard(mine)
    w_stage_one(1)
    tmp_arrival(1).wait_recv()
    for j in range(4):
        tok_arrival(1, j).wait_recv()
    normalise(3 - mine, False)
    project(3 - mine)
    put_shard(3 - mine)
    tmp_arrival(2).wait_recv()
    tmp_copy(3).start()
    for j in range(4):
        tok_arrival(2, j).wait_recv()
        tok_copy(3, j).start()
    w_stage_two(1)
    w_stage_one(2)
    normalise(far, False)
    project(far)
    put_shard(far)
    w_stage_one(3)
    tmp_arrival(3).wait_recv()
    for j in range(4):
        tok_arrival(3, j).wait_recv()
    normalise(3 - far, False)
    project(3 - far)
    put_shard(3 - far)
    w_stage_two(2)
    w_stage_two(3)
    for w in (1, 2, 3):
        w_stage_three(w)
    for w in (1, 2, 3):
        w_stage_four(w)
        own_put(w).wait()

    @pl.when(jnp.logical_not(stay))
    def _():
        tmp_copy(0).wait_send()
        for j in range(4):
            tok_copy(0, j).wait_send()

    for kind in (1, 2, 3):
        tmp_copy(kind).wait_send()
        for j in range(4):
            tok_copy(kind, j).wait_send()
    for d in range(3):
        v_copy(d).wait_send()
        for w in range(4):
            for kind in range(9):
                w_copy(w, d, kind).wait_send()
    vec_put.wait()
    tmp_put.wait()
    for copy in outs:
        copy.wait()


def front(tok, tmp, vec, spatial, wq, wo, wu, wd):
    bf, f32 = jnp.bfloat16, jnp.float32
    S = jax.ShapeDtypeStruct
    hb = pl.BlockSpec(memory_space=pltpu.HBM)
    regs = [(w.shape[0] // 4, w.shape[1] // 2) for w in (wq, wo, wu, wd)]
    full = [(4 * w.shape[0], w.shape[1]) for w in (wq, wo, wu, wd)]
    dma = pltpu.SemaphoreType.DMA
    return pl.pallas_call(
        front_kernel,
        out_shape=(
            S((4, SP, D), bf), S((4, 4, SP, D), bf), S((4, 4, SP, D), bf), S((4, 4, SP, D), bf), S((4, SP, D), f32),
            S((4, VEC_ROWS, D), bf), S((8, D), f32),
        ) + tuple(S(s, bf) for s in full),
        in_specs=[hb, hb, hb, VM, hb, hb, hb, hb],
        out_specs=(hb,) * 11,
        scratch_shapes=[
            pltpu.VMEM((4, 4, SP, D), bf), pltpu.VMEM((4, 8, D), f32), pltpu.VMEM((4, VEC_ROWS, D), bf),
            pltpu.VMEM((4, 4, SP, D), bf), pltpu.VMEM((4, SP, D), bf), pltpu.VMEM((4, 4, SP, D), bf),
            pltpu.VMEM((4, 4, SP, D), bf), pltpu.VMEM((4, SP, D), f32), pltpu.VMEM(full[0], bf),
        ]
        + [pltpu.VMEM(r, f32) for r in regs] + [pltpu.VMEM(r, bf) for r in regs]
        + [pltpu.VMEM(w.shape, f32) for w in (wq, wo, wu, wd)] + [pltpu.VMEM(w.shape, bf) for w in (wq, wo, wu, wd)]
        + [dma((4, 4)), dma((4, 4)), dma((4,)), dma((4,)), dma((3,)), dma((3,)), dma((4, 3, 9)), dma((4, 3, 9)),
           dma((4,)), dma((4,)), dma((4,)), dma((6,)), dma((16,))],
        compiler_params=pltpu.CompilerParams(
            collective_id=1, has_side_effects=True, vmem_limit_bytes=62 * 2**20),
        cost_estimate=pl.CostEstimate(flops=2 * 9 * 784 * 768 * 768, bytes_accessed=40 * 2**20, transcendentals=0),
        name="front",
    )(tok, tmp, vec, spatial, wq, wo, wu, wd)


def tail_kernel(
    n_items, gd, gu, go, dk, dv, n_all, dq, x_in, dh, wq, vec, vp,
    tg_out, vec_out, gq_out, go_out, gu_out, gd_out,
    dk_s, dv_s, n_s, dq_s, x_s, dh_s, wq_s, vec_s, vp_s, nt_s, part_s, far_s, near_s, far_e, vb_s, gq_s,
    sq, so, su, sd, cq, co, cu, cd, aq, ao, au, ad, bq, bo, bu, bd, zq, zo, zu, zd, fq, fo, fu, fd, eq, eo, eu, ed,
    load_sem, n_sem, dh_sem, half_sem, put_sem, out_sem, p_send, p_recv, vb_send, vb_recv, g_send, g_recv, e_send, e_recv,
):
    bf, f32 = jnp.bfloat16, jnp.float32
    i, f, core, stay, mine, other, far, flip = place()
    ix, iy = halves(core, flip(i, 2), flip(i, 4)), halves(core, flip(i, 4), flip(i, 2))
    xy = (i // 2) % 4
    xy_x, xy_y = halves(core, flip(xy, 1), flip(xy, 2)), halves(core, flip(xy, 2), flip(xy, 1))
    diag = flip(flip(xy, 1), 2)
    c_dev, x_dev, y_dev, e_dev = (flip(i, 1), f), (ix, f), (iy, f), (i, other)
    zs = [flip(f, 1), flip(f, 2), flip(flip(f, 1), 2)]
    extra = []
    bit = 8
    while bit < n_items:
        extra.append(bit)
        bit *= 2

    barrier = pltpu.get_barrier_semaphore()
    partners = [c_dev, (flip(i, 2), f), (flip(i, 4), f)] + [(i, z) for z in zs] + [(flip(i, b), f) for b in extra]
    for dev in partners:
        pl.semaphore_signal(barrier, inc=1, device_id=dev, device_id_type=MESH)

    loads = [pltpu.make_async_copy(a, b, load_sem.at[n]) for n, (a, b) in enumerate(
        [(dk, dk_s), (dv, dv_s), (dq, dq_s), (x_in, x_s), (wq, wq_s), (vec, vec_s), (vp, vp_s)])]
    for copy in loads:
        copy.start()
    def n_load(s):
        return pltpu.make_async_copy(n_all.at[s], n_s.at[s % 2], n_sem.at[s % 2])

    n_load(0).start()
    n_load(1).start()
    grads = (gq_s, go, gu, gd)
    sums, crecv, r1, r2, r3, fin, ext = ((sq, so, su, sd), (cq, co, cu, cd), (aq, ao, au, ad), (bq, bo, bu, bd),
                                         (zq, zo, zu, zd), (fq, fo, fu, fd), (eq, eo, eu, ed))
    outs = (gq_out, go_out, gu_out, gd_out)

    def cols_of(w, half):
        width = sums[w].shape[-1]
        return pl.ds(pl.multiple_of(half * width, 128), width)

    def half_load(w):
        return pltpu.make_async_copy(grads[w].at[:, :, :, cols_of(w, core)], sums[w], half_sem.at[w])

    for w in (3, 2, 1):
        half_load(w).start()
    pl.semaphore_wait(barrier, len(partners))

    def remote(src, dst, ssem, rsem, dev):
        return pltpu.make_async_remote_copy(
            src_ref=src, dst_ref=dst, send_sem=ssem, recv_sem=rsem, device_id=dev, device_id_type=MESH)

    def rows_of(w):
        unit = sums[w].shape[2] // 3
        return (pl.ds(0, 2 * unit), pl.ds(2 * unit, unit))

    def g_copies(w, stage):
        s, base = sums[w], 0
        ra, rb = rows_of(w)
        found = []

        def add(src, dst, dev):
            found.append((src, dst, dev))

        if stage == 0:
            for z in range(4):
                add(grads[w].at[z, :, :, cols_of(w, 1 - core)], crecv[w].at[z], c_dev)
        elif stage == 1:
            base = 4
            for z in range(4):
                add(s.at[z, xy_x, ra], r1[w].at[z, 0, ra], x_dev)
                add(s.at[z, diag, ra], r1[w].at[z, 1, ra], x_dev)
                add(s.at[z, xy_y, rb], r1[w].at[z, 0, rb], y_dev)
                add(s.at[z, diag, rb], r1[w].at[z, 1, rb], y_dev)
        elif stage == 2:
            base = 20
            for z in range(4):
                add(s.at[z, xy_y, ra], r2[w].at[z, ra], y_dev)
                add(s.at[z, xy_x, rb], r2[w].at[z, rb], x_dev)
        elif stage == 3:
            base = 28
            for d in range(3):
                add(s.at[zs[d], xy], r3[w].at[d], (i, zs[d]))
        return [remote(src, dst, g_send.at[w, base + n], g_recv.at[w, base + n], dev)
                for n, (src, dst, dev) in enumerate(found)]

    AX, AY, AC0, ADA, ADB, AC1, AC2, AC3 = range(31, 39)

    def region(w, at, half, piece):
        rows = sums[w].shape[2]
        unit = rows // 3
        start, count = at * rows, rows
        if piece == 1:
            count = 2 * unit
        elif piece == 2:
            start, count = start + 2 * unit, unit
        return outs[w].at[pl.ds(pl.multiple_of(start, 16), count), cols_of(w, half)]

    def a_copy(w, kind):
        at = {AX: xy, AY: xy, AC0: xy, ADA: xy_x, ADB: xy_y, AC1: xy_x, AC2: xy_y, AC3: diag}[kind]
        piece = {ADA: 1, ADB: 2}.get(kind, 0)
        dev = {AX: x_dev, AY: y_dev, ADA: y_dev, ADB: x_dev}.get(kind, c_dev)
        dst = region(w, at, core, piece)
        src = fin[w] if kind in (AX, AY, AC0) else dst
        return remote(src, dst, g_send.at[w, kind], g_recv.at[w, kind], dev)

    def a_arrival(w, kind):
        at = {AX: xy_x, AY: xy_y, ADA: diag, ADB: diag, AC0: xy, AC1: xy_y, AC2: xy_x, AC3: diag}[kind]
        piece = {ADA: 1, ADB: 2}.get(kind, 0)
        ref = region(w, at, (1 - core) if kind >= AC1 or kind == AC0 else core, piece)
        return remote(ref, ref, g_send.at[w, kind], g_recv.at[w, kind], c_dev)

    def start(copies):
        for copy in copies:
            copy.start()

    def plus(ref, where, other_ref, other_where):
        ref[where] = (ref[where].astype(f32) + other_ref[other_where].astype(f32)).astype(bf)

    def g_step(w, stage):
        ra, rb = rows_of(w)
        for copy in g_copies(w, stage):
            copy.wait_recv()
        s = sums[w]
        if stage == 0:
            half_load(w).wait()

            def one(n, _):
                plus(s, (n // 4, n % 4), crecv[w], (n // 4, n % 4))
                return 0
            lax.fori_loop(0, 16, one, 0)
        elif stage == 1:
            def one(z, _):
                plus(s, (z, xy, ra), r1[w], (z, 0, ra))
                plus(s, (z, xy_y, ra), r1[w], (z, 1, ra))
                plus(s, (z, xy, rb), r1[w], (z, 0, rb))
                plus(s, (z, xy_x, rb), r1[w], (z, 1, rb))
                return 0
            lax.fori_loop(0, 4, one, 0)
        elif stage == 2:
            def one(z, _):
                plus(s, (z, xy), r2[w], (z,))
                return 0
            lax.fori_loop(0, 4, one, 0)
        elif stage == 3:
            total = s[f, xy].astype(f32)
            for d in range(3):
                total = total + r3[w][d].astype(f32)
            fin[w][...] = total.astype(bf)
            for n, b in enumerate(extra):
                copy = remote(fin[w], ext[w].at[n], e_send.at[w, n], e_recv.at[w, n], (flip(i, b), f))
                copy.start()
                copy.wait()
                fin[w][...] = (fin[w][...].astype(f32) + ext[w][n].astype(f32)).astype(bf)
            pltpu.make_async_copy(fin[w], region(w, xy, core, 0), put_sem.at[w]).start()
            start([a_copy(w, kind) for kind in (AX, AY, AC0)])
        if stage < 3:
            start(g_copies(w, stage + 1))

    def a_step_one(w):
        a_arrival(w, AX).wait_recv()
        start([a_copy(w, ADA), a_copy(w, AC1)])
        a_arrival(w, AY).wait_recv()
        start([a_copy(w, ADB), a_copy(w, AC2)])

    def a_step_two(w):
        a_arrival(w, ADA).wait_recv()
        a_arrival(w, ADB).wait_recv()
        a_copy(w, AC3).start()

    def a_step_three(w):
        for kind in (AC0, AC1, AC2, AC3):
            a_arrival(w, kind).wait_recv()
        pltpu.make_async_copy(fin[w], region(w, xy, core, 0), put_sem.at[w]).wait()

    def partial_rows(shard):
        def tile(t, _):
            at = pl.multiple_of(t * 256, 256)
            keys = mm(dk_s[shard].reshape(4 * SP, D), wq_s[pl.ds(at, 256), D : 2 * D], NT)
            values = mm(dv_s[shard].reshape(4 * SP, D), wq_s[pl.ds(at, 256), 2 * D :], NT)
            part_s[shard, :, :, pl.ds(at, 256)] = (keys + values).astype(bf).reshape(4, SP, 256)
            return 0
        lax.fori_loop(0, 3, tile, 0)

    far_copy = remote(part_s.at[3 - far], far_s, p_send.at[0], p_recv.at[0], c_dev)
    near_copy = remote(part_s.at[3 - mine], near_s, p_send.at[1], p_recv.at[1], c_dev)
    chip_copy = remote(part_s.at[far], far_e, p_send.at[2], p_recv.at[2], e_dev)

    for w in (3, 2, 1):
        start(g_copies(w, 0))
    for n in (0, 1, 4):
        loads[n].wait()
    partial_rows(3 - far)
    far_copy.start()
    partial_rows(far)
    far_copy.wait_recv()

    def add_far(j, _):
        plus(part_s, (far, j), far_s, (j,))
        return 0
    lax.fori_loop(0, 4, add_far, 0)
    chip_copy.start()
    g_step(3, 0)
    g_step(2, 0)
    g_step(1, 0)
    loads[2].wait()
    for s in range(4):
        n_load(s).wait()
        nt_s[s] = jnp.transpose(n_s[s % 2].reshape(4 * SP, D))
        if s < 2:
            n_load(s + 2).start()

    def grad_q(t, _):
        cols = pl.ds(pl.multiple_of(t * 256, 256), 256)
        g = mm(nt_s[mine], dq_s[:, :, cols].reshape(4 * SP, 256))
        gq_s[:, :, :, cols] = g.astype(bf).reshape(4, 4, D // 16, 256)
        return 0
    lax.fori_loop(0, 3, grad_q, 0)

    def grad_kv(t, _):
        cols = pl.ds(pl.multiple_of(t * 256, 256), 256)
        gk = jnp.zeros((D, 256), f32)
        gv = jnp.zeros((D, 256), f32)
        for s in range(4):
            gk = gk + mm(nt_s[s], dk_s[s, :, :, cols].reshape(4 * SP, 256))
            gv = gv + mm(nt_s[s], dv_s[s, :, :, cols].reshape(4 * SP, 256))
        gq_s[:, :, :, pl.ds(pl.multiple_of(D + t * 256, 256), 256)] = gk.astype(bf).reshape(4, 4, D // 16, 256)
        gq_s[:, :, :, pl.ds(pl.multiple_of(2 * D + t * 256, 256), 256)] = gv.astype(bf).reshape(4, 4, D // 16, 256)
        return 0
    lax.fori_loop(0, 3, grad_kv, 0)
    half_load(0).start()
    start(g_copies(0, 0))
    g_step(3, 1)
    partial_rows(3 - mine)
    near_copy.start()
    partial_rows(mine)
    g_step(0, 0)
    g_step(2, 1)
    g_step(1, 1)
    g_step(3, 2)
    for n in (3, 5, 6):
        loads[n].wait()
    near_copy.wait_recv()
    chip_copy.wait_recv()
    gain = vec_s[0, 0:1, :].astype(f32)

    def column_sums(j, carry):
        bias_q, bias_v = carry
        bias_q = bias_q + jnp.sum(dq_s[j].astype(f32), axis=0, keepdims=True)
        for s in range(4):
            bias_v = bias_v + jnp.sum(dv_s[s, j].astype(f32), axis=0, keepdims=True)
        return bias_q, bias_v
    zero = jnp.zeros((1, D), f32)
    bias_q, bias_v = lax.fori_loop(0, 4, column_sums, (zero, zero))
    vp_s[0, 2:3, :] = bias_q
    vp_s[1, 0:1, :] = bias_v

    def dh_load(j):
        return pltpu.make_async_copy(dh.at[j], dh_s.at[j % 2], dh_sem.at[j % 2])

    dh_load(0).start()

    def norm_back(j, carry):
        gains, shifts = carry

        @pl.when(j < 3)
        def _():
            dh_load(j + 1).start()

        dh_load(j).wait()
        dn = mm(dq_s[j], wq_s[:, :D], NT) + part_s[mine, j].astype(f32) + near_s[j].astype(f32) + far_e[j].astype(f32)
        x = x_s[j]
        centred = x - jnp.mean(x, axis=-1, keepdims=True)
        scale = lax.rsqrt(jnp.mean(centred * centred, axis=-1, keepdims=True) + 1e-06)
        unit = centred * scale
        gains = gains + jnp.sum(dn * unit, axis=0, keepdims=True)
        shifts = shifts + jnp.sum(dn, axis=0, keepdims=True)
        dn = dn * gain
        back = dn - jnp.mean(dn, axis=-1, keepdims=True) - unit * jnp.mean(dn * unit, axis=-1, keepdims=True)
        x_s[j] = dh_s[j % 2] + back * scale
        return gains, shifts
    gains, shifts = lax.fori_loop(0, 4, norm_back, (zero, zero))
    vp_s[0, 0:1, :] = gains
    vp_s[0, 1:2, :] = shifts

    tg_put = pltpu.make_async_copy(x_s, tg_out, out_sem.at[0])
    tg_put.start()

    ring = [c_dev, (flip(i, 2), f), (flip(i, 4), f), (i, zs[0]), (i, zs[1])] + [(flip(i, b), f) for b in extra]

    def v_copy(n):
        return remote(vp_s, vb_s.at[n], vb_send.at[n], vb_recv.at[n], ring[n])

    def v_step(n):
        v_copy(n).wait()
        vp_s[...] = vp_s[...] + vb_s[n]
        if n + 1 < len(ring):
            v_copy(n + 1).start()

    v_copy(0).start()
    g_step(2, 2)
    v_step(0)
    g_step(1, 2)
    v_step(1)
    g_step(0, 1)
    v_step(2)
    g_step(3, 3)
    g_step(2, 3)
    v_step(3)
    g_step(1, 3)
    a_step_one(3)
    a_step_one(2)
    g_step(0, 2)
    for n in range(4, len(ring)):
        v_step(n)
    a_step_one(1)
    a_step_two(3)
    a_step_two(2)
    g_step(0, 3)
    a_step_two(1)
    a_step_three(3)
    a_step_three(2)
    a_step_one(0)
    a_step_three(1)
    a_step_two(0)
    a_step_three(0)
    vec_put = pltpu.make_async_copy(vp_s.at[f], vec_out, out_sem.at[1])
    vec_put.start()
    for w in range(4):
        for stage in range(4):
            for copy in g_copies(w, stage):
                copy.wait_send()
        for kind in (AX, AY, AC0, ADA, ADB, AC1, AC2, AC3):
            a_copy(w, kind).wait_send()
    far_copy.wait_send()
    near_copy.wait_send()
    chip_copy.wait_send()
    tg_put.wait()
    vec_put.wait()


def tail(n_items, gd, gu, go, dk, dv, n_all, dq, x_in, dh, wq, vec, vp):
    bf, f32 = jnp.bfloat16, jnp.float32
    S = jax.ShapeDtypeStruct
    hb = pl.BlockSpec(memory_space=pltpu.HBM)
    dma = pltpu.SemaphoreType.DMA
    n_extra = 0
    while 8 * 2**n_extra < n_items:
        n_extra += 1
    shapes = [(D // 16, 3 * D // 2)] + [(g.shape[2], g.shape[3] // 2) for g in (go, gu, gd)]
    v = lambda shape, dtype=bf: pltpu.VMEM(shape, dtype)
    rows = (4, SP, D)
    return pl.pallas_call(
        functools.partial(tail_kernel, n_items),
        out_shape=(S(rows, f32), S((8, D), f32), S((D // 4, 3 * D), bf))
        + tuple(S((4 * g.shape[2], g.shape[3]), bf) for g in (go, gu, gd)),
        in_specs=[hb] * 12,
        out_specs=(hb,) * 6,
        scratch_shapes=[
            v((4,) + rows), v((4,) + rows), v((2,) + rows), v(rows), v(rows, f32), v((2, SP, D), f32), v((D, 3 * D)),
            v((4, VEC_ROWS, D)), v((4, 8, D), f32), v((4, D, 4 * SP)), v((4,) + rows), v(rows), v(rows), v(rows),
            v((5 + n_extra, 4, 8, D), f32), v((4, 4, D // 16, 3 * D)),
        ]
        + [v((4, 4) + s) for s in shapes] + [v((4, 4) + s) for s in shapes] + [v((4, 2) + s) for s in shapes]
        + [v((4,) + s) for s in shapes] + [v((3,) + s) for s in shapes] + [v(s) for s in shapes]
        + [v((max(n_extra, 1),) + (s if n_extra else (16, 128))) for s in shapes]
        + [dma((7,)), dma((2,)), dma((2,)), dma((4,)), dma((4,)), dma((2,)), dma((3,)), dma((3,)), dma((5 + n_extra,)), dma((5 + n_extra,)),
           dma((4, 39)), dma((4, 39)), dma((4, max(n_extra, 1))), dma((4, max(n_extra, 1)))],
        compiler_params=pltpu.CompilerParams(
            collective_id=2, has_side_effects=True, vmem_limit_bytes=63 * 2**20),
        cost_estimate=pl.CostEstimate(flops=2 * 14 * 784 * 768 * 768, bytes_accessed=60 * 2**20, transcendentals=0),
        name="tail",
    )(gd, gu, go, dk, dv, n_all, dq, x_in, dh, wq, vec, vp)


def on_device(
    tokens,
    cotangent,
    date_year,
    date_day,
    item_dates,
    slot_frame,
    frame_mask,
    qkv_weight,
    qkv_first,
    qkv_second,
    out_weight,
    out_first,
    out_second,
    up_weight,
    up_first,
    up_second,
    down_weight,
    down_first,
    down_second,
    vectors,
    vector_first,
    vector_second,
):
    bf, f32 = jnp.bfloat16, jnp.float32
    n_items = lax.axis_size("items")
    i, f, core, stay, mine, other, far, flip = place()
    swap = []
    for k in range(n_items):
        for z in range(4):
            if k % 2 != z // 2:
                swap.append((k * 4 + z, (k ^ 1) * 4 + 3 - z))

    def to_worker(array):
        return jnp.where(stay, array, lax.ppermute(array, ("items", "frames"), swap))

    pad = lambda a: jnp.pad(a[0], ((0, 0), (0, SP - FRAME_TOK), (0, 0)))
    item_index, is_valid = slot_items(item_dates[0], slot_frame[0], frame_mask[0])
    own_items = lax.dynamic_slice_in_dim(item_index, f * 4, 4)
    tables = jnp.concatenate(key_tables(item_index, is_valid, own_items)).astype(f32)
    tmp = jnp.concatenate([temporal_rows(date_year[0], date_day[0]), jnp.pad(tables[None], ((0, 3), (0, D - 8 * NK)))])
    vec = jnp.pad(vectors.astype(bf).reshape(3, D), ((0, VEC_ROWS - 3), (0, 0)))
    q3, k4, v4, n4, x3, vec_all, tmp_own, wq, wo, wu, wd = front(
        pad(tokens), tmp, vec, jnp.asarray(spatial_rows()), qkv_weight, out_weight, up_weight, down_weight)
    tables = tmp_own[4, : 8 * NK].astype(jnp.int32)
    idx, val = tables[: 4 * NK], tables[4 * NK :]
    k3, v3 = k4.reshape(16, SP, D), v4.reshape(16, SP, D)
    o3, lse = attn_fwd(idx, val, q3, k3, v3)
    grad_out_low = to_worker(pad(cotangent)).reshape(4 * SP, D)
    v_rows = vec_all[:, :3].astype(f32).reshape(12, D)
    bias_output, gain_two, shift_two, bias_down = v_rows[4], v_rows[5], v_rows[6], v_rows[7]
    bias_up = v_rows[8:].reshape(4 * D)
    residual_in = x3.reshape(4 * SP, D)
    attended_low = o3.reshape(4 * SP, D)
    branch = mm(attended_low, wo) + bias_output
    hidden = residual_in + branch
    normed_two, norm_two_back = jax.vjp(layer_norm, hidden, gain_two, shift_two)
    normed_two_low = normed_two.astype(bf)
    inner = mm(normed_two_low, wu) + bias_up
    active, gelu_back = jax.vjp(exact_gelu, inner)
    active_low = active.astype(bf)
    mlp_out = mm(active_low, wd) + bias_down
    block_out = to_worker((hidden + mlp_out).astype(bf))
    grad_out = grad_out_low.astype(f32)
    TN = (((0,), (0,)), ((), ()))
    down_grad = mm(active_low, grad_out_low, TN)
    bias_down_grad = jnp.sum(grad_out, axis=0)
    (inner_grad,) = gelu_back(mm(grad_out_low, wd, NT))
    inner_grad_low = inner_grad.astype(bf)
    up_grad = mm(normed_two_low, inner_grad_low, TN)
    bias_up_grad = jnp.sum(inner_grad_low.astype(f32), axis=0)
    hidden_from_norm, gain_two_grad, shift_two_grad = norm_two_back(mm(inner_grad_low, wu, NT))
    hidden_grad = grad_out + hidden_from_norm
    branch_grad_low = hidden_grad.astype(bf)
    out_grad = mm(attended_low, branch_grad_low, TN)
    bias_output_grad = jnp.sum(branch_grad_low.astype(f32), axis=0)
    attended_grad_low = mm(branch_grad_low, wo, NT).astype(bf)
    dq3, dk3, dv3 = attn_bwd(idx, val, q3, k3, v3, o3, attended_grad_low.reshape(4, SP, D), lse)
    zero = jnp.zeros((4 * D,), f32)
    vector_part = jnp.concatenate([zero, bias_output_grad, gain_two_grad, shift_two_grad, bias_down_grad, bias_up_grad])
    vector_part = jnp.pad(vector_part.reshape(4, 3, D), ((0, 0), (0, 5), (0, 0)))
    blocks = lambda g: g.astype(bf).reshape(4, 4, g.shape[0] // 16, g.shape[1])
    token_grad, vector_sum, qkv_sum, out_sum, up_sum, down_sum = tail(
        n_items, blocks(down_grad), blocks(up_grad), blocks(out_grad), dk3.reshape(4, 4, SP, D), dv3.reshape(4, 4, SP, D),
        n4, dq3, x3, hidden_grad.reshape(4, SP, D), wq, vec_all, vector_part)
    token_grad = jnp.where(
        stay, token_grad, lax.ppermute(token_grad.astype(bf), ("items", "frames"), swap).astype(f32))
    qkv_new = adamw(qkv_weight, qkv_first, qkv_second, qkv_sum.astype(f32), 0.05, 0.05)
    out_new = adamw(out_weight, out_first, out_second, out_sum.astype(f32), 0.5, 0.05)
    up_new = adamw(up_weight, up_first, up_second, up_sum.astype(f32), 0.05, 0.05)
    down_new = adamw(down_weight, down_first, down_second, down_sum.astype(f32), 0.03, 0.05)
    vector_new = adamw(vectors, vector_first, vector_second, vector_sum[:3].reshape(3 * D), 0.3, 0.0)
    cut = lambda a: a.reshape(1, 4, SP, D)[:, :, :FRAME_TOK]
    return (cut(block_out), cut(token_grad)) + qkv_new + out_new + up_new + down_new + vector_new


def solution(mesh):
    placed = (
        P("items", "frames", None, None),
        P("items", "frames", None, None),
        P("items", "frames"),
        P("items", "frames"),
        P("items", None),
        P("items", None),
        P("items", None),
        P("frames", None),
        P("frames", None),
        P("frames", None),
        P("frames", None),
        P("frames", None),
        P("frames", None),
        P("frames", None),
        P("frames", None),
        P("frames", None),
        P("frames", None),
        P("frames", None),
        P("frames", None),
        P("frames"),
        P("frames"),
        P("frames"),
    )
    return jax.shard_map(
        on_device,
        mesh=mesh,
        in_specs=placed,
        out_specs=(
            P("items", "frames", None, None),
            P("items", "frames", None, None),
            P("frames", None),
            P("frames", None),
            P("frames", None),
            P("frames", None),
            P("frames", None),
            P("frames", None),
            P("frames", None),
            P("frames", None),
            P("frames", None),
            P("frames", None),
            P("frames", None),
            P("frames", None),
            P("frames"),
            P("frames"),
            P("frames"),
        ),
        check_vma=False,
    )
```

```python
import functools

import jax
import jax.numpy as jnp
import numpy as np
from jax import lax
from jax.experimental import pallas as pl
from jax.experimental.pallas import tpu as pltpu
from jax.sharding import PartitionSpec as P

D = 768
HEADS = 12
HEAD = 64
GRID = 14
STEP = 10
FRAME_TOK = 196


beta_one = 0.9
beta_two = 0.999


def sincos(values, length_out):
    half_width = length_out // 2
    frequency = 1.0 / 10000.0 ** (jnp.arange(half_width, dtype=jnp.float32) / half_width)
    angles = values[..., None] * frequency
    return jnp.concatenate([jnp.sin(angles), jnp.cos(angles)], axis=-1)


def temporal_rows(year_values, day_values):
    dates = jnp.concatenate(
        [
            sincos((year_values - 2000).astype(jnp.float32), D // 8),
            sincos(day_values.astype(jnp.float32), D // 8),
        ],
        axis=-1,
    )
    return jnp.pad(dates, ((0, 0), (3 * D // 4, 0)))


def spatial_rows():
    half = 3 * D // 16
    frequency = (1.0 / np.float32(10000.0) ** (np.arange(half, dtype=np.float32) / np.float32(half))).astype(np.float32)
    cells = np.arange(FRAME_TOK)
    parts = []
    for values in (cells // GRID, cells % GRID):
        angles = values.astype(np.float32)[:, None] * frequency
        parts += [np.sin(angles), np.cos(angles)]
    rows = np.zeros((SP, D), np.float32)
    rows[:FRAME_TOK, : 3 * D // 4] = np.concatenate(parts, axis=-1)
    return rows


def slot_items(dates_group, frames_group, mask_group):
    item_ends = jnp.cumsum(dates_group)
    starts = item_ends - dates_group
    item_index = jnp.sum((frames_group[:, None] >= item_ends[None, :]).astype(jnp.int32), axis=1)
    is_first = jnp.any(frames_group[:, None] == starts[None, :], axis=1)
    is_valid = jnp.logical_or(mask_group > 0, is_first)
    return (item_index, is_valid)


SP = 208
NK = 6
NEG = -1e30
NT = (((1,), (1,)), ((), ()))
NN = (((1,), (0,)), ((), ()))


def mm(a, b, dims=NN):
    return lax.dot_general(a, b, dims, preferred_element_type=jnp.float32)


def augmented_keys(parts, valid, bias_lane, mine):
    row = lax.broadcasted_iota(jnp.int32, (SP, 128), 0)
    lane = lax.broadcasted_iota(jnp.int32, (SP, 128), 1)
    blocks = []
    for part, live in zip(parts, valid):
        bias = jnp.where(row >= FRAME_TOK, NEG, live).astype(jnp.bfloat16)
        blocks.append(jnp.where(mine, part, jnp.where(lane == bias_lane, bias, jnp.zeros_like(part))))
    return jnp.concatenate(blocks, axis=0)


def attn_fwd_kernel(idx_ref, val_ref, q_ref, k_ref, v_ref, o_ref, lse_ref):
    lane = lax.broadcasted_iota(jnp.int32, (SP, 128), 1)

    def one(step, _):
        j, b = step // 6, step % 6
        cols = pl.ds(pl.multiple_of(b * 128, 128), 128)
        parts = [k_ref[idx_ref[j * NK + t], :, cols] for t in range(NK)]
        valid = [jnp.where(val_ref[j * NK + t] > 0, 0.0, NEG) for t in range(NK)]
        vg = jnp.concatenate([v_ref[idx_ref[j * NK + t], :, cols] for t in range(NK)], axis=0)
        q = q_ref[j, :, cols]
        scores = []
        for h in range(2):
            mine = (lane < 64) if h == 0 else (lane >= 64)
            spare = 64 if h == 0 else 0
            ka = augmented_keys(parts, valid, spare, mine)
            qa = jnp.where(mine, q, jnp.where(lane == spare, jnp.ones_like(q), jnp.zeros_like(q)))
            scores.append(mm(qa, ka, NT))
        peaks = [jnp.max(s, axis=1, keepdims=True) for s in scores]
        probs = [jnp.exp(s - m) for s, m in zip(scores, peaks)]
        sums = [jnp.sum(p, axis=1, keepdims=True) for p in probs]
        outs = [mm(p.astype(jnp.bfloat16), vg) / total for p, total in zip(probs, sums)]
        o_ref[j, :, cols] = jnp.where(lane < 64, outs[0], outs[1]).astype(jnp.bfloat16)
        logs = [m + jnp.log(total) for m, total in zip(peaks, sums)]
        lse_ref[j, b] = jnp.transpose(jnp.where(lane == 0, logs[0], logs[1]))[:8]
        return 0

    lax.fori_loop(0, 24, one, 0)


VM = pl.BlockSpec(memory_space=pltpu.VMEM)
SM = pl.BlockSpec(memory_space=pltpu.SMEM)


def attn_fwd(idx, val, q, k, v):
    return pl.pallas_call(
        attn_fwd_kernel,
        out_shape=(
            jax.ShapeDtypeStruct((4, SP, D), jnp.bfloat16),
            jax.ShapeDtypeStruct((4, 6, 8, SP), jnp.float32),
        ),
        in_specs=[SM, SM, VM, VM, VM],
        out_specs=(VM, VM),
        compiler_params=pltpu.CompilerParams(vmem_limit_bytes=60 * 2**20),
        cost_estimate=pl.CostEstimate(
            flops=2 * 2 * 24 * 12 * SP * SP * 256,
            bytes_accessed=14 * 2**20,
            transcendentals=24 * 12 * SP * SP,
        ),
        name="attn_fwd",
    )(idx, val, q, k, v)


def key_tables(item_index, is_valid, q_items):
    match = (q_items[:, None] == item_index[None, :]) & is_valid[None, :]
    rank = jnp.cumsum(match.astype(jnp.int32), axis=1) - 1
    count = jnp.sum(match.astype(jnp.int32), axis=1)
    place = jnp.arange(NK, dtype=jnp.int32)
    hit = match[:, None, :] & (rank[:, None, :] == place[None, :, None])
    slots = jnp.arange(item_index.shape[0], dtype=jnp.int32)
    idx = jnp.sum(jnp.where(hit, slots[None, None, :], 0), axis=2)
    val = (place[None, :] < count[:, None]).astype(jnp.int32)
    place_of = jnp.arange(4 * NK, dtype=jnp.int32)
    held = (idx.reshape(-1)[None, :] == slots[:, None]) & (val.reshape(-1)[None, :] > 0)
    first = jnp.min(jnp.where(held, place_of[None, :], 4 * NK), axis=1)
    last = jnp.max(jnp.where(held, place_of[None, :], -1), axis=1)
    has_first, has_last = first < 4 * NK, last > first
    rows = [jnp.where(has_first, first, 0), jnp.where(has_last, last, 0), has_first, has_last]
    return jnp.concatenate([idx.reshape(-1), val.reshape(-1)] + [r.astype(jnp.int32) for r in rows])


def adamw(weight, first_moment, second, gradient, step_rate, decay):
    first_new = beta_one * first_moment + (1.0 - beta_one) * gradient
    second_new = beta_two * second + (1.0 - beta_two) * gradient * gradient
    first_hat = first_new / (1.0 - beta_one**STEP)
    second_hat = second_new / (1.0 - beta_two**STEP)
    weight_new = weight - step_rate * (first_hat / (jnp.sqrt(second_hat) + 1e-08) + decay * weight)
    return (first_new, second_new, weight_new)


VEC_ROWS = 16
MESH = pl.DeviceIdType.MESH
Z, X, Y, DA, DB, C0, C1, C2, C3 = range(9)


def norm_rows(x):
    mean = jnp.mean(x, axis=-1, keepdims=True)
    centred = x - mean
    spread = jnp.mean(centred * centred, axis=-1, keepdims=True)
    return centred * lax.rsqrt(spread + 1e-06)


def place():
    i, f = lax.axis_index("items"), lax.axis_index("frames")
    core = i % 2
    upper = f // 2
    stay = core == upper
    mine = jnp.where(stay, f, 3 - f)
    other = f + 1 - 2 * (f % 2)
    far = jnp.where(stay, other, 3 - other)
    flip = lambda v, bit: v + bit - 2 * bit * ((v // bit) % 2)
    return i, f, core, stay, mine, other, far, flip


def halves(core, a, b):
    return jnp.where(core == 0, a, b)


def front_kernel(
    tok, tmp, vec, spatial, wq, wo, wu, wd,
    q_out, k_out, v_out, nt_out, x_out, vec_out, tmp_out, wq_out, wo_out, wu_out, wd_out,
    t_s, tmp_s, vec_s, n_s, nt_s, q_s, k_s, v_s, x_s, wq_s,
    rq32, ro32, ru32, rd32, rq, ro, ru, rd, sq32, so32, su32, sd32, sq, so, su, sd,
    t_send, t_recv, m_send, m_recv, v_send, v_recv, w_send, w_recv, reg_sem, own_sem, put_sem, loc_sem, out_sem,
):
    bf, f32 = jnp.bfloat16, jnp.float32
    i, f, core, stay, mine, other, far, flip = place()
    c_dev = (flip(i, 1), f)
    x_dev = (halves(core, flip(i, 2), flip(i, 4)), f)
    y_dev = (halves(core, flip(i, 4), flip(i, 2)), f)
    e_dev = (i, other)
    m_dev = (flip(i, 1), 3 - f)
    xy = (i // 2) % 4
    xy_x, xy_y = halves(core, flip(xy, 1), flip(xy, 2)), halves(core, flip(xy, 2), flip(xy, 1))
    diag = flip(flip(xy, 1), 2)
    zs = [flip(f, 1), flip(f, 2), flip(flip(f, 1), 2)]

    barrier = pltpu.get_barrier_semaphore()
    partners = [c_dev, x_dev, y_dev, m_dev] + [(i, z) for z in zs]
    for dev in partners:
        pl.semaphore_signal(barrier, inc=1, device_id=dev, device_id_type=MESH)

    weights = [(wq, wq_out, rq32, rq, sq32, sq), (wo, wo_out, ro32, ro, so32, so),
               (wu, wu_out, ru32, ru, su32, su), (wd, wd_out, rd32, rd, sd32, sd)]

    def region_load(w):
        src, _, r32, _, _, _ = weights[w]
        rows, cols = r32.shape
        return pltpu.make_async_copy(
            src.at[pl.ds(pl.multiple_of(xy * rows, rows), rows), pl.ds(pl.multiple_of(core * cols, 128), cols)],
            r32, reg_sem.at[w])

    def own_load(w):
        return pltpu.make_async_copy(weights[w][0], weights[w][4], own_sem.at[w])

    def own_put(w):
        out, small = weights[w][1], weights[w][5]
        rows = small.shape[0]
        return pltpu.make_async_copy(small, out.at[pl.ds(pl.multiple_of(f * rows, rows), rows), :], put_sem.at[w])

    for w in range(4):
        region_load(w).start()
    for w in range(4):
        own_load(w).start()
    tok_load = pltpu.make_async_copy(tok, t_s.at[mine], loc_sem.at[0])
    tmp_load = pltpu.make_async_copy(tmp, tmp_s.at[mine], loc_sem.at[1])
    vec_load = pltpu.make_async_copy(vec, vec_s.at[f], loc_sem.at[2])

    @pl.when(stay)
    def _():
        tok_load.start()
        tmp_load.start()

    vec_load.start()
    pl.semaphore_wait(barrier, len(partners))

    def remote(src, dst, ssem, rsem, dev):
        return pltpu.make_async_remote_copy(
            src_ref=src, dst_ref=dst, send_sem=ssem, recv_sem=rsem, device_id=dev, device_id_type=MESH)

    def tok_copy(kind, j):
        if kind == 0:
            return remote(tok.at[j], t_s.at[f, j], t_send.at[0, j], t_recv.at[0, j], m_dev)
        if kind == 3:
            return remote(t_s.at[far, j], t_s.at[far, j], t_send.at[3, j], t_recv.at[3, j], c_dev)
        return remote(t_s.at[mine, j], t_s.at[mine, j], t_send.at[kind, j], t_recv.at[kind, j],
                      c_dev if kind == 1 else e_dev)

    def tok_arrival(kind, j):
        shard = (mine, 3 - mine, far, 3 - far)[kind]
        return remote(t_s.at[shard, j], t_s.at[shard, j], t_send.at[kind, j], t_recv.at[kind, j], c_dev)

    def tmp_copy(kind):
        if kind == 0:
            return remote(tmp, tmp_s.at[f], m_send.at[0], m_recv.at[0], m_dev)
        if kind == 3:
            return remote(tmp_s.at[far], tmp_s.at[far], m_send.at[3], m_recv.at[3], c_dev)
        return remote(tmp_s.at[mine], tmp_s.at[mine], m_send.at[kind], m_recv.at[kind], c_dev if kind == 1 else e_dev)

    def tmp_arrival(kind):
        shard = (mine, 3 - mine, far, 3 - far)[kind]
        return remote(tmp_s.at[shard], tmp_s.at[shard], m_send.at[kind], m_recv.at[kind], c_dev)

    def part(w, z, at, half, piece):
        out, r = weights[w][1], weights[w][3]
        rows, cols = r.shape
        unit = rows // 3
        start = z * 4 * rows + at * rows
        if piece == 0:
            return out.at[pl.ds(pl.multiple_of(start, 16), rows), pl.ds(pl.multiple_of(half * cols, 128), cols)]
        if piece == 1:
            return out.at[pl.ds(pl.multiple_of(start, 16), 2 * unit), pl.ds(pl.multiple_of(half * cols, 128), cols)]
        return out.at[pl.ds(pl.multiple_of(start + 2 * unit, 16), unit), pl.ds(pl.multiple_of(half * cols, 128), cols)]

    def w_copy(w, d, kind):
        sems = (w_send.at[w, d, kind], w_recv.at[w, d, kind])
        z = zs[d]
        if kind == Z:
            return remote(weights[w][3], part(w, f, xy, core, 0), *sems, (i, z))
        at = {X: xy, Y: xy, DA: xy_x, DB: xy_y, C0: xy, C1: xy_x, C2: xy_y, C3: diag}[kind]
        piece = {DA: 1, DB: 2}.get(kind, 0)
        dev = {X: x_dev, Y: y_dev, DA: y_dev, DB: x_dev}.get(kind, c_dev)
        ref = part(w, z, at, core, piece)
        return remote(ref, ref, *sems, dev)

    def w_arrival(w, d, kind):
        sems = (w_send.at[w, d, kind], w_recv.at[w, d, kind])
        z = zs[d]
        at = {Z: xy, X: xy_x, Y: xy_y, DA: diag, DB: diag, C0: xy, C1: xy_y, C2: xy_x, C3: diag}[kind]
        piece = {DA: 1, DB: 2}.get(kind, 0)
        half = (1 - core) if kind >= C0 else core
        ref = part(w, z, at, half, piece)
        return remote(ref, ref, *sems, c_dev)

    def w_send_region(w):
        region_load(w).wait()
        weights[w][3][...] = weights[w][2][...].astype(bf)
        for d in range(3):
            w_copy(w, d, Z).start()

    def w_stage_one(w):
        for d in range(3):
            w_arrival(w, d, Z).wait_recv()
            for kind in (X, Y, C0):
                w_copy(w, d, kind).start()

    def w_stage_two(w):
        for d in range(3):
            w_arrival(w, d, X).wait_recv()
            w_copy(w, d, DA).start()
            w_copy(w, d, C1).start()
            w_arrival(w, d, Y).wait_recv()
            w_copy(w, d, DB).start()
            w_copy(w, d, C2).start()

    def w_stage_three(w):
        for d in range(3):
            w_arrival(w, d, DA).wait_recv()
            w_arrival(w, d, DB).wait_recv()
            w_copy(w, d, C3).start()

    def w_stage_four(w):
        for d in range(3):
            for kind in (C0, C1, C2, C3):
                w_arrival(w, d, kind).wait_recv()

    def w_own(w):
        own_load(w).wait()
        weights[w][5][...] = weights[w][4][...].astype(bf)
        own_put(w).start()

    w_send_region(0)

    @pl.when(jnp.logical_not(stay))
    def _():
        tmp_copy(0).start()
        for j in range(4):
            tok_copy(0, j).start()

    @pl.when(stay)
    def _():
        tok_load.wait()
        tmp_load.wait()
        for kind in (2, 1):
            tmp_copy(kind).start()
            for j in range(4):
                tok_copy(kind, j).start()

    vec_load.wait()
    def v_copy(d):
        return remote(vec_s.at[f], vec_s.at[f], v_send.at[d], v_recv.at[d], (i, zs[d]))
    def v_arrival(d):
        return remote(vec_s.at[zs[d]], vec_s.at[zs[d]], v_send.at[d], v_recv.at[d], (i, zs[d]))
    for d in range(3):
        v_copy(d).start()
    for w in range(4):
        w_own(w)
    w_stage_one(0)
    w_stage_two(0)
    w_stage_three(0)

    @pl.when(jnp.logical_not(stay))
    def _():
        tmp_arrival(0).wait_recv()
        for kind in (2, 1):
            tmp_copy(kind).start()
        for j in range(4):
            tok_arrival(0, j).wait_recv()
            for kind in (2, 1):
                tok_copy(kind, j).start()

    for w in (1, 2, 3):
        w_send_region(w)
    w_stage_four(0)
    own_put(0).wait()
    wq_load = pltpu.make_async_copy(wq_out, wq_s, loc_sem.at[3])
    wq_load.start()
    for d in range(3):
        v_arrival(d).wait_recv()
    vec_put = pltpu.make_async_copy(vec_s, vec_out, loc_sem.at[4])
    vec_put.start()
    tmp_put = pltpu.make_async_copy(tmp_s.at[mine], tmp_out, loc_sem.at[5])
    tmp_put.start()
    gain = vec_s[0, 0:1, :].astype(f32)
    shift = vec_s[0, 1:2, :].astype(f32)
    bias_q = vec_s[0, 2:3, :].astype(f32)
    bias_v = vec_s[1, 0:1, :].astype(f32)
    wq_load.wait()

    def normalise(shard, keep_x):
        def slot(j, _):
            x = t_s[shard, j].astype(f32) + (spatial[...] + tmp_s[shard, pl.ds(j, 1), :])
            if keep_x:
                x_s[j] = x
            n_s[shard, j] = (norm_rows(x) * gain + shift).astype(bf)
            return 0
        lax.fori_loop(0, 4, slot, 0)

    def project(shard):
        rows = n_s[shard].reshape(4 * SP, D)
        def keys(t, _):
            cols = pl.ds(pl.multiple_of(t * 256, 256), 256)
            k_s[shard, :, :, cols] = mm(rows, wq_s[:, pl.ds(pl.multiple_of(D + t * 256, 256), 256)]).astype(bf).reshape(4, SP, 256)
            v_s[shard, :, :, cols] = (mm(rows, wq_s[:, pl.ds(pl.multiple_of(2 * D + t * 256, 256), 256)])
                                      + vec_s[1, 0:1, cols].astype(f32)).astype(bf).reshape(4, SP, 256)
            return 0
        lax.fori_loop(0, 3, keys, 0)

    def project_q(shard):
        rows = n_s[shard].reshape(4 * SP, D)
        def queries(t, _):
            cols = pl.ds(pl.multiple_of(t * 256, 256), 256)
            q = (mm(rows, wq_s[:, cols]) + vec_s[0, 2:3, cols].astype(f32)).astype(bf)
            q_s[:, :, cols] = (q.astype(f32) * 0.125).astype(bf).reshape(4, SP, 256)
            return 0
        lax.fori_loop(0, 3, queries, 0)

    outs = []
    def put(src, dst):
        copy = pltpu.make_async_copy(src, dst, out_sem.at[len(outs)])
        copy.start()
        outs.append(copy)

    def put_shard(shard):
        nt_s[shard] = jnp.transpose(n_s[shard].reshape(4 * SP, D))
        put(nt_s.at[shard], nt_out.at[shard])
        put(k_s.at[shard], k_out.at[shard])
        put(v_s.at[shard], v_out.at[shard])

    normalise(mine, True)
    put(x_s, x_out)
    project_q(mine)
    put(q_s, q_out)
    project(mine)
    put_shard(mine)
    w_stage_one(1)
    tmp_arrival(1).wait_recv()
    for j in range(4):
        tok_arrival(1, j).wait_recv()
    normalise(3 - mine, False)
    project(3 - mine)
    put_shard(3 - mine)
    tmp_arrival(2).wait_recv()
    tmp_copy(3).start()
    for j in range(4):
        tok_arrival(2, j).wait_recv()
        tok_copy(3, j).start()
    w_stage_two(1)
    w_stage_one(2)
    normalise(far, False)
    project(far)
    put_shard(far)
    w_stage_one(3)
    tmp_arrival(3).wait_recv()
    for j in range(4):
        tok_arrival(3, j).wait_recv()
    normalise(3 - far, False)
    project(3 - far)
    put_shard(3 - far)
    w_stage_two(2)
    w_stage_two(3)
    for w in (1, 2, 3):
        w_stage_three(w)
    for w in (1, 2, 3):
        w_stage_four(w)
        own_put(w).wait()

    @pl.when(jnp.logical_not(stay))
    def _():
        tmp_copy(0).wait_send()
        for j in range(4):
            tok_copy(0, j).wait_send()

    for kind in (1, 2, 3):
        tmp_copy(kind).wait_send()
        for j in range(4):
            tok_copy(kind, j).wait_send()
    for d in range(3):
        v_copy(d).wait_send()
        for w in range(4):
            for kind in range(9):
                w_copy(w, d, kind).wait_send()
    vec_put.wait()
    tmp_put.wait()
    for copy in outs:
        copy.wait()


def front(tok, tmp, vec, spatial, wq, wo, wu, wd):
    bf, f32 = jnp.bfloat16, jnp.float32
    S = jax.ShapeDtypeStruct
    hb = pl.BlockSpec(memory_space=pltpu.HBM)
    regs = [(w.shape[0] // 4, w.shape[1] // 2) for w in (wq, wo, wu, wd)]
    full = [(4 * w.shape[0], w.shape[1]) for w in (wq, wo, wu, wd)]
    dma = pltpu.SemaphoreType.DMA
    return pl.pallas_call(
        front_kernel,
        out_shape=(
            S((4, SP, D), bf), S((4, 4, SP, D), bf), S((4, 4, SP, D), bf), S((4, D, 4 * SP), bf), S((4, SP, D), f32),
            S((4, VEC_ROWS, D), bf), S((8, D), f32),
        ) + tuple(S(s, bf) for s in full),
        in_specs=[hb, hb, hb, VM, hb, hb, hb, hb],
        out_specs=(hb,) * 11,
        scratch_shapes=[
            pltpu.VMEM((4, 4, SP, D), bf), pltpu.VMEM((4, 8, D), f32), pltpu.VMEM((4, VEC_ROWS, D), bf),
            pltpu.VMEM((4, 4, SP, D), bf), pltpu.VMEM((4, D, 4 * SP), bf), pltpu.VMEM((4, SP, D), bf), pltpu.VMEM((4, 4, SP, D), bf),
            pltpu.VMEM((4, 4, SP, D), bf), pltpu.VMEM((4, SP, D), f32), pltpu.VMEM(full[0], bf),
        ]
        + [pltpu.VMEM(r, f32) for r in regs] + [pltpu.VMEM(r, bf) for r in regs]
        + [pltpu.VMEM(w.shape, f32) for w in (wq, wo, wu, wd)] + [pltpu.VMEM(w.shape, bf) for w in (wq, wo, wu, wd)]
        + [dma((4, 4)), dma((4, 4)), dma((4,)), dma((4,)), dma((3,)), dma((3,)), dma((4, 3, 9)), dma((4, 3, 9)),
           dma((4,)), dma((4,)), dma((4,)), dma((6,)), dma((16,))],
        compiler_params=pltpu.CompilerParams(
            collective_id=1, has_side_effects=True, vmem_limit_bytes=62 * 2**20),
        cost_estimate=pl.CostEstimate(flops=2 * 9 * 784 * 768 * 768, bytes_accessed=40 * 2**20, transcendentals=0),
        name="front",
    )(tok, tmp, vec, spatial, wq, wo, wu, wd)


def norm_parts(x):
    centred = x - jnp.mean(x, axis=-1, keepdims=True)
    scale = lax.rsqrt(jnp.mean(centred * centred, axis=-1, keepdims=True) + 1e-06)
    return centred * scale, scale


def norm_grad(dn, unit, scale):
    return (dn - jnp.mean(dn, axis=-1, keepdims=True) - unit * jnp.mean(dn * unit, axis=-1, keepdims=True)) * scale


def mid_kernel(
    o_in, x_in, dy_in, vec, wo, wu, wd,
    y_out, dh_out, do_out, gd_out, gu_out, go_out, vp_out,
    o_s, h_s, dy_s, vec_s, wo_s, wu_s, wd_s, n_s, nt_s, a_s, du_s, mlp_s, dn_s, gd_s, gu_s, go_s, y_s, db_s, do_s, vp_s,
    bu_s, gbu_s, in_sem, out_sem,
):
    bf, f32 = jnp.bfloat16, jnp.float32
    loads = [pltpu.make_async_copy(a, b, in_sem.at[n]) for n, (a, b) in enumerate(
        [(o_in, o_s), (wo, wo_s), (vec, vec_s), (x_in, h_s), (dy_in, dy_s), (wu, wu_s), (wd, wd_s)])]
    for copy in loads:
        copy.start()
    vp_s[...] = jnp.zeros_like(vp_s)
    zero = jnp.zeros((1, D), f32)
    for n in range(4):
        loads[n].wait()
    flat = lambda ref: ref[...].reshape(4 * SP, D)

    def branch(t, _):
        cols = pl.ds(pl.multiple_of(t * 256, 256), 256)
        out = mm(flat(o_s), wo_s[:, cols]) + vec_s[1, 1:2, cols].astype(f32)
        h_s[:, :, cols] = h_s[:, :, cols] + out.reshape(4, SP, 256)
        return 0
    lax.fori_loop(0, 3, branch, 0)
    gain, shift = vec_s[1, 2:3, :].astype(f32), vec_s[2, 0:1, :].astype(f32)

    def norm(j, _):
        unit, _scale = norm_parts(h_s[j])
        n_s[j] = (unit * gain + shift).astype(bf)
        return 0
    lax.fori_loop(0, 4, norm, 0)
    nt_s[...] = jnp.transpose(flat(n_s))
    spots = [(n, (n // 3 + 8) // 3, (n // 3 + 8) % 3, (n % 3) * 256) for n in range(12)]
    for n, z, r, at in spots:
        bu_s[n, 0:1, :] = vec_s[z, r : r + 1, at : at + 256].astype(f32)
    mlp_s[...] = jnp.zeros_like(mlp_s)
    dn_s[...] = jnp.zeros_like(dn_s)
    for n in range(4, 7):
        loads[n].wait()

    def tile(n, _):
        at = pl.multiple_of(n * 256, 256)
        cols = pl.ds(at, 256)
        low = pl.ds(pl.multiple_of((n % 3) * 256, 256), 256)
        u = mm(flat(n_s), wu_s[:, cols]) + bu_s[n, 0:1, :]
        cdf = 0.5 * (1.0 + lax.erf(u * 0.7071067811865476))
        a = (u * cdf).astype(bf)
        slope = cdf + u * (jnp.exp(u * u * -0.5) * 0.3989422804014327)
        da = mm(flat(dy_s), wd_s[cols, :], NT)
        du = (da * slope).astype(bf)
        a_s[:, low] = a
        du_s[:, low] = du
        gd_s[cols, :] = mm(jnp.transpose(a), flat(dy_s)).astype(bf)
        gu_s[:, cols] = mm(nt_s[...], du).astype(bf)
        gbu_s[n, 0:1, :] = jnp.sum(du.astype(f32), axis=0, keepdims=True)

        @pl.when(n % 3 == 2)
        def _():
            start = pl.multiple_of((n // 3) * D, D)

            def add(t, _):
                out = pl.ds(pl.multiple_of(t * 256, 256), 256)
                mlp_s[:, out] += mm(a_s[...], wd_s[pl.ds(start, D), out])
                dn_s[:, out] += mm(du_s[...], wu_s[out, pl.ds(start, D)], NT)
                return 0
            lax.fori_loop(0, 3, add, 0)
        return 0
    lax.fori_loop(0, 12, tile, 0)
    for n, z, r, at in spots:
        vp_s[z, r : r + 1, at : at + 256] = gbu_s[n, 0:1, :]
    puts = []

    def put(src, dst):
        copy = pltpu.make_async_copy(src, dst, out_sem.at[len(puts)])
        copy.start()
        puts.append(copy)

    put(gd_s, gd_out)
    put(gu_s, gu_out)
    bias_down = vec_s[2, 1:2, :].astype(f32)

    def back(j, carry):
        gains, shifts, bias_o, bias_d = carry
        rows = pl.ds(pl.multiple_of(j * SP, 16), SP)
        h = h_s[j]
        y_s[j] = (h + (mlp_s[rows, :] + bias_down)).astype(bf)
        unit, scale = norm_parts(h)
        dn = dn_s[rows, :]
        gains = gains + jnp.sum(dn * unit, axis=0, keepdims=True)
        shifts = shifts + jnp.sum(dn, axis=0, keepdims=True)
        dy = dy_s[j].astype(f32)
        dh = dy + norm_grad(dn * gain, unit, scale)
        h_s[j] = dh
        db = dh.astype(bf)
        db_s[j] = db
        bias_o = bias_o + jnp.sum(db.astype(f32), axis=0, keepdims=True)
        return gains, shifts, bias_o, bias_d + jnp.sum(dy, axis=0, keepdims=True)
    gains, shifts, bias_o, bias_d = lax.fori_loop(0, 4, back, (zero,) * 4)
    put(y_s, y_out)
    put(h_s, dh_out)
    vp_s[1, 1:2, :] = bias_o
    vp_s[1, 2:3, :] = gains
    vp_s[2, 0:1, :] = shifts
    vp_s[2, 1:2, :] = bias_d
    put(vp_s, vp_out)

    def attended(t, _):
        cols = pl.ds(pl.multiple_of(t * 256, 256), 256)
        do_s[:, :, cols] = mm(flat(db_s), wo_s[cols, :], NT).astype(bf).reshape(4, SP, 256)
        return 0
    lax.fori_loop(0, 3, attended, 0)
    put(do_s, do_out)

    def out_grad(t, _):
        cols = pl.ds(pl.multiple_of(t * 256, 256), 256)
        turned = jnp.transpose(o_s[:, :, cols].reshape(4 * SP, 256))
        go_s[cols, :] = mm(turned, flat(db_s)).astype(bf)
        return 0
    lax.fori_loop(0, 3, out_grad, 0)
    put(go_s, go_out)
    for copy in puts:
        copy.wait()


def mid(o, x, dy, vec, wo, wu, wd):
    bf, f32 = jnp.bfloat16, jnp.float32
    S = jax.ShapeDtypeStruct
    hb = pl.BlockSpec(memory_space=pltpu.HBM)
    dma = pltpu.SemaphoreType.DMA
    v = lambda shape, dtype=bf: pltpu.VMEM(shape, dtype)
    rows = (4, SP, D)
    return pl.pallas_call(
        mid_kernel,
        out_shape=(S(rows, bf), S(rows, f32), S(rows, bf), S((4 * D, D), bf), S((D, 4 * D), bf), S((D, D), bf),
                   S((4, 8, D), f32)),
        in_specs=[hb] * 7,
        out_specs=(hb,) * 7,
        scratch_shapes=[
            v(rows), v(rows, f32), v(rows), v((4, VEC_ROWS, D)), v((D, D)), v((D, 4 * D)), v((4 * D, D)),
            v(rows), v((D, 4 * SP)), v((4 * SP, D)), v((4 * SP, D)), v((4 * SP, D), f32), v((4 * SP, D), f32),
            v((4 * D, D)), v((D, 4 * D)), v((D, D)), v(rows), v(rows), v(rows), v((4, 8, D), f32),
            v((12, 8, 256), f32), v((12, 8, 256), f32), dma((7,)), dma((7,)),
        ],
        compiler_params=pltpu.CompilerParams(vmem_limit_bytes=62 * 2**20),
        cost_estimate=pl.CostEstimate(flops=2 * 27 * 832 * 768 * 768, bytes_accessed=40 * 2**20, transcendentals=832 * 3072 * 2),
        name="mid",
    )(o, x, dy, vec, wo, wu, wd)


class Sums:
    AX, AY, AC0, ADA, ADB, AC1, AC2, AC3 = range(31, 39)

    def __init__(self, n_items, grads, outs, bufs, sems):
        self.grads, self.outs = grads, outs
        self.sums, self.crecv, self.r1, self.r2, self.r3, self.fin, self.ext = bufs
        self.g_send, self.g_recv, self.e_send, self.e_recv, self.half_sem, self.put_sem = sems
        i, f, core, stay, mine, other, far, flip = place()
        self.i, self.f, self.core, self.flip = i, f, core, flip
        xy = (i // 2) % 4
        self.xy, self.diag = xy, flip(flip(xy, 1), 2)
        self.xy_x, self.xy_y = halves(core, flip(xy, 1), flip(xy, 2)), halves(core, flip(xy, 2), flip(xy, 1))
        self.c_dev = (flip(i, 1), f)
        self.x_dev = (halves(core, flip(i, 2), flip(i, 4)), f)
        self.y_dev = (halves(core, flip(i, 4), flip(i, 2)), f)
        self.e_dev = (i, other)
        self.zs = [flip(f, 1), flip(f, 2), flip(flip(f, 1), 2)]
        self.extra = []
        bit = 8
        while bit < n_items:
            self.extra.append(bit)
            bit *= 2

    def greet(self):
        barrier = pltpu.get_barrier_semaphore()
        partners = [self.c_dev, self.x_dev, self.y_dev] + [(self.i, z) for z in self.zs]
        partners += [(self.flip(self.i, b), self.f) for b in self.extra]
        for dev in partners:
            pl.semaphore_signal(barrier, inc=1, device_id=dev, device_id_type=MESH)
        return lambda: pl.semaphore_wait(barrier, len(partners))

    @staticmethod
    def remote(src, dst, ssem, rsem, dev):
        return pltpu.make_async_remote_copy(
            src_ref=src, dst_ref=dst, send_sem=ssem, recv_sem=rsem, device_id=dev, device_id_type=MESH)

    def cols_of(self, w, half):
        width = self.sums[w].shape[-1]
        return pl.ds(pl.multiple_of(half * width, 128), width)

    def half_load(self, w):
        return pltpu.make_async_copy(
            self.grads[w].at[:, :, :, self.cols_of(w, self.core)], self.sums[w], self.half_sem.at[w])

    def rows_of(self, w):
        unit = self.sums[w].shape[2] // 3
        return (pl.ds(0, 2 * unit), pl.ds(2 * unit, unit))

    def copies(self, w, stage):
        s, base = self.sums[w], (0, 4, 20, 28)[stage]
        ra, rb = self.rows_of(w)
        found = []
        if stage == 0:
            for z in range(4):
                found.append((self.grads[w].at[z, :, :, self.cols_of(w, 1 - self.core)], self.crecv[w].at[z], self.c_dev))
        elif stage == 1:
            for z in range(4):
                found.append((s.at[z, self.xy_x, ra], self.r1[w].at[z, 0, ra], self.x_dev))
                found.append((s.at[z, self.diag, ra], self.r1[w].at[z, 1, ra], self.x_dev))
                found.append((s.at[z, self.xy_y, rb], self.r1[w].at[z, 0, rb], self.y_dev))
                found.append((s.at[z, self.diag, rb], self.r1[w].at[z, 1, rb], self.y_dev))
        elif stage == 2:
            for z in range(4):
                found.append((s.at[z, self.xy_y, ra], self.r2[w].at[z, ra], self.y_dev))
                found.append((s.at[z, self.xy_x, rb], self.r2[w].at[z, rb], self.x_dev))
        else:
            for d in range(3):
                found.append((s.at[self.zs[d], self.xy], self.r3[w].at[d], (self.i, self.zs[d])))
        return [self.remote(src, dst, self.g_send.at[w, base + n], self.g_recv.at[w, base + n], dev)
                for n, (src, dst, dev) in enumerate(found)]

    def region(self, w, at, half, piece):
        rows = self.sums[w].shape[2]
        unit = rows // 3
        start, count = at * rows, rows
        if piece == 1:
            count = 2 * unit
        elif piece == 2:
            start, count = start + 2 * unit, unit
        return self.outs[w].at[pl.ds(pl.multiple_of(start, 16), count), self.cols_of(w, half)]

    def a_copy(self, w, kind):
        at = {self.AX: self.xy, self.AY: self.xy, self.AC0: self.xy, self.ADA: self.xy_x, self.ADB: self.xy_y,
              self.AC1: self.xy_x, self.AC2: self.xy_y, self.AC3: self.diag}[kind]
        piece = {self.ADA: 1, self.ADB: 2}.get(kind, 0)
        dev = {self.AX: self.x_dev, self.AY: self.y_dev, self.ADA: self.y_dev, self.ADB: self.x_dev}.get(kind, self.c_dev)
        dst = self.region(w, at, self.core, piece)
        src = self.fin[w] if kind in (self.AX, self.AY, self.AC0) else dst
        return self.remote(src, dst, self.g_send.at[w, kind], self.g_recv.at[w, kind], dev)

    def a_arrival(self, w, kind):
        at = {self.AX: self.xy_x, self.AY: self.xy_y, self.ADA: self.diag, self.ADB: self.diag, self.AC0: self.xy,
              self.AC1: self.xy_y, self.AC2: self.xy_x, self.AC3: self.diag}[kind]
        piece = {self.ADA: 1, self.ADB: 2}.get(kind, 0)
        half = (1 - self.core) if kind in (self.AC0, self.AC1, self.AC2, self.AC3) else self.core
        ref = self.region(w, at, half, piece)
        return self.remote(ref, ref, self.g_send.at[w, kind], self.g_recv.at[w, kind], self.c_dev)

    def begin(self, w):
        self.half_load(w).start()
        for copy in self.copies(w, 0):
            copy.start()

    @staticmethod
    def plus(ref, where, other_ref, other_where):
        ref[where] = (ref[where].astype(jnp.float32) + other_ref[other_where].astype(jnp.float32)).astype(jnp.bfloat16)

    def step(self, w, stage):
        f32 = jnp.float32
        ra, rb = self.rows_of(w)
        plus, s, xy, xy_x, xy_y = self.plus, self.sums[w], self.xy, self.xy_x, self.xy_y
        for copy in self.copies(w, stage):
            copy.wait_recv()
        if stage == 0:
            self.half_load(w).wait()

            def one(n, _):
                plus(s, (n // 4, n % 4), self.crecv[w], (n // 4, n % 4))
                return 0
            lax.fori_loop(0, 16, one, 0)
        elif stage == 1:
            def one(z, _):
                plus(s, (z, xy, ra), self.r1[w], (z, 0, ra))
                plus(s, (z, xy_y, ra), self.r1[w], (z, 1, ra))
                plus(s, (z, xy, rb), self.r1[w], (z, 0, rb))
                plus(s, (z, xy_x, rb), self.r1[w], (z, 1, rb))
                return 0
            lax.fori_loop(0, 4, one, 0)
        elif stage == 2:
            def one(z, _):
                plus(s, (z, xy), self.r2[w], (z,))
                return 0
            lax.fori_loop(0, 4, one, 0)
        else:
            fin = self.fin[w]
            total = s[self.f, xy].astype(f32)
            for d in range(3):
                total = total + self.r3[w][d].astype(f32)
            fin[...] = total.astype(jnp.bfloat16)
            for n, b in enumerate(self.extra):
                copy = self.remote(fin, self.ext[w].at[n], self.e_send.at[w, n], self.e_recv.at[w, n],
                                   (self.flip(self.i, b), self.f))
                copy.start()
                copy.wait()
                fin[...] = (fin[...].astype(f32) + self.ext[w][n].astype(f32)).astype(jnp.bfloat16)
            pltpu.make_async_copy(fin, self.region(w, xy, self.core, 0), self.put_sem.at[w]).start()
            for kind in (self.AX, self.AY, self.AC0):
                self.a_copy(w, kind).start()
        if stage < 3:
            for copy in self.copies(w, stage + 1):
                copy.start()

    def gather_one(self, w):
        self.a_arrival(w, self.AX).wait_recv()
        self.a_copy(w, self.ADA).start()
        self.a_copy(w, self.AC1).start()
        self.a_arrival(w, self.AY).wait_recv()
        self.a_copy(w, self.ADB).start()
        self.a_copy(w, self.AC2).start()

    def gather_two(self, w):
        self.a_arrival(w, self.ADA).wait_recv()
        self.a_arrival(w, self.ADB).wait_recv()
        self.a_copy(w, self.AC3).start()

    def gather_three(self, w):
        for kind in (self.AC0, self.AC1, self.AC2, self.AC3):
            self.a_arrival(w, kind).wait_recv()
        pltpu.make_async_copy(self.fin[w], self.region(w, self.xy, self.core, 0), self.put_sem.at[w]).wait()

    def finish(self, w):
        for stage in range(4):
            for copy in self.copies(w, stage):
                copy.wait_send()
        for kind in range(self.AX, self.AC3 + 1):
            self.a_copy(w, kind).wait_send()


def sums_scratch(n_items, shapes):
    v = lambda shape: pltpu.VMEM(shape, jnp.bfloat16)
    dma = pltpu.SemaphoreType.DMA
    n_extra, n = 0, len(shapes)
    while 8 * 2**n_extra < n_items:
        n_extra += 1
    bufs = []
    for lead in ((4, 4), (4, 4), (4, 2), (4,), (3,), ()):
        bufs += [v(lead + s) for s in shapes]
    bufs += [v((n_extra,) + s) if n_extra else v((1, 16, 128)) for s in shapes]
    sems = [dma((n, 39)), dma((n, 39)), dma((n, max(n_extra, 1))), dma((n, max(n_extra, 1))), dma((n,)), dma((n,))]
    return bufs, sems


def split_refs(refs, n):
    return [refs[k * n : (k + 1) * n] for k in range(7)]


def back_kernel(
    n_items, idx_ref, val_ref, src_ref, q_in, k_in, v_in, o_in, do_in, lse_in, nt_in, wq_in, gd, gu, go,
    dq_out, part_out, gq_out, bias_out, gd_out, gu_out, go_out,
    q_s, k_s, v_s, o_s, do_s, lse_s, nt_s, wq_s, pk_s, pv_s, gq_s, bias_s, load_sem, out_sem, *rest,
):
    bf, f32 = jnp.bfloat16, jnp.float32
    net = Sums(n_items, (gd, gu, go), (gd_out, gu_out, go_out), split_refs(rest[:21], 3), rest[21:])
    ready = net.greet()
    loads = [pltpu.make_async_copy(a, b, load_sem.at[n]) for n, (a, b) in enumerate(
        [(q_in, q_s), (k_in, k_s), (v_in, v_s), (o_in, o_s), (do_in, do_s), (lse_in, lse_s), (nt_in, nt_s), (wq_in, wq_s)])]
    for copy in loads:
        copy.start()
    ready()
    for w in range(3):
        net.begin(w)
    for n in range(6):
        loads[n].wait()
    lane = lax.broadcasted_iota(jnp.int32, (SP, 128), 1)
    row = lax.broadcasted_iota(jnp.int32, (SP, D), 0)
    plan = ((2, 0, 0), (4, 1, 0), (6, 2, 0), (9, 0, 1), (14, 1, 1), (16, 2, 1), (18, 0, 2), (22, 1, 2))

    def one(step, _):
        for at, w, stage in plan:
            @pl.when(step == at)
            def _():
                net.step(w, stage)
        j, b = step // 6, step % 6
        cols = pl.ds(pl.multiple_of(b * 128, 128), 128)
        parts = [k_s[idx_ref[j * NK + t], :, cols] for t in range(NK)]
        valid = [jnp.where(val_ref[j * NK + t] > 0, 0.0, NEG) for t in range(NK)]
        kg = jnp.concatenate(parts, axis=0)
        vg = jnp.concatenate([v_s[idx_ref[j * NK + t], :, cols] for t in range(NK)], axis=0)
        kg_t = jnp.transpose(kg)
        q, do, o = q_s[j, :, cols], do_s[j, :, cols], o_s[j, :, cols]
        prod_t = jnp.transpose(do.astype(f32) * o.astype(f32))
        logs = lse_s[j, b]
        dk = jnp.zeros((NK * SP, 128), f32)
        dv = jnp.zeros((NK * SP, 128), f32)
        dq_t = []
        for h in range(2):
            mine = (lane < 64) if h == 0 else (lane >= 64)
            spare = 64 if h == 0 else 0
            ka = augmented_keys(parts, valid, spare, mine)
            qm = jnp.where(mine, q, jnp.zeros_like(q))
            qa = jnp.where(lane == spare, jnp.ones_like(q), qm)
            dom = jnp.where(mine, do, jnp.zeros_like(do))
            centre = jnp.sum(prod_t[h * 64 : (h + 1) * 64], axis=0, keepdims=True)
            s_t = mm(ka, qa, NT)
            da_t = mm(vg, dom, NT)
            p = jnp.exp(s_t - logs[h : h + 1])
            ds = (p * (da_t - centre)).astype(bf)
            dv = dv + mm(p.astype(bf), dom)
            dk = dk + mm(ds, qm)
            dq_t.append(mm(kg_t, ds))
        dq = jnp.transpose(jnp.concatenate([dq_t[0][:64], dq_t[1][64:]], axis=0))
        q_s[j, :, cols] = (dq * 0.125).astype(bf)
        for t in range(NK):
            pk_s[j * NK + t, :, cols] = dk[t * SP : (t + 1) * SP].astype(bf)
            pv_s[j * NK + t, :, cols] = dv[t * SP : (t + 1) * SP].astype(bf)
        return 0

    lax.fori_loop(0, 24, one, 0)
    puts = []

    def put(src, dst):
        copy = pltpu.make_async_copy(src, dst, out_sem.at[len(puts)])
        copy.start()
        puts.append(copy)

    put(q_s, dq_out)
    net.step(2, 2)

    def combine(slot, _):
        first, second = src_ref[slot], src_ref[16 + slot]
        keep_a = jnp.logical_and(row < FRAME_TOK, src_ref[32 + slot] > 0)
        keep_b = jnp.logical_and(row < FRAME_TOK, src_ref[48 + slot] > 0)
        for out, part in ((k_s, pk_s), (v_s, pv_s)):
            total = jnp.where(keep_a, part[first].astype(f32), 0.0) + jnp.where(keep_b, part[second].astype(f32), 0.0)
            out[slot] = total.astype(bf)
        return 0

    lax.fori_loop(0, 16, combine, 0)
    net.step(0, 3)
    for n in (6, 7):
        loads[n].wait()

    def slots(ref, shard):
        return ref[pl.ds(4 * shard, 4)].reshape(4 * SP, D)

    def partial_rows(shard, _):
        def tile(t, _):
            at = pl.multiple_of(t * 256, 256)
            keys = mm(slots(k_s, shard), wq_s[pl.ds(at, 256), D : 2 * D], NT)
            values = mm(slots(v_s, shard), wq_s[pl.ds(at, 256), 2 * D :], NT)
            pk_s[pl.ds(4 * shard, 4), :, pl.ds(at, 256)] = (keys + values).astype(bf).reshape(4, SP, 256)
            return 0
        lax.fori_loop(0, 3, tile, 0)
        return 0

    lax.fori_loop(0, 2, partial_rows, 0)
    net.step(1, 3)
    net.step(2, 3)
    lax.fori_loop(2, 4, partial_rows, 0)
    put(pk_s.at[pl.ds(0, 16)], part_out)
    net.gather_one(0)
    mine = place()[4]

    def grad_q(t, _):
        cols = pl.ds(pl.multiple_of(t * 256, 256), 256)
        g = mm(nt_s[mine], q_s[:, :, cols].reshape(4 * SP, 256))
        gq_s[:, :, :, cols] = g.astype(bf).reshape(4, 4, D // 16, 256)
        return 0
    lax.fori_loop(0, 3, grad_q, 0)

    def grad_kv(t, _):
        cols = pl.ds(pl.multiple_of((t % 3) * 256, 256), 256)
        for at, ref in ((0, k_s), (1, v_s)):
            @pl.when(t // 3 == at)
            def _():
                g = jnp.zeros((D, 256), f32)
                for s in range(4):
                    g = g + mm(nt_s[s], ref[4 * s : 4 * s + 4, :, cols].reshape(4 * SP, 256))
                gq_s[:, :, :, pl.ds(pl.multiple_of(D + t * 256, 256), 256)] = g.astype(bf).reshape(4, 4, D // 16, 256)
        return 0
    lax.fori_loop(0, 3, grad_kv, 0)
    net.gather_one(1)
    net.gather_two(0)
    lax.fori_loop(3, 6, grad_kv, 0)
    put(gq_s, gq_out)
    net.gather_one(2)

    def bias_sums(slot, carry):
        bias_q, bias_v = carry
        bias_v = bias_v + jnp.sum(v_s[slot].astype(f32), axis=0, keepdims=True)
        return bias_q, bias_v
    zero = jnp.zeros((1, D), f32)
    bias_q, bias_v = lax.fori_loop(0, 16, bias_sums, (zero, zero))
    for j in range(4):
        bias_q = bias_q + jnp.sum(q_s[j].astype(f32), axis=0, keepdims=True)
    bias_s[0:1, :] = bias_q
    bias_s[1:2, :] = bias_v
    bias_s[2:8, :] = jnp.zeros((6, D), f32)
    put(bias_s, bias_out)
    net.gather_two(1)
    net.gather_two(2)
    for w in range(3):
        net.gather_three(w)
    for w in range(3):
        net.finish(w)
    for copy in puts:
        copy.wait()


def back(n_items, idx, val, src, q, k, v_, o, do, lse, nt, wq, gd, gu, go):
    bf, f32 = jnp.bfloat16, jnp.float32
    S = jax.ShapeDtypeStruct
    hb = pl.BlockSpec(memory_space=pltpu.HBM)
    dma = pltpu.SemaphoreType.DMA
    v = lambda shape, dtype=bf: pltpu.VMEM(shape, dtype)
    rows = (4, SP, D)
    bufs, sems = sums_scratch(n_items, [(g.shape[2], g.shape[3] // 2) for g in (gd, gu, go)])
    return pl.pallas_call(
        functools.partial(back_kernel, n_items),
        out_shape=(S(rows, bf), S((16, SP, D), bf), S((4, 4, D // 16, 3 * D), bf), S((8, D), f32))
        + tuple(S((4 * g.shape[2], g.shape[3]), bf) for g in (gd, gu, go)),
        in_specs=[SM, SM, SM] + [hb] * 11,
        out_specs=(hb,) * 7,
        scratch_shapes=[
            v(rows), v((16, SP, D)), v((16, SP, D)), v(rows), v(rows), v((4, 6, 8, SP), f32), v((4, D, 4 * SP)),
            v((D, 3 * D)), v((24, SP, D)), v((24, SP, D)), v((4, 4, D // 16, 3 * D)), v((8, D), f32), dma((8,)), dma((4,)),
        ] + bufs + sems,
        compiler_params=pltpu.CompilerParams(
            collective_id=3, has_side_effects=True, vmem_limit_bytes=63 * 2**20),
        cost_estimate=pl.CostEstimate(
            flops=2 * 5 * 24 * 12 * SP * SP * 256, bytes_accessed=60 * 2**20, transcendentals=24 * 12 * SP * SP),
        name="back",
    )(idx, val, src, q, k, v_, o, do, lse, nt, wq, gd, gu, go)


def tail_kernel(
    n_items, gq, part, dq, x_in, dh, wq, vec, vp, bias,
    tg_out, vec_out, gq_out,
    dq_s, x_s, dh_s, wq_s, vec_s, vp_s, bias_s, mine_s, far_mine_s, far_s, near_s, far_e, vb_s,
    load_sem, out_sem, p_send, p_recv, vb_send, vb_recv, *rest,
):
    bf, f32 = jnp.bfloat16, jnp.float32
    net = Sums(n_items, (gq,), (gq_out,), split_refs(rest[:7], 1), rest[7:])
    i, f, core, stay, mine, other, far, flip = place()
    ready = net.greet()
    loads = [pltpu.make_async_copy(a, b, load_sem.at[n]) for n, (a, b) in enumerate(
        [(part.at[far], far_mine_s), (dq, dq_s), (wq.at[:, pl.ds(0, D)], wq_s), (part.at[mine], mine_s), (vec, vec_s),
         (vp, vp_s), (bias, bias_s), (x_in, x_s), (dh, dh_s)])]
    for copy in loads:
        copy.start()
    ready()

    def far_copy(j):
        return net.remote(part.at[3 - far, j], far_s.at[j], p_send.at[0, j], p_recv.at[0, j], net.c_dev)

    def near_copy(j):
        return net.remote(part.at[3 - mine, j], near_s.at[j], p_send.at[1, j], p_recv.at[1, j], net.c_dev)

    def chip_copy(j):
        return net.remote(far_mine_s.at[j], far_e.at[j], p_send.at[2, j], p_recv.at[2, j], net.e_dev)

    for j in range(4):
        far_copy(j).start()
    net.begin(0)
    for j in range(4):
        near_copy(j).start()
    loads[0].wait()
    for j in range(4):
        far_copy(j).wait_recv()
        net.plus(far_mine_s, (j,), far_s, (j,))
        chip_copy(j).start()
    net.step(0, 0)
    for n in range(1, 9):
        loads[n].wait()
    zero = jnp.zeros((1, D), f32)
    gain = vec_s[0, 0:1, :].astype(f32)
    vp_s[0, 2:3, :] = bias_s[0:1, :]
    vp_s[1, 0:1, :] = bias_s[1:2, :]

    def norm_back(j, carry):
        gains, shifts = carry
        near_copy(j).wait_recv()
        dn = mm(dq_s[j], wq_s[...], NT) + mine_s[j].astype(f32) + near_s[j].astype(f32)
        unit, scale = norm_parts(x_s[j])
        chip_copy(j).wait_recv()
        dn = dn + far_e[j].astype(f32)
        gains = gains + jnp.sum(dn * unit, axis=0, keepdims=True)
        shifts = shifts + jnp.sum(dn, axis=0, keepdims=True)
        x_s[j] = dh_s[j] + norm_grad(dn * gain, unit, scale)
        return gains, shifts

    def slot_out(j):
        return pltpu.make_async_copy(x_s.at[j], tg_out.at[j], out_sem.at[j])

    carry = (zero, zero)
    for j in range(4):
        if j == 2:
            net.step(0, 1)
        carry = norm_back(j, carry)
        slot_out(j).start()
    vp_s[0, 0:1, :] = carry[0]
    vp_s[0, 1:2, :] = carry[1]
    ring = [net.c_dev, net.x_dev, net.y_dev, (i, net.zs[0]), (i, net.zs[1])] + [(flip(i, b), f) for b in net.extra]

    def v_copy(n):
        return net.remote(vp_s, vb_s.at[n], vb_send.at[n], vb_recv.at[n], ring[n])

    def v_step(n):
        v_copy(n).wait()
        vp_s[...] = vp_s[...] + vb_s[n]
        if n + 1 < len(ring):
            v_copy(n + 1).start()

    v_copy(0).start()
    net.step(0, 2)
    v_step(0)
    v_step(1)
    net.step(0, 3)
    v_step(2)
    net.gather_one(0)
    v_step(3)
    net.gather_two(0)
    for n in range(4, len(ring)):
        v_step(n)
    vec_put = pltpu.make_async_copy(vp_s.at[f], vec_out, out_sem.at[4])
    vec_put.start()
    net.gather_three(0)
    net.finish(0)
    for j in range(4):
        far_copy(j).wait_send()
        near_copy(j).wait_send()
        chip_copy(j).wait_send()
        slot_out(j).wait()
    vec_put.wait()


def tail(n_items, gq, part, dq, x_in, dh, wq, vec, vp, bias):
    bf, f32 = jnp.bfloat16, jnp.float32
    S = jax.ShapeDtypeStruct
    hb = pl.BlockSpec(memory_space=pltpu.HBM)
    dma = pltpu.SemaphoreType.DMA
    v = lambda shape, dtype=bf: pltpu.VMEM(shape, dtype)
    rows = (4, SP, D)
    bufs, sems = sums_scratch(n_items, [(gq.shape[2], gq.shape[3] // 2)])
    steps = 5
    while 2 ** (steps - 2) < n_items:
        steps += 1
    return pl.pallas_call(
        functools.partial(tail_kernel, n_items),
        out_shape=(S(rows, f32), S((8, D), f32), S((D // 4, 3 * D), bf)),
        in_specs=[hb] * 9,
        out_specs=(hb,) * 3,
        scratch_shapes=[
            v(rows), v(rows, f32), v(rows, f32), v((D, D)), v((4, VEC_ROWS, D)), v((4, 8, D), f32), v((8, D), f32),
            v(rows), v(rows), v(rows), v(rows), v(rows), v((steps, 4, 8, D), f32),
            dma((9,)), dma((5,)), dma((3, 4)), dma((3, 4)), dma((steps,)), dma((steps,)),
        ] + bufs + sems,
        compiler_params=pltpu.CompilerParams(
            collective_id=2, has_side_effects=True, vmem_limit_bytes=60 * 2**20),
        cost_estimate=pl.CostEstimate(flops=2 * 14 * 784 * 768 * 768, bytes_accessed=60 * 2**20, transcendentals=0),
        name="tail",
    )(gq, part, dq, x_in, dh, wq, vec, vp, bias)


def on_device(
    tokens,
    cotangent,
    date_year,
    date_day,
    item_dates,
    slot_frame,
    frame_mask,
    qkv_weight,
    qkv_first,
    qkv_second,
    out_weight,
    out_first,
    out_second,
    up_weight,
    up_first,
    up_second,
    down_weight,
    down_first,
    down_second,
    vectors,
    vector_first,
    vector_second,
):
    bf, f32 = jnp.bfloat16, jnp.float32
    n_items = lax.axis_size("items")
    i, f, core, stay, mine, other, far, flip = place()
    swap = []
    for k in range(n_items):
        for z in range(4):
            if k % 2 != z // 2:
                swap.append((k * 4 + z, (k ^ 1) * 4 + 3 - z))

    def to_worker(array):
        return jnp.where(stay, array, lax.ppermute(array, ("items", "frames"), swap))

    pad = lambda a: jnp.pad(a[0], ((0, 0), (0, SP - FRAME_TOK), (0, 0)))
    item_index, is_valid = slot_items(item_dates[0], slot_frame[0], frame_mask[0])
    own_items = lax.dynamic_slice_in_dim(item_index, f * 4, 4)
    tables = key_tables(item_index, is_valid, own_items).astype(f32)
    tmp = jnp.concatenate([temporal_rows(date_year[0], date_day[0]), jnp.pad(tables[None], ((0, 3), (0, D - tables.shape[0])))])
    vec = jnp.pad(vectors.astype(bf).reshape(3, D), ((0, VEC_ROWS - 3), (0, 0)))
    q3, k4, v4, nt, x3, vec_all, tmp_own, wq, wo, wu, wd = front(
        pad(tokens), tmp, vec, jnp.asarray(spatial_rows()), qkv_weight, out_weight, up_weight, down_weight)
    tables = tmp_own[4, : 8 * NK + 64].astype(jnp.int32)
    idx, val, src = tables[: 4 * NK], tables[4 * NK : 8 * NK], tables[8 * NK :]
    k3, v3 = k4.reshape(16, SP, D), v4.reshape(16, SP, D)
    o3, lse = attn_fwd(idx, val, q3, k3, v3)
    block_out, hidden_grad, do3, down_grad, up_grad, out_grad, vector_part = mid(
        o3, x3, to_worker(pad(cotangent)), vec_all, wo, wu, wd)
    block_out = to_worker(block_out)
    blocks = lambda g: g.reshape(4, 4, g.shape[0] // 16, g.shape[1])
    dq3, part, gq, bias_part, down_sum, up_sum, out_sum = back(
        n_items, idx, val, src, q3, k3, v3, o3, do3, lse, nt, wq, blocks(down_grad), blocks(up_grad), blocks(out_grad))
    token_grad, vector_sum, qkv_sum = tail(
        n_items, gq, part.reshape(4, 4, SP, D), dq3, x3, hidden_grad, wq, vec_all, vector_part, bias_part)
    token_grad = jnp.where(
        stay, token_grad, lax.ppermute(token_grad.astype(bf), ("items", "frames"), swap).astype(f32))
    qkv_new = adamw(qkv_weight, qkv_first, qkv_second, qkv_sum.astype(f32), 0.05, 0.05)
    out_new = adamw(out_weight, out_first, out_second, out_sum.astype(f32), 0.5, 0.05)
    up_new = adamw(up_weight, up_first, up_second, up_sum.astype(f32), 0.05, 0.05)
    down_new = adamw(down_weight, down_first, down_second, down_sum.astype(f32), 0.03, 0.05)
    vector_new = adamw(vectors, vector_first, vector_second, vector_sum[:3].reshape(3 * D), 0.3, 0.0)
    cut = lambda a: a.reshape(1, 4, SP, D)[:, :, :FRAME_TOK]
    return (cut(block_out), cut(token_grad)) + qkv_new + out_new + up_new + down_new + vector_new


def solution(mesh):
    placed = (
        P("items", "frames", None, None),
        P("items", "frames", None, None),
        P("items", "frames"),
        P("items", "frames"),
        P("items", None),
        P("items", None),
        P("items", None),
        P("frames", None),
        P("frames", None),
        P("frames", None),
        P("frames", None),
        P("frames", None),
        P("frames", None),
        P("frames", None),
        P("frames", None),
        P("frames", None),
        P("frames", None),
        P("frames", None),
        P("frames", None),
        P("frames"),
        P("frames"),
        P("frames"),
    )
    return jax.shard_map(
        on_device,
        mesh=mesh,
        in_specs=placed,
        out_specs=(
            P("items", "frames", None, None),
            P("items", "frames", None, None),
            P("frames", None),
            P("frames", None),
            P("frames", None),
            P("frames", None),
            P("frames", None),
            P("frames", None),
            P("frames", None),
            P("frames", None),
            P("frames", None),
            P("frames", None),
            P("frames", None),
            P("frames", None),
            P("frames"),
            P("frames"),
            P("frames"),
        ),
        check_vma=False,
    )
```

```python
import functools

import jax
import jax.numpy as jnp
import numpy as np
from jax import lax
from jax.experimental import pallas as pl
from jax.experimental.pallas import tpu as pltpu
from jax.sharding import PartitionSpec as P

D = 768
HEADS = 12
HEAD = 64
GRID = 14
STEP = 10
FRAME_TOK = 196


beta_one = 0.9
beta_two = 0.999


def sincos(values, length_out):
    half_width = length_out // 2
    frequency = 1.0 / 10000.0 ** (jnp.arange(half_width, dtype=jnp.float32) / half_width)
    angles = values[..., None] * frequency
    return jnp.concatenate([jnp.sin(angles), jnp.cos(angles)], axis=-1)


def temporal_rows(year_values, day_values):
    dates = jnp.concatenate(
        [
            sincos((year_values - 2000).astype(jnp.float32), D // 8),
            sincos(day_values.astype(jnp.float32), D // 8),
        ],
        axis=-1,
    )
    return jnp.pad(dates, ((0, 0), (3 * D // 4, 0)))


def spatial_rows():
    half = 3 * D // 16
    frequency = (1.0 / np.float32(10000.0) ** (np.arange(half, dtype=np.float32) / np.float32(half))).astype(np.float32)
    cells = np.arange(FRAME_TOK)
    parts = []
    for values in (cells // GRID, cells % GRID):
        angles = values.astype(np.float32)[:, None] * frequency
        parts += [np.sin(angles), np.cos(angles)]
    rows = np.zeros((SP, D), np.float32)
    rows[:FRAME_TOK, : 3 * D // 4] = np.concatenate(parts, axis=-1)
    return rows


def slot_items(dates_group, frames_group, mask_group):
    item_ends = jnp.cumsum(dates_group)
    starts = item_ends - dates_group
    item_index = jnp.sum((frames_group[:, None] >= item_ends[None, :]).astype(jnp.int32), axis=1)
    is_first = jnp.any(frames_group[:, None] == starts[None, :], axis=1)
    is_valid = jnp.logical_or(mask_group > 0, is_first)
    return (item_index, is_valid)


SP = 208
NK = 6
NEG = -1e30
NT = (((1,), (1,)), ((), ()))
NN = (((1,), (0,)), ((), ()))


def mm(a, b, dims=NN):
    return lax.dot_general(a, b, dims, preferred_element_type=jnp.float32)


def augmented_keys(parts, valid, bias_lane, mine):
    row = lax.broadcasted_iota(jnp.int32, (SP, 128), 0)
    lane = lax.broadcasted_iota(jnp.int32, (SP, 128), 1)
    blocks = []
    for part, live in zip(parts, valid):
        bias = jnp.where(row >= FRAME_TOK, NEG, live).astype(jnp.bfloat16)
        blocks.append(jnp.where(mine, part, jnp.where(lane == bias_lane, bias, jnp.zeros_like(part))))
    return jnp.concatenate(blocks, axis=0)


def attention_step(step, tab_ref, q_ref, k_ref, v_ref, o_ref, lse_ref):
    lane = lax.broadcasted_iota(jnp.int32, (SP, 128), 1)
    j, b = step // 6, step % 6
    cols = pl.ds(pl.multiple_of(b * 128, 128), 128)
    parts = [k_ref[tab_ref[0, j * NK + t], :, cols] for t in range(NK)]
    valid = [jnp.where(tab_ref[0, (4 + j) * NK + t] > 0, 0.0, NEG) for t in range(NK)]
    vg = jnp.concatenate([v_ref[tab_ref[0, j * NK + t], :, cols] for t in range(NK)], axis=0)
    q = q_ref[j, :, cols]
    scores = []
    for h in range(2):
        mine = (lane < 64) if h == 0 else (lane >= 64)
        spare = 64 if h == 0 else 0
        ka = augmented_keys(parts, valid, spare, mine)
        qa = jnp.where(mine, q, jnp.where(lane == spare, jnp.ones_like(q), jnp.zeros_like(q)))
        scores.append(mm(qa, ka, NT))
    peaks = [jnp.max(s, axis=1, keepdims=True) for s in scores]
    probs = [jnp.exp(s - m) for s, m in zip(scores, peaks)]
    sums = [jnp.sum(p, axis=1, keepdims=True) for p in probs]
    outs = [mm(p.astype(jnp.bfloat16), vg) / total for p, total in zip(probs, sums)]
    o_ref[j, :, cols] = jnp.where(lane < 64, outs[0], outs[1]).astype(jnp.bfloat16)
    logs = [m + jnp.log(total) for m, total in zip(peaks, sums)]
    lse_ref[j, b] = jnp.transpose(jnp.where(lane == 0, logs[0], logs[1]))[:8]


VM = pl.BlockSpec(memory_space=pltpu.VMEM)
SM = pl.BlockSpec(memory_space=pltpu.SMEM)


def key_tables(item_index, is_valid, q_items):
    match = (q_items[:, None] == item_index[None, :]) & is_valid[None, :]
    rank = jnp.cumsum(match.astype(jnp.int32), axis=1) - 1
    count = jnp.sum(match.astype(jnp.int32), axis=1)
    place = jnp.arange(NK, dtype=jnp.int32)
    hit = match[:, None, :] & (rank[:, None, :] == place[None, :, None])
    slots = jnp.arange(item_index.shape[0], dtype=jnp.int32)
    idx = jnp.sum(jnp.where(hit, slots[None, None, :], 0), axis=2)
    val = (place[None, :] < count[:, None]).astype(jnp.int32)
    place_of = jnp.arange(4 * NK, dtype=jnp.int32)
    held = (idx.reshape(-1)[None, :] == slots[:, None]) & (val.reshape(-1)[None, :] > 0)
    first = jnp.min(jnp.where(held, place_of[None, :], 4 * NK), axis=1)
    last = jnp.max(jnp.where(held, place_of[None, :], -1), axis=1)
    has_first, has_last = first < 4 * NK, last > first
    rows = [jnp.where(has_first, first, 0), jnp.where(has_last, last, 0), has_first, has_last]
    return jnp.concatenate([idx.reshape(-1), val.reshape(-1)] + [r.astype(jnp.int32) for r in rows])


def adamw(weight, first_moment, second, gradient, step_rate, decay):
    first_new = beta_one * first_moment + (1.0 - beta_one) * gradient
    second_new = beta_two * second + (1.0 - beta_two) * gradient * gradient
    first_hat = first_new / (1.0 - beta_one**STEP)
    second_hat = second_new / (1.0 - beta_two**STEP)
    weight_new = weight - step_rate * (first_hat / (jnp.sqrt(second_hat) + 1e-08) + decay * weight)
    return (first_new, second_new, weight_new)


VEC_ROWS = 16
MESH = pl.DeviceIdType.MESH
Z, X, Y, DA, DB, C0, C1, C2, C3 = range(9)


def norm_rows(x):
    mean = jnp.mean(x, axis=-1, keepdims=True)
    centred = x - mean
    spread = jnp.mean(centred * centred, axis=-1, keepdims=True)
    return centred * lax.rsqrt(spread + 1e-06)


def place():
    i, f = lax.axis_index("items"), lax.axis_index("frames")
    core = i % 2
    upper = f // 2
    stay = core == upper
    mine = jnp.where(stay, f, 3 - f)
    other = f + 1 - 2 * (f % 2)
    far = jnp.where(stay, other, 3 - other)
    flip = lambda v, bit: v + bit - 2 * bit * ((v // bit) % 2)
    return i, f, core, stay, mine, other, far, flip


def halves(core, a, b):
    return jnp.where(core == 0, a, b)


def front_kernel(
    tok, cot, tmp, tab, vec, spatial, wq, wo, wu, wd,
    q_out, k_out, v_out, o_out, lse_out, nt_out, x_out, dy_out, vec_out, tab_out, wq_out, wo_out, wu_out, wd_out,
    t_s, tmp_s, vec_s, n_s, nt_s, q_s, k_s, v_s, o_s, lse_s, x_s, tab_s, wq_s,
    rq32, ro32, ru32, rd32, rq, ro, ru, rd, sq32, so32, su32, sd32, sq, so, su, sd,
    t_send, t_recv, m_send, m_recv, d_send, d_recv, v_send, v_recv, w_send, w_recv, z_send, z_recv,
    reg_sem, own_sem, put_sem, loc_sem, out_sem, nt_sem,
):
    bf, f32 = jnp.bfloat16, jnp.float32
    i, f, core, stay, mine, other, far, flip = place()
    c_dev = (flip(i, 1), f)
    x_dev = (halves(core, flip(i, 2), flip(i, 4)), f)
    y_dev = (halves(core, flip(i, 4), flip(i, 2)), f)
    e_dev = (i, other)
    m_dev = (flip(i, 1), 3 - f)
    xy = (i // 2) % 4
    xy_x, xy_y = halves(core, flip(xy, 1), flip(xy, 2)), halves(core, flip(xy, 2), flip(xy, 1))
    diag = flip(flip(xy, 1), 2)
    zs = [flip(f, 1), jnp.where(f < 2, 2, 1), jnp.where(f < 2, 3, 0)]

    barrier = pltpu.get_barrier_semaphore()
    partners = [c_dev, x_dev, y_dev, m_dev] + [(i, z) for z in zs]
    for dev in partners:
        pl.semaphore_signal(barrier, inc=1, device_id=dev, device_id_type=MESH)

    weights = [(wq, wq_out, rq32, rq, sq32, sq), (wo, wo_out, ro32, ro, so32, so),
               (wu, wu_out, ru32, ru, su32, su), (wd, wd_out, rd32, rd, sd32, sd)]

    def region_load(w):
        src, _, r32, _, _, _ = weights[w]
        rows, cols = r32.shape
        return pltpu.make_async_copy(
            src.at[pl.ds(pl.multiple_of(xy * rows, rows), rows), pl.ds(pl.multiple_of(core * cols, 128), cols)],
            r32, reg_sem.at[w])

    def own_load(w):
        return pltpu.make_async_copy(weights[w][0], weights[w][4], own_sem.at[w])

    def own_put(w):
        out, small = weights[w][1], weights[w][5]
        rows = small.shape[0]
        return pltpu.make_async_copy(small, out.at[pl.ds(pl.multiple_of(f * rows, rows), rows), :], put_sem.at[w])

    for w in range(4):
        region_load(w).start()
    for w in range(4):
        own_load(w).start()
    tok_load = pltpu.make_async_copy(tok, t_s.at[mine], loc_sem.at[0])
    tmp_load = pltpu.make_async_copy(tmp, tmp_s.at[mine], loc_sem.at[1])
    tab_load = pltpu.make_async_copy(tab, tab_out, loc_sem.at[5])
    cot_load = pltpu.make_async_copy(cot, dy_out, loc_sem.at[6])
    vec_load = pltpu.make_async_copy(vec, vec_s.at[f], loc_sem.at[2])

    @pl.when(stay)
    def _():
        tok_load.start()
        tmp_load.start()
        tab_load.start()

    vec_load.start()
    pl.semaphore_wait(barrier, len(partners))

    def remote(src, dst, ssem, rsem, dev):
        return pltpu.make_async_remote_copy(
            src_ref=src, dst_ref=dst, send_sem=ssem, recv_sem=rsem, device_id=dev, device_id_type=MESH)

    def tok_copy(kind, j):
        if kind == 0:
            return remote(tok.at[j], t_s.at[f, j], t_send.at[0, j], t_recv.at[0, j], m_dev)
        if kind == 3:
            return remote(t_s.at[far, j], t_s.at[far, j], t_send.at[3, j], t_recv.at[3, j], c_dev)
        return remote(t_s.at[mine, j], t_s.at[mine, j], t_send.at[kind, j], t_recv.at[kind, j],
                      c_dev if kind == 1 else e_dev)

    def tok_arrival(kind, j):
        shard = (mine, 3 - mine, far, 3 - far)[kind]
        return remote(t_s.at[shard, j], t_s.at[shard, j], t_send.at[kind, j], t_recv.at[kind, j], c_dev)

    def tmp_copy(kind):
        if kind == 0:
            return remote(tmp, tmp_s.at[f], m_send.at[0], m_recv.at[0], m_dev)
        if kind == 3:
            return remote(tmp_s.at[far], tmp_s.at[far], m_send.at[3], m_recv.at[3], c_dev)
        return remote(tmp_s.at[mine], tmp_s.at[mine], m_send.at[kind], m_recv.at[kind], c_dev if kind == 1 else e_dev)

    def tmp_arrival(kind):
        shard = (mine, 3 - mine, far, 3 - far)[kind]
        return remote(tmp_s.at[shard], tmp_s.at[shard], m_send.at[kind], m_recv.at[kind], c_dev)

    def tab_copy():
        return remote(tab, tab_out, d_send.at[4], d_recv.at[4], m_dev)

    def cot_copy(j):
        return remote(cot.at[j], dy_out.at[j], d_send.at[j], d_recv.at[j], m_dev)

    def part(w, z, at, half, piece):
        out, r = weights[w][1], weights[w][3]
        rows, cols = r.shape
        unit = rows // 3
        start = z * 4 * rows + at * rows
        if piece == 0:
            return out.at[pl.ds(pl.multiple_of(start, 16), rows), pl.ds(pl.multiple_of(half * cols, 128), cols)]
        if piece == 1:
            return out.at[pl.ds(pl.multiple_of(start, 16), 2 * unit), pl.ds(pl.multiple_of(half * cols, 128), cols)]
        return out.at[pl.ds(pl.multiple_of(start + 2 * unit, 16), unit), pl.ds(pl.multiple_of(half * cols, 128), cols)]

    def w_copy(w, d, kind):
        sems = (w_send.at[w, d, kind], w_recv.at[w, d, kind])
        z = zs[d]
        at = {X: xy, Y: xy, DA: xy_x, DB: xy_y, C0: xy, C1: xy_x, C2: xy_y, C3: diag}[kind]
        piece = {DA: 1, DB: 2}.get(kind, 0)
        dev = {X: x_dev, Y: y_dev, DA: y_dev, DB: x_dev}.get(kind, c_dev)
        ref = part(w, z, at, core, piece)
        return remote(ref, ref, *sems, dev)

    def w_arrival(w, d, kind):
        sems = (w_send.at[w, d, kind], w_recv.at[w, d, kind])
        z = zs[d]
        at = {X: xy_x, Y: xy_y, DA: diag, DB: diag, C0: xy, C1: xy_y, C2: xy_x, C3: diag}[kind]
        piece = {DA: 1, DB: 2}.get(kind, 0)
        half = (1 - core) if kind >= C0 else core
        ref = part(w, z, at, half, piece)
        return remote(ref, ref, *sems, c_dev)

    def z_copy(w, d):
        return remote(weights[w][3], part(w, f, xy, core, 0), z_send.at[w, d], z_recv.at[w, f], (i, zs[d]))

    def z_arrival(w, d):
        ref = part(w, zs[d], xy, core, 0)
        return remote(ref, ref, z_send.at[w, d], z_recv.at[w, zs[d]], (i, zs[d]))

    def w_send_region(w):
        region_load(w).wait()
        weights[w][3][...] = weights[w][2][...].astype(bf)
        for d in range(3):
            z_copy(w, d).start()

    def w_stage_one(w):
        for d in range(3):
            z_arrival(w, d).wait_recv()
            for kind in (X, Y, C0):
                w_copy(w, d, kind).start()

    def w_stage_two(w):
        for d in range(3):
            w_arrival(w, d, X).wait_recv()
            w_copy(w, d, DA).start()
            w_copy(w, d, C1).start()
            w_arrival(w, d, Y).wait_recv()
            w_copy(w, d, DB).start()
            w_copy(w, d, C2).start()

    def w_stage_three(w):
        for d in range(3):
            w_arrival(w, d, DA).wait_recv()
            w_arrival(w, d, DB).wait_recv()
            w_copy(w, d, C3).start()

    def w_stage_four(w):
        for d in range(3):
            for kind in (C0, C1, C2, C3):
                w_arrival(w, d, kind).wait_recv()

    def w_own(w):
        own_load(w).wait()
        weights[w][5][...] = weights[w][4][...].astype(bf)
        own_put(w).start()

    w_send_region(0)
    vec_load.wait()

    def v_copy(d):
        return remote(vec_s.at[f], vec_s.at[f], v_send.at[d], v_recv.at[f], (i, zs[d]))

    def v_arrival(d):
        return remote(vec_s.at[zs[d]], vec_s.at[zs[d]], v_send.at[d], v_recv.at[zs[d]], (i, zs[d]))

    for d in range(3):
        v_copy(d).start()

    @pl.when(jnp.logical_not(stay))
    def _():
        tmp_copy(0).start()
        tab_copy().start()

    @pl.when(stay)
    def _():
        tok_load.wait()
        tmp_load.wait()
        for kind in (2, 1):
            tmp_copy(kind).start()
        for j in range(4):
            tok_copy(1, j).start()

    w_own(0)
    w_stage_one(0)

    @pl.when(jnp.logical_not(stay))
    def _():
        for j in range(4):
            tok_copy(0, j).start()

    @pl.when(stay)
    def _():
        for j in range(4):
            tok_copy(2, j).start()

    for w in (1, 2, 3):
        w_own(w)
    w_stage_two(0)
    w_stage_three(0)
    w_stage_four(0)
    own_put(0).wait()
    wq_load = pltpu.make_async_copy(wq_out, wq_s, loc_sem.at[3])
    wq_load.start()
    for d in range(3):
        v_arrival(d).wait_recv()
    vec_put = pltpu.make_async_copy(vec_s, vec_out, loc_sem.at[4])
    vec_put.start()
    gain = vec_s[0, 0:1, :].astype(f32)
    shift = vec_s[0, 1:2, :].astype(f32)
    bias_q = vec_s[0, 2:3, :].astype(f32)
    bias_v = vec_s[1, 0:1, :].astype(f32)
    wq_load.wait()

    def normalise(shard):
        def slot(j, _):
            x = t_s[shard, j].astype(f32) + (spatial[...] + tmp_s[shard, pl.ds(j, 1), :])

            @pl.when(shard == mine)
            def _():
                x_s[j] = x
            n_s[j] = (norm_rows(x) * gain + shift).astype(bf)
            return 0
        lax.fori_loop(0, 4, slot, 0)

    def project(shard):
        rows = n_s[...].reshape(4 * SP, D)
        at = pl.ds(4 * shard, 4)
        def keys(t, _):
            cols = pl.ds(pl.multiple_of(t * 256, 256), 256)
            k_s[at, :, cols] = mm(rows, wq_s[:, pl.ds(pl.multiple_of(D + t * 256, 256), 256)]).astype(bf).reshape(4, SP, 256)
            v_s[at, :, cols] = (mm(rows, wq_s[:, pl.ds(pl.multiple_of(2 * D + t * 256, 256), 256)])
                                      + vec_s[1, 0:1, cols].astype(f32)).astype(bf).reshape(4, SP, 256)
            return 0
        lax.fori_loop(0, 3, keys, 0)

    def project_q(shard):
        rows = n_s[...].reshape(4 * SP, D)
        def queries(t, _):
            cols = pl.ds(pl.multiple_of(t * 256, 256), 256)
            q = (mm(rows, wq_s[:, cols]) + vec_s[0, 2:3, cols].astype(f32)).astype(bf)
            q_s[:, :, cols] = (q.astype(f32) * 0.125).astype(bf).reshape(4, SP, 256)
            return 0
        lax.fori_loop(0, 3, queries, 0)

    outs = []
    def put(src, dst):
        copy = pltpu.make_async_copy(src, dst, out_sem.at[len(outs)])
        copy.start()
        outs.append(copy)

    turned = []

    def put_shard(shard):
        n = len(turned)
        if n >= 2:
            turned[n - 2].wait()
        nt_s[n % 2] = jnp.transpose(n_s[...].reshape(4 * SP, D))
        copy = pltpu.make_async_copy(nt_s.at[n % 2], nt_out.at[shard], nt_sem.at[n % 2])
        copy.start()
        turned.append(copy)
        at = pl.ds(4 * shard, 4)
        put(k_s.at[at], k_out.at[at])
        put(v_s.at[at], v_out.at[at])

    moved = jnp.logical_not(stay)

    def arrive(kind):
        tmp_arrival(kind).wait_recv()
        if kind == 2:
            tmp_copy(3).start()
        if kind == 0:
            for then in (2, 1):
                tmp_copy(then).start()
        for j in range(4):
            tok_arrival(kind, j).wait_recv()
            if kind == 2:
                tok_copy(3, j).start()
            if kind == 0:
                for then in (2, 1):
                    tok_copy(then, j).start()

    def work(shard):
        normalise(shard)

        @pl.when(shard == mine)
        def _():
            project_q(shard)

        project(shard)
        put_shard(shard)

    stayed_here, stayed_there = jnp.where(stay, mine, 3 - mine), jnp.where(stay, far, 3 - far)

    @pl.when(moved)
    def _():
        arrive(1)

    work(stayed_here)

    @pl.when(moved)
    def _():
        arrive(0)

    @pl.when(stay)
    def _():
        arrive(1)

    for w in (1, 2, 3):
        w_send_region(w)
    work(3 - stayed_here)
    put(x_s, x_out)
    put(q_s, q_out)

    @pl.when(stay)
    def _():
        arrive(2)

    @pl.when(moved)
    def _():
        arrive(3)

    work(stayed_there)

    @pl.when(moved)
    def _():
        arrive(2)

    @pl.when(stay)
    def _():
        arrive(3)

    @pl.when(moved)
    def _():
        for j in range(4):
            cot_copy(j).start()

    @pl.when(stay)
    def _():
        cot_load.start()

    work(3 - stayed_there)

    @pl.when(stay)
    def _():
        tab_load.wait()

    @pl.when(jnp.logical_not(stay))
    def _():
        tab_copy().wait_recv()

    to_scalars = pltpu.make_async_copy(tab_out, tab_s, loc_sem.at[7])
    to_scalars.start()
    to_scalars.wait()
    plan = ((0, w_stage_one, 1), (3, w_stage_one, 2), (5, w_stage_two, 1), (8, w_stage_one, 3), (14, w_stage_two, 2), (16, w_stage_three, 1), (22, w_stage_two, 3))

    def attend(step, _):
        for at, act, w in plan:
            @pl.when(step == at)
            def _():
                act(w)
        attention_step(step, tab_s, q_s, k_s, v_s, o_s, lse_s)
        return 0

    lax.fori_loop(0, 24, attend, 0)
    put(o_s, o_out)
    put(lse_s, lse_out)
    for act, w in ((w_stage_three, 2), (w_stage_three, 3)):
        act(w)
    for w in (1, 2, 3):
        w_stage_four(w)
        own_put(w).wait()

    @pl.when(jnp.logical_not(stay))
    def _():
        tmp_copy(0).wait_send()
        tab_copy().wait_send()
        for j in range(4):
            tok_copy(0, j).wait_send()
            cot_copy(j).wait()

    @pl.when(stay)
    def _():
        cot_load.wait()

    for kind in (1, 2, 3):
        tmp_copy(kind).wait_send()
        for j in range(4):
            tok_copy(kind, j).wait_send()
    for d in range(3):
        v_copy(d).wait_send()
        for w in range(4):
            z_copy(w, d).wait_send()
            for kind in range(X, C3 + 1):
                w_copy(w, d, kind).wait_send()
    for copy in turned[2:]:
        copy.wait()
    vec_put.wait()
    for copy in outs:
        copy.wait()


def front(tok, cot, tmp, tab, vec, spatial, wq, wo, wu, wd):
    bf, f32 = jnp.bfloat16, jnp.float32
    S = jax.ShapeDtypeStruct
    hb = pl.BlockSpec(memory_space=pltpu.HBM)
    regs = [(w.shape[0] // 4, w.shape[1] // 2) for w in (wq, wo, wu, wd)]
    full = [(4 * w.shape[0], w.shape[1]) for w in (wq, wo, wu, wd)]
    dma = pltpu.SemaphoreType.DMA
    v = lambda shape, dtype=bf: pltpu.VMEM(shape, dtype)
    rows, every, stats = (4, SP, D), (16, SP, D), (4, 6, 8, SP)
    return pl.pallas_call(
        front_kernel,
        out_shape=(
            S(rows, bf), S(every, bf), S(every, bf), S(rows, bf), S(stats, f32), S((4, D, 4 * SP), bf), S(rows, f32),
            S(rows, bf), S((4, VEC_ROWS, D), bf), S(tab.shape, jnp.int32),
        ) + tuple(S(s, bf) for s in full),
        in_specs=[hb] * 5 + [VM] + [hb] * 4,
        out_specs=(hb,) * 14,
        scratch_shapes=[
            v((4,) + rows), v((4, 8, D), f32), v((4, VEC_ROWS, D)), v(rows), v((2, D, 4 * SP)), v(rows), v(every), v(every),
            v(rows), v(stats, f32), v(rows, f32), pltpu.SMEM(tab.shape, jnp.int32), v(full[0]),
        ]
        + [v(r, f32) for r in regs] + [v(r) for r in regs]
        + [v(w.shape, f32) for w in (wq, wo, wu, wd)] + [v(w.shape) for w in (wq, wo, wu, wd)]
        + [dma((4, 4)), dma((4, 4)), dma((4,)), dma((4,)), dma((5,)), dma((5,)), dma((3,)), dma((4,)), dma((4, 3, 9)),
           dma((4, 3, 9)), dma((4, 3)), dma((4, 4)), dma((4,)), dma((4,)), dma((4,)), dma((8,)), dma((16,)),
           dma((2,))],
        compiler_params=pltpu.CompilerParams(
            collective_id=1, has_side_effects=True, vmem_limit_bytes=62 * 2**20),
        cost_estimate=pl.CostEstimate(
            flops=2 * 9 * 784 * 768 * 768, bytes_accessed=40 * 2**20, transcendentals=24 * 12 * SP * SP),
        name="front",
    )(tok, cot, tmp, tab, vec, spatial, wq, wo, wu, wd)


def norm_parts(x):
    centred = x - jnp.mean(x, axis=-1, keepdims=True)
    scale = lax.rsqrt(jnp.mean(centred * centred, axis=-1, keepdims=True) + 1e-06)
    return centred * scale, scale


def norm_grad(dn, unit, scale):
    return (dn - jnp.mean(dn, axis=-1, keepdims=True) - unit * jnp.mean(dn * unit, axis=-1, keepdims=True)) * scale


def mid_kernel(
    o_in, x_in, dy_in, vec, wo, wu, wd,
    y_out, dh_out, do_out, gd_out, gu_out, go_out, vp_out,
    o_s, h_s, dy_s, vec_s, wo_s, wu_s, wd_s, n_s, nt_s, a_s, du_s, mlp_s, dn_s, gd_s, gu_s, go_s, y_s, db_s, do_s, vp_s,
    bu_s, gbu_s, in_sem, out_sem,
):
    bf, f32 = jnp.bfloat16, jnp.float32
    loads = [pltpu.make_async_copy(a, b, in_sem.at[n]) for n, (a, b) in enumerate(
        [(o_in, o_s), (wo, wo_s), (vec, vec_s), (x_in, h_s), (dy_in, dy_s), (wu, wu_s), (wd, wd_s)])]
    for copy in loads:
        copy.start()
    vp_s[...] = jnp.zeros_like(vp_s)
    zero = jnp.zeros((1, D), f32)
    for n in range(4):
        loads[n].wait()
    flat = lambda ref: ref[...].reshape(4 * SP, D)

    def branch(t, _):
        cols = pl.ds(pl.multiple_of(t * 256, 256), 256)
        out = mm(flat(o_s), wo_s[:, cols]) + vec_s[1, 1:2, cols].astype(f32)
        h_s[:, :, cols] = h_s[:, :, cols] + out.reshape(4, SP, 256)
        return 0
    lax.fori_loop(0, 3, branch, 0)
    gain, shift = vec_s[1, 2:3, :].astype(f32), vec_s[2, 0:1, :].astype(f32)

    def norm(j, _):
        unit, _scale = norm_parts(h_s[j])
        n_s[j] = (unit * gain + shift).astype(bf)
        return 0
    lax.fori_loop(0, 4, norm, 0)
    nt_s[...] = jnp.transpose(flat(n_s))
    spots = [(n, (n // 3 + 8) // 3, (n // 3 + 8) % 3, (n % 3) * 256) for n in range(12)]
    for n, z, r, at in spots:
        bu_s[n, 0:1, :] = vec_s[z, r : r + 1, at : at + 256].astype(f32)
    mlp_s[...] = jnp.zeros_like(mlp_s)
    dn_s[...] = jnp.zeros_like(dn_s)
    for n in range(4, 7):
        loads[n].wait()

    def tile(n, _):
        at = pl.multiple_of(n * 256, 256)
        cols = pl.ds(at, 256)
        low = pl.ds(pl.multiple_of((n % 3) * 256, 256), 256)
        u = mm(flat(n_s), wu_s[:, cols]) + bu_s[n, 0:1, :]
        cdf = 0.5 * (1.0 + lax.erf(u * 0.7071067811865476))
        a = (u * cdf).astype(bf)
        slope = cdf + u * (jnp.exp(u * u * -0.5) * 0.3989422804014327)
        da = mm(flat(dy_s), wd_s[cols, :], NT)
        du = (da * slope).astype(bf)
        a_s[:, low] = a
        du_s[:, low] = du
        gd_s[cols, :] = mm(jnp.transpose(a), flat(dy_s)).astype(bf)
        gu_s[:, cols] = mm(nt_s[...], du).astype(bf)
        gbu_s[n, 0:1, :] = jnp.sum(du.astype(f32), axis=0, keepdims=True)

        @pl.when(n % 3 == 2)
        def _():
            start = pl.multiple_of((n // 3) * D, D)

            def add(t, _):
                out = pl.ds(pl.multiple_of(t * 256, 256), 256)
                mlp_s[:, out] += mm(a_s[...], wd_s[pl.ds(start, D), out])
                dn_s[:, out] += mm(du_s[...], wu_s[out, pl.ds(start, D)], NT)
                return 0
            lax.fori_loop(0, 3, add, 0)
        return 0
    lax.fori_loop(0, 12, tile, 0)
    for n, z, r, at in spots:
        vp_s[z, r : r + 1, at : at + 256] = gbu_s[n, 0:1, :]
    puts = []

    def put(src, dst):
        copy = pltpu.make_async_copy(src, dst, out_sem.at[len(puts)])
        copy.start()
        puts.append(copy)

    put(gd_s, gd_out)
    put(gu_s, gu_out)
    bias_down = vec_s[2, 1:2, :].astype(f32)

    def back(j, carry):
        gains, shifts, bias_o, bias_d = carry
        rows = pl.ds(pl.multiple_of(j * SP, 16), SP)
        h = h_s[j]
        y_s[j] = (h + (mlp_s[rows, :] + bias_down)).astype(bf)
        unit, scale = norm_parts(h)
        dn = dn_s[rows, :]
        gains = gains + jnp.sum(dn * unit, axis=0, keepdims=True)
        shifts = shifts + jnp.sum(dn, axis=0, keepdims=True)
        dy = dy_s[j].astype(f32)
        dh = dy + norm_grad(dn * gain, unit, scale)
        h_s[j] = dh
        db = dh.astype(bf)
        db_s[j] = db
        bias_o = bias_o + jnp.sum(db.astype(f32), axis=0, keepdims=True)
        return gains, shifts, bias_o, bias_d + jnp.sum(dy, axis=0, keepdims=True)
    gains, shifts, bias_o, bias_d = lax.fori_loop(0, 4, back, (zero,) * 4)
    put(y_s, y_out)
    put(h_s, dh_out)
    vp_s[1, 1:2, :] = bias_o
    vp_s[1, 2:3, :] = gains
    vp_s[2, 0:1, :] = shifts
    vp_s[2, 1:2, :] = bias_d
    put(vp_s, vp_out)

    def attended(t, _):
        cols = pl.ds(pl.multiple_of(t * 256, 256), 256)
        do_s[:, :, cols] = mm(flat(db_s), wo_s[cols, :], NT).astype(bf).reshape(4, SP, 256)
        return 0
    lax.fori_loop(0, 3, attended, 0)
    put(do_s, do_out)

    def out_grad(t, _):
        cols = pl.ds(pl.multiple_of(t * 256, 256), 256)
        turned = jnp.transpose(o_s[:, :, cols].reshape(4 * SP, 256))
        go_s[cols, :] = mm(turned, flat(db_s)).astype(bf)
        return 0
    lax.fori_loop(0, 3, out_grad, 0)
    put(go_s, go_out)
    for copy in puts:
        copy.wait()


def mid(o, x, dy, vec, wo, wu, wd):
    bf, f32 = jnp.bfloat16, jnp.float32
    S = jax.ShapeDtypeStruct
    hb = pl.BlockSpec(memory_space=pltpu.HBM)
    dma = pltpu.SemaphoreType.DMA
    v = lambda shape, dtype=bf: pltpu.VMEM(shape, dtype)
    rows = (4, SP, D)
    return pl.pallas_call(
        mid_kernel,
        out_shape=(S(rows, bf), S(rows, f32), S(rows, bf), S((4 * D, D), bf), S((D, 4 * D), bf), S((D, D), bf),
                   S((4, 8, D), f32)),
        in_specs=[hb] * 7,
        out_specs=(hb,) * 7,
        scratch_shapes=[
            v(rows), v(rows, f32), v(rows), v((4, VEC_ROWS, D)), v((D, D)), v((D, 4 * D)), v((4 * D, D)),
            v(rows), v((D, 4 * SP)), v((4 * SP, D)), v((4 * SP, D)), v((4 * SP, D), f32), v((4 * SP, D), f32),
            v((4 * D, D)), v((D, 4 * D)), v((D, D)), v(rows), v(rows), v(rows), v((4, 8, D), f32),
            v((12, 8, 256), f32), v((12, 8, 256), f32), dma((7,)), dma((7,)),
        ],
        compiler_params=pltpu.CompilerParams(vmem_limit_bytes=62 * 2**20),
        cost_estimate=pl.CostEstimate(flops=2 * 27 * 832 * 768 * 768, bytes_accessed=40 * 2**20, transcendentals=832 * 3072 * 2),
        name="mid",
    )(o, x, dy, vec, wo, wu, wd)


class Sums:
    AX, AY, AC0, ADA, ADB, AC1, AC2, AC3 = range(31, 39)

    def __init__(self, n_items, grads, outs, bufs, sems):
        self.grads, self.outs = grads, outs
        self.sums, self.crecv, self.r1, self.r2, self.r3, self.fin, self.ext = bufs
        self.g_send, self.g_recv, self.e_send, self.e_recv, self.half_sem, self.put_sem = sems
        i, f, core, stay, mine, other, far, flip = place()
        self.i, self.f, self.core, self.flip = i, f, core, flip
        xy = (i // 2) % 4
        self.xy, self.diag = xy, flip(flip(xy, 1), 2)
        self.xy_x, self.xy_y = halves(core, flip(xy, 1), flip(xy, 2)), halves(core, flip(xy, 2), flip(xy, 1))
        self.c_dev = (flip(i, 1), f)
        self.x_dev = (halves(core, flip(i, 2), flip(i, 4)), f)
        self.y_dev = (halves(core, flip(i, 4), flip(i, 2)), f)
        self.e_dev = (i, other)
        self.zs = [flip(f, 1), flip(f, 2), flip(flip(f, 1), 2)]
        self.extra = []
        bit = 8
        while bit < n_items:
            self.extra.append(bit)
            bit *= 2

    def greet(self):
        barrier = pltpu.get_barrier_semaphore()
        partners = [self.c_dev, self.x_dev, self.y_dev] + [(self.i, z) for z in self.zs]
        partners += [(self.flip(self.i, b), self.f) for b in self.extra]
        for dev in partners:
            pl.semaphore_signal(barrier, inc=1, device_id=dev, device_id_type=MESH)
        return lambda: pl.semaphore_wait(barrier, len(partners))

    @staticmethod
    def remote(src, dst, ssem, rsem, dev):
        return pltpu.make_async_remote_copy(
            src_ref=src, dst_ref=dst, send_sem=ssem, recv_sem=rsem, device_id=dev, device_id_type=MESH)

    def cols_of(self, w, half):
        width = self.sums[w].shape[-1]
        return pl.ds(pl.multiple_of(half * width, 128), width)

    def half_load(self, w):
        return pltpu.make_async_copy(
            self.grads[w].at[:, :, :, self.cols_of(w, self.core)], self.sums[w], self.half_sem.at[w])

    def rows_of(self, w):
        unit = self.sums[w].shape[2] // 3
        return (pl.ds(0, 2 * unit), pl.ds(2 * unit, unit))

    def copies(self, w, stage):
        s, base = self.sums[w], (0, 4, 20, 28)[stage]
        ra, rb = self.rows_of(w)
        found = []
        if stage == 0:
            for z in range(4):
                found.append((self.grads[w].at[z, :, :, self.cols_of(w, 1 - self.core)], self.crecv[w].at[z], self.c_dev))
        elif stage == 1:
            for z in range(4):
                found.append((s.at[z, self.xy_x, ra], self.r1[w].at[z, 0, ra], self.x_dev))
                found.append((s.at[z, self.diag, ra], self.r1[w].at[z, 1, ra], self.x_dev))
                found.append((s.at[z, self.xy_y, rb], self.r1[w].at[z, 0, rb], self.y_dev))
                found.append((s.at[z, self.diag, rb], self.r1[w].at[z, 1, rb], self.y_dev))
        elif stage == 2:
            for z in range(4):
                found.append((s.at[z, self.xy_y, ra], self.r2[w].at[z, ra], self.y_dev))
                found.append((s.at[z, self.xy_x, rb], self.r2[w].at[z, rb], self.x_dev))
        else:
            for d in range(3):
                found.append((s.at[self.zs[d], self.xy], self.r3[w].at[d], (self.i, self.zs[d])))
        return [self.remote(src, dst, self.g_send.at[w, base + n], self.g_recv.at[w, base + n], dev)
                for n, (src, dst, dev) in enumerate(found)]

    def region(self, w, at, half, piece):
        rows = self.sums[w].shape[2]
        unit = rows // 3
        start, count = at * rows, rows
        if piece == 1:
            count = 2 * unit
        elif piece == 2:
            start, count = start + 2 * unit, unit
        return self.outs[w].at[pl.ds(pl.multiple_of(start, 16), count), self.cols_of(w, half)]

    def a_copy(self, w, kind):
        at = {self.AX: self.xy, self.AY: self.xy, self.AC0: self.xy, self.ADA: self.xy_x, self.ADB: self.xy_y,
              self.AC1: self.xy_x, self.AC2: self.xy_y, self.AC3: self.diag}[kind]
        piece = {self.ADA: 1, self.ADB: 2}.get(kind, 0)
        dev = {self.AX: self.x_dev, self.AY: self.y_dev, self.ADA: self.y_dev, self.ADB: self.x_dev}.get(kind, self.c_dev)
        dst = self.region(w, at, self.core, piece)
        src = self.fin[w] if kind in (self.AX, self.AY, self.AC0) else dst
        return self.remote(src, dst, self.g_send.at[w, kind], self.g_recv.at[w, kind], dev)

    def a_arrival(self, w, kind):
        at = {self.AX: self.xy_x, self.AY: self.xy_y, self.ADA: self.diag, self.ADB: self.diag, self.AC0: self.xy,
              self.AC1: self.xy_y, self.AC2: self.xy_x, self.AC3: self.diag}[kind]
        piece = {self.ADA: 1, self.ADB: 2}.get(kind, 0)
        half = (1 - self.core) if kind in (self.AC0, self.AC1, self.AC2, self.AC3) else self.core
        ref = self.region(w, at, half, piece)
        return self.remote(ref, ref, self.g_send.at[w, kind], self.g_recv.at[w, kind], self.c_dev)

    def begin(self, w):
        self.half_load(w).start()
        for copy in self.copies(w, 0):
            copy.start()

    @staticmethod
    def plus(ref, where, other_ref, other_where):
        ref[where] = (ref[where].astype(jnp.float32) + other_ref[other_where].astype(jnp.float32)).astype(jnp.bfloat16)

    def step(self, w, stage):
        f32 = jnp.float32
        ra, rb = self.rows_of(w)
        plus, s, xy, xy_x, xy_y = self.plus, self.sums[w], self.xy, self.xy_x, self.xy_y
        for copy in self.copies(w, stage):
            copy.wait_recv()
        if stage == 0:
            self.half_load(w).wait()

            def one(n, _):
                plus(s, (n // 4, n % 4), self.crecv[w], (n // 4, n % 4))
                return 0
            lax.fori_loop(0, 16, one, 0)
        elif stage == 1:
            def one(z, _):
                plus(s, (z, xy, ra), self.r1[w], (z, 0, ra))
                plus(s, (z, xy_y, ra), self.r1[w], (z, 1, ra))
                plus(s, (z, xy, rb), self.r1[w], (z, 0, rb))
                plus(s, (z, xy_x, rb), self.r1[w], (z, 1, rb))
                return 0
            lax.fori_loop(0, 4, one, 0)
        elif stage == 2:
            def one(z, _):
                plus(s, (z, xy), self.r2[w], (z,))
                return 0
            lax.fori_loop(0, 4, one, 0)
        else:
            fin = self.fin[w]
            total = s[self.f, xy].astype(f32)
            for d in range(3):
                total = total + self.r3[w][d].astype(f32)
            fin[...] = total.astype(jnp.bfloat16)
            for n, b in enumerate(self.extra):
                copy = self.remote(fin, self.ext[w].at[n], self.e_send.at[w, n], self.e_recv.at[w, n],
                                   (self.flip(self.i, b), self.f))
                copy.start()
                copy.wait()
                fin[...] = (fin[...].astype(f32) + self.ext[w][n].astype(f32)).astype(jnp.bfloat16)
            pltpu.make_async_copy(fin, self.region(w, xy, self.core, 0), self.put_sem.at[w]).start()
            for kind in (self.AX, self.AY, self.AC0):
                self.a_copy(w, kind).start()
        if stage < 3:
            for copy in self.copies(w, stage + 1):
                copy.start()

    def gather_one(self, w):
        self.a_arrival(w, self.AX).wait_recv()
        self.a_copy(w, self.ADA).start()
        self.a_copy(w, self.AC1).start()
        self.a_arrival(w, self.AY).wait_recv()
        self.a_copy(w, self.ADB).start()
        self.a_copy(w, self.AC2).start()

    def gather_two(self, w):
        self.a_arrival(w, self.ADA).wait_recv()
        self.a_arrival(w, self.ADB).wait_recv()
        self.a_copy(w, self.AC3).start()

    def gather_three(self, w):
        for kind in (self.AC0, self.AC1, self.AC2, self.AC3):
            self.a_arrival(w, kind).wait_recv()
        pltpu.make_async_copy(self.fin[w], self.region(w, self.xy, self.core, 0), self.put_sem.at[w]).wait()

    def finish(self, w):
        for stage in range(4):
            for copy in self.copies(w, stage):
                copy.wait_send()
        for kind in range(self.AX, self.AC3 + 1):
            self.a_copy(w, kind).wait_send()


def sums_scratch(n_items, shapes):
    v = lambda shape: pltpu.VMEM(shape, jnp.bfloat16)
    dma = pltpu.SemaphoreType.DMA
    n_extra, n = 0, len(shapes)
    while 8 * 2**n_extra < n_items:
        n_extra += 1
    bufs = []
    for lead in ((4, 4), (4, 4), (4, 2), (4,), (3,), ()):
        bufs += [v(lead + s) for s in shapes]
    bufs += [v((n_extra,) + s) if n_extra else v((1, 16, 128)) for s in shapes]
    sems = [dma((n, 39)), dma((n, 39)), dma((n, max(n_extra, 1))), dma((n, max(n_extra, 1))), dma((n,)), dma((n,))]
    return bufs, sems


def split_refs(refs, n):
    return [refs[k * n : (k + 1) * n] for k in range(7)]


def back_kernel(
    n_items, tab_ref, q_in, k_in, v_in, o_in, do_in, lse_in, nt_in, wq_in, gd, gu, go,
    dq_out, part_out, gq_out, bias_out, gd_out, gu_out, go_out,
    q_s, k_s, v_s, o_s, do_s, lse_s, nt_s, wq_s, pk_s, pv_s, gq_s, bias_s, load_sem, out_sem, *rest,
):
    bf, f32 = jnp.bfloat16, jnp.float32
    net = Sums(n_items, (gd, gu, go), (gd_out, gu_out, go_out), split_refs(rest[:21], 3), rest[21:])
    ready = net.greet()
    loads = [pltpu.make_async_copy(a, b, load_sem.at[n]) for n, (a, b) in enumerate(
        [(q_in, q_s), (k_in, k_s), (v_in, v_s), (o_in, o_s), (do_in, do_s), (lse_in, lse_s), (nt_in, nt_s), (wq_in, wq_s)])]
    for copy in loads:
        copy.start()
    ready()
    for w in range(3):
        net.begin(w)
    for n in range(6):
        loads[n].wait()
    lane = lax.broadcasted_iota(jnp.int32, (SP, 128), 1)
    row = lax.broadcasted_iota(jnp.int32, (SP, D), 0)
    plan = ((2, 0, 0), (4, 1, 0), (6, 2, 0), (9, 0, 1), (14, 1, 1), (16, 2, 1), (18, 0, 2), (22, 1, 2))

    def one(step, _):
        for at, w, stage in plan:
            @pl.when(step == at)
            def _():
                net.step(w, stage)
        j, b = step // 6, step % 6
        cols = pl.ds(pl.multiple_of(b * 128, 128), 128)
        parts = [k_s[tab_ref[0, j * NK + t], :, cols] for t in range(NK)]
        valid = [jnp.where(tab_ref[0, (4 + j) * NK + t] > 0, 0.0, NEG) for t in range(NK)]
        kg = jnp.concatenate(parts, axis=0)
        vg = jnp.concatenate([v_s[tab_ref[0, j * NK + t], :, cols] for t in range(NK)], axis=0)
        kg_t = jnp.transpose(kg)
        q, do, o = q_s[j, :, cols], do_s[j, :, cols], o_s[j, :, cols]
        prod_t = jnp.transpose(do.astype(f32) * o.astype(f32))
        logs = lse_s[j, b]
        dk = jnp.zeros((NK * SP, 128), f32)
        dv = jnp.zeros((NK * SP, 128), f32)
        dq_t = []
        for h in range(2):
            mine = (lane < 64) if h == 0 else (lane >= 64)
            spare = 64 if h == 0 else 0
            ka = augmented_keys(parts, valid, spare, mine)
            qm = jnp.where(mine, q, jnp.zeros_like(q))
            qa = jnp.where(lane == spare, jnp.ones_like(q), qm)
            dom = jnp.where(mine, do, jnp.zeros_like(do))
            centre = jnp.sum(prod_t[h * 64 : (h + 1) * 64], axis=0, keepdims=True)
            s_t = mm(ka, qa, NT)
            da_t = mm(vg, dom, NT)
            p = jnp.exp(s_t - logs[h : h + 1])
            ds = (p * (da_t - centre)).astype(bf)
            dv = dv + mm(p.astype(bf), dom)
            dk = dk + mm(ds, qm)
            dq_t.append(mm(kg_t, ds))
        dq = jnp.transpose(jnp.concatenate([dq_t[0][:64], dq_t[1][64:]], axis=0))
        q_s[j, :, cols] = (dq * 0.125).astype(bf)
        for t in range(NK):
            pk_s[j * NK + t, :, cols] = dk[t * SP : (t + 1) * SP].astype(bf)
            pv_s[j * NK + t, :, cols] = dv[t * SP : (t + 1) * SP].astype(bf)
        return 0

    lax.fori_loop(0, 24, one, 0)
    puts = []

    def put(src, dst):
        copy = pltpu.make_async_copy(src, dst, out_sem.at[len(puts)])
        copy.start()
        puts.append(copy)

    put(q_s, dq_out)
    net.step(2, 2)

    def combine(slot, _):
        first, second = tab_ref[0, 8 * NK + slot], tab_ref[0, 8 * NK + 16 + slot]
        keep_a = jnp.logical_and(row < FRAME_TOK, tab_ref[0, 8 * NK + 32 + slot] > 0)
        keep_b = jnp.logical_and(row < FRAME_TOK, tab_ref[0, 8 * NK + 48 + slot] > 0)
        for out, part in ((k_s, pk_s), (v_s, pv_s)):
            total = jnp.where(keep_a, part[first].astype(f32), 0.0) + jnp.where(keep_b, part[second].astype(f32), 0.0)
            out[slot] = total.astype(bf)
        return 0

    lax.fori_loop(0, 16, combine, 0)
    net.step(0, 3)
    for n in (6, 7):
        loads[n].wait()

    def slots(ref, shard):
        return ref[pl.ds(4 * shard, 4)].reshape(4 * SP, D)

    def partial_rows(shard, _):
        def tile(t, _):
            at = pl.multiple_of(t * 256, 256)
            keys = mm(slots(k_s, shard), wq_s[pl.ds(at, 256), D : 2 * D], NT)
            values = mm(slots(v_s, shard), wq_s[pl.ds(at, 256), 2 * D :], NT)
            pk_s[pl.ds(4 * shard, 4), :, pl.ds(at, 256)] = (keys + values).astype(bf).reshape(4, SP, 256)
            return 0
        lax.fori_loop(0, 3, tile, 0)
        return 0

    lax.fori_loop(0, 2, partial_rows, 0)
    net.step(1, 3)
    net.step(2, 3)
    lax.fori_loop(2, 4, partial_rows, 0)
    put(pk_s.at[pl.ds(0, 16)], part_out)
    net.gather_one(0)
    mine = place()[4]

    def grad_q(t, _):
        cols = pl.ds(pl.multiple_of(t * 256, 256), 256)
        g = mm(nt_s[mine], q_s[:, :, cols].reshape(4 * SP, 256))
        gq_s[:, :, :, cols] = g.astype(bf).reshape(4, 4, D // 16, 256)
        return 0
    lax.fori_loop(0, 3, grad_q, 0)

    def grad_kv(t, _):
        cols = pl.ds(pl.multiple_of((t % 3) * 256, 256), 256)
        for at, ref in ((0, k_s), (1, v_s)):
            @pl.when(t // 3 == at)
            def _():
                g = jnp.zeros((D, 256), f32)
                for s in range(4):
                    g = g + mm(nt_s[s], ref[4 * s : 4 * s + 4, :, cols].reshape(4 * SP, 256))
                gq_s[:, :, :, pl.ds(pl.multiple_of(D + t * 256, 256), 256)] = g.astype(bf).reshape(4, 4, D // 16, 256)
        return 0
    lax.fori_loop(0, 3, grad_kv, 0)
    net.gather_one(1)
    net.gather_two(0)
    lax.fori_loop(3, 6, grad_kv, 0)
    put(gq_s, gq_out)
    net.gather_one(2)

    def bias_sums(slot, carry):
        bias_q, bias_v = carry
        bias_v = bias_v + jnp.sum(v_s[slot].astype(f32), axis=0, keepdims=True)
        return bias_q, bias_v
    zero = jnp.zeros((1, D), f32)
    bias_q, bias_v = lax.fori_loop(0, 16, bias_sums, (zero, zero))
    for j in range(4):
        bias_q = bias_q + jnp.sum(q_s[j].astype(f32), axis=0, keepdims=True)
    bias_s[0:1, :] = bias_q
    bias_s[1:2, :] = bias_v
    bias_s[2:8, :] = jnp.zeros((6, D), f32)
    put(bias_s, bias_out)
    net.gather_two(1)
    net.gather_two(2)
    for w in range(3):
        net.gather_three(w)
    for w in range(3):
        net.finish(w)
    for copy in puts:
        copy.wait()


def back(n_items, tab, q, k, v_, o, do, lse, nt, wq, gd, gu, go):
    bf, f32 = jnp.bfloat16, jnp.float32
    S = jax.ShapeDtypeStruct
    hb = pl.BlockSpec(memory_space=pltpu.HBM)
    dma = pltpu.SemaphoreType.DMA
    v = lambda shape, dtype=bf: pltpu.VMEM(shape, dtype)
    rows = (4, SP, D)
    bufs, sems = sums_scratch(n_items, [(g.shape[2], g.shape[3] // 2) for g in (gd, gu, go)])
    return pl.pallas_call(
        functools.partial(back_kernel, n_items),
        out_shape=(S(rows, bf), S((16, SP, D), bf), S((4, 4, D // 16, 3 * D), bf), S((8, D), f32))
        + tuple(S((4 * g.shape[2], g.shape[3]), bf) for g in (gd, gu, go)),
        in_specs=[SM] + [hb] * 11,
        out_specs=(hb,) * 7,
        scratch_shapes=[
            v(rows), v((16, SP, D)), v((16, SP, D)), v(rows), v(rows), v((4, 6, 8, SP), f32), v((4, D, 4 * SP)),
            v((D, 3 * D)), v((24, SP, D)), v((24, SP, D)), v((4, 4, D // 16, 3 * D)), v((8, D), f32), dma((8,)), dma((4,)),
        ] + bufs + sems,
        compiler_params=pltpu.CompilerParams(
            collective_id=3, has_side_effects=True, vmem_limit_bytes=63 * 2**20),
        cost_estimate=pl.CostEstimate(
            flops=2 * 5 * 24 * 12 * SP * SP * 256, bytes_accessed=60 * 2**20, transcendentals=24 * 12 * SP * SP),
        name="back",
    )(tab, q, k, v_, o, do, lse, nt, wq, gd, gu, go)


def tail_kernel(
    n_items, gq, part, dq, x_in, dh, wq, vec, vp, bias,
    tg_out, vec_out, gq_out,
    dq_s, x_s, dh_s, wq_s, vec_s, vp_s, bias_s, mine_s, far_mine_s, far_s, near_s, far_e, vb_s,
    load_sem, out_sem, p_send, p_recv, vb_send, vb_recv, *rest,
):
    bf, f32 = jnp.bfloat16, jnp.float32
    net = Sums(n_items, (gq,), (gq_out,), split_refs(rest[:7], 1), rest[7:])
    i, f, core, stay, mine, other, far, flip = place()
    ready = net.greet()
    loads = [pltpu.make_async_copy(a, b, load_sem.at[n]) for n, (a, b) in enumerate(
        [(part.at[far], far_mine_s), (dq, dq_s), (wq.at[:, pl.ds(0, D)], wq_s), (part.at[mine], mine_s), (vec, vec_s),
         (vp, vp_s), (bias, bias_s), (x_in, x_s), (dh, dh_s)])]
    for copy in loads:
        copy.start()
    ready()

    def far_copy(j):
        return net.remote(part.at[3 - far, j], far_s.at[j], p_send.at[0, j], p_recv.at[0, j], net.c_dev)

    def near_copy(j):
        return net.remote(part.at[3 - mine, j], near_s.at[j], p_send.at[1, j], p_recv.at[1, j], net.c_dev)

    def chip_copy(j):
        return net.remote(far_mine_s.at[j], far_e.at[j], p_send.at[2, j], p_recv.at[2, j], net.e_dev)

    for j in range(4):
        far_copy(j).start()
    net.begin(0)
    for j in range(4):
        near_copy(j).start()
    loads[0].wait()
    for j in range(4):
        far_copy(j).wait_recv()
        net.plus(far_mine_s, (j,), far_s, (j,))
        chip_copy(j).start()
    net.step(0, 0)
    for n in range(1, 9):
        loads[n].wait()
    zero = jnp.zeros((1, D), f32)
    gain = vec_s[0, 0:1, :].astype(f32)
    vp_s[0, 2:3, :] = bias_s[0:1, :]
    vp_s[1, 0:1, :] = bias_s[1:2, :]

    def norm_back(j, carry):
        gains, shifts = carry
        near_copy(j).wait_recv()
        dn = mm(dq_s[j], wq_s[...], NT) + mine_s[j].astype(f32) + near_s[j].astype(f32)
        unit, scale = norm_parts(x_s[j])
        chip_copy(j).wait_recv()
        dn = dn + far_e[j].astype(f32)
        gains = gains + jnp.sum(dn * unit, axis=0, keepdims=True)
        shifts = shifts + jnp.sum(dn, axis=0, keepdims=True)
        x_s[j] = dh_s[j] + norm_grad(dn * gain, unit, scale)
        return gains, shifts

    def slot_out(j):
        return pltpu.make_async_copy(x_s.at[j], tg_out.at[j], out_sem.at[j])

    carry = (zero, zero)
    for j in range(4):
        if j == 2:
            net.step(0, 1)
        carry = norm_back(j, carry)
        slot_out(j).start()
    vp_s[0, 0:1, :] = carry[0]
    vp_s[0, 1:2, :] = carry[1]
    ring = [net.c_dev, net.x_dev, net.y_dev, (i, net.zs[0]), (i, net.zs[1])] + [(flip(i, b), f) for b in net.extra]

    def v_copy(n):
        return net.remote(vp_s, vb_s.at[n], vb_send.at[n], vb_recv.at[n], ring[n])

    def v_step(n):
        v_copy(n).wait()
        vp_s[...] = vp_s[...] + vb_s[n]
        if n + 1 < len(ring):
            v_copy(n + 1).start()

    v_copy(0).start()
    net.step(0, 2)
    v_step(0)
    v_step(1)
    net.step(0, 3)
    v_step(2)
    net.gather_one(0)
    v_step(3)
    net.gather_two(0)
    for n in range(4, len(ring)):
        v_step(n)
    vec_put = pltpu.make_async_copy(vp_s.at[f], vec_out, out_sem.at[4])
    vec_put.start()
    net.gather_three(0)
    net.finish(0)
    for j in range(4):
        far_copy(j).wait_send()
        near_copy(j).wait_send()
        chip_copy(j).wait_send()
        slot_out(j).wait()
    vec_put.wait()


def tail(n_items, gq, part, dq, x_in, dh, wq, vec, vp, bias):
    bf, f32 = jnp.bfloat16, jnp.float32
    S = jax.ShapeDtypeStruct
    hb = pl.BlockSpec(memory_space=pltpu.HBM)
    dma = pltpu.SemaphoreType.DMA
    v = lambda shape, dtype=bf: pltpu.VMEM(shape, dtype)
    rows = (4, SP, D)
    bufs, sems = sums_scratch(n_items, [(gq.shape[2], gq.shape[3] // 2)])
    steps = 5
    while 2 ** (steps - 2) < n_items:
        steps += 1
    return pl.pallas_call(
        functools.partial(tail_kernel, n_items),
        out_shape=(S(rows, f32), S((8, D), f32), S((D // 4, 3 * D), bf)),
        in_specs=[hb] * 9,
        out_specs=(hb,) * 3,
        scratch_shapes=[
            v(rows), v(rows, f32), v(rows, f32), v((D, D)), v((4, VEC_ROWS, D)), v((4, 8, D), f32), v((8, D), f32),
            v(rows), v(rows), v(rows), v(rows), v(rows), v((steps, 4, 8, D), f32),
            dma((9,)), dma((5,)), dma((3, 4)), dma((3, 4)), dma((steps,)), dma((steps,)),
        ] + bufs + sems,
        compiler_params=pltpu.CompilerParams(
            collective_id=2, has_side_effects=True, vmem_limit_bytes=60 * 2**20),
        cost_estimate=pl.CostEstimate(flops=2 * 14 * 784 * 768 * 768, bytes_accessed=60 * 2**20, transcendentals=0),
        name="tail",
    )(gq, part, dq, x_in, dh, wq, vec, vp, bias)


def on_device(
    tokens,
    cotangent,
    date_year,
    date_day,
    item_dates,
    slot_frame,
    frame_mask,
    qkv_weight,
    qkv_first,
    qkv_second,
    out_weight,
    out_first,
    out_second,
    up_weight,
    up_first,
    up_second,
    down_weight,
    down_first,
    down_second,
    vectors,
    vector_first,
    vector_second,
):
    bf, f32 = jnp.bfloat16, jnp.float32
    n_items = lax.axis_size("items")
    i, f, core, stay, mine, other, far, flip = place()
    swap = []
    for k in range(n_items):
        for z in range(4):
            if k % 2 != z // 2:
                swap.append((k * 4 + z, (k ^ 1) * 4 + 3 - z))

    def to_worker(array):
        return jnp.where(stay, array, lax.ppermute(array, ("items", "frames"), swap))

    pad = lambda a: jnp.pad(a[0], ((0, 0), (0, SP - FRAME_TOK), (0, 0)))
    item_index, is_valid = slot_items(item_dates[0], slot_frame[0], frame_mask[0])
    own_items = lax.dynamic_slice_in_dim(item_index, f * 4, 4)
    tables = key_tables(item_index, is_valid, own_items)
    tab = jnp.pad(tables[None], ((0, 7), (0, 128 - tables.shape[0])))
    tmp = jnp.pad(temporal_rows(date_year[0], date_day[0]), ((0, 4), (0, 0)))
    vec = jnp.pad(vectors.astype(bf).reshape(3, D), ((0, VEC_ROWS - 3), (0, 0)))
    q3, k3, v3, o3, lse, nt, x3, dy, vec_all, tab_own, wq, wo, wu, wd = front(
        pad(tokens), pad(cotangent), tmp, tab, vec, jnp.asarray(spatial_rows()),
        qkv_weight, out_weight, up_weight, down_weight)
    block_out, hidden_grad, do3, down_grad, up_grad, out_grad, vector_part = mid(
        o3, x3, dy, vec_all, wo, wu, wd)
    block_out = to_worker(block_out)
    blocks = lambda g: g.reshape(4, 4, g.shape[0] // 16, g.shape[1])
    dq3, part, gq, bias_part, down_sum, up_sum, out_sum = back(
        n_items, tab_own, q3, k3, v3, o3, do3, lse, nt, wq, blocks(down_grad), blocks(up_grad), blocks(out_grad))
    token_grad, vector_sum, qkv_sum = tail(
        n_items, gq, part.reshape(4, 4, SP, D), dq3, x3, hidden_grad, wq, vec_all, vector_part, bias_part)
    token_grad = jnp.where(
        stay, token_grad, lax.ppermute(token_grad.astype(bf), ("items", "frames"), swap).astype(f32))
    qkv_new = adamw(qkv_weight, qkv_first, qkv_second, qkv_sum.astype(f32), 0.05, 0.05)
    out_new = adamw(out_weight, out_first, out_second, out_sum.astype(f32), 0.5, 0.05)
    up_new = adamw(up_weight, up_first, up_second, up_sum.astype(f32), 0.05, 0.05)
    down_new = adamw(down_weight, down_first, down_second, down_sum.astype(f32), 0.03, 0.05)
    vector_new = adamw(vectors, vector_first, vector_second, vector_sum[:3].reshape(3 * D), 0.3, 0.0)
    cut = lambda a: a.reshape(1, 4, SP, D)[:, :, :FRAME_TOK]
    return (cut(block_out), cut(token_grad)) + qkv_new + out_new + up_new + down_new + vector_new


def solution(mesh):
    placed = (
        P("items", "frames", None, None),
        P("items", "frames", None, None),
        P("items", "frames"),
        P("items", "frames"),
        P("items", None),
        P("items", None),
        P("items", None),
        P("frames", None),
        P("frames", None),
        P("frames", None),
        P("frames", None),
        P("frames", None),
        P("frames", None),
        P("frames", None),
        P("frames", None),
        P("frames", None),
        P("frames", None),
        P("frames", None),
        P("frames", None),
        P("frames"),
        P("frames"),
        P("frames"),
    )
    return jax.shard_map(
        on_device,
        mesh=mesh,
        in_specs=placed,
        out_specs=(
            P("items", "frames", None, None),
            P("items", "frames", None, None),
            P("frames", None),
            P("frames", None),
            P("frames", None),
            P("frames", None),
            P("frames", None),
            P("frames", None),
            P("frames", None),
            P("frames", None),
            P("frames", None),
            P("frames", None),
            P("frames", None),
            P("frames", None),
            P("frames"),
            P("frames"),
            P("frames"),
        ),
        check_vma=False,
    )
```

```python
import functools

import jax
import jax.numpy as jnp
import numpy as np
from jax import lax
from jax.experimental import pallas as pl
from jax.experimental.pallas import tpu as pltpu
from jax.sharding import PartitionSpec as P

D = 768
HEADS = 12
HEAD = 64
GRID = 14
STEP = 10
FRAME_TOK = 196


beta_one = 0.9
beta_two = 0.999


def sincos(values, length_out):
    half_width = length_out // 2
    frequency = 1.0 / 10000.0 ** (jnp.arange(half_width, dtype=jnp.float32) / half_width)
    angles = values[..., None] * frequency
    return jnp.concatenate([jnp.sin(angles), jnp.cos(angles)], axis=-1)


def temporal_rows(year_values, day_values):
    dates = jnp.concatenate(
        [
            sincos((year_values - 2000).astype(jnp.float32), D // 8),
            sincos(day_values.astype(jnp.float32), D // 8),
        ],
        axis=-1,
    )
    return jnp.pad(dates, ((0, 0), (3 * D // 4, 0)))


def spatial_rows():
    half = 3 * D // 16
    frequency = (1.0 / np.float32(10000.0) ** (np.arange(half, dtype=np.float32) / np.float32(half))).astype(np.float32)
    cells = np.arange(FRAME_TOK)
    parts = []
    for values in (cells // GRID, cells % GRID):
        angles = values.astype(np.float32)[:, None] * frequency
        parts += [np.sin(angles), np.cos(angles)]
    rows = np.zeros((SP, D), np.float32)
    rows[:FRAME_TOK, : 3 * D // 4] = np.concatenate(parts, axis=-1)
    return rows


def slot_items(dates_group, frames_group, mask_group):
    item_ends = jnp.cumsum(dates_group)
    starts = item_ends - dates_group
    item_index = jnp.sum((frames_group[:, None] >= item_ends[None, :]).astype(jnp.int32), axis=1)
    is_first = jnp.any(frames_group[:, None] == starts[None, :], axis=1)
    is_valid = jnp.logical_or(mask_group > 0, is_first)
    return (item_index, is_valid)


SP = 208
NK = 6
NEG = -1e30
NT = (((1,), (1,)), ((), ()))
NN = (((1,), (0,)), ((), ()))


def mm(a, b, dims=NN):
    return lax.dot_general(a, b, dims, preferred_element_type=jnp.float32)


def augmented_keys(parts, valid, bias_lane, mine):
    row = lax.broadcasted_iota(jnp.int32, (SP, 128), 0)
    lane = lax.broadcasted_iota(jnp.int32, (SP, 128), 1)
    blocks = []
    for part, live in zip(parts, valid):
        bias = jnp.where(row >= FRAME_TOK, NEG, live).astype(jnp.bfloat16)
        blocks.append(jnp.where(mine, part, jnp.where(lane == bias_lane, bias, jnp.zeros_like(part))))
    return jnp.concatenate(blocks, axis=0)


def attention_step(step, tab_ref, q_ref, k_ref, v_ref, o_ref, lse_ref):
    lane = lax.broadcasted_iota(jnp.int32, (SP, 128), 1)
    j, b = step // 6, step % 6
    cols = pl.ds(pl.multiple_of(b * 128, 128), 128)
    parts = [k_ref[tab_ref[0, j * NK + t], :, cols] for t in range(NK)]
    valid = [jnp.where(tab_ref[0, (4 + j) * NK + t] > 0, 0.0, NEG) for t in range(NK)]
    vg = jnp.concatenate([v_ref[tab_ref[0, j * NK + t], :, cols] for t in range(NK)], axis=0)
    q = q_ref[j, :, cols]
    scores = []
    for h in range(2):
        mine = (lane < 64) if h == 0 else (lane >= 64)
        spare = 64 if h == 0 else 0
        ka = augmented_keys(parts, valid, spare, mine)
        qa = jnp.where(mine, q, jnp.where(lane == spare, jnp.ones_like(q), jnp.zeros_like(q)))
        scores.append(mm(qa, ka, NT))
    peaks = [jnp.max(s, axis=1, keepdims=True) for s in scores]
    probs = [jnp.exp(s - m) for s, m in zip(scores, peaks)]
    sums = [jnp.sum(p, axis=1, keepdims=True) for p in probs]
    outs = [mm(p.astype(jnp.bfloat16), vg) / total for p, total in zip(probs, sums)]
    o_ref[j, :, cols] = jnp.where(lane < 64, outs[0], outs[1]).astype(jnp.bfloat16)
    logs = [m + jnp.log(total) for m, total in zip(peaks, sums)]
    lse_ref[j, b] = jnp.transpose(jnp.where(lane == 0, logs[0], logs[1]))[:8]


VM = pl.BlockSpec(memory_space=pltpu.VMEM)
SM = pl.BlockSpec(memory_space=pltpu.SMEM)


def key_tables(item_index, is_valid, q_items):
    match = (q_items[:, None] == item_index[None, :]) & is_valid[None, :]
    rank = jnp.cumsum(match.astype(jnp.int32), axis=1) - 1
    count = jnp.sum(match.astype(jnp.int32), axis=1)
    place = jnp.arange(NK, dtype=jnp.int32)
    hit = match[:, None, :] & (rank[:, None, :] == place[None, :, None])
    slots = jnp.arange(item_index.shape[0], dtype=jnp.int32)
    idx = jnp.sum(jnp.where(hit, slots[None, None, :], 0), axis=2)
    val = (place[None, :] < count[:, None]).astype(jnp.int32)
    place_of = jnp.arange(4 * NK, dtype=jnp.int32)
    held = (idx.reshape(-1)[None, :] == slots[:, None]) & (val.reshape(-1)[None, :] > 0)
    first = jnp.min(jnp.where(held, place_of[None, :], 4 * NK), axis=1)
    last = jnp.max(jnp.where(held, place_of[None, :], -1), axis=1)
    has_first, has_last = first < 4 * NK, last > first
    rows = [jnp.where(has_first, first, 0), jnp.where(has_last, last, 0), has_first, has_last]
    return jnp.concatenate([idx.reshape(-1), val.reshape(-1)] + [r.astype(jnp.int32) for r in rows])


def adamw(weight, first_moment, second, gradient, step_rate, decay):
    first_new = beta_one * first_moment + (1.0 - beta_one) * gradient
    second_new = beta_two * second + (1.0 - beta_two) * gradient * gradient
    first_hat = first_new / (1.0 - beta_one**STEP)
    second_hat = second_new / (1.0 - beta_two**STEP)
    weight_new = weight - step_rate * (first_hat / (jnp.sqrt(second_hat) + 1e-08) + decay * weight)
    return (first_new, second_new, weight_new)


VEC_ROWS = 16
MESH = pl.DeviceIdType.MESH
Z, X, Y, DA, DB, C0, C1, C2, C3 = range(9)


def norm_rows(x):
    mean = jnp.mean(x, axis=-1, keepdims=True)
    centred = x - mean
    spread = jnp.mean(centred * centred, axis=-1, keepdims=True)
    return centred * lax.rsqrt(spread + 1e-06)


def place():
    i, f = lax.axis_index("items"), lax.axis_index("frames")
    core = i % 2
    upper = f // 2
    stay = core == upper
    mine = jnp.where(stay, f, 3 - f)
    other = f + 1 - 2 * (f % 2)
    far = jnp.where(stay, other, 3 - other)
    flip = lambda v, bit: v + bit - 2 * bit * ((v // bit) % 2)
    return i, f, core, stay, mine, other, far, flip


def halves(core, a, b):
    return jnp.where(core == 0, a, b)


def front_kernel(
    tok, cot, tmp, tab, vec, spatial, wq, wo, wu, wd,
    q_out, k_out, v_out, o_out, lse_out, nt_out, x_out, dy_out, vec_out, tab_out, wq_out, wo_out, wu_out, wd_out,
    t_s, tmp_s, vec_s, n_s, nt_s, q_s, k_s, v_s, o_s, lse_s, x_s, tab_s, wq_s,
    rq32, ro32, ru32, rd32, rq, ro, ru, rd, sq32, so32, su32, sd32, sq, so, su, sd,
    t_send, t_recv, m_send, m_recv, d_send, d_recv, v_send, v_recv, w_send, w_recv, z_send, z_recv,
    reg_sem, own_sem, put_sem, loc_sem, out_sem, nt_sem,
):
    bf, f32 = jnp.bfloat16, jnp.float32
    i, f, core, stay, mine, other, far, flip = place()
    c_dev = (flip(i, 1), f)
    x_dev = (halves(core, flip(i, 2), flip(i, 4)), f)
    y_dev = (halves(core, flip(i, 4), flip(i, 2)), f)
    e_dev = (i, other)
    m_dev = (flip(i, 1), 3 - f)
    xy = (i // 2) % 4
    xy_x, xy_y = halves(core, flip(xy, 1), flip(xy, 2)), halves(core, flip(xy, 2), flip(xy, 1))
    diag = flip(flip(xy, 1), 2)
    zs = [flip(f, 1), jnp.where(f < 2, 2, 1), jnp.where(f < 2, 3, 0)]

    barrier = pltpu.get_barrier_semaphore()
    partners = [c_dev, x_dev, y_dev, m_dev] + [(i, z) for z in zs]
    for dev in partners:
        pl.semaphore_signal(barrier, inc=1, device_id=dev, device_id_type=MESH)

    weights = [(wq, wq_out, rq32, rq, sq32, sq), (wo, wo_out, ro32, ro, so32, so),
               (wu, wu_out, ru32, ru, su32, su), (wd, wd_out, rd32, rd, sd32, sd)]

    def region_load(w):
        src, _, r32, _, _, _ = weights[w]
        rows, cols = r32.shape
        return pltpu.make_async_copy(
            src.at[pl.ds(pl.multiple_of(xy * rows, rows), rows), pl.ds(pl.multiple_of(core * cols, 128), cols)],
            r32, reg_sem.at[w])

    def own_load(w):
        return pltpu.make_async_copy(weights[w][0], weights[w][4], own_sem.at[w])

    def own_put(w):
        out, small = weights[w][1], weights[w][5]
        rows = small.shape[0]
        return pltpu.make_async_copy(small, out.at[pl.ds(pl.multiple_of(f * rows, rows), rows), :], put_sem.at[w])

    for w in range(4):
        region_load(w).start()
    for w in range(4):
        own_load(w).start()
    tok_load = pltpu.make_async_copy(tok, t_s.at[mine], loc_sem.at[0])
    tmp_load = pltpu.make_async_copy(tmp, tmp_s.at[mine], loc_sem.at[1])
    tab_load = pltpu.make_async_copy(tab, tab_out, loc_sem.at[5])
    cot_load = pltpu.make_async_copy(cot, dy_out, loc_sem.at[6])
    vec_load = pltpu.make_async_copy(vec, vec_s.at[f], loc_sem.at[2])

    @pl.when(stay)
    def _():
        tok_load.start()
        tmp_load.start()
        tab_load.start()

    vec_load.start()
    pl.semaphore_wait(barrier, len(partners))

    def remote(src, dst, ssem, rsem, dev):
        return pltpu.make_async_remote_copy(
            src_ref=src, dst_ref=dst, send_sem=ssem, recv_sem=rsem, device_id=dev, device_id_type=MESH)

    def tok_copy(kind, j):
        if kind == 0:
            return remote(tok.at[j], t_s.at[f, j], t_send.at[0, j], t_recv.at[0, j], m_dev)
        if kind == 3:
            return remote(t_s.at[far, j], t_s.at[far, j], t_send.at[3, j], t_recv.at[3, j], c_dev)
        return remote(t_s.at[mine, j], t_s.at[mine, j], t_send.at[kind, j], t_recv.at[kind, j],
                      c_dev if kind == 1 else e_dev)

    def tok_arrival(kind, j):
        shard = (mine, 3 - mine, far, 3 - far)[kind]
        return remote(t_s.at[shard, j], t_s.at[shard, j], t_send.at[kind, j], t_recv.at[kind, j], c_dev)

    def tmp_copy(kind):
        if kind == 0:
            return remote(tmp, tmp_s.at[f], m_send.at[0], m_recv.at[0], m_dev)
        if kind == 3:
            return remote(tmp_s.at[far], tmp_s.at[far], m_send.at[3], m_recv.at[3], c_dev)
        return remote(tmp_s.at[mine], tmp_s.at[mine], m_send.at[kind], m_recv.at[kind], c_dev if kind == 1 else e_dev)

    def tmp_arrival(kind):
        shard = (mine, 3 - mine, far, 3 - far)[kind]
        return remote(tmp_s.at[shard], tmp_s.at[shard], m_send.at[kind], m_recv.at[kind], c_dev)

    def tab_copy():
        return remote(tab, tab_out, d_send.at[4], d_recv.at[4], m_dev)

    def cot_copy(j):
        return remote(cot.at[j], dy_out.at[j], d_send.at[j], d_recv.at[j], m_dev)

    def part(w, z, at, half, piece):
        out, r = weights[w][1], weights[w][3]
        rows, cols = r.shape
        unit = rows // 3
        start = z * 4 * rows + at * rows
        if piece == 0:
            return out.at[pl.ds(pl.multiple_of(start, 16), rows), pl.ds(pl.multiple_of(half * cols, 128), cols)]
        if piece == 1:
            return out.at[pl.ds(pl.multiple_of(start, 16), 2 * unit), pl.ds(pl.multiple_of(half * cols, 128), cols)]
        return out.at[pl.ds(pl.multiple_of(start + 2 * unit, 16), unit), pl.ds(pl.multiple_of(half * cols, 128), cols)]

    def w_copy(w, d, kind):
        sems = (w_send.at[w, d, kind], w_recv.at[w, d, kind])
        z = zs[d]
        at = {X: xy, Y: xy, DA: xy_x, DB: xy_y, C0: xy, C1: xy_x, C2: xy_y, C3: diag}[kind]
        piece = {DA: 1, DB: 2}.get(kind, 0)
        dev = {X: x_dev, Y: y_dev, DA: y_dev, DB: x_dev}.get(kind, c_dev)
        ref = part(w, z, at, core, piece)
        return remote(ref, ref, *sems, dev)

    def w_arrival(w, d, kind):
        sems = (w_send.at[w, d, kind], w_recv.at[w, d, kind])
        z = zs[d]
        at = {X: xy_x, Y: xy_y, DA: diag, DB: diag, C0: xy, C1: xy_y, C2: xy_x, C3: diag}[kind]
        piece = {DA: 1, DB: 2}.get(kind, 0)
        half = (1 - core) if kind >= C0 else core
        ref = part(w, z, at, half, piece)
        return remote(ref, ref, *sems, c_dev)

    def z_copy(w, d):
        return remote(weights[w][3], part(w, f, xy, core, 0), z_send.at[w, d], z_recv.at[w, f], (i, zs[d]))

    def z_arrival(w, d):
        ref = part(w, zs[d], xy, core, 0)
        return remote(ref, ref, z_send.at[w, d], z_recv.at[w, zs[d]], (i, zs[d]))

    def w_send_region(w):
        region_load(w).wait()
        weights[w][3][...] = weights[w][2][...].astype(bf)
        for d in range(3):
            z_copy(w, d).start()

    def w_stage_one(w):
        for d in range(3):
            z_arrival(w, d).wait_recv()
            for kind in (X, Y, C0):
                w_copy(w, d, kind).start()

    def w_stage_two(w):
        for d in range(3):
            w_arrival(w, d, X).wait_recv()
            w_copy(w, d, DA).start()
            w_copy(w, d, C1).start()
            w_arrival(w, d, Y).wait_recv()
            w_copy(w, d, DB).start()
            w_copy(w, d, C2).start()

    def w_stage_three(w):
        for d in range(3):
            w_arrival(w, d, DA).wait_recv()
            w_arrival(w, d, DB).wait_recv()
            w_copy(w, d, C3).start()

    def w_stage_four(w):
        for d in range(3):
            for kind in (C0, C1, C2, C3):
                w_arrival(w, d, kind).wait_recv()

    def w_own(w):
        own_load(w).wait()
        weights[w][5][...] = weights[w][4][...].astype(bf)
        own_put(w).start()

    w_send_region(0)
    vec_load.wait()

    def v_copy(d):
        return remote(vec_s.at[f], vec_s.at[f], v_send.at[d], v_recv.at[f], (i, zs[d]))

    def v_arrival(d):
        return remote(vec_s.at[zs[d]], vec_s.at[zs[d]], v_send.at[d], v_recv.at[zs[d]], (i, zs[d]))

    for d in range(3):
        v_copy(d).start()

    @pl.when(jnp.logical_not(stay))
    def _():
        tmp_copy(0).start()
        tab_copy().start()

    @pl.when(stay)
    def _():
        tok_load.wait()
        tmp_load.wait()
        for kind in (2, 1):
            tmp_copy(kind).start()
        for j in range(4):
            tok_copy(1, j).start()

    w_own(0)
    w_stage_one(0)

    @pl.when(jnp.logical_not(stay))
    def _():
        for j in range(4):
            tok_copy(0, j).start()

    @pl.when(stay)
    def _():
        for j in range(4):
            tok_copy(2, j).start()

    for w in (1, 2, 3):
        w_own(w)
    w_stage_two(0)
    w_stage_three(0)
    w_stage_four(0)
    own_put(0).wait()
    wq_load = pltpu.make_async_copy(wq_out, wq_s, loc_sem.at[3])
    wq_load.start()
    for d in range(3):
        v_arrival(d).wait_recv()
    vec_put = pltpu.make_async_copy(vec_s, vec_out, loc_sem.at[4])
    vec_put.start()
    gain = vec_s[0, 0:1, :].astype(f32)
    shift = vec_s[0, 1:2, :].astype(f32)
    bias_q = vec_s[0, 2:3, :].astype(f32)
    bias_v = vec_s[1, 0:1, :].astype(f32)
    wq_load.wait()

    def normalise(shard):
        def slot(j, _):
            x = t_s[shard, j].astype(f32) + (spatial[...] + tmp_s[shard, pl.ds(j, 1), :])

            @pl.when(shard == mine)
            def _():
                x_s[j] = x
            n_s[j] = (norm_rows(x) * gain + shift).astype(bf)
            return 0
        lax.fori_loop(0, 4, slot, 0)

    def project(shard):
        rows = n_s[...].reshape(4 * SP, D)
        at = pl.ds(4 * shard, 4)
        def keys(t, _):
            cols = pl.ds(pl.multiple_of(t * 256, 256), 256)
            k_s[at, :, cols] = mm(rows, wq_s[:, pl.ds(pl.multiple_of(D + t * 256, 256), 256)]).astype(bf).reshape(4, SP, 256)
            v_s[at, :, cols] = (mm(rows, wq_s[:, pl.ds(pl.multiple_of(2 * D + t * 256, 256), 256)])
                                      + vec_s[1, 0:1, cols].astype(f32)).astype(bf).reshape(4, SP, 256)
            return 0
        lax.fori_loop(0, 3, keys, 0)

    def project_q(shard):
        rows = n_s[...].reshape(4 * SP, D)
        def queries(t, _):
            cols = pl.ds(pl.multiple_of(t * 256, 256), 256)
            q = (mm(rows, wq_s[:, cols]) + vec_s[0, 2:3, cols].astype(f32)).astype(bf)
            q_s[:, :, cols] = (q.astype(f32) * 0.125).astype(bf).reshape(4, SP, 256)
            return 0
        lax.fori_loop(0, 3, queries, 0)

    outs = []
    def put(src, dst):
        copy = pltpu.make_async_copy(src, dst, out_sem.at[len(outs)])
        copy.start()
        outs.append(copy)

    turned = []

    def put_shard(shard):
        n = len(turned)
        if n >= 2:
            turned[n - 2].wait()
        nt_s[n % 2] = jnp.transpose(n_s[...].reshape(4 * SP, D))
        copy = pltpu.make_async_copy(nt_s.at[n % 2], nt_out.at[shard], nt_sem.at[n % 2])
        copy.start()
        turned.append(copy)
        at = pl.ds(4 * shard, 4)
        put(k_s.at[at], k_out.at[at])
        put(v_s.at[at], v_out.at[at])

    moved = jnp.logical_not(stay)

    def arrive(kind):
        tmp_arrival(kind).wait_recv()
        if kind == 2:
            tmp_copy(3).start()
        if kind == 0:
            for then in (2, 1):
                tmp_copy(then).start()
        for j in range(4):
            tok_arrival(kind, j).wait_recv()
            if kind == 2:
                tok_copy(3, j).start()
            if kind == 0:
                for then in (2, 1):
                    tok_copy(then, j).start()

    def work(shard):
        normalise(shard)

        @pl.when(shard == mine)
        def _():
            project_q(shard)

        project(shard)
        put_shard(shard)

    stayed_here, stayed_there = jnp.where(stay, mine, 3 - mine), jnp.where(stay, far, 3 - far)

    @pl.when(moved)
    def _():
        arrive(1)

    work(stayed_here)

    @pl.when(moved)
    def _():
        arrive(0)

    @pl.when(stay)
    def _():
        arrive(1)

    for w in (1, 2, 3):
        w_send_region(w)
    work(3 - stayed_here)
    put(x_s, x_out)
    put(q_s, q_out)

    @pl.when(stay)
    def _():
        arrive(2)

    @pl.when(moved)
    def _():
        arrive(3)

    work(stayed_there)

    @pl.when(moved)
    def _():
        arrive(2)

    @pl.when(stay)
    def _():
        arrive(3)

    @pl.when(moved)
    def _():
        for j in range(4):
            cot_copy(j).start()

    @pl.when(stay)
    def _():
        cot_load.start()

    work(3 - stayed_there)

    @pl.when(stay)
    def _():
        tab_load.wait()

    @pl.when(jnp.logical_not(stay))
    def _():
        tab_copy().wait_recv()

    to_scalars = pltpu.make_async_copy(tab_out, tab_s, loc_sem.at[7])
    to_scalars.start()
    to_scalars.wait()
    plan = ((0, w_stage_one, 1), (3, w_stage_one, 2), (5, w_stage_two, 1), (8, w_stage_one, 3), (14, w_stage_two, 2), (16, w_stage_three, 1), (22, w_stage_two, 3))

    def attend(step, _):
        for at, act, w in plan:
            @pl.when(step == at)
            def _():
                act(w)
        attention_step(step, tab_s, q_s, k_s, v_s, o_s, lse_s)
        return 0

    lax.fori_loop(0, 24, attend, 0)
    put(o_s, o_out)
    put(lse_s, lse_out)
    for act, w in ((w_stage_three, 2), (w_stage_three, 3)):
        act(w)
    for w in (1, 2, 3):
        w_stage_four(w)
        own_put(w).wait()

    @pl.when(jnp.logical_not(stay))
    def _():
        tmp_copy(0).wait_send()
        tab_copy().wait_send()
        for j in range(4):
            tok_copy(0, j).wait_send()
            cot_copy(j).wait()

    @pl.when(stay)
    def _():
        cot_load.wait()

    for kind in (1, 2, 3):
        tmp_copy(kind).wait_send()
        for j in range(4):
            tok_copy(kind, j).wait_send()
    for d in range(3):
        v_copy(d).wait_send()
        for w in range(4):
            z_copy(w, d).wait_send()
            for kind in range(X, C3 + 1):
                w_copy(w, d, kind).wait_send()
    for copy in turned[2:]:
        copy.wait()
    vec_put.wait()
    for copy in outs:
        copy.wait()


def front(tok, cot, tmp, tab, vec, spatial, wq, wo, wu, wd):
    bf, f32 = jnp.bfloat16, jnp.float32
    S = jax.ShapeDtypeStruct
    hb = pl.BlockSpec(memory_space=pltpu.HBM)
    regs = [(w.shape[0] // 4, w.shape[1] // 2) for w in (wq, wo, wu, wd)]
    full = [(4 * w.shape[0], w.shape[1]) for w in (wq, wo, wu, wd)]
    dma = pltpu.SemaphoreType.DMA
    v = lambda shape, dtype=bf: pltpu.VMEM(shape, dtype)
    rows, every, stats = (4, SP, D), (16, SP, D), (4, 6, 8, SP)
    return pl.pallas_call(
        front_kernel,
        out_shape=(
            S(rows, bf), S(every, bf), S(every, bf), S(rows, bf), S(stats, f32), S((4, D, 4 * SP), bf), S(rows, f32),
            S(rows, bf), S((4, VEC_ROWS, D), bf), S(tab.shape, jnp.int32),
        ) + tuple(S(s, bf) for s in full),
        in_specs=[hb] * 5 + [VM] + [hb] * 4,
        out_specs=(hb,) * 14,
        scratch_shapes=[
            v((4,) + rows), v((4, 8, D), f32), v((4, VEC_ROWS, D)), v(rows), v((2, D, 4 * SP)), v(rows), v(every), v(every),
            v(rows), v(stats, f32), v(rows, f32), pltpu.SMEM(tab.shape, jnp.int32), v(full[0]),
        ]
        + [v(r, f32) for r in regs] + [v(r) for r in regs]
        + [v(w.shape, f32) for w in (wq, wo, wu, wd)] + [v(w.shape) for w in (wq, wo, wu, wd)]
        + [dma((4, 4)), dma((4, 4)), dma((4,)), dma((4,)), dma((5,)), dma((5,)), dma((3,)), dma((4,)), dma((4, 3, 9)),
           dma((4, 3, 9)), dma((4, 3)), dma((4, 4)), dma((4,)), dma((4,)), dma((4,)), dma((8,)), dma((16,)),
           dma((2,))],
        compiler_params=pltpu.CompilerParams(
            collective_id=1, has_side_effects=True, vmem_limit_bytes=62 * 2**20),
        cost_estimate=pl.CostEstimate(
            flops=2 * 9 * 784 * 768 * 768, bytes_accessed=40 * 2**20, transcendentals=24 * 12 * SP * SP),
        name="front",
    )(tok, cot, tmp, tab, vec, spatial, wq, wo, wu, wd)


def norm_parts(x):
    centred = x - jnp.mean(x, axis=-1, keepdims=True)
    scale = lax.rsqrt(jnp.mean(centred * centred, axis=-1, keepdims=True) + 1e-06)
    return centred * scale, scale


def norm_grad(dn, unit, scale):
    return (dn - jnp.mean(dn, axis=-1, keepdims=True) - unit * jnp.mean(dn * unit, axis=-1, keepdims=True)) * scale


def mid_kernel(
    o_in, x_in, dy_in, vec, wo, wu, wd,
    y_out, dh_out, do_out, gd_out, gu_out, go_out, vp_out,
    o_s, h_s, dy_s, vec_s, wo_s, wu_s, wd_s, n_s, nt_s, a_s, du_s, mlp_s, dn_s, gd_s, gu_s, go_s, y_s, db_s, do_s, vp_s,
    bu_s, gbu_s, in_sem, out_sem,
):
    bf, f32 = jnp.bfloat16, jnp.float32
    loads = [pltpu.make_async_copy(a, b, in_sem.at[n]) for n, (a, b) in enumerate(
        [(o_in, o_s), (wo, wo_s), (vec, vec_s), (x_in, h_s), (dy_in, dy_s), (wu, wu_s), (wd, wd_s)])]
    for copy in loads[:4]:
        copy.start()
    vp_s[...] = jnp.zeros_like(vp_s)
    zero = jnp.zeros((1, D), f32)
    for n in range(4):
        loads[n].wait()
    for copy in loads[4:]:
        copy.start()
    flat = lambda ref: ref[...].reshape(4 * SP, D)

    def branch(t, _):
        cols = pl.ds(pl.multiple_of(t * 256, 256), 256)
        out = mm(flat(o_s), wo_s[:, cols]) + vec_s[1, 1:2, cols].astype(f32)
        h_s[:, :, cols] = h_s[:, :, cols] + out.reshape(4, SP, 256)
        return 0
    lax.fori_loop(0, 3, branch, 0)
    gain, shift = vec_s[1, 2:3, :].astype(f32), vec_s[2, 0:1, :].astype(f32)

    def norm(j, _):
        unit, _scale = norm_parts(h_s[j])
        n_s[j] = (unit * gain + shift).astype(bf)
        return 0
    lax.fori_loop(0, 4, norm, 0)
    nt_s[...] = jnp.transpose(flat(n_s))
    spots = [(n, (n // 3 + 8) // 3, (n // 3 + 8) % 3, (n % 3) * 256) for n in range(12)]
    for n, z, r, at in spots:
        bu_s[n, 0:1, :] = vec_s[z, r : r + 1, at : at + 256].astype(f32)
    mlp_s[...] = jnp.zeros_like(mlp_s)
    dn_s[...] = jnp.zeros_like(dn_s)
    for n in range(4, 7):
        loads[n].wait()

    def group(g, _):
        start = pl.multiple_of(g * D, D)
        for k in range(3):
            n, low = 3 * g + k, slice(256 * k, 256 * k + 256)
            cols = pl.ds(pl.multiple_of(g * D + k * 256, 256), 256)
            u = mm(flat(n_s), wu_s[:, cols]) + bu_s[n, 0:1, :]
            cdf = 0.5 * (1.0 + lax.erf(u * 0.7071067811865476))
            a = (u * cdf).astype(bf)
            slope = cdf + u * (jnp.exp(u * u * -0.5) * 0.3989422804014327)
            da = mm(flat(dy_s), wd_s[cols, :], NT)
            du = (da * slope).astype(bf)
            a_s[:, low] = a
            du_s[:, low] = du
            gd_s[cols, :] = mm(jnp.transpose(a), flat(dy_s)).astype(bf)
            gu_s[:, cols] = mm(nt_s[...], du).astype(bf)
            gbu_s[n, 0:1, :] = jnp.sum(du.astype(f32), axis=0, keepdims=True)
        for t in range(3):
            out = slice(256 * t, 256 * t + 256)
            mlp_s[:, out] += mm(a_s[...], wd_s[pl.ds(start, D), out])
            dn_s[:, out] += mm(du_s[...], wu_s[out, pl.ds(start, D)], NT)
        return 0

    lax.fori_loop(0, 4, group, 0)
    for n, z, r, at in spots:
        vp_s[z, r : r + 1, at : at + 256] = gbu_s[n, 0:1, :]
    puts = []

    def put(src, dst):
        copy = pltpu.make_async_copy(src, dst, out_sem.at[len(puts)])
        copy.start()
        puts.append(copy)

    put(gd_s, gd_out)
    put(gu_s, gu_out)
    bias_down = vec_s[2, 1:2, :].astype(f32)

    def back(j, carry):
        gains, shifts, bias_o, bias_d = carry
        rows = pl.ds(pl.multiple_of(j * SP, 16), SP)
        h = h_s[j]
        y_s[j] = (h + (mlp_s[rows, :] + bias_down)).astype(bf)
        unit, scale = norm_parts(h)
        dn = dn_s[rows, :]
        gains = gains + jnp.sum(dn * unit, axis=0, keepdims=True)
        shifts = shifts + jnp.sum(dn, axis=0, keepdims=True)
        dy = dy_s[j].astype(f32)
        dh = dy + norm_grad(dn * gain, unit, scale)
        h_s[j] = dh
        db = dh.astype(bf)
        db_s[j] = db
        bias_o = bias_o + jnp.sum(db.astype(f32), axis=0, keepdims=True)
        return gains, shifts, bias_o, bias_d + jnp.sum(dy, axis=0, keepdims=True)
    gains, shifts, bias_o, bias_d = lax.fori_loop(0, 4, back, (zero,) * 4)
    put(y_s, y_out)
    put(h_s, dh_out)
    vp_s[1, 1:2, :] = bias_o
    vp_s[1, 2:3, :] = gains
    vp_s[2, 0:1, :] = shifts
    vp_s[2, 1:2, :] = bias_d
    put(vp_s, vp_out)

    def attended(t, _):
        cols = pl.ds(pl.multiple_of(t * 256, 256), 256)
        do_s[:, :, cols] = mm(flat(db_s), wo_s[cols, :], NT).astype(bf).reshape(4, SP, 256)
        return 0
    lax.fori_loop(0, 3, attended, 0)
    put(do_s, do_out)

    def out_grad(t, _):
        cols = pl.ds(pl.multiple_of(t * 256, 256), 256)
        turned = jnp.transpose(o_s[:, :, cols].reshape(4 * SP, 256))
        go_s[cols, :] = mm(turned, flat(db_s)).astype(bf)
        return 0
    lax.fori_loop(0, 3, out_grad, 0)
    put(go_s, go_out)
    for copy in puts:
        copy.wait()


def mid(o, x, dy, vec, wo, wu, wd):
    bf, f32 = jnp.bfloat16, jnp.float32
    S = jax.ShapeDtypeStruct
    hb = pl.BlockSpec(memory_space=pltpu.HBM)
    dma = pltpu.SemaphoreType.DMA
    v = lambda shape, dtype=bf: pltpu.VMEM(shape, dtype)
    rows = (4, SP, D)
    return pl.pallas_call(
        mid_kernel,
        out_shape=(S(rows, bf), S(rows, f32), S(rows, bf), S((4 * D, D), bf), S((D, 4 * D), bf), S((D, D), bf),
                   S((4, 8, D), f32)),
        in_specs=[hb] * 7,
        out_specs=(hb,) * 7,
        scratch_shapes=[
            v(rows), v(rows, f32), v(rows), v((4, VEC_ROWS, D)), v((D, D)), v((D, 4 * D)), v((4 * D, D)),
            v(rows), v((D, 4 * SP)), v((4 * SP, D)), v((4 * SP, D)), v((4 * SP, D), f32), v((4 * SP, D), f32),
            v((4 * D, D)), v((D, 4 * D)), v((D, D)), v(rows), v(rows), v(rows), v((4, 8, D), f32),
            v((12, 8, 256), f32), v((12, 8, 256), f32), dma((7,)), dma((7,)),
        ],
        compiler_params=pltpu.CompilerParams(vmem_limit_bytes=62 * 2**20),
        cost_estimate=pl.CostEstimate(flops=2 * 27 * 832 * 768 * 768, bytes_accessed=40 * 2**20, transcendentals=832 * 3072 * 2),
        name="mid",
    )(o, x, dy, vec, wo, wu, wd)


class Sums:
    AX, AY, AC0, ADA, ADB, AC1, AC2, AC3 = range(31, 39)

    def __init__(self, n_items, grads, outs, bufs, sems, gathers=True):
        self.gathers = gathers
        self.grads, self.outs = grads, outs
        self.sums, self.crecv, self.r1, self.r2, self.r3, self.fin, self.ext = bufs
        self.g_send, self.g_recv, self.e_send, self.e_recv, self.half_sem, self.put_sem = sems
        i, f, core, stay, mine, other, far, flip = place()
        self.i, self.f, self.core, self.flip = i, f, core, flip
        xy = (i // 2) % 4
        self.xy, self.diag = xy, flip(flip(xy, 1), 2)
        self.xy_x, self.xy_y = halves(core, flip(xy, 1), flip(xy, 2)), halves(core, flip(xy, 2), flip(xy, 1))
        self.c_dev = (flip(i, 1), f)
        self.x_dev = (halves(core, flip(i, 2), flip(i, 4)), f)
        self.y_dev = (halves(core, flip(i, 4), flip(i, 2)), f)
        self.e_dev = (i, other)
        self.zs = [flip(f, 1), flip(f, 2), flip(flip(f, 1), 2)]
        self.extra = []
        bit = 8
        while bit < n_items:
            self.extra.append(bit)
            bit *= 2

    def greet(self, *more):
        barrier = pltpu.get_barrier_semaphore()
        partners = [self.c_dev, self.x_dev, self.y_dev] + [(self.i, z) for z in self.zs]
        partners += [(self.flip(self.i, b), self.f) for b in self.extra] + list(more)
        for dev in partners:
            pl.semaphore_signal(barrier, inc=1, device_id=dev, device_id_type=MESH)
        return lambda: pl.semaphore_wait(barrier, len(partners))

    @staticmethod
    def remote(src, dst, ssem, rsem, dev):
        return pltpu.make_async_remote_copy(
            src_ref=src, dst_ref=dst, send_sem=ssem, recv_sem=rsem, device_id=dev, device_id_type=MESH)

    def cols_of(self, w, half):
        width = self.sums[w].shape[-1]
        return pl.ds(pl.multiple_of(half * width, 128), width)

    def half_load(self, w):
        return pltpu.make_async_copy(
            self.grads[w].at[:, :, :, self.cols_of(w, self.core)], self.sums[w], self.half_sem.at[w])

    def rows_of(self, w):
        unit = self.sums[w].shape[2] // 3
        return (pl.ds(0, 2 * unit), pl.ds(2 * unit, unit))

    def copies(self, w, stage):
        s, base = self.sums[w], (0, 4, 20, 28)[stage]
        ra, rb = self.rows_of(w)
        found = []
        if stage == 0:
            for z in range(4):
                found.append((self.grads[w].at[z, :, :, self.cols_of(w, 1 - self.core)], self.crecv[w].at[z], self.c_dev))
        elif stage == 1:
            for z in range(4):
                found.append((s.at[z, self.xy_x, ra], self.r1[w].at[z, 0, ra], self.x_dev))
                found.append((s.at[z, self.diag, ra], self.r1[w].at[z, 1, ra], self.x_dev))
                found.append((s.at[z, self.xy_y, rb], self.r1[w].at[z, 0, rb], self.y_dev))
                found.append((s.at[z, self.diag, rb], self.r1[w].at[z, 1, rb], self.y_dev))
        elif stage == 2:
            for z in range(4):
                found.append((s.at[z, self.xy_y, ra], self.r2[w].at[z, ra], self.y_dev))
                found.append((s.at[z, self.xy_x, rb], self.r2[w].at[z, rb], self.x_dev))
        else:
            for d in range(3):
                found.append((s.at[self.zs[d], self.xy], self.r3[w].at[d], (self.i, self.zs[d])))
        return [self.remote(src, dst, self.g_send.at[w, base + n], self.g_recv.at[w, base + n], dev)
                for n, (src, dst, dev) in enumerate(found)]

    def region(self, w, at, half, piece):
        rows = self.sums[w].shape[2]
        unit = rows // 3
        start, count = at * rows, rows
        if piece == 1:
            count = 2 * unit
        elif piece == 2:
            start, count = start + 2 * unit, unit
        return self.outs[w].at[pl.ds(pl.multiple_of(start, 16), count), self.cols_of(w, half)]

    def a_copy(self, w, kind):
        at = {self.AX: self.xy, self.AY: self.xy, self.AC0: self.xy, self.ADA: self.xy_x, self.ADB: self.xy_y,
              self.AC1: self.xy_x, self.AC2: self.xy_y, self.AC3: self.diag}[kind]
        piece = {self.ADA: 1, self.ADB: 2}.get(kind, 0)
        dev = {self.AX: self.x_dev, self.AY: self.y_dev, self.ADA: self.y_dev, self.ADB: self.x_dev}.get(kind, self.c_dev)
        dst = self.region(w, at, self.core, piece)
        src = self.fin[w] if kind in (self.AX, self.AY, self.AC0) else dst
        return self.remote(src, dst, self.g_send.at[w, kind], self.g_recv.at[w, kind], dev)

    def a_arrival(self, w, kind):
        at = {self.AX: self.xy_x, self.AY: self.xy_y, self.ADA: self.diag, self.ADB: self.diag, self.AC0: self.xy,
              self.AC1: self.xy_y, self.AC2: self.xy_x, self.AC3: self.diag}[kind]
        piece = {self.ADA: 1, self.ADB: 2}.get(kind, 0)
        half = (1 - self.core) if kind in (self.AC0, self.AC1, self.AC2, self.AC3) else self.core
        ref = self.region(w, at, half, piece)
        return self.remote(ref, ref, self.g_send.at[w, kind], self.g_recv.at[w, kind], self.c_dev)

    def begin(self, w):
        self.half_load(w).start()
        for copy in self.copies(w, 0):
            copy.start()

    @staticmethod
    def plus(ref, where, other_ref, other_where):
        ref[where] = ref[where] + other_ref[other_where]

    def step(self, w, stage):
        f32 = jnp.float32
        ra, rb = self.rows_of(w)
        plus, s, xy, xy_x, xy_y = self.plus, self.sums[w], self.xy, self.xy_x, self.xy_y
        for copy in self.copies(w, stage):
            copy.wait_recv()
        if stage == 0:
            self.half_load(w).wait()

            def one(n, _):
                plus(s, (n // 4, n % 4), self.crecv[w], (n // 4, n % 4))
                return 0
            lax.fori_loop(0, 16, one, 0)
        elif stage == 1:
            def one(z, _):
                plus(s, (z, xy, ra), self.r1[w], (z, 0, ra))
                plus(s, (z, xy_y, ra), self.r1[w], (z, 1, ra))
                plus(s, (z, xy, rb), self.r1[w], (z, 0, rb))
                plus(s, (z, xy_x, rb), self.r1[w], (z, 1, rb))
                return 0
            lax.fori_loop(0, 4, one, 0)
        elif stage == 2:
            def one(z, _):
                plus(s, (z, xy), self.r2[w], (z,))
                return 0
            lax.fori_loop(0, 4, one, 0)
        else:
            fin = self.fin[w]
            total = s[self.f, xy].astype(f32)
            for d in range(3):
                total = total + self.r3[w][d].astype(f32)
            fin[...] = total.astype(jnp.bfloat16)
            for n, b in enumerate(self.extra):
                copy = self.remote(fin, self.ext[w].at[n], self.e_send.at[w, n], self.e_recv.at[w, n],
                                   (self.flip(self.i, b), self.f))
                copy.start()
                copy.wait()
                fin[...] = (fin[...].astype(f32) + self.ext[w][n].astype(f32)).astype(jnp.bfloat16)
            if self.gathers:
                self.gather_begin(w)
            else:
                self.fin_put(w).start()
        if stage < 3:
            for copy in self.copies(w, stage + 1):
                copy.start()

    def fin_put(self, w):
        dst = self.region(w, self.xy, self.core, 0) if self.gathers else self.outs[w]
        return pltpu.make_async_copy(self.fin[w], dst, self.put_sem.at[w])

    def gather_begin(self, w):
        self.fin_put(w).start()
        for kind in (self.AX, self.AY, self.AC0):
            self.a_copy(w, kind).start()

    def gather_one(self, w):
        self.a_arrival(w, self.AX).wait_recv()
        self.a_copy(w, self.ADA).start()
        self.a_copy(w, self.AC1).start()
        self.a_arrival(w, self.AY).wait_recv()
        self.a_copy(w, self.ADB).start()
        self.a_copy(w, self.AC2).start()

    def gather_two(self, w):
        self.a_arrival(w, self.ADA).wait_recv()
        self.a_arrival(w, self.ADB).wait_recv()
        self.a_copy(w, self.AC3).start()

    def gather_three(self, w):
        for kind in (self.AC0, self.AC1, self.AC2, self.AC3):
            self.a_arrival(w, kind).wait_recv()
        self.fin_put(w).wait()

    def finish(self, w, sums=True):
        if sums:
            for stage in range(4):
                for copy in self.copies(w, stage):
                    copy.wait_send()
        if self.gathers:
            for kind in range(self.AX, self.AC3 + 1):
                self.a_copy(w, kind).wait_send()
        else:
            self.fin_put(w).wait()


def sums_scratch(n_items, shapes):
    v = lambda shape: pltpu.VMEM(shape, jnp.bfloat16)
    dma = pltpu.SemaphoreType.DMA
    n_extra, n = 0, len(shapes)
    while 8 * 2**n_extra < n_items:
        n_extra += 1
    bufs = []
    for lead in ((4, 4), (4, 4), (4, 2), (4,), (3,), ()):
        bufs += [v(lead + s) for s in shapes]
    bufs += [v((n_extra,) + s) if n_extra else v((1, 16, 128)) for s in shapes]
    sems = [dma((n, 39)), dma((n, 39)), dma((n, max(n_extra, 1))), dma((n, max(n_extra, 1))), dma((n,)), dma((n,))]
    return bufs, sems


def split_refs(refs, n):
    return [refs[k * n : (k + 1) * n] for k in range(7)]


def back_kernel(
    n_items, tab_ref, q_in, k_in, v_in, o_in, do_in, lse_in, nt_in, wq_in, y_in, gd, gu, go,
    y_out, dq_out, part_out, gq_out, bias_out, gd_out, gu_out, go_out,
    q_s, k_s, v_s, o_s, do_s, lse_s, nt_s, wq_s, pk_s, pv_s, gq_s, bias_s, load_sem, out_sem, y_send, y_recv, *rest,
):
    bf, f32 = jnp.bfloat16, jnp.float32
    net = Sums(n_items, (gd, gu, go), (gd_out, gu_out, go_out), split_refs(rest[:21], 3), rest[21:], False)
    i, f, core, stay, mine, other, far, flip = place()
    m_dev = (flip(i, 1), 3 - f)
    ready = net.greet(m_dev)
    loads = [pltpu.make_async_copy(a, b, load_sem.at[n]) for n, (a, b) in enumerate(
        [(q_in, q_s), (k_in, k_s), (v_in, v_s), (o_in, o_s), (do_in, do_s), (lse_in, lse_s), (nt_in, nt_s), (wq_in, wq_s)])]
    for copy in loads[:6]:
        copy.start()
    ready()
    for w in range(3):
        net.begin(w)
    y_stay = pltpu.make_async_copy(y_in, y_out, y_send.at[0])

    def y_copy(j):
        return net.remote(y_in.at[j], y_out.at[j], y_send.at[j], y_recv.at[j], m_dev)

    @pl.when(stay)
    def _():
        y_stay.start()

    @pl.when(jnp.logical_not(stay))
    def _():
        for j in range(4):
            y_copy(j).start()

    for n in range(6):
        loads[n].wait()
    for copy in loads[6:]:
        copy.start()
    lane = lax.broadcasted_iota(jnp.int32, (SP, 128), 1)
    row = lax.broadcasted_iota(jnp.int32, (SP, D), 0)
    plan = ((1, 0, 0), (2, 1, 0), (3, 2, 0), (5, 0, 1), (7, 1, 1), (8, 2, 1), (9, 0, 2), (11, 1, 2))

    def attend_back(step):
        j, b = step // 6, step % 6
        cols = pl.ds(pl.multiple_of(b * 128, 128), 128)
        parts = [k_s[tab_ref[0, j * NK + t], :, cols] for t in range(NK)]
        valid = [jnp.where(tab_ref[0, (4 + j) * NK + t] > 0, 0.0, NEG) for t in range(NK)]
        kg = jnp.concatenate(parts, axis=0)
        vg = jnp.concatenate([v_s[tab_ref[0, j * NK + t], :, cols] for t in range(NK)], axis=0)
        kg_t = jnp.transpose(kg)
        q, do, o = q_s[j, :, cols], do_s[j, :, cols], o_s[j, :, cols]
        prod_t = jnp.transpose(do.astype(f32) * o.astype(f32))
        logs = lse_s[j, b]
        dk = jnp.zeros((NK * SP, 128), f32)
        dv = jnp.zeros((NK * SP, 128), f32)
        dq_t = []
        for h in range(2):
            mine = (lane < 64) if h == 0 else (lane >= 64)
            spare = 64 if h == 0 else 0
            ka = augmented_keys(parts, valid, spare, mine)
            qm = jnp.where(mine, q, jnp.zeros_like(q))
            qa = jnp.where(lane == spare, jnp.ones_like(q), qm)
            dom = jnp.where(mine, do, jnp.zeros_like(do))
            centre = jnp.sum(prod_t[h * 64 : (h + 1) * 64], axis=0, keepdims=True)
            s_t = mm(ka, qa, NT)
            da_t = mm(vg, dom, NT)
            p = jnp.exp(s_t - logs[h : h + 1])
            ds = (p * (da_t - centre)).astype(bf)
            dv = dv + mm(p.astype(bf), dom)
            dk = dk + mm(ds, qm)
            dq_t.append(mm(kg_t, ds))
        dq = jnp.transpose(jnp.concatenate([dq_t[0][:64], dq_t[1][64:]], axis=0))
        q_s[j, :, cols] = (dq * 0.125).astype(bf)
        for t in range(NK):
            pk_s[j * NK + t, :, cols] = dk[t * SP : (t + 1) * SP].astype(bf)
            pv_s[j * NK + t, :, cols] = dv[t * SP : (t + 1) * SP].astype(bf)

    def one(step, _):
        for at, w, stage in plan:
            @pl.when(step == at)
            def _():
                net.step(w, stage)
        for half in range(2):
            attend_back(2 * step + half)
        return 0

    lax.fori_loop(0, 12, one, 0)
    puts = []

    def put(src, dst):
        copy = pltpu.make_async_copy(src, dst, out_sem.at[len(puts)])
        copy.start()
        puts.append(copy)

    put(q_s, dq_out)
    net.step(2, 2)

    def combine(slot, _):
        first, second = tab_ref[0, 8 * NK + slot], tab_ref[0, 8 * NK + 16 + slot]
        keep_a = jnp.logical_and(row < FRAME_TOK, tab_ref[0, 8 * NK + 32 + slot] > 0)
        keep_b = jnp.logical_and(row < FRAME_TOK, tab_ref[0, 8 * NK + 48 + slot] > 0)
        for out, part in ((k_s, pk_s), (v_s, pv_s)):
            total = jnp.where(keep_a, part[first].astype(f32), 0.0) + jnp.where(keep_b, part[second].astype(f32), 0.0)
            out[slot] = total.astype(bf)
        return 0

    lax.fori_loop(0, 16, combine, 0)
    net.step(0, 3)
    for n in (6, 7):
        loads[n].wait()

    def slots(ref, shard):
        return ref[pl.ds(4 * shard, 4)].reshape(4 * SP, D)

    def partial_rows(shard, _):
        def tile(t, _):
            at = pl.multiple_of(t * 256, 256)
            keys = mm(slots(k_s, shard), wq_s[pl.ds(at, 256), D : 2 * D], NT)
            values = mm(slots(v_s, shard), wq_s[pl.ds(at, 256), 2 * D :], NT)
            pk_s[pl.ds(4 * shard, 4), :, pl.ds(at, 256)] = (keys + values).astype(bf).reshape(4, SP, 256)
            return 0
        lax.fori_loop(0, 3, tile, 0)
        return 0

    lax.fori_loop(0, 2, partial_rows, 0)
    net.step(1, 3)
    net.step(2, 3)
    lax.fori_loop(2, 4, partial_rows, 0)
    put(pk_s.at[pl.ds(0, 16)], part_out)

    def grad_q(t, _):
        cols = pl.ds(pl.multiple_of(t * 256, 256), 256)
        g = mm(nt_s[mine], q_s[:, :, cols].reshape(4 * SP, 256))
        gq_s[:, :, :, cols] = g.astype(bf).reshape(4, 4, D // 16, 256)
        return 0
    lax.fori_loop(0, 3, grad_q, 0)

    def grad_kv(t, _):
        cols = pl.ds(pl.multiple_of((t % 3) * 256, 256), 256)
        for at, ref in ((0, k_s), (1, v_s)):
            @pl.when(t // 3 == at)
            def _():
                g = jnp.zeros((D, 256), f32)
                for s in range(4):
                    g = g + mm(nt_s[s], ref[4 * s : 4 * s + 4, :, cols].reshape(4 * SP, 256))
                gq_s[:, :, :, pl.ds(pl.multiple_of(D + t * 256, 256), 256)] = g.astype(bf).reshape(4, 4, D // 16, 256)
        return 0
    lax.fori_loop(0, 3, grad_kv, 0)
    lax.fori_loop(3, 6, grad_kv, 0)
    put(gq_s, gq_out)

    def bias_sums(slot, carry):
        bias_q, bias_v = carry
        bias_v = bias_v + jnp.sum(v_s[slot].astype(f32), axis=0, keepdims=True)
        return bias_q, bias_v
    zero = jnp.zeros((1, D), f32)
    bias_q, bias_v = lax.fori_loop(0, 16, bias_sums, (zero, zero))
    for j in range(4):
        bias_q = bias_q + jnp.sum(q_s[j].astype(f32), axis=0, keepdims=True)
    bias_s[0:1, :] = bias_q
    bias_s[1:2, :] = bias_v
    bias_s[2:8, :] = jnp.zeros((6, D), f32)
    put(bias_s, bias_out)
    for w in range(3):
        net.finish(w)

    @pl.when(stay)
    def _():
        y_stay.wait()

    @pl.when(jnp.logical_not(stay))
    def _():
        for j in range(4):
            y_copy(j).wait()

    for copy in puts:
        copy.wait()


def back(n_items, tab, q, k, v_, o, do, lse, nt, wq, y, gd, gu, go):
    bf, f32 = jnp.bfloat16, jnp.float32
    S = jax.ShapeDtypeStruct
    hb = pl.BlockSpec(memory_space=pltpu.HBM)
    dma = pltpu.SemaphoreType.DMA
    v = lambda shape, dtype=bf: pltpu.VMEM(shape, dtype)
    rows = (4, SP, D)
    bufs, sems = sums_scratch(n_items, [(g.shape[2], g.shape[3] // 2) for g in (gd, gu, go)])
    return pl.pallas_call(
        functools.partial(back_kernel, n_items),
        out_shape=(S(rows, bf), S(rows, bf), S((16, SP, D), bf), S((4, 4, D // 16, 3 * D), bf), S((8, D), f32))
        + tuple(S((g.shape[2], g.shape[3] // 2), bf) for g in (gd, gu, go)),
        in_specs=[SM] + [hb] * 12,
        out_specs=(hb,) * 8,
        scratch_shapes=[
            v(rows), v((16, SP, D)), v((16, SP, D)), v(rows), v(rows), v((4, 6, 8, SP), f32), v((4, D, 4 * SP)),
            v((D, 3 * D)), v((24, SP, D)), v((24, SP, D)), v((4, 4, D // 16, 3 * D)), v((8, D), f32), dma((8,)), dma((4,)), dma((4,)), dma((4,)),
        ] + bufs + sems,
        compiler_params=pltpu.CompilerParams(
            collective_id=3, has_side_effects=True, vmem_limit_bytes=63 * 2**20),
        cost_estimate=pl.CostEstimate(
            flops=2 * 5 * 24 * 12 * SP * SP * 256, bytes_accessed=60 * 2**20, transcendentals=24 * 12 * SP * SP),
        name="back",
    )(tab, q, k, v_, o, do, lse, nt, wq, y, gd, gu, go)


def tail_kernel(
    n_items, gq, part, dq, x_in, dh, wq, vec, vp, bias, fd, fu, fo,
    tg_out, tb_out, vec_out, gq_out, gd_out, gu_out, go_out,
    dq_s, x_s, dh_s, wq_s, vec_s, vp_s, bias_s, mine_s, far_mine_s, far_s, near_s, far_e, cut_s, vb_s,
    load_sem, out_sem, low_sem, late_send, late_recv, late_put, p_send, p_recv, vb_send, vb_recv, *rest,
):
    bf, f32 = jnp.bfloat16, jnp.float32
    net = Sums(n_items, (gq,), (gq_out,), split_refs(rest[:7], 1), rest[7:])
    i, f, core, stay, mine, other, far, flip = place()
    shapes = [jax.ShapeDtypeStruct((4, 4) + r.shape, bf) for r in (fd, fu, fo)]
    late = Sums(n_items, (None,) * 3, (gd_out, gu_out, go_out), (shapes,) + (None,) * 4 + ((fd, fu, fo), None),
                (late_send, late_recv, None, None, None, late_put))
    late.AX, late.AY, late.AC0, late.ADA, late.ADB, late.AC1, late.AC2, late.AC3 = range(8)
    ready = net.greet()
    loads = [pltpu.make_async_copy(a, b, load_sem.at[n]) for n, (a, b) in enumerate(
        [(part.at[far], far_mine_s), (dq, dq_s), (wq.at[:, pl.ds(0, D)], wq_s), (part.at[mine], mine_s), (vec, vec_s),
         (vp, vp_s), (bias, bias_s), (x_in, x_s), (dh, dh_s)])]
    for copy in loads:
        copy.start()
    ready()

    def far_copy(j):
        return net.remote(part.at[3 - far, j], far_s.at[j], p_send.at[0, j], p_recv.at[0, j], net.c_dev)

    def near_copy(j):
        return net.remote(part.at[3 - mine, j], near_s.at[j], p_send.at[1, j], p_recv.at[1, j], net.c_dev)

    def chip_copy(j):
        return net.remote(far_mine_s.at[j], far_e.at[j], p_send.at[2, j], p_recv.at[2, j], net.e_dev)

    for j in range(4):
        far_copy(j).start()
    net.begin(0)
    for w in range(3):
        late.gather_begin(w)
    for j in range(4):
        near_copy(j).start()
    loads[0].wait()
    for j in range(4):
        far_copy(j).wait_recv()
        net.plus(far_mine_s, (j,), far_s, (j,))
        chip_copy(j).start()
    net.step(0, 0)
    late.gather_one(2)
    for n in range(1, 9):
        loads[n].wait()
    zero = jnp.zeros((1, D), f32)
    gain = vec_s[0, 0:1, :].astype(f32)
    vp_s[0, 2:3, :] = bias_s[0:1, :]
    vp_s[1, 0:1, :] = bias_s[1:2, :]

    def norm_back(j, carry):
        gains, shifts = carry
        near_copy(j).wait_recv()
        dn = mm(dq_s[j], wq_s[...], NT) + mine_s[j].astype(f32) + near_s[j].astype(f32)
        unit, scale = norm_parts(x_s[j])
        chip_copy(j).wait_recv()
        dn = dn + far_e[j].astype(f32)
        gains = gains + jnp.sum(dn * unit, axis=0, keepdims=True)
        shifts = shifts + jnp.sum(dn, axis=0, keepdims=True)
        grad = dh_s[j] + norm_grad(dn * gain, unit, scale)
        cut_s[j] = grad[:FRAME_TOK]
        dq_s[j] = grad.astype(bf)
        return gains, shifts

    def slot_out(j):
        return pltpu.make_async_copy(cut_s.at[j], tg_out.at[j], out_sem.at[j])

    def low_out(j):
        return pltpu.make_async_copy(dq_s.at[j], tb_out.at[j], low_sem.at[j])

    carry = (zero, zero)
    for j in range(4):
        if j == 2:
            net.step(0, 1)
            late.gather_one(0)
            late.gather_one(1)
        carry = norm_back(j, carry)
        slot_out(j).start()
        low_out(j).start()
    vp_s[0, 0:1, :] = carry[0]
    vp_s[0, 1:2, :] = carry[1]
    ring = [net.c_dev, net.x_dev, net.y_dev, (i, net.zs[0]), (i, net.zs[1])] + [(flip(i, b), f) for b in net.extra]

    def v_copy(n):
        return net.remote(vp_s, vb_s.at[n], vb_send.at[n], vb_recv.at[n], ring[n])

    def v_step(n):
        v_copy(n).wait()
        vp_s[...] = vp_s[...] + vb_s[n]
        if n + 1 < len(ring):
            v_copy(n + 1).start()

    v_copy(0).start()
    net.step(0, 2)
    for w in range(3):
        late.gather_two(w)
    v_step(0)
    v_step(1)
    net.step(0, 3)
    v_step(2)
    net.gather_one(0)
    v_step(3)
    net.gather_two(0)
    for n in range(4, len(ring)):
        v_step(n)
    vec_put = pltpu.make_async_copy(vp_s.at[f], vec_out, out_sem.at[4])
    vec_put.start()
    net.gather_three(0)
    net.finish(0)
    for w in range(3):
        late.gather_three(w)
        late.finish(w, False)
    for j in range(4):
        far_copy(j).wait_send()
        near_copy(j).wait_send()
        chip_copy(j).wait_send()
        slot_out(j).wait()
        low_out(j).wait()
    vec_put.wait()


def tail(n_items, gq, part, dq, x_in, dh, wq, vec, vp, bias, fd, fu, fo):
    bf, f32 = jnp.bfloat16, jnp.float32
    S = jax.ShapeDtypeStruct
    hb = pl.BlockSpec(memory_space=pltpu.HBM)
    dma = pltpu.SemaphoreType.DMA
    v = lambda shape, dtype=bf: pltpu.VMEM(shape, dtype)
    rows = (4, SP, D)
    bufs, sems = sums_scratch(n_items, [(gq.shape[2], gq.shape[3] // 2)])
    steps = 5
    while 2 ** (steps - 2) < n_items:
        steps += 1
    return pl.pallas_call(
        functools.partial(tail_kernel, n_items),
        out_shape=(S((4, FRAME_TOK, D), f32), S(rows, bf), S((8, D), f32), S((D // 4, 3 * D), bf))
        + tuple(S((4 * r.shape[0], 2 * r.shape[1]), bf) for r in (fd, fu, fo)),
        in_specs=[hb] * 12,
        out_specs=(hb,) * 7,
        scratch_shapes=[
            v(rows), v(rows, f32), v(rows, f32), v((D, D)), v((4, VEC_ROWS, D)), v((4, 8, D), f32), v((8, D), f32),
            v(rows), v(rows), v(rows), v(rows), v(rows), v((4, FRAME_TOK, D), f32), v((steps, 4, 8, D), f32),
            dma((9,)), dma((5,)), dma((4,)), dma((3, 8)), dma((3, 8)), dma((3,)), dma((3, 4)), dma((3, 4)), dma((steps,)), dma((steps,)),
        ] + bufs + sems,
        compiler_params=pltpu.CompilerParams(
            collective_id=2, has_side_effects=True, vmem_limit_bytes=60 * 2**20),
        cost_estimate=pl.CostEstimate(flops=2 * 14 * 784 * 768 * 768, bytes_accessed=60 * 2**20, transcendentals=0),
        name="tail",
    )(gq, part, dq, x_in, dh, wq, vec, vp, bias, fd, fu, fo)


def on_device(
    tokens,
    cotangent,
    date_year,
    date_day,
    item_dates,
    slot_frame,
    frame_mask,
    qkv_weight,
    qkv_first,
    qkv_second,
    out_weight,
    out_first,
    out_second,
    up_weight,
    up_first,
    up_second,
    down_weight,
    down_first,
    down_second,
    vectors,
    vector_first,
    vector_second,
):
    bf, f32 = jnp.bfloat16, jnp.float32
    n_items = lax.axis_size("items")
    i, f, core, stay, mine, other, far, flip = place()
    swap = []
    for k in range(n_items):
        for z in range(4):
            if k % 2 != z // 2:
                swap.append((k * 4 + z, (k ^ 1) * 4 + 3 - z))

    pad = lambda a: jnp.pad(a[0], ((0, 0), (0, SP - FRAME_TOK), (0, 0)))
    item_index, is_valid = slot_items(item_dates[0], slot_frame[0], frame_mask[0])
    own_items = lax.dynamic_slice_in_dim(item_index, f * 4, 4)
    tables = key_tables(item_index, is_valid, own_items)
    tab = jnp.pad(tables[None], ((0, 7), (0, 128 - tables.shape[0])))
    tmp = jnp.pad(temporal_rows(date_year[0], date_day[0]), ((0, 4), (0, 0)))
    vec = jnp.pad(vectors.astype(bf).reshape(3, D), ((0, VEC_ROWS - 3), (0, 0)))
    q3, k3, v3, o3, lse, nt, x3, dy, vec_all, tab_own, wq, wo, wu, wd = front(
        pad(tokens), pad(cotangent), tmp, tab, vec, jnp.asarray(spatial_rows()),
        qkv_weight, out_weight, up_weight, down_weight)
    block_out, hidden_grad, do3, down_grad, up_grad, out_grad, vector_part = mid(
        o3, x3, dy, vec_all, wo, wu, wd)
    blocks = lambda g: g.reshape(4, 4, g.shape[0] // 16, g.shape[1])
    block_out, dq3, part, gq, bias_part, *regions = back(
        n_items, tab_own, q3, k3, v3, o3, do3, lse, nt, wq, block_out, blocks(down_grad), blocks(up_grad), blocks(out_grad))
    token_grad, token_low, vector_sum, qkv_sum, down_sum, up_sum, out_sum = tail(
        n_items, gq, part.reshape(4, 4, SP, D), dq3, x3, hidden_grad, wq, vec_all, vector_part, bias_part, *regions)
    home = lax.ppermute(token_low, ("items", "frames"), swap)
    token_grad = jnp.where(stay, token_grad, home[:, :FRAME_TOK].astype(f32))
    qkv_new = adamw(qkv_weight, qkv_first, qkv_second, qkv_sum.astype(f32), 0.05, 0.05)
    out_new = adamw(out_weight, out_first, out_second, out_sum.astype(f32), 0.5, 0.05)
    up_new = adamw(up_weight, up_first, up_second, up_sum.astype(f32), 0.05, 0.05)
    down_new = adamw(down_weight, down_first, down_second, down_sum.astype(f32), 0.03, 0.05)
    vector_new = adamw(vectors, vector_first, vector_second, vector_sum[:3].reshape(3 * D), 0.3, 0.0)
    cut = lambda a: a.reshape(1, 4, SP, D)[:, :, :FRAME_TOK]
    return (cut(block_out), token_grad[None]) + qkv_new + out_new + up_new + down_new + vector_new


def solution(mesh):
    placed = (
        P("items", "frames", None, None),
        P("items", "frames", None, None),
        P("items", "frames"),
        P("items", "frames"),
        P("items", None),
        P("items", None),
        P("items", None),
        P("frames", None),
        P("frames", None),
        P("frames", None),
        P("frames", None),
        P("frames", None),
        P("frames", None),
        P("frames", None),
        P("frames", None),
        P("frames", None),
        P("frames", None),
        P("frames", None),
        P("frames", None),
        P("frames"),
        P("frames"),
        P("frames"),
    )
    return jax.shard_map(
        on_device,
        mesh=mesh,
        in_specs=placed,
        out_specs=(
            P("items", "frames", None, None),
            P("items", "frames", None, None),
            P("frames", None),
            P("frames", None),
            P("frames", None),
            P("frames", None),
            P("frames", None),
            P("frames", None),
            P("frames", None),
            P("frames", None),
            P("frames", None),
            P("frames", None),
            P("frames", None),
            P("frames", None),
            P("frames"),
            P("frames"),
            P("frames"),
        ),
        check_vma=False,
    )
```

```python
import functools

import jax
import jax.numpy as jnp
import numpy as np
from jax import lax
from jax.experimental import pallas as pl
from jax.experimental.pallas import tpu as pltpu
from jax.sharding import PartitionSpec as P

D = 768
HEADS = 12
HEAD = 64
GRID = 14
STEP = 10
FRAME_TOK = 196


beta_one = 0.9
beta_two = 0.999


def sincos(values, length_out):
    half_width = length_out // 2
    frequency = 1.0 / 10000.0 ** (jnp.arange(half_width, dtype=jnp.float32) / half_width)
    angles = values[..., None] * frequency
    return jnp.concatenate([jnp.sin(angles), jnp.cos(angles)], axis=-1)


def temporal_rows(year_values, day_values):
    dates = jnp.concatenate(
        [
            sincos((year_values - 2000).astype(jnp.float32), D // 8),
            sincos(day_values.astype(jnp.float32), D // 8),
        ],
        axis=-1,
    )
    return jnp.pad(dates, ((0, 0), (3 * D // 4, 0)))


def spatial_rows():
    half = 3 * D // 16
    frequency = (1.0 / np.float32(10000.0) ** (np.arange(half, dtype=np.float32) / np.float32(half))).astype(np.float32)
    cells = np.arange(FRAME_TOK)
    parts = []
    for values in (cells // GRID, cells % GRID):
        angles = values.astype(np.float32)[:, None] * frequency
        parts += [np.sin(angles), np.cos(angles)]
    rows = np.zeros((SP, D), np.float32)
    rows[:FRAME_TOK, : 3 * D // 4] = np.concatenate(parts, axis=-1)
    return rows


def slot_items(dates_group, frames_group, mask_group):
    item_ends = jnp.cumsum(dates_group)
    starts = item_ends - dates_group
    item_index = jnp.sum((frames_group[:, None] >= item_ends[None, :]).astype(jnp.int32), axis=1)
    is_first = jnp.any(frames_group[:, None] == starts[None, :], axis=1)
    is_valid = jnp.logical_or(mask_group > 0, is_first)
    return (item_index, is_valid)


SP = 208
NK = 6
NEG = -1e30
NT = (((1,), (1,)), ((), ()))
NN = (((1,), (0,)), ((), ()))


def mm(a, b, dims=NN):
    return lax.dot_general(a, b, dims, preferred_element_type=jnp.float32)


def augmented_keys(parts, valid, bias_lane, mine):
    row = lax.broadcasted_iota(jnp.int32, (SP, 128), 0)
    lane = lax.broadcasted_iota(jnp.int32, (SP, 128), 1)
    blocks = []
    for part, live in zip(parts, valid):
        bias = jnp.where(row >= FRAME_TOK, NEG, live).astype(jnp.bfloat16)
        blocks.append(jnp.where(mine, part, jnp.where(lane == bias_lane, bias, jnp.zeros_like(part))))
    return jnp.concatenate(blocks, axis=0)


def attention_step(step, tab_ref, q_ref, k_ref, v_ref, o_ref, lse_ref):
    lane = lax.broadcasted_iota(jnp.int32, (SP, 128), 1)
    j, b = step // 6, step % 6
    cols = pl.ds(pl.multiple_of(b * 128, 128), 128)
    parts = [k_ref[tab_ref[0, j * NK + t], :, cols] for t in range(NK)]
    valid = [jnp.where(tab_ref[0, (4 + j) * NK + t] > 0, 0.0, NEG) for t in range(NK)]
    vg = jnp.concatenate([v_ref[tab_ref[0, j * NK + t], :, cols] for t in range(NK)], axis=0)
    q = q_ref[j, :, cols]
    scores = []
    for h in range(2):
        mine = (lane < 64) if h == 0 else (lane >= 64)
        spare = 64 if h == 0 else 0
        ka = augmented_keys(parts, valid, spare, mine)
        qa = jnp.where(mine, q, jnp.where(lane == spare, jnp.ones_like(q), jnp.zeros_like(q)))
        scores.append(mm(qa, ka, NT))
    peaks = [jnp.max(s, axis=1, keepdims=True) for s in scores]
    probs = [jnp.exp(s - m) for s, m in zip(scores, peaks)]
    sums = [jnp.sum(p, axis=1, keepdims=True) for p in probs]
    outs = [mm(p.astype(jnp.bfloat16), vg) / total for p, total in zip(probs, sums)]
    o_ref[j, :, cols] = jnp.where(lane < 64, outs[0], outs[1]).astype(jnp.bfloat16)
    logs = [m + jnp.log(total) for m, total in zip(peaks, sums)]
    lse_ref[j, b] = jnp.transpose(jnp.where(lane == 0, logs[0], logs[1]))[:8]


VM = pl.BlockSpec(memory_space=pltpu.VMEM)
SM = pl.BlockSpec(memory_space=pltpu.SMEM)


def key_tables(item_index, is_valid, q_items):
    match = (q_items[:, None] == item_index[None, :]) & is_valid[None, :]
    rank = jnp.cumsum(match.astype(jnp.int32), axis=1) - 1
    count = jnp.sum(match.astype(jnp.int32), axis=1)
    place = jnp.arange(NK, dtype=jnp.int32)
    hit = match[:, None, :] & (rank[:, None, :] == place[None, :, None])
    slots = jnp.arange(item_index.shape[0], dtype=jnp.int32)
    idx = jnp.sum(jnp.where(hit, slots[None, None, :], 0), axis=2)
    val = (place[None, :] < count[:, None]).astype(jnp.int32)
    place_of = jnp.arange(4 * NK, dtype=jnp.int32)
    held = (idx.reshape(-1)[None, :] == slots[:, None]) & (val.reshape(-1)[None, :] > 0)
    first = jnp.min(jnp.where(held, place_of[None, :], 4 * NK), axis=1)
    last = jnp.max(jnp.where(held, place_of[None, :], -1), axis=1)
    has_first, has_last = first < 4 * NK, last > first
    rows = [jnp.where(has_first, first, 0), jnp.where(has_last, last, 0), has_first, has_last]
    return jnp.concatenate([idx.reshape(-1), val.reshape(-1)] + [r.astype(jnp.int32) for r in rows])


def adamw(weight, first_moment, second, gradient, step_rate, decay):
    first_new = beta_one * first_moment + (1.0 - beta_one) * gradient
    second_new = beta_two * second + (1.0 - beta_two) * gradient * gradient
    first_hat = first_new / (1.0 - beta_one**STEP)
    second_hat = second_new / (1.0 - beta_two**STEP)
    weight_new = weight - step_rate * (first_hat / (jnp.sqrt(second_hat) + 1e-08) + decay * weight)
    return (first_new, second_new, weight_new)


VEC_ROWS = 16
MESH = pl.DeviceIdType.MESH
Z, X, Y, DA, DB, C0, C1, C2, C3 = range(9)


def norm_rows(x):
    mean = jnp.mean(x, axis=-1, keepdims=True)
    centred = x - mean
    spread = jnp.mean(centred * centred, axis=-1, keepdims=True)
    return centred * lax.rsqrt(spread + 1e-06)


def place():
    i, f = lax.axis_index("items"), lax.axis_index("frames")
    core = i % 2
    upper = f // 2
    stay = core == upper
    mine = jnp.where(stay, f, 3 - f)
    other = f + 1 - 2 * (f % 2)
    far = jnp.where(stay, other, 3 - other)
    flip = lambda v, bit: v + bit - 2 * bit * ((v // bit) % 2)
    return i, f, core, stay, mine, other, far, flip


def halves(core, a, b):
    return jnp.where(core == 0, a, b)


def front_kernel(
    tok, cot, tmp, tab, vec, spatial, wq, wo, wu, wd,
    q_out, k_out, v_out, o_out, lse_out, nt_out, x_out, dy_out, vec_out, tab_out, wq_out, wo_out, wu_out, wd_out,
    t_s, tmp_s, vec_s, n_s, nt_s, q_s, k_s, v_s, o_s, lse_s, x_s, tab_s, wq_s,
    rq32, ro32, ru32, rd32, rq, ro, ru, rd, sq32, so32, su32, sd32, sq, so, su, sd,
    t_send, t_recv, m_send, m_recv, d_send, d_recv, v_send, v_recv, w_send, w_recv, z_send, z_recv,
    reg_sem, own_sem, put_sem, loc_sem, out_sem, nt_sem,
):
    bf, f32 = jnp.bfloat16, jnp.float32
    i, f, core, stay, mine, other, far, flip = place()
    c_dev = (flip(i, 1), f)
    x_dev = (halves(core, flip(i, 2), flip(i, 4)), f)
    y_dev = (halves(core, flip(i, 4), flip(i, 2)), f)
    e_dev = (i, other)
    m_dev = (flip(i, 1), 3 - f)
    xy = (i // 2) % 4
    xy_x, xy_y = halves(core, flip(xy, 1), flip(xy, 2)), halves(core, flip(xy, 2), flip(xy, 1))
    diag = flip(flip(xy, 1), 2)
    zs = [flip(f, 1), jnp.where(f < 2, 2, 1), jnp.where(f < 2, 3, 0)]

    barrier = pltpu.get_barrier_semaphore()
    partners = [c_dev, x_dev, y_dev, m_dev] + [(i, z) for z in zs]
    for dev in partners:
        pl.semaphore_signal(barrier, inc=1, device_id=dev, device_id_type=MESH)

    weights = [(wq, wq_out, rq32, rq, sq32, sq), (wo, wo_out, ro32, ro, so32, so),
               (wu, wu_out, ru32, ru, su32, su), (wd, wd_out, rd32, rd, sd32, sd)]

    def region_load(w):
        src, _, r32, _, _, _ = weights[w]
        rows, cols = r32.shape
        return pltpu.make_async_copy(
            src.at[pl.ds(pl.multiple_of(xy * rows, rows), rows), pl.ds(pl.multiple_of(core * cols, 128), cols)],
            r32, reg_sem.at[w])

    def own_load(w):
        return pltpu.make_async_copy(weights[w][0], weights[w][4], own_sem.at[w])

    def own_put(w):
        out, small = weights[w][1], weights[w][5]
        rows = small.shape[0]
        return pltpu.make_async_copy(small, out.at[pl.ds(pl.multiple_of(f * rows, rows), rows), :], put_sem.at[w])

    for w in range(4):
        region_load(w).start()
    for w in range(4):
        own_load(w).start()
    tok_load = pltpu.make_async_copy(tok, t_s.at[mine], loc_sem.at[0])
    tmp_load = pltpu.make_async_copy(tmp, tmp_s.at[mine], loc_sem.at[1])
    tab_load = pltpu.make_async_copy(tab, tab_out, loc_sem.at[5])
    cot_load = pltpu.make_async_copy(cot, dy_out, loc_sem.at[6])
    vec_load = pltpu.make_async_copy(vec, vec_s.at[f], loc_sem.at[2])

    @pl.when(stay)
    def _():
        tok_load.start()
        tmp_load.start()
        tab_load.start()

    vec_load.start()
    pl.semaphore_wait(barrier, len(partners))

    def remote(src, dst, ssem, rsem, dev):
        return pltpu.make_async_remote_copy(
            src_ref=src, dst_ref=dst, send_sem=ssem, recv_sem=rsem, device_id=dev, device_id_type=MESH)

    def tok_copy(kind, j):
        if kind == 0:
            return remote(tok.at[j], t_s.at[f, j], t_send.at[0, j], t_recv.at[0, j], m_dev)
        if kind == 3:
            return remote(t_s.at[far, j], t_s.at[far, j], t_send.at[3, j], t_recv.at[3, j], c_dev)
        return remote(t_s.at[mine, j], t_s.at[mine, j], t_send.at[kind, j], t_recv.at[kind, j],
                      c_dev if kind == 1 else e_dev)

    def tok_arrival(kind, j):
        shard = (mine, 3 - mine, far, 3 - far)[kind]
        return remote(t_s.at[shard, j], t_s.at[shard, j], t_send.at[kind, j], t_recv.at[kind, j], c_dev)

    def tmp_copy(kind):
        if kind == 0:
            return remote(tmp, tmp_s.at[f], m_send.at[0], m_recv.at[0], m_dev)
        if kind == 3:
            return remote(tmp_s.at[far], tmp_s.at[far], m_send.at[3], m_recv.at[3], c_dev)
        return remote(tmp_s.at[mine], tmp_s.at[mine], m_send.at[kind], m_recv.at[kind], c_dev if kind == 1 else e_dev)

    def tmp_arrival(kind):
        shard = (mine, 3 - mine, far, 3 - far)[kind]
        return remote(tmp_s.at[shard], tmp_s.at[shard], m_send.at[kind], m_recv.at[kind], c_dev)

    def tab_copy():
        return remote(tab, tab_out, d_send.at[4], d_recv.at[4], m_dev)

    def cot_copy(j):
        return remote(cot.at[j], dy_out.at[j], d_send.at[j], d_recv.at[j], m_dev)

    def part(w, z, at, half, piece):
        out, r = weights[w][1], weights[w][3]
        rows, cols = r.shape
        unit = rows // 3
        start = z * 4 * rows + at * rows
        if piece == 0:
            return out.at[pl.ds(pl.multiple_of(start, 16), rows), pl.ds(pl.multiple_of(half * cols, 128), cols)]
        if piece == 1:
            return out.at[pl.ds(pl.multiple_of(start, 16), 2 * unit), pl.ds(pl.multiple_of(half * cols, 128), cols)]
        return out.at[pl.ds(pl.multiple_of(start + 2 * unit, 16), unit), pl.ds(pl.multiple_of(half * cols, 128), cols)]

    def w_copy(w, d, kind):
        sems = (w_send.at[w, d, kind], w_recv.at[w, d, kind])
        z = zs[d]
        at = {X: xy, Y: xy, DA: xy_x, DB: xy_y, C0: xy, C1: xy_x, C2: xy_y, C3: diag}[kind]
        piece = {DA: 1, DB: 2}.get(kind, 0)
        dev = {X: x_dev, Y: y_dev, DA: y_dev, DB: x_dev}.get(kind, c_dev)
        ref = part(w, z, at, core, piece)
        return remote(ref, ref, *sems, dev)

    def w_arrival(w, d, kind):
        sems = (w_send.at[w, d, kind], w_recv.at[w, d, kind])
        z = zs[d]
        at = {X: xy_x, Y: xy_y, DA: diag, DB: diag, C0: xy, C1: xy_y, C2: xy_x, C3: diag}[kind]
        piece = {DA: 1, DB: 2}.get(kind, 0)
        half = (1 - core) if kind >= C0 else core
        ref = part(w, z, at, half, piece)
        return remote(ref, ref, *sems, c_dev)

    def z_copy(w, d):
        return remote(weights[w][3], part(w, f, xy, core, 0), z_send.at[w, d], z_recv.at[w, f], (i, zs[d]))

    def z_arrival(w, d):
        ref = part(w, zs[d], xy, core, 0)
        return remote(ref, ref, z_send.at[w, d], z_recv.at[w, zs[d]], (i, zs[d]))

    def w_send_region(w):
        region_load(w).wait()
        weights[w][3][...] = weights[w][2][...].astype(bf)
        for d in range(3):
            z_copy(w, d).start()

    def w_stage_one(w):
        for d in range(3):
            z_arrival(w, d).wait_recv()
            for kind in (X, Y, C0):
                w_copy(w, d, kind).start()

    def w_stage_two(w):
        for d in range(3):
            w_arrival(w, d, X).wait_recv()
            w_copy(w, d, DA).start()
            w_copy(w, d, C1).start()
            w_arrival(w, d, Y).wait_recv()
            w_copy(w, d, DB).start()
            w_copy(w, d, C2).start()

    def w_stage_three(w):
        for d in range(3):
            w_arrival(w, d, DA).wait_recv()
            w_arrival(w, d, DB).wait_recv()
            w_copy(w, d, C3).start()

    def w_stage_four(w):
        for d in range(3):
            for kind in (C0, C1, C2, C3):
                w_arrival(w, d, kind).wait_recv()

    def w_own(w):
        own_load(w).wait()
        weights[w][5][...] = weights[w][4][...].astype(bf)
        own_put(w).start()

    w_send_region(0)
    vec_load.wait()

    def v_copy(d):
        return remote(vec_s.at[f], vec_s.at[f], v_send.at[d], v_recv.at[f], (i, zs[d]))

    def v_arrival(d):
        return remote(vec_s.at[zs[d]], vec_s.at[zs[d]], v_send.at[d], v_recv.at[zs[d]], (i, zs[d]))

    for d in range(3):
        v_copy(d).start()

    @pl.when(jnp.logical_not(stay))
    def _():
        tmp_copy(0).start()
        tab_copy().start()

    @pl.when(stay)
    def _():
        tok_load.wait()
        tmp_load.wait()
        for kind in (2, 1):
            tmp_copy(kind).start()
        for j in range(4):
            tok_copy(1, j).start()

    w_own(0)
    w_stage_one(0)

    @pl.when(jnp.logical_not(stay))
    def _():
        for j in range(4):
            tok_copy(0, j).start()

    @pl.when(stay)
    def _():
        for j in range(4):
            tok_copy(2, j).start()

    for w in (1, 2, 3):
        w_own(w)
    w_stage_two(0)
    w_stage_three(0)
    w_stage_four(0)
    own_put(0).wait()
    wq_load = pltpu.make_async_copy(wq_out, wq_s, loc_sem.at[3])
    wq_load.start()
    for d in range(3):
        v_arrival(d).wait_recv()
    vec_put = pltpu.make_async_copy(vec_s, vec_out, loc_sem.at[4])
    vec_put.start()
    gain = vec_s[0, 0:1, :].astype(f32)
    shift = vec_s[0, 1:2, :].astype(f32)
    bias_q = vec_s[0, 2:3, :].astype(f32)
    bias_v = vec_s[1, 0:1, :].astype(f32)
    wq_load.wait()

    def normalise(shard):
        def slot(j, _):
            x = t_s[shard, j].astype(f32) + (spatial[...] + tmp_s[shard, pl.ds(j, 1), :])

            @pl.when(shard == mine)
            def _():
                x_s[j] = x
            n_s[j] = (norm_rows(x) * gain + shift).astype(bf)
            return 0
        lax.fori_loop(0, 4, slot, 0)

    def project(shard):
        rows = n_s[...].reshape(4 * SP, D)
        at = pl.ds(4 * shard, 4)
        def keys(t, _):
            cols = pl.ds(pl.multiple_of(t * 256, 256), 256)
            k_s[at, :, cols] = mm(rows, wq_s[:, pl.ds(pl.multiple_of(D + t * 256, 256), 256)]).astype(bf).reshape(4, SP, 256)
            v_s[at, :, cols] = (mm(rows, wq_s[:, pl.ds(pl.multiple_of(2 * D + t * 256, 256), 256)])
                                      + vec_s[1, 0:1, cols].astype(f32)).astype(bf).reshape(4, SP, 256)
            return 0
        lax.fori_loop(0, 3, keys, 0)

    def project_q(shard):
        rows = n_s[...].reshape(4 * SP, D)
        def queries(t, _):
            cols = pl.ds(pl.multiple_of(t * 256, 256), 256)
            q = (mm(rows, wq_s[:, cols]) + vec_s[0, 2:3, cols].astype(f32)).astype(bf)
            q_s[:, :, cols] = (q.astype(f32) * 0.125).astype(bf).reshape(4, SP, 256)
            return 0
        lax.fori_loop(0, 3, queries, 0)

    outs = []
    def put(src, dst):
        copy = pltpu.make_async_copy(src, dst, out_sem.at[len(outs)])
        copy.start()
        outs.append(copy)

    turned = []

    def put_shard(shard):
        n = len(turned)
        if n >= 2:
            turned[n - 2].wait()
        nt_s[n % 2] = jnp.transpose(n_s[...].reshape(4 * SP, D))
        copy = pltpu.make_async_copy(nt_s.at[n % 2], nt_out.at[shard], nt_sem.at[n % 2])
        copy.start()
        turned.append(copy)
        at = pl.ds(4 * shard, 4)
        put(k_s.at[at], k_out.at[at])
        put(v_s.at[at], v_out.at[at])

    moved = jnp.logical_not(stay)

    def arrive(kind):
        tmp_arrival(kind).wait_recv()
        if kind == 2:
            tmp_copy(3).start()
        if kind == 0:
            for then in (2, 1):
                tmp_copy(then).start()
        for j in range(4):
            tok_arrival(kind, j).wait_recv()
            if kind == 2:
                tok_copy(3, j).start()
            if kind == 0:
                for then in (2, 1):
                    tok_copy(then, j).start()

    def work(shard):
        normalise(shard)

        @pl.when(shard == mine)
        def _():
            project_q(shard)

        project(shard)
        put_shard(shard)

    stayed_here, stayed_there = jnp.where(stay, mine, 3 - mine), jnp.where(stay, far, 3 - far)

    @pl.when(moved)
    def _():
        arrive(1)

    work(stayed_here)

    @pl.when(moved)
    def _():
        arrive(0)

    @pl.when(stay)
    def _():
        arrive(1)

    for w in (1, 2, 3):
        w_send_region(w)
    work(3 - stayed_here)
    put(x_s, x_out)
    put(q_s, q_out)

    @pl.when(stay)
    def _():
        arrive(2)

    @pl.when(moved)
    def _():
        arrive(3)

    work(stayed_there)

    @pl.when(moved)
    def _():
        arrive(2)

    @pl.when(stay)
    def _():
        arrive(3)

    @pl.when(moved)
    def _():
        for j in range(4):
            cot_copy(j).start()

    @pl.when(stay)
    def _():
        cot_load.start()

    work(3 - stayed_there)

    @pl.when(stay)
    def _():
        tab_load.wait()

    @pl.when(jnp.logical_not(stay))
    def _():
        tab_copy().wait_recv()

    to_scalars = pltpu.make_async_copy(tab_out, tab_s, loc_sem.at[7])
    to_scalars.start()
    to_scalars.wait()
    plan = ((0, w_stage_one, 1), (3, w_stage_one, 2), (5, w_stage_two, 1), (8, w_stage_one, 3), (14, w_stage_two, 2), (16, w_stage_three, 1), (22, w_stage_two, 3))

    def attend(step, _):
        for at, act, w in plan:
            @pl.when(step == at)
            def _():
                act(w)
        attention_step(step, tab_s, q_s, k_s, v_s, o_s, lse_s)
        return 0

    lax.fori_loop(0, 24, attend, 0)
    put(o_s, o_out)
    put(lse_s, lse_out)
    for act, w in ((w_stage_three, 2), (w_stage_three, 3)):
        act(w)
    for w in (1, 2, 3):
        w_stage_four(w)
        own_put(w).wait()

    @pl.when(jnp.logical_not(stay))
    def _():
        tmp_copy(0).wait_send()
        tab_copy().wait_send()
        for j in range(4):
            tok_copy(0, j).wait_send()
            cot_copy(j).wait()

    @pl.when(stay)
    def _():
        cot_load.wait()

    for kind in (1, 2, 3):
        tmp_copy(kind).wait_send()
        for j in range(4):
            tok_copy(kind, j).wait_send()
    for d in range(3):
        v_copy(d).wait_send()
        for w in range(4):
            z_copy(w, d).wait_send()
            for kind in range(X, C3 + 1):
                w_copy(w, d, kind).wait_send()
    for copy in turned[2:]:
        copy.wait()
    vec_put.wait()
    for copy in outs:
        copy.wait()


def front(tok, cot, tmp, tab, vec, spatial, wq, wo, wu, wd):
    bf, f32 = jnp.bfloat16, jnp.float32
    S = jax.ShapeDtypeStruct
    hb = pl.BlockSpec(memory_space=pltpu.HBM)
    regs = [(w.shape[0] // 4, w.shape[1] // 2) for w in (wq, wo, wu, wd)]
    full = [(4 * w.shape[0], w.shape[1]) for w in (wq, wo, wu, wd)]
    dma = pltpu.SemaphoreType.DMA
    v = lambda shape, dtype=bf: pltpu.VMEM(shape, dtype)
    rows, every, stats = (4, SP, D), (16, SP, D), (4, 6, 8, SP)
    return pl.pallas_call(
        front_kernel,
        out_shape=(
            S(rows, bf), S(every, bf), S(every, bf), S(rows, bf), S(stats, f32), S((4, D, 4 * SP), bf), S(rows, f32),
            S(rows, bf), S((4, VEC_ROWS, D), bf), S(tab.shape, jnp.int32),
        ) + tuple(S(s, bf) for s in full),
        in_specs=[hb] * 5 + [VM] + [hb] * 4,
        out_specs=(hb,) * 14,
        scratch_shapes=[
            v((4,) + rows), v((4, 8, D), f32), v((4, VEC_ROWS, D)), v(rows), v((2, D, 4 * SP)), v(rows), v(every), v(every),
            v(rows), v(stats, f32), v(rows, f32), pltpu.SMEM(tab.shape, jnp.int32), v(full[0]),
        ]
        + [v(r, f32) for r in regs] + [v(r) for r in regs]
        + [v(w.shape, f32) for w in (wq, wo, wu, wd)] + [v(w.shape) for w in (wq, wo, wu, wd)]
        + [dma((4, 4)), dma((4, 4)), dma((4,)), dma((4,)), dma((5,)), dma((5,)), dma((3,)), dma((4,)), dma((4, 3, 9)),
           dma((4, 3, 9)), dma((4, 3)), dma((4, 4)), dma((4,)), dma((4,)), dma((4,)), dma((8,)), dma((16,)),
           dma((2,))],
        compiler_params=pltpu.CompilerParams(
            collective_id=1, has_side_effects=True, vmem_limit_bytes=62 * 2**20),
        cost_estimate=pl.CostEstimate(
            flops=2 * 9 * 784 * 768 * 768, bytes_accessed=40 * 2**20, transcendentals=24 * 12 * SP * SP),
        name="front",
    )(tok, cot, tmp, tab, vec, spatial, wq, wo, wu, wd)


def norm_parts(x):
    centred = x - jnp.mean(x, axis=-1, keepdims=True)
    scale = lax.rsqrt(jnp.mean(centred * centred, axis=-1, keepdims=True) + 1e-06)
    return centred * scale, scale


def norm_grad(dn, unit, scale):
    return (dn - jnp.mean(dn, axis=-1, keepdims=True) - unit * jnp.mean(dn * unit, axis=-1, keepdims=True)) * scale


def mid_kernel(
    o_in, x_in, dy_in, vec, wo, wu, wd,
    y_out, dh_out, do_out, gd_out, gu_out, go_out, vp_out,
    o_s, h_s, dy_s, vec_s, wo_s, wu_s, wd_s, n_s, nt_s, a_s, du_s, mlp_s, dn_s, gd_s, gu_s, go_s, y_s, db_s, do_s, vp_s,
    bu_s, gbu_s, in_sem, out_sem,
):
    bf, f32 = jnp.bfloat16, jnp.float32
    loads = [pltpu.make_async_copy(a, b, in_sem.at[n]) for n, (a, b) in enumerate(
        [(o_in, o_s), (wo, wo_s), (vec, vec_s), (x_in, h_s), (dy_in, dy_s), (wu, wu_s), (wd, wd_s)])]
    for copy in loads[:4]:
        copy.start()
    vp_s[...] = jnp.zeros_like(vp_s)
    zero = jnp.zeros((1, D), f32)
    for n in range(4):
        loads[n].wait()
    for copy in loads[4:]:
        copy.start()
    flat = lambda ref: ref[...].reshape(4 * SP, D)

    def branch(t, _):
        cols = pl.ds(pl.multiple_of(t * 256, 256), 256)
        out = mm(flat(o_s), wo_s[:, cols]) + vec_s[1, 1:2, cols].astype(f32)
        h_s[:, :, cols] = h_s[:, :, cols] + out.reshape(4, SP, 256)
        return 0
    lax.fori_loop(0, 3, branch, 0)
    gain, shift = vec_s[1, 2:3, :].astype(f32), vec_s[2, 0:1, :].astype(f32)

    def norm(j, _):
        unit, _scale = norm_parts(h_s[j])
        n_s[j] = (unit * gain + shift).astype(bf)
        return 0
    lax.fori_loop(0, 4, norm, 0)
    nt_s[...] = jnp.transpose(flat(n_s))
    spots = [(n, (n // 3 + 8) // 3, (n // 3 + 8) % 3, (n % 3) * 256) for n in range(12)]
    for n, z, r, at in spots:
        bu_s[n, 0:1, :] = vec_s[z, r : r + 1, at : at + 256].astype(f32)
    mlp_s[...] = jnp.zeros_like(mlp_s)
    dn_s[...] = jnp.zeros_like(dn_s)
    for n in range(4, 7):
        loads[n].wait()

    def group(g, _):
        start = pl.multiple_of(g * D, D)
        for k in range(3):
            n, low = 3 * g + k, slice(256 * k, 256 * k + 256)
            cols = pl.ds(pl.multiple_of(g * D + k * 256, 256), 256)
            u = mm(flat(n_s), wu_s[:, cols]) + bu_s[n, 0:1, :]
            cdf = 0.5 * (1.0 + lax.erf(u * 0.7071067811865476))
            a = (u * cdf).astype(bf)
            slope = cdf + u * (jnp.exp(u * u * -0.5) * 0.3989422804014327)
            da = mm(flat(dy_s), wd_s[cols, :], NT)
            du = (da * slope).astype(bf)
            a_s[:, low] = a
            du_s[:, low] = du
            gd_s[cols, :] = mm(jnp.transpose(a), flat(dy_s)).astype(bf)
            gu_s[:, cols] = mm(nt_s[...], du).astype(bf)
            gbu_s[n, 0:1, :] = jnp.sum(du.astype(f32), axis=0, keepdims=True)
        for t in range(3):
            out = slice(256 * t, 256 * t + 256)
            mlp_s[:, out] += mm(a_s[...], wd_s[pl.ds(start, D), out])
            dn_s[:, out] += mm(du_s[...], wu_s[out, pl.ds(start, D)], NT)
        return 0

    lax.fori_loop(0, 4, group, 0)
    for n, z, r, at in spots:
        vp_s[z, r : r + 1, at : at + 256] = gbu_s[n, 0:1, :]
    puts = []

    def put(src, dst):
        copy = pltpu.make_async_copy(src, dst, out_sem.at[len(puts)])
        copy.start()
        puts.append(copy)

    put(gd_s, gd_out)
    put(gu_s, gu_out)
    bias_down = vec_s[2, 1:2, :].astype(f32)

    def back(j, carry):
        gains, shifts, bias_o, bias_d = carry
        rows = pl.ds(pl.multiple_of(j * SP, 16), SP)
        h = h_s[j]
        y_s[j] = (h + (mlp_s[rows, :] + bias_down)).astype(bf)
        unit, scale = norm_parts(h)
        dn = dn_s[rows, :]
        gains = gains + jnp.sum(dn * unit, axis=0, keepdims=True)
        shifts = shifts + jnp.sum(dn, axis=0, keepdims=True)
        dy = dy_s[j].astype(f32)
        dh = dy + norm_grad(dn * gain, unit, scale)
        h_s[j] = dh
        db = dh.astype(bf)
        db_s[j] = db
        bias_o = bias_o + jnp.sum(db.astype(f32), axis=0, keepdims=True)
        return gains, shifts, bias_o, bias_d + jnp.sum(dy, axis=0, keepdims=True)
    gains, shifts, bias_o, bias_d = lax.fori_loop(0, 4, back, (zero,) * 4)
    put(y_s, y_out)
    put(h_s, dh_out)
    vp_s[1, 1:2, :] = bias_o
    vp_s[1, 2:3, :] = gains
    vp_s[2, 0:1, :] = shifts
    vp_s[2, 1:2, :] = bias_d
    put(vp_s, vp_out)

    def attended(t, _):
        cols = pl.ds(pl.multiple_of(t * 256, 256), 256)
        do_s[:, :, cols] = mm(flat(db_s), wo_s[cols, :], NT).astype(bf).reshape(4, SP, 256)
        return 0
    lax.fori_loop(0, 3, attended, 0)
    put(do_s, do_out)

    def out_grad(t, _):
        cols = pl.ds(pl.multiple_of(t * 256, 256), 256)
        turned = jnp.transpose(o_s[:, :, cols].reshape(4 * SP, 256))
        go_s[cols, :] = mm(turned, flat(db_s)).astype(bf)
        return 0
    lax.fori_loop(0, 3, out_grad, 0)
    put(go_s, go_out)
    for copy in puts:
        copy.wait()


def mid(o, x, dy, vec, wo, wu, wd):
    bf, f32 = jnp.bfloat16, jnp.float32
    S = jax.ShapeDtypeStruct
    hb = pl.BlockSpec(memory_space=pltpu.HBM)
    dma = pltpu.SemaphoreType.DMA
    v = lambda shape, dtype=bf: pltpu.VMEM(shape, dtype)
    rows = (4, SP, D)
    return pl.pallas_call(
        mid_kernel,
        out_shape=(S(rows, bf), S(rows, f32), S(rows, bf), S((4 * D, D), bf), S((D, 4 * D), bf), S((D, D), bf),
                   S((4, 8, D), f32)),
        in_specs=[hb] * 7,
        out_specs=(hb,) * 7,
        scratch_shapes=[
            v(rows), v(rows, f32), v(rows), v((4, VEC_ROWS, D)), v((D, D)), v((D, 4 * D)), v((4 * D, D)),
            v(rows), v((D, 4 * SP)), v((4 * SP, D)), v((4 * SP, D)), v((4 * SP, D), f32), v((4 * SP, D), f32),
            v((4 * D, D)), v((D, 4 * D)), v((D, D)), v(rows), v(rows), v(rows), v((4, 8, D), f32),
            v((12, 8, 256), f32), v((12, 8, 256), f32), dma((7,)), dma((7,)),
        ],
        compiler_params=pltpu.CompilerParams(vmem_limit_bytes=62 * 2**20),
        cost_estimate=pl.CostEstimate(flops=2 * 27 * 832 * 768 * 768, bytes_accessed=40 * 2**20, transcendentals=832 * 3072 * 2),
        name="mid",
    )(o, x, dy, vec, wo, wu, wd)


class Sums:
    AX, AY, AC0, ADA, ADB, AC1, AC2, AC3 = range(31, 39)

    def __init__(self, n_items, grads, outs, bufs, sems, gathers=True):
        self.gathers = gathers
        self.grads, self.outs = grads, outs
        self.sums, self.crecv, self.r1, self.r2, self.r3, self.fin, self.ext = bufs
        self.g_send, self.g_recv, self.e_send, self.e_recv, self.half_sem, self.put_sem = sems
        i, f, core, stay, mine, other, far, flip = place()
        self.i, self.f, self.core, self.flip = i, f, core, flip
        xy = (i // 2) % 4
        self.xy, self.diag = xy, flip(flip(xy, 1), 2)
        self.xy_x, self.xy_y = halves(core, flip(xy, 1), flip(xy, 2)), halves(core, flip(xy, 2), flip(xy, 1))
        self.c_dev = (flip(i, 1), f)
        self.x_dev = (halves(core, flip(i, 2), flip(i, 4)), f)
        self.y_dev = (halves(core, flip(i, 4), flip(i, 2)), f)
        self.e_dev = (i, other)
        self.zs = [flip(f, 1), flip(f, 2), flip(flip(f, 1), 2)]
        self.extra = []
        bit = 8
        while bit < n_items:
            self.extra.append(bit)
            bit *= 2

    def greet(self, *more):
        barrier = pltpu.get_barrier_semaphore()
        partners = [self.c_dev, self.x_dev, self.y_dev] + [(self.i, z) for z in self.zs]
        partners += [(self.flip(self.i, b), self.f) for b in self.extra] + list(more)
        for dev in partners:
            pl.semaphore_signal(barrier, inc=1, device_id=dev, device_id_type=MESH)
        return lambda: pl.semaphore_wait(barrier, len(partners))

    @staticmethod
    def remote(src, dst, ssem, rsem, dev):
        return pltpu.make_async_remote_copy(
            src_ref=src, dst_ref=dst, send_sem=ssem, recv_sem=rsem, device_id=dev, device_id_type=MESH)

    def cols_of(self, w, half):
        width = self.sums[w].shape[-1]
        return pl.ds(pl.multiple_of(half * width, 128), width)

    def half_load(self, w):
        return pltpu.make_async_copy(
            self.grads[w].at[:, :, :, self.cols_of(w, self.core)], self.sums[w], self.half_sem.at[w])

    def rows_of(self, w):
        unit = self.sums[w].shape[2] // 3
        return (pl.ds(0, 2 * unit), pl.ds(2 * unit, unit))

    def copies(self, w, stage):
        s, base = self.sums[w], (0, 4, 20, 28)[stage]
        ra, rb = self.rows_of(w)
        found = []
        if stage == 0:
            for z in range(4):
                found.append((self.grads[w].at[z, :, :, self.cols_of(w, 1 - self.core)], self.crecv[w].at[z], self.c_dev))
        elif stage == 1:
            for z in range(4):
                found.append((s.at[z, self.xy_x, ra], self.r1[w].at[z, 0, ra], self.x_dev))
                found.append((s.at[z, self.diag, ra], self.r1[w].at[z, 1, ra], self.x_dev))
                found.append((s.at[z, self.xy_y, rb], self.r1[w].at[z, 0, rb], self.y_dev))
                found.append((s.at[z, self.diag, rb], self.r1[w].at[z, 1, rb], self.y_dev))
        elif stage == 2:
            for z in range(4):
                found.append((s.at[z, self.xy_y, ra], self.r2[w].at[z, ra], self.y_dev))
                found.append((s.at[z, self.xy_x, rb], self.r2[w].at[z, rb], self.x_dev))
        else:
            for d in range(3):
                found.append((s.at[self.zs[d], self.xy], self.r3[w].at[d], (self.i, self.zs[d])))
        return [self.remote(src, dst, self.g_send.at[w, base + n], self.g_recv.at[w, base + n], dev)
                for n, (src, dst, dev) in enumerate(found)]

    def region(self, w, at, half, piece):
        rows = self.sums[w].shape[2]
        unit = rows // 3
        start, count = at * rows, rows
        if piece == 1:
            count = 2 * unit
        elif piece == 2:
            start, count = start + 2 * unit, unit
        return self.outs[w].at[pl.ds(pl.multiple_of(start, 16), count), self.cols_of(w, half)]

    def a_copy(self, w, kind):
        at = {self.AX: self.xy, self.AY: self.xy, self.AC0: self.xy, self.ADA: self.xy_x, self.ADB: self.xy_y,
              self.AC1: self.xy_x, self.AC2: self.xy_y, self.AC3: self.diag}[kind]
        piece = {self.ADA: 1, self.ADB: 2}.get(kind, 0)
        dev = {self.AX: self.x_dev, self.AY: self.y_dev, self.ADA: self.y_dev, self.ADB: self.x_dev}.get(kind, self.c_dev)
        dst = self.region(w, at, self.core, piece)
        src = self.fin[w] if kind in (self.AX, self.AY, self.AC0) else dst
        return self.remote(src, dst, self.g_send.at[w, kind], self.g_recv.at[w, kind], dev)

    def a_arrival(self, w, kind):
        at = {self.AX: self.xy_x, self.AY: self.xy_y, self.ADA: self.diag, self.ADB: self.diag, self.AC0: self.xy,
              self.AC1: self.xy_y, self.AC2: self.xy_x, self.AC3: self.diag}[kind]
        piece = {self.ADA: 1, self.ADB: 2}.get(kind, 0)
        half = (1 - self.core) if kind in (self.AC0, self.AC1, self.AC2, self.AC3) else self.core
        ref = self.region(w, at, half, piece)
        return self.remote(ref, ref, self.g_send.at[w, kind], self.g_recv.at[w, kind], self.c_dev)

    def begin(self, w):
        self.half_load(w).start()
        for copy in self.copies(w, 0):
            copy.start()

    @staticmethod
    def plus(ref, where, other_ref, other_where):
        ref[where] = ref[where] + other_ref[other_where]

    def step(self, w, stage):
        f32 = jnp.float32
        ra, rb = self.rows_of(w)
        plus, s, xy, xy_x, xy_y = self.plus, self.sums[w], self.xy, self.xy_x, self.xy_y
        for copy in self.copies(w, stage):
            copy.wait_recv()
        if stage == 0:
            self.half_load(w).wait()

            def one(n, _):
                plus(s, (n // 4, n % 4), self.crecv[w], (n // 4, n % 4))
                return 0
            lax.fori_loop(0, 16, one, 0)
        elif stage == 1:
            def one(z, _):
                plus(s, (z, xy, ra), self.r1[w], (z, 0, ra))
                plus(s, (z, xy_y, ra), self.r1[w], (z, 1, ra))
                plus(s, (z, xy, rb), self.r1[w], (z, 0, rb))
                plus(s, (z, xy_x, rb), self.r1[w], (z, 1, rb))
                return 0
            lax.fori_loop(0, 4, one, 0)
        elif stage == 2:
            def one(z, _):
                plus(s, (z, xy), self.r2[w], (z,))
                return 0
            lax.fori_loop(0, 4, one, 0)
        else:
            fin = self.fin[w]
            total = s[self.f, xy].astype(f32)
            for d in range(3):
                total = total + self.r3[w][d].astype(f32)
            fin[...] = total.astype(jnp.bfloat16)
            for n, b in enumerate(self.extra):
                copy = self.remote(fin, self.ext[w].at[n], self.e_send.at[w, n], self.e_recv.at[w, n],
                                   (self.flip(self.i, b), self.f))
                copy.start()
                copy.wait()
                fin[...] = (fin[...].astype(f32) + self.ext[w][n].astype(f32)).astype(jnp.bfloat16)
            if self.gathers:
                self.gather_begin(w)
            else:
                self.fin_put(w).start()
        if stage < 3:
            for copy in self.copies(w, stage + 1):
                copy.start()

    def fin_put(self, w):
        dst = self.region(w, self.xy, self.core, 0) if self.gathers else self.outs[w]
        return pltpu.make_async_copy(self.fin[w], dst, self.put_sem.at[w])

    def gather_begin(self, w):
        self.fin_put(w).start()
        for kind in (self.AX, self.AY, self.AC0):
            self.a_copy(w, kind).start()

    def gather_one(self, w):
        self.a_arrival(w, self.AX).wait_recv()
        self.a_copy(w, self.ADA).start()
        self.a_copy(w, self.AC1).start()
        self.a_arrival(w, self.AY).wait_recv()
        self.a_copy(w, self.ADB).start()
        self.a_copy(w, self.AC2).start()

    def gather_two(self, w):
        self.a_arrival(w, self.ADA).wait_recv()
        self.a_arrival(w, self.ADB).wait_recv()
        self.a_copy(w, self.AC3).start()

    def gather_three(self, w):
        for kind in (self.AC0, self.AC1, self.AC2, self.AC3):
            self.a_arrival(w, kind).wait_recv()
        self.fin_put(w).wait()

    def finish(self, w, sums=True):
        if sums:
            for stage in range(4):
                for copy in self.copies(w, stage):
                    copy.wait_send()
        if self.gathers:
            for kind in range(self.AX, self.AC3 + 1):
                self.a_copy(w, kind).wait_send()
        else:
            self.fin_put(w).wait()


def sums_scratch(n_items, shapes):
    v = lambda shape: pltpu.VMEM(shape, jnp.bfloat16)
    dma = pltpu.SemaphoreType.DMA
    n_extra, n = 0, len(shapes)
    while 8 * 2**n_extra < n_items:
        n_extra += 1
    bufs = []
    for lead in ((4, 4), (4, 4), (4, 2), (4,), (3,), ()):
        bufs += [v(lead + s) for s in shapes]
    bufs += [v((n_extra,) + s) if n_extra else v((1, 16, 128)) for s in shapes]
    sems = [dma((n, 39)), dma((n, 39)), dma((n, max(n_extra, 1))), dma((n, max(n_extra, 1))), dma((n,)), dma((n,))]
    return bufs, sems


def split_refs(refs, n):
    return [refs[k * n : (k + 1) * n] for k in range(7)]


def back_kernel(
    n_items, tab_ref, q_in, k_in, v_in, o_in, do_in, lse_in, nt_in, wq_in, y_in, gd, gu, go,
    y_out, dq_out, part_out, gq_out, bias_out, gd_out, gu_out, go_out,
    q_s, k_s, v_s, o_s, do_s, lse_s, nt_s, wq_s, pk_s, pv_s, gq_s, bias_s, load_sem, out_sem, y_send, y_recv, *rest,
):
    bf, f32 = jnp.bfloat16, jnp.float32
    net = Sums(n_items, (gd, gu, go), (gd_out, gu_out, go_out), split_refs(rest[:21], 3), rest[21:], False)
    i, f, core, stay, mine, other, far, flip = place()
    m_dev = (flip(i, 1), 3 - f)
    ready = net.greet(m_dev)
    loads = [pltpu.make_async_copy(a, b, load_sem.at[n]) for n, (a, b) in enumerate(
        [(q_in, q_s), (k_in, k_s), (v_in, v_s), (o_in, o_s), (do_in, do_s), (lse_in, lse_s), (nt_in, nt_s), (wq_in, wq_s)])]
    for copy in loads[:6]:
        copy.start()
    ready()
    for w in range(3):
        net.begin(w)
    y_stay = pltpu.make_async_copy(y_in, y_out, y_send.at[0])

    def y_copy(j):
        return net.remote(y_in.at[j], y_out.at[j], y_send.at[j], y_recv.at[j], m_dev)

    @pl.when(stay)
    def _():
        y_stay.start()

    @pl.when(jnp.logical_not(stay))
    def _():
        for j in range(4):
            y_copy(j).start()

    for n in range(6):
        loads[n].wait()
    for copy in loads[6:]:
        copy.start()
    lane = lax.broadcasted_iota(jnp.int32, (SP, 128), 1)
    plan = ((1, 0, 0), (2, 1, 0), (3, 2, 0), (5, 0, 1), (7, 1, 1), (8, 2, 1), (9, 0, 2), (11, 1, 2))

    def attend_back(step):
        j, b = step // 6, step % 6
        cols = pl.ds(pl.multiple_of(b * 128, 128), 128)
        parts = [k_s[tab_ref[0, j * NK + t], :, cols] for t in range(NK)]
        valid = [jnp.where(tab_ref[0, (4 + j) * NK + t] > 0, 0.0, NEG) for t in range(NK)]
        kg = jnp.concatenate(parts, axis=0)
        vg = jnp.concatenate([v_s[tab_ref[0, j * NK + t], :, cols] for t in range(NK)], axis=0)
        kg_t = jnp.transpose(kg)
        q, do, o = q_s[j, :, cols], do_s[j, :, cols], o_s[j, :, cols]
        prod_t = jnp.transpose(do.astype(f32) * o.astype(f32))
        logs = lse_s[j, b]
        dk_h, dv_h, dq_t = [], [], []
        for h in range(2):
            mine = (lane < 64) if h == 0 else (lane >= 64)
            spare = 64 if h == 0 else 0
            ka = augmented_keys(parts, valid, spare, mine)
            qm = jnp.where(mine, q, jnp.zeros_like(q))
            qa = jnp.where(lane == spare, jnp.ones_like(q), qm)
            dom = jnp.where(mine, do, jnp.zeros_like(do))
            centre = jnp.sum(prod_t[h * 64 : (h + 1) * 64], axis=0, keepdims=True)
            s_t = mm(ka, qa, NT)
            da_t = mm(vg, dom, NT)
            p = jnp.exp(s_t - logs[h : h + 1])
            ds = (p * (da_t - centre)).astype(bf)
            dv_h.append(mm(p.astype(bf), dom))
            dk_h.append(mm(ds, qm))
            dq_t.append(mm(kg_t, ds))
        dq = jnp.transpose(jnp.concatenate([dq_t[0][:64], dq_t[1][64:]], axis=0))
        dk, dv = dk_h[0] + dk_h[1], dv_h[0] + dv_h[1]
        q_s[j, :, cols] = (dq * 0.125).astype(bf)
        for t in range(NK):
            pk_s[j * NK + t, :, cols] = dk[t * SP : (t + 1) * SP].astype(bf)
            pv_s[j * NK + t, :, cols] = dv[t * SP : (t + 1) * SP].astype(bf)

    def one(step, _):
        for at, w, stage in plan:
            @pl.when(step == at)
            def _():
                net.step(w, stage)
        for half in range(2):
            attend_back(2 * step + half)
        return 0

    lax.fori_loop(0, 12, one, 0)
    puts = []

    def put(src, dst):
        copy = pltpu.make_async_copy(src, dst, out_sem.at[len(puts)])
        copy.start()
        puts.append(copy)

    put(q_s, dq_out)
    net.step(2, 2)

    def combine(slot, _):
        first, second = tab_ref[0, 8 * NK + slot], tab_ref[0, 8 * NK + 16 + slot]
        keep_a, keep_b = tab_ref[0, 8 * NK + 32 + slot] > 0, tab_ref[0, 8 * NK + 48 + slot] > 0
        none = jnp.zeros((SP, D), bf)
        for out, part in ((k_s, pk_s), (v_s, pv_s)):
            out[slot] = jnp.where(keep_a, part[first], none) + jnp.where(keep_b, part[second], none)
        return 0

    lax.fori_loop(0, 16, combine, 0)
    net.step(0, 3)
    for n in (6, 7):
        loads[n].wait()

    def slots(ref, shard):
        return ref[pl.ds(4 * shard, 4)].reshape(4 * SP, D)

    def partial_rows(shard, _):
        def tile(t, _):
            at = pl.multiple_of(t * 256, 256)
            keys = mm(slots(k_s, shard), wq_s[pl.ds(at, 256), D : 2 * D], NT)
            values = mm(slots(v_s, shard), wq_s[pl.ds(at, 256), 2 * D :], NT)
            pk_s[pl.ds(4 * shard, 4), :, pl.ds(at, 256)] = (keys + values).astype(bf).reshape(4, SP, 256)
            return 0
        lax.fori_loop(0, 3, tile, 0)
        return 0

    lax.fori_loop(0, 2, partial_rows, 0)
    net.step(1, 3)
    net.step(2, 3)
    lax.fori_loop(2, 4, partial_rows, 0)
    put(pk_s.at[pl.ds(0, 16)], part_out)

    def grad_q(t, _):
        cols = pl.ds(pl.multiple_of(t * 256, 256), 256)
        g = mm(nt_s[mine], q_s[:, :, cols].reshape(4 * SP, 256))
        gq_s[:, :, :, cols] = g.astype(bf).reshape(4, 4, D // 16, 256)
        return 0
    lax.fori_loop(0, 3, grad_q, 0)

    def grad_kv(t, _):
        cols = pl.ds(pl.multiple_of((t % 3) * 256, 256), 256)
        for at, ref in ((0, k_s), (1, v_s)):
            @pl.when(t // 3 == at)
            def _():
                g = jnp.zeros((D, 256), f32)
                for s in range(4):
                    g = g + mm(nt_s[s], ref[4 * s : 4 * s + 4, :, cols].reshape(4 * SP, 256))
                gq_s[:, :, :, pl.ds(pl.multiple_of(D + t * 256, 256), 256)] = g.astype(bf).reshape(4, 4, D // 16, 256)
        return 0
    lax.fori_loop(0, 3, grad_kv, 0)
    lax.fori_loop(3, 6, grad_kv, 0)
    put(gq_s, gq_out)

    def bias_sums(slot, carry):
        bias_q, bias_v = carry
        bias_v = bias_v + jnp.sum(v_s[slot].astype(f32), axis=0, keepdims=True)
        return bias_q, bias_v
    zero = jnp.zeros((1, D), f32)
    bias_q, bias_v = lax.fori_loop(0, 16, bias_sums, (zero, zero))
    for j in range(4):
        bias_q = bias_q + jnp.sum(q_s[j].astype(f32), axis=0, keepdims=True)
    bias_s[0:1, :] = bias_q
    bias_s[1:2, :] = bias_v
    bias_s[2:8, :] = jnp.zeros((6, D), f32)
    put(bias_s, bias_out)
    for w in range(3):
        net.finish(w)

    @pl.when(stay)
    def _():
        y_stay.wait()

    @pl.when(jnp.logical_not(stay))
    def _():
        for j in range(4):
            y_copy(j).wait()

    for copy in puts:
        copy.wait()


def back(n_items, tab, q, k, v_, o, do, lse, nt, wq, y, gd, gu, go):
    bf, f32 = jnp.bfloat16, jnp.float32
    S = jax.ShapeDtypeStruct
    hb = pl.BlockSpec(memory_space=pltpu.HBM)
    dma = pltpu.SemaphoreType.DMA
    v = lambda shape, dtype=bf: pltpu.VMEM(shape, dtype)
    rows = (4, SP, D)
    bufs, sems = sums_scratch(n_items, [(g.shape[2], g.shape[3] // 2) for g in (gd, gu, go)])
    return pl.pallas_call(
        functools.partial(back_kernel, n_items),
        out_shape=(S(rows, bf), S(rows, bf), S((16, SP, D), bf), S((4, 4, D // 16, 3 * D), bf), S((8, D), f32))
        + tuple(S((g.shape[2], g.shape[3] // 2), bf) for g in (gd, gu, go)),
        in_specs=[SM] + [hb] * 12,
        out_specs=(hb,) * 8,
        scratch_shapes=[
            v(rows), v((16, SP, D)), v((16, SP, D)), v(rows), v(rows), v((4, 6, 8, SP), f32), v((4, D, 4 * SP)),
            v((D, 3 * D)), v((24, SP, D)), v((24, SP, D)), v((4, 4, D // 16, 3 * D)), v((8, D), f32), dma((8,)), dma((4,)), dma((4,)), dma((4,)),
        ] + bufs + sems,
        compiler_params=pltpu.CompilerParams(
            collective_id=3, has_side_effects=True, vmem_limit_bytes=63 * 2**20),
        cost_estimate=pl.CostEstimate(
            flops=2 * 5 * 24 * 12 * SP * SP * 256, bytes_accessed=60 * 2**20, transcendentals=24 * 12 * SP * SP),
        name="back",
    )(tab, q, k, v_, o, do, lse, nt, wq, y, gd, gu, go)


def tail_kernel(
    n_items, gq, part, dq, x_in, dh, wq, vec, vp, bias, fd, fu, fo,
    tg_out, tb_out, vec_out, gq_out, gd_out, gu_out, go_out,
    dq_s, x_s, dh_s, wq_s, vec_s, vp_s, bias_s, mine_s, far_mine_s, far_s, near_s, far_e, cut_s, vb_s,
    load_sem, out_sem, low_sem, late_send, late_recv, late_put, p_send, p_recv, vb_send, vb_recv, *rest,
):
    bf, f32 = jnp.bfloat16, jnp.float32
    net = Sums(n_items, (gq,), (gq_out,), split_refs(rest[:7], 1), rest[7:])
    i, f, core, stay, mine, other, far, flip = place()
    shapes = [jax.ShapeDtypeStruct((4, 4) + r.shape, bf) for r in (fd, fu, fo)]
    late = Sums(n_items, (None,) * 3, (gd_out, gu_out, go_out), (shapes,) + (None,) * 4 + ((fd, fu, fo), None),
                (late_send, late_recv, None, None, None, late_put))
    late.AX, late.AY, late.AC0, late.ADA, late.ADB, late.AC1, late.AC2, late.AC3 = range(8)
    ready = net.greet()
    loads = [pltpu.make_async_copy(a, b, load_sem.at[n]) for n, (a, b) in enumerate(
        [(part.at[far], far_mine_s), (dq, dq_s), (wq.at[:, pl.ds(0, D)], wq_s), (part.at[mine], mine_s), (vec, vec_s),
         (vp, vp_s), (bias, bias_s), (x_in, x_s), (dh, dh_s)])]
    for copy in loads:
        copy.start()
    ready()

    def far_copy(j):
        return net.remote(part.at[3 - far, j], far_s.at[j], p_send.at[0, j], p_recv.at[0, j], net.c_dev)

    def near_copy(j):
        return net.remote(part.at[3 - mine, j], near_s.at[j], p_send.at[1, j], p_recv.at[1, j], net.c_dev)

    def chip_copy(j):
        return net.remote(far_mine_s.at[j], far_e.at[j], p_send.at[2, j], p_recv.at[2, j], net.e_dev)

    for j in range(4):
        far_copy(j).start()
    net.begin(0)
    for w in range(3):
        late.gather_begin(w)
    for j in range(4):
        near_copy(j).start()
    loads[0].wait()
    for j in range(4):
        far_copy(j).wait_recv()
        net.plus(far_mine_s, (j,), far_s, (j,))
        chip_copy(j).start()
    net.step(0, 0)
    late.gather_one(2)
    for n in range(1, 9):
        loads[n].wait()
    zero = jnp.zeros((1, D), f32)
    gain = vec_s[0, 0:1, :].astype(f32)
    vp_s[0, 2:3, :] = bias_s[0:1, :]
    vp_s[1, 0:1, :] = bias_s[1:2, :]

    def norm_back(j, carry):
        gains, shifts = carry
        near_copy(j).wait_recv()
        dn = mm(dq_s[j], wq_s[...], NT) + mine_s[j].astype(f32) + near_s[j].astype(f32)
        unit, scale = norm_parts(x_s[j])
        chip_copy(j).wait_recv()
        dn = dn + far_e[j].astype(f32)
        gains = gains + jnp.sum(dn * unit, axis=0, keepdims=True)
        shifts = shifts + jnp.sum(dn, axis=0, keepdims=True)
        grad = dh_s[j] + norm_grad(dn * gain, unit, scale)
        cut_s[j] = grad[:FRAME_TOK]
        dq_s[j] = grad.astype(bf)
        return gains, shifts

    def slot_out(j):
        return pltpu.make_async_copy(cut_s.at[j], tg_out.at[j], out_sem.at[j])

    def low_out(j):
        return pltpu.make_async_copy(dq_s.at[j], tb_out.at[j], low_sem.at[j])

    carry = (zero, zero)
    for j in range(4):
        if j == 1:
            net.step(0, 1)
            late.gather_one(0)
            late.gather_one(1)
        if j == 3:
            net.step(0, 2)
            for w in range(3):
                late.gather_two(w)
        carry = norm_back(j, carry)
        slot_out(j).start()
        low_out(j).start()
    vp_s[0, 0:1, :] = carry[0]
    vp_s[0, 1:2, :] = carry[1]
    ring = [net.c_dev, net.x_dev, net.y_dev, (i, net.zs[0]), (i, net.zs[1])] + [(flip(i, b), f) for b in net.extra]

    def v_copy(n):
        return net.remote(vp_s, vb_s.at[n], vb_send.at[n], vb_recv.at[n], ring[n])

    def v_step(n):
        v_copy(n).wait()
        vp_s[...] = vp_s[...] + vb_s[n]
        if n + 1 < len(ring):
            v_copy(n + 1).start()

    v_copy(0).start()
    v_step(0)
    v_step(1)
    net.step(0, 3)
    v_step(2)
    net.gather_one(0)
    v_step(3)
    net.gather_two(0)
    for n in range(4, len(ring)):
        v_step(n)
    vec_put = pltpu.make_async_copy(vp_s.at[f], vec_out, out_sem.at[4])
    vec_put.start()
    net.gather_three(0)
    net.finish(0)
    for w in range(3):
        late.gather_three(w)
        late.finish(w, False)
    for j in range(4):
        far_copy(j).wait_send()
        near_copy(j).wait_send()
        chip_copy(j).wait_send()
        slot_out(j).wait()
        low_out(j).wait()
    vec_put.wait()


def tail(n_items, gq, part, dq, x_in, dh, wq, vec, vp, bias, fd, fu, fo):
    bf, f32 = jnp.bfloat16, jnp.float32
    S = jax.ShapeDtypeStruct
    hb = pl.BlockSpec(memory_space=pltpu.HBM)
    dma = pltpu.SemaphoreType.DMA
    v = lambda shape, dtype=bf: pltpu.VMEM(shape, dtype)
    rows = (4, SP, D)
    bufs, sems = sums_scratch(n_items, [(gq.shape[2], gq.shape[3] // 2)])
    steps = 5
    while 2 ** (steps - 2) < n_items:
        steps += 1
    return pl.pallas_call(
        functools.partial(tail_kernel, n_items),
        out_shape=(S((4, FRAME_TOK, D), f32), S(rows, bf), S((8, D), f32), S((D // 4, 3 * D), bf))
        + tuple(S((4 * r.shape[0], 2 * r.shape[1]), bf) for r in (fd, fu, fo)),
        in_specs=[hb] * 12,
        out_specs=(hb,) * 7,
        scratch_shapes=[
            v(rows), v(rows, f32), v(rows, f32), v((D, D)), v((4, VEC_ROWS, D)), v((4, 8, D), f32), v((8, D), f32),
            v(rows), v(rows), v(rows), v(rows), v(rows), v((4, FRAME_TOK, D), f32), v((steps, 4, 8, D), f32),
            dma((9,)), dma((5,)), dma((4,)), dma((3, 8)), dma((3, 8)), dma((3,)), dma((3, 4)), dma((3, 4)), dma((steps,)), dma((steps,)),
        ] + bufs + sems,
        compiler_params=pltpu.CompilerParams(
            collective_id=2, has_side_effects=True, vmem_limit_bytes=60 * 2**20),
        cost_estimate=pl.CostEstimate(flops=2 * 14 * 784 * 768 * 768, bytes_accessed=60 * 2**20, transcendentals=0),
        name="tail",
    )(gq, part, dq, x_in, dh, wq, vec, vp, bias, fd, fu, fo)


def on_device(
    tokens,
    cotangent,
    date_year,
    date_day,
    item_dates,
    slot_frame,
    frame_mask,
    qkv_weight,
    qkv_first,
    qkv_second,
    out_weight,
    out_first,
    out_second,
    up_weight,
    up_first,
    up_second,
    down_weight,
    down_first,
    down_second,
    vectors,
    vector_first,
    vector_second,
):
    bf, f32 = jnp.bfloat16, jnp.float32
    n_items = lax.axis_size("items")
    i, f, core, stay, mine, other, far, flip = place()
    swap = []
    for k in range(n_items):
        for z in range(4):
            if k % 2 != z // 2:
                swap.append((k * 4 + z, (k ^ 1) * 4 + 3 - z))

    pad = lambda a: jnp.pad(a[0], ((0, 0), (0, SP - FRAME_TOK), (0, 0)))
    item_index, is_valid = slot_items(item_dates[0], slot_frame[0], frame_mask[0])
    own_items = lax.dynamic_slice_in_dim(item_index, f * 4, 4)
    tables = key_tables(item_index, is_valid, own_items)
    tab = jnp.pad(tables[None], ((0, 7), (0, 128 - tables.shape[0])))
    tmp = jnp.pad(temporal_rows(date_year[0], date_day[0]), ((0, 4), (0, 0)))
    vec = jnp.pad(vectors.astype(bf).reshape(3, D), ((0, VEC_ROWS - 3), (0, 0)))
    q3, k3, v3, o3, lse, nt, x3, dy, vec_all, tab_own, wq, wo, wu, wd = front(
        pad(tokens), pad(cotangent), tmp, tab, vec, jnp.asarray(spatial_rows()),
        qkv_weight, out_weight, up_weight, down_weight)
    block_out, hidden_grad, do3, down_grad, up_grad, out_grad, vector_part = mid(
        o3, x3, dy, vec_all, wo, wu, wd)
    blocks = lambda g: g.reshape(4, 4, g.shape[0] // 16, g.shape[1])
    block_out, dq3, part, gq, bias_part, *regions = back(
        n_items, tab_own, q3, k3, v3, o3, do3, lse, nt, wq, block_out, blocks(down_grad), blocks(up_grad), blocks(out_grad))
    token_grad, token_low, vector_sum, qkv_sum, down_sum, up_sum, out_sum = tail(
        n_items, gq, part.reshape(4, 4, SP, D), dq3, x3, hidden_grad, wq, vec_all, vector_part, bias_part, *regions)
    home = lax.ppermute(token_low, ("items", "frames"), swap)
    token_grad = jnp.where(stay, token_grad, home[:, :FRAME_TOK].astype(f32))
    qkv_new = adamw(qkv_weight, qkv_first, qkv_second, qkv_sum.astype(f32), 0.05, 0.05)
    out_new = adamw(out_weight, out_first, out_second, out_sum.astype(f32), 0.5, 0.05)
    up_new = adamw(up_weight, up_first, up_second, up_sum.astype(f32), 0.05, 0.05)
    down_new = adamw(down_weight, down_first, down_second, down_sum.astype(f32), 0.03, 0.05)
    vector_new = adamw(vectors, vector_first, vector_second, vector_sum[:3].reshape(3 * D), 0.3, 0.0)
    cut = lambda a: a.reshape(1, 4, SP, D)[:, :, :FRAME_TOK]
    return (cut(block_out), token_grad[None]) + qkv_new + out_new + up_new + down_new + vector_new


def solution(mesh):
    placed = (
        P("items", "frames", None, None),
        P("items", "frames", None, None),
        P("items", "frames"),
        P("items", "frames"),
        P("items", None),
        P("items", None),
        P("items", None),
        P("frames", None),
        P("frames", None),
        P("frames", None),
        P("frames", None),
        P("frames", None),
        P("frames", None),
        P("frames", None),
        P("frames", None),
        P("frames", None),
        P("frames", None),
        P("frames", None),
        P("frames", None),
        P("frames"),
        P("frames"),
        P("frames"),
    )
    return jax.shard_map(
        on_device,
        mesh=mesh,
        in_specs=placed,
        out_specs=(
            P("items", "frames", None, None),
            P("items", "frames", None, None),
            P("frames", None),
            P("frames", None),
            P("frames", None),
            P("frames", None),
            P("frames", None),
            P("frames", None),
            P("frames", None),
            P("frames", None),
            P("frames", None),
            P("frames", None),
            P("frames", None),
            P("frames", None),
            P("frames"),
            P("frames"),
            P("frames"),
        ),
        check_vma=False,
    )
```

```python
import functools

import jax
import jax.numpy as jnp
import numpy as np
from jax import lax
from jax.experimental import pallas as pl
from jax.experimental.pallas import tpu as pltpu
from jax.sharding import PartitionSpec as P

D = 768
HEADS = 12
HEAD = 64
GRID = 14
STEP = 10
FRAME_TOK = 196


beta_one = 0.9
beta_two = 0.999


def sincos(values, length_out):
    half_width = length_out // 2
    frequency = 1.0 / 10000.0 ** (jnp.arange(half_width, dtype=jnp.float32) / half_width)
    angles = values[..., None] * frequency
    return jnp.concatenate([jnp.sin(angles), jnp.cos(angles)], axis=-1)


def temporal_rows(year_values, day_values):
    dates = jnp.concatenate(
        [
            sincos((year_values - 2000).astype(jnp.float32), D // 8),
            sincos(day_values.astype(jnp.float32), D // 8),
        ],
        axis=-1,
    )
    return jnp.pad(dates, ((0, 0), (3 * D // 4, 0)))


def spatial_rows():
    half = 3 * D // 16
    frequency = (1.0 / np.float32(10000.0) ** (np.arange(half, dtype=np.float32) / np.float32(half))).astype(np.float32)
    cells = np.arange(FRAME_TOK)
    parts = []
    for values in (cells // GRID, cells % GRID):
        angles = values.astype(np.float32)[:, None] * frequency
        parts += [np.sin(angles), np.cos(angles)]
    rows = np.zeros((SP, D), np.float32)
    rows[:FRAME_TOK, : 3 * D // 4] = np.concatenate(parts, axis=-1)
    return rows


def slot_items(dates_group, frames_group, mask_group):
    item_ends = jnp.cumsum(dates_group)
    starts = item_ends - dates_group
    item_index = jnp.sum((frames_group[:, None] >= item_ends[None, :]).astype(jnp.int32), axis=1)
    is_first = jnp.any(frames_group[:, None] == starts[None, :], axis=1)
    is_valid = jnp.logical_or(mask_group > 0, is_first)
    return (item_index, is_valid)


SP = 208
NK = 6
NEG = -1e30
NT = (((1,), (1,)), ((), ()))
NN = (((1,), (0,)), ((), ()))


def mm(a, b, dims=NN):
    return lax.dot_general(a, b, dims, preferred_element_type=jnp.float32)


def augmented_keys(parts, valid, bias_lane, mine):
    row = lax.broadcasted_iota(jnp.int32, (SP, 128), 0)
    lane = lax.broadcasted_iota(jnp.int32, (SP, 128), 1)
    blocks = []
    for part, live in zip(parts, valid):
        bias = jnp.where(row >= FRAME_TOK, NEG, live).astype(jnp.bfloat16)
        blocks.append(jnp.where(mine, part, jnp.where(lane == bias_lane, bias, jnp.zeros_like(part))))
    return jnp.concatenate(blocks, axis=0)


def attention_step(step, tab_ref, q_ref, k_ref, v_ref, o_ref, lse_ref):
    lane = lax.broadcasted_iota(jnp.int32, (SP, 128), 1)
    j, b = step // 6, step % 6
    cols = pl.ds(pl.multiple_of(b * 128, 128), 128)
    parts = [k_ref[tab_ref[0, j * NK + t], :, cols] for t in range(NK)]
    valid = [jnp.where(tab_ref[0, (4 + j) * NK + t] > 0, 0.0, NEG) for t in range(NK)]
    vg = jnp.concatenate([v_ref[tab_ref[0, j * NK + t], :, cols] for t in range(NK)], axis=0)
    q = q_ref[j, :, cols]
    scores = []
    for h in range(2):
        mine = (lane < 64) if h == 0 else (lane >= 64)
        spare = 64 if h == 0 else 0
        ka = augmented_keys(parts, valid, spare, mine)
        qa = jnp.where(mine, q, jnp.where(lane == spare, jnp.ones_like(q), jnp.zeros_like(q)))
        scores.append(mm(qa, ka, NT))
    peaks = [jnp.max(s, axis=1, keepdims=True) for s in scores]
    probs = [jnp.exp(s - m) for s, m in zip(scores, peaks)]
    sums = [jnp.sum(p, axis=1, keepdims=True) for p in probs]
    outs = [mm(p.astype(jnp.bfloat16), vg) / total for p, total in zip(probs, sums)]
    o_ref[j, :, cols] = jnp.where(lane < 64, outs[0], outs[1]).astype(jnp.bfloat16)
    logs = [m + jnp.log(total) for m, total in zip(peaks, sums)]
    lse_ref[j, b] = jnp.transpose(jnp.where(lane == 0, logs[0], logs[1]))[:8]


VM = pl.BlockSpec(memory_space=pltpu.VMEM)
SM = pl.BlockSpec(memory_space=pltpu.SMEM)


def key_tables(item_index, is_valid, q_items):
    match = (q_items[:, None] == item_index[None, :]) & is_valid[None, :]
    rank = jnp.cumsum(match.astype(jnp.int32), axis=1) - 1
    count = jnp.sum(match.astype(jnp.int32), axis=1)
    place = jnp.arange(NK, dtype=jnp.int32)
    hit = match[:, None, :] & (rank[:, None, :] == place[None, :, None])
    slots = jnp.arange(item_index.shape[0], dtype=jnp.int32)
    idx = jnp.sum(jnp.where(hit, slots[None, None, :], 0), axis=2)
    val = (place[None, :] < count[:, None]).astype(jnp.int32)
    place_of = jnp.arange(4 * NK, dtype=jnp.int32)
    held = (idx.reshape(-1)[None, :] == slots[:, None]) & (val.reshape(-1)[None, :] > 0)
    first = jnp.min(jnp.where(held, place_of[None, :], 4 * NK), axis=1)
    last = jnp.max(jnp.where(held, place_of[None, :], -1), axis=1)
    has_first, has_last = first < 4 * NK, last > first
    rows = [jnp.where(has_first, first, 0), jnp.where(has_last, last, 0), has_first, has_last]
    return jnp.concatenate([idx.reshape(-1), val.reshape(-1)] + [r.astype(jnp.int32) for r in rows])


def adamw(weight, first_moment, second, gradient, step_rate, decay):
    first_new = beta_one * first_moment + (1.0 - beta_one) * gradient
    second_new = beta_two * second + (1.0 - beta_two) * gradient * gradient
    first_hat = first_new / (1.0 - beta_one**STEP)
    second_hat = second_new / (1.0 - beta_two**STEP)
    weight_new = weight - step_rate * (first_hat / (jnp.sqrt(second_hat) + 1e-08) + decay * weight)
    return (first_new, second_new, weight_new)


VEC_ROWS = 16
MESH = pl.DeviceIdType.MESH
Z, X, Y, DA, DB, C0, C1, C2, C3 = range(9)


def norm_rows(x):
    mean = jnp.mean(x, axis=-1, keepdims=True)
    centred = x - mean
    spread = jnp.mean(centred * centred, axis=-1, keepdims=True)
    return centred * lax.rsqrt(spread + 1e-06)


def place():
    i, f = lax.axis_index("items"), lax.axis_index("frames")
    core = i % 2
    upper = f // 2
    stay = core == upper
    mine = jnp.where(stay, f, 3 - f)
    other = f + 1 - 2 * (f % 2)
    far = jnp.where(stay, other, 3 - other)
    flip = lambda v, bit: v + bit - 2 * bit * ((v // bit) % 2)
    return i, f, core, stay, mine, other, far, flip


def halves(core, a, b):
    return jnp.where(core == 0, a, b)


def front_kernel(
    tok, cot, tmp, tab, vec, spatial, wq, wo, wu, wd,
    q_out, k_out, v_out, o_out, lse_out, nt_out, x_out, dy_out, vec_out, tab_out, wq_out, wo_out, wu_out, wd_out,
    t_s, tmp_s, vec_s, n_s, nt_s, q_s, k_s, v_s, o_s, lse_s, x_s, tab_s, wq_s,
    rq32, ro32, ru32, rd32, rq, ro, ru, rd, sq32, so32, su32, sd32, sq, so, su, sd,
    t_send, t_recv, m_send, m_recv, d_send, d_recv, v_send, v_recv, w_send, w_recv, z_send, z_recv,
    reg_sem, own_sem, put_sem, loc_sem, out_sem, nt_sem,
):
    bf, f32 = jnp.bfloat16, jnp.float32
    i, f, core, stay, mine, other, far, flip = place()
    c_dev = (flip(i, 1), f)
    x_dev = (halves(core, flip(i, 2), flip(i, 4)), f)
    y_dev = (halves(core, flip(i, 4), flip(i, 2)), f)
    e_dev = (i, other)
    m_dev = (flip(i, 1), 3 - f)
    xy = (i // 2) % 4
    xy_x, xy_y = halves(core, flip(xy, 1), flip(xy, 2)), halves(core, flip(xy, 2), flip(xy, 1))
    diag = flip(flip(xy, 1), 2)
    zs = [flip(f, 1), jnp.where(f < 2, 2, 1), jnp.where(f < 2, 3, 0)]

    barrier = pltpu.get_barrier_semaphore()
    partners = [c_dev, x_dev, y_dev, m_dev] + [(i, z) for z in zs]
    for dev in partners:
        pl.semaphore_signal(barrier, inc=1, device_id=dev, device_id_type=MESH)

    weights = [(wq, wq_out, rq32, rq, sq32, sq), (wo, wo_out, ro32, ro, so32, so),
               (wu, wu_out, ru32, ru, su32, su), (wd, wd_out, rd32, rd, sd32, sd)]

    def region_load(w):
        src, _, r32, _, _, _ = weights[w]
        rows, cols = r32.shape
        return pltpu.make_async_copy(
            src.at[pl.ds(pl.multiple_of(xy * rows, rows), rows), pl.ds(pl.multiple_of(core * cols, 128), cols)],
            r32, reg_sem.at[w])

    def own_load(w):
        return pltpu.make_async_copy(weights[w][0], weights[w][4], own_sem.at[w])

    def own_put(w):
        out, small = weights[w][1], weights[w][5]
        rows = small.shape[0]
        return pltpu.make_async_copy(small, out.at[pl.ds(pl.multiple_of(f * rows, rows), rows), :], put_sem.at[w])

    for w in range(4):
        region_load(w).start()
    for w in range(4):
        own_load(w).start()
    tok_load = pltpu.make_async_copy(tok, t_s.at[mine], loc_sem.at[0])
    tmp_load = pltpu.make_async_copy(tmp, tmp_s.at[mine], loc_sem.at[1])
    tab_load = pltpu.make_async_copy(tab, tab_out, loc_sem.at[5])
    cot_load = pltpu.make_async_copy(cot, dy_out, loc_sem.at[6])
    vec_load = pltpu.make_async_copy(vec, vec_s.at[f], loc_sem.at[2])

    @pl.when(stay)
    def _():
        tok_load.start()
        tmp_load.start()
        tab_load.start()

    vec_load.start()
    pl.semaphore_wait(barrier, len(partners))

    def remote(src, dst, ssem, rsem, dev):
        return pltpu.make_async_remote_copy(
            src_ref=src, dst_ref=dst, send_sem=ssem, recv_sem=rsem, device_id=dev, device_id_type=MESH)

    def tok_copy(kind, j):
        if kind == 0:
            return remote(tok.at[j], t_s.at[f, j], t_send.at[0, j], t_recv.at[0, j], m_dev)
        if kind == 3:
            return remote(t_s.at[far, j], t_s.at[far, j], t_send.at[3, j], t_recv.at[3, j], c_dev)
        return remote(t_s.at[mine, j], t_s.at[mine, j], t_send.at[kind, j], t_recv.at[kind, j],
                      c_dev if kind == 1 else e_dev)

    def tok_arrival(kind, j):
        shard = (mine, 3 - mine, far, 3 - far)[kind]
        return remote(t_s.at[shard, j], t_s.at[shard, j], t_send.at[kind, j], t_recv.at[kind, j], c_dev)

    def tmp_copy(kind):
        if kind == 0:
            return remote(tmp, tmp_s.at[f], m_send.at[0], m_recv.at[0], m_dev)
        if kind == 3:
            return remote(tmp_s.at[far], tmp_s.at[far], m_send.at[3], m_recv.at[3], c_dev)
        return remote(tmp_s.at[mine], tmp_s.at[mine], m_send.at[kind], m_recv.at[kind], c_dev if kind == 1 else e_dev)

    def tmp_arrival(kind):
        shard = (mine, 3 - mine, far, 3 - far)[kind]
        return remote(tmp_s.at[shard], tmp_s.at[shard], m_send.at[kind], m_recv.at[kind], c_dev)

    def tab_copy():
        return remote(tab, tab_out, d_send.at[4], d_recv.at[4], m_dev)

    def cot_copy(j):
        return remote(cot.at[j], dy_out.at[j], d_send.at[j], d_recv.at[j], m_dev)

    def part(w, z, at, half, piece):
        out, r = weights[w][1], weights[w][3]
        rows, cols = r.shape
        unit = rows // 3
        start = z * 4 * rows + at * rows
        if piece == 0:
            return out.at[pl.ds(pl.multiple_of(start, 16), rows), pl.ds(pl.multiple_of(half * cols, 128), cols)]
        if piece == 1:
            return out.at[pl.ds(pl.multiple_of(start, 16), 2 * unit), pl.ds(pl.multiple_of(half * cols, 128), cols)]
        return out.at[pl.ds(pl.multiple_of(start + 2 * unit, 16), unit), pl.ds(pl.multiple_of(half * cols, 128), cols)]

    def w_copy(w, d, kind):
        sems = (w_send.at[w, d, kind], w_recv.at[w, d, kind])
        z = zs[d]
        at = {X: xy, Y: xy, DA: xy_x, DB: xy_y, C0: xy, C1: xy_x, C2: xy_y, C3: diag}[kind]
        piece = {DA: 1, DB: 2}.get(kind, 0)
        dev = {X: x_dev, Y: y_dev, DA: y_dev, DB: x_dev}.get(kind, c_dev)
        ref = part(w, z, at, core, piece)
        return remote(ref, ref, *sems, dev)

    def w_arrival(w, d, kind):
        sems = (w_send.at[w, d, kind], w_recv.at[w, d, kind])
        z = zs[d]
        at = {X: xy_x, Y: xy_y, DA: diag, DB: diag, C0: xy, C1: xy_y, C2: xy_x, C3: diag}[kind]
        piece = {DA: 1, DB: 2}.get(kind, 0)
        half = (1 - core) if kind >= C0 else core
        ref = part(w, z, at, half, piece)
        return remote(ref, ref, *sems, c_dev)

    def z_copy(w, d):
        return remote(weights[w][3], part(w, f, xy, core, 0), z_send.at[w, d], z_recv.at[w, f], (i, zs[d]))

    def z_arrival(w, d):
        ref = part(w, zs[d], xy, core, 0)
        return remote(ref, ref, z_send.at[w, d], z_recv.at[w, zs[d]], (i, zs[d]))

    def w_send_region(w):
        region_load(w).wait()
        weights[w][3][...] = weights[w][2][...].astype(bf)
        for d in range(3):
            z_copy(w, d).start()

    def w_stage_one(w):
        for d in range(3):
            z_arrival(w, d).wait_recv()
            for kind in (X, Y, C0):
                w_copy(w, d, kind).start()

    def w_stage_two(w):
        for d in range(3):
            w_arrival(w, d, X).wait_recv()
            w_copy(w, d, DA).start()
            w_copy(w, d, C1).start()
            w_arrival(w, d, Y).wait_recv()
            w_copy(w, d, DB).start()
            w_copy(w, d, C2).start()

    def w_stage_three(w):
        for d in range(3):
            w_arrival(w, d, DA).wait_recv()
            w_arrival(w, d, DB).wait_recv()
            w_copy(w, d, C3).start()

    def w_stage_four(w):
        for d in range(3):
            for kind in (C0, C1, C2, C3):
                w_arrival(w, d, kind).wait_recv()

    def w_own(w):
        own_load(w).wait()
        weights[w][5][...] = weights[w][4][...].astype(bf)
        own_put(w).start()

    w_send_region(0)
    vec_load.wait()

    def v_copy(d):
        return remote(vec_s.at[f], vec_s.at[f], v_send.at[d], v_recv.at[f], (i, zs[d]))

    def v_arrival(d):
        return remote(vec_s.at[zs[d]], vec_s.at[zs[d]], v_send.at[d], v_recv.at[zs[d]], (i, zs[d]))

    for d in range(3):
        v_copy(d).start()

    @pl.when(jnp.logical_not(stay))
    def _():
        tmp_copy(0).start()
        tab_copy().start()

    @pl.when(stay)
    def _():
        tok_load.wait()
        tmp_load.wait()
        for kind in (2, 1):
            tmp_copy(kind).start()
        for j in range(4):
            tok_copy(1, j).start()

    w_own(0)
    w_stage_one(0)

    @pl.when(jnp.logical_not(stay))
    def _():
        for j in range(4):
            tok_copy(0, j).start()

    @pl.when(stay)
    def _():
        for j in range(4):
            tok_copy(2, j).start()

    for w in (1, 2, 3):
        w_own(w)
    w_stage_two(0)
    w_stage_three(0)
    w_stage_four(0)
    own_put(0).wait()
    wq_load = pltpu.make_async_copy(wq_out, wq_s, loc_sem.at[3])
    wq_load.start()
    for d in range(3):
        v_arrival(d).wait_recv()
    vec_put = pltpu.make_async_copy(vec_s, vec_out, loc_sem.at[4])
    vec_put.start()
    gain = vec_s[0, 0:1, :].astype(f32)
    shift = vec_s[0, 1:2, :].astype(f32)
    bias_q = vec_s[0, 2:3, :].astype(f32)
    bias_v = vec_s[1, 0:1, :].astype(f32)
    wq_load.wait()

    def normalise(shard):
        def slot(j, _):
            x = t_s[shard, j].astype(f32) + (spatial[...] + tmp_s[shard, pl.ds(j, 1), :])

            @pl.when(shard == mine)
            def _():
                x_s[j] = x
            n_s[j] = (norm_rows(x) * gain + shift).astype(bf)
            return 0
        lax.fori_loop(0, 4, slot, 0)

    def project(shard):
        rows = n_s[...].reshape(4 * SP, D)
        at = pl.ds(4 * shard, 4)
        def keys(t, _):
            cols = pl.ds(pl.multiple_of(t * 256, 256), 256)
            k_s[at, :, cols] = mm(rows, wq_s[:, pl.ds(pl.multiple_of(D + t * 256, 256), 256)]).astype(bf).reshape(4, SP, 256)
            v_s[at, :, cols] = (mm(rows, wq_s[:, pl.ds(pl.multiple_of(2 * D + t * 256, 256), 256)])
                                      + vec_s[1, 0:1, cols].astype(f32)).astype(bf).reshape(4, SP, 256)
            return 0
        lax.fori_loop(0, 3, keys, 0)

    def project_q(shard):
        rows = n_s[...].reshape(4 * SP, D)
        def queries(t, _):
            cols = pl.ds(pl.multiple_of(t * 256, 256), 256)
            q = (mm(rows, wq_s[:, cols]) + vec_s[0, 2:3, cols].astype(f32)).astype(bf)
            q_s[:, :, cols] = (q.astype(f32) * 0.125).astype(bf).reshape(4, SP, 256)
            return 0
        lax.fori_loop(0, 3, queries, 0)

    outs = []
    def put(src, dst):
        copy = pltpu.make_async_copy(src, dst, out_sem.at[len(outs)])
        copy.start()
        outs.append(copy)

    turned = []

    def put_shard(shard):
        n = len(turned)
        if n >= 2:
            turned[n - 2].wait()
        nt_s[n % 2] = jnp.transpose(n_s[...].reshape(4 * SP, D))
        copy = pltpu.make_async_copy(nt_s.at[n % 2], nt_out.at[shard], nt_sem.at[n % 2])
        copy.start()
        turned.append(copy)
        at = pl.ds(4 * shard, 4)
        put(k_s.at[at], k_out.at[at])
        put(v_s.at[at], v_out.at[at])

    moved = jnp.logical_not(stay)

    def arrive(kind):
        tmp_arrival(kind).wait_recv()
        if kind == 2:
            tmp_copy(3).start()
        if kind == 0:
            for then in (2, 1):
                tmp_copy(then).start()
        for j in range(4):
            tok_arrival(kind, j).wait_recv()
            if kind == 2:
                tok_copy(3, j).start()
            if kind == 0:
                for then in (2, 1):
                    tok_copy(then, j).start()

    def work(shard):
        normalise(shard)

        @pl.when(shard == mine)
        def _():
            project_q(shard)

        project(shard)
        put_shard(shard)

    stayed_here, stayed_there = jnp.where(stay, mine, 3 - mine), jnp.where(stay, far, 3 - far)

    @pl.when(moved)
    def _():
        arrive(1)

    work(stayed_here)

    @pl.when(moved)
    def _():
        arrive(0)

    @pl.when(stay)
    def _():
        arrive(1)

    for w in (1, 2, 3):
        w_send_region(w)
    work(3 - stayed_here)
    put(x_s, x_out)
    put(q_s, q_out)

    @pl.when(stay)
    def _():
        arrive(2)

    @pl.when(moved)
    def _():
        arrive(3)

    work(stayed_there)

    @pl.when(moved)
    def _():
        arrive(2)

    @pl.when(stay)
    def _():
        arrive(3)

    @pl.when(moved)
    def _():
        for j in range(4):
            cot_copy(j).start()

    @pl.when(stay)
    def _():
        cot_load.start()

    work(3 - stayed_there)

    @pl.when(stay)
    def _():
        tab_load.wait()

    @pl.when(jnp.logical_not(stay))
    def _():
        tab_copy().wait_recv()

    to_scalars = pltpu.make_async_copy(tab_out, tab_s, loc_sem.at[7])
    to_scalars.start()
    to_scalars.wait()
    plan = ((0, w_stage_one, 1), (3, w_stage_one, 2), (5, w_stage_two, 1), (8, w_stage_one, 3), (14, w_stage_two, 2), (16, w_stage_three, 1), (22, w_stage_two, 3))

    def attend(step, _):
        for at, act, w in plan:
            @pl.when(step == at)
            def _():
                act(w)
        attention_step(step, tab_s, q_s, k_s, v_s, o_s, lse_s)
        return 0

    lax.fori_loop(0, 24, attend, 0)
    put(o_s, o_out)
    put(lse_s, lse_out)
    for act, w in ((w_stage_three, 2), (w_stage_three, 3)):
        act(w)
    for w in (1, 2, 3):
        w_stage_four(w)
        own_put(w).wait()

    @pl.when(jnp.logical_not(stay))
    def _():
        tmp_copy(0).wait_send()
        tab_copy().wait_send()
        for j in range(4):
            tok_copy(0, j).wait_send()
            cot_copy(j).wait()

    @pl.when(stay)
    def _():
        cot_load.wait()

    for kind in (1, 2, 3):
        tmp_copy(kind).wait_send()
        for j in range(4):
            tok_copy(kind, j).wait_send()
    for d in range(3):
        v_copy(d).wait_send()
        for w in range(4):
            z_copy(w, d).wait_send()
            for kind in range(X, C3 + 1):
                w_copy(w, d, kind).wait_send()
    for copy in turned[2:]:
        copy.wait()
    vec_put.wait()
    for copy in outs:
        copy.wait()


def front(tok, cot, tmp, tab, vec, spatial, wq, wo, wu, wd):
    bf, f32 = jnp.bfloat16, jnp.float32
    S = jax.ShapeDtypeStruct
    hb = pl.BlockSpec(memory_space=pltpu.HBM)
    regs = [(w.shape[0] // 4, w.shape[1] // 2) for w in (wq, wo, wu, wd)]
    full = [(4 * w.shape[0], w.shape[1]) for w in (wq, wo, wu, wd)]
    dma = pltpu.SemaphoreType.DMA
    v = lambda shape, dtype=bf: pltpu.VMEM(shape, dtype)
    rows, every, stats = (4, SP, D), (16, SP, D), (4, 6, 8, SP)
    return pl.pallas_call(
        front_kernel,
        out_shape=(
            S(rows, bf), S(every, bf), S(every, bf), S(rows, bf), S(stats, f32), S((4, D, 4 * SP), bf), S(rows, f32),
            S(rows, bf), S((4, VEC_ROWS, D), bf), S(tab.shape, jnp.int32),
        ) + tuple(S(s, bf) for s in full),
        in_specs=[hb] * 5 + [VM] + [hb] * 4,
        out_specs=(hb,) * 14,
        scratch_shapes=[
            v((4,) + rows), v((4, 8, D), f32), v((4, VEC_ROWS, D)), v(rows), v((2, D, 4 * SP)), v(rows), v(every), v(every),
            v(rows), v(stats, f32), v(rows, f32), pltpu.SMEM(tab.shape, jnp.int32), v(full[0]),
        ]
        + [v(r, f32) for r in regs] + [v(r) for r in regs]
        + [v(w.shape, f32) for w in (wq, wo, wu, wd)] + [v(w.shape) for w in (wq, wo, wu, wd)]
        + [dma((4, 4)), dma((4, 4)), dma((4,)), dma((4,)), dma((5,)), dma((5,)), dma((3,)), dma((4,)), dma((4, 3, 9)),
           dma((4, 3, 9)), dma((4, 3)), dma((4, 4)), dma((4,)), dma((4,)), dma((4,)), dma((8,)), dma((16,)),
           dma((2,))],
        compiler_params=pltpu.CompilerParams(
            collective_id=1, has_side_effects=True, vmem_limit_bytes=62 * 2**20),
        cost_estimate=pl.CostEstimate(
            flops=2 * 9 * 784 * 768 * 768, bytes_accessed=40 * 2**20, transcendentals=24 * 12 * SP * SP),
        name="front",
    )(tok, cot, tmp, tab, vec, spatial, wq, wo, wu, wd)


def norm_parts(x):
    centred = x - jnp.mean(x, axis=-1, keepdims=True)
    scale = lax.rsqrt(jnp.mean(centred * centred, axis=-1, keepdims=True) + 1e-06)
    return centred * scale, scale


def norm_grad(dn, unit, scale):
    return (dn - jnp.mean(dn, axis=-1, keepdims=True) - unit * jnp.mean(dn * unit, axis=-1, keepdims=True)) * scale


def mid_kernel(
    o_in, x_in, dy_in, vec, wo, wu, wd,
    y_out, dh_out, do_out, gd_out, gu_out, go_out, vp_out,
    o_s, h_s, dy_s, vec_s, wo_s, wu_s, wd_s, n_s, nt_s, a_s, du_s, mlp_s, dn_s, gd_s, gu_s, go_s, y_s, db_s, do_s, vp_s,
    bu_s, gbu_s, in_sem, out_sem,
):
    bf, f32 = jnp.bfloat16, jnp.float32
    loads = [pltpu.make_async_copy(a, b, in_sem.at[n]) for n, (a, b) in enumerate(
        [(o_in, o_s), (wo, wo_s), (vec, vec_s), (x_in, h_s), (dy_in, dy_s), (wu, wu_s), (wd, wd_s)])]
    for copy in loads[:4]:
        copy.start()
    vp_s[...] = jnp.zeros_like(vp_s)
    zero = jnp.zeros((1, D), f32)
    for n in range(4):
        loads[n].wait()
    for copy in loads[4:]:
        copy.start()
    flat = lambda ref: ref[...].reshape(4 * SP, D)

    def branch(t, _):
        cols = pl.ds(pl.multiple_of(t * 256, 256), 256)
        out = mm(flat(o_s), wo_s[:, cols]) + vec_s[1, 1:2, cols].astype(f32)
        h_s[:, :, cols] = h_s[:, :, cols] + out.reshape(4, SP, 256)
        return 0
    lax.fori_loop(0, 3, branch, 0)
    gain, shift = vec_s[1, 2:3, :].astype(f32), vec_s[2, 0:1, :].astype(f32)

    def norm(j, _):
        unit, _scale = norm_parts(h_s[j])
        n_s[j] = (unit * gain + shift).astype(bf)
        return 0
    lax.fori_loop(0, 4, norm, 0)
    nt_s[...] = jnp.transpose(flat(n_s))
    spots = [(n, (n // 3 + 8) // 3, (n // 3 + 8) % 3, (n % 3) * 256) for n in range(12)]
    for n, z, r, at in spots:
        bu_s[n, 0:1, :] = vec_s[z, r : r + 1, at : at + 256].astype(f32)
    mlp_s[...] = jnp.zeros_like(mlp_s)
    dn_s[...] = jnp.zeros_like(dn_s)
    for n in range(4, 7):
        loads[n].wait()

    def group(g, _):
        start = pl.multiple_of(g * D, D)
        for k in range(3):
            n, low = 3 * g + k, slice(256 * k, 256 * k + 256)
            cols = pl.ds(pl.multiple_of(g * D + k * 256, 256), 256)
            u = mm(flat(n_s), wu_s[:, cols]) + bu_s[n, 0:1, :]
            cdf = 0.5 * (1.0 + lax.erf(u * 0.7071067811865476))
            a = (u * cdf).astype(bf)
            slope = cdf + u * (jnp.exp(u * u * -0.5) * 0.3989422804014327)
            da = mm(flat(dy_s), wd_s[cols, :], NT)
            du = (da * slope).astype(bf)
            a_s[:, low] = a
            du_s[:, low] = du
            gd_s[cols, :] = mm(jnp.transpose(a), flat(dy_s)).astype(bf)
            gu_s[:, cols] = mm(nt_s[...], du).astype(bf)
            gbu_s[n, 0:1, :] = jnp.sum(du.astype(f32), axis=0, keepdims=True)
        for t in range(3):
            out = slice(256 * t, 256 * t + 256)
            mlp_s[:, out] += mm(a_s[...], wd_s[pl.ds(start, D), out])
            dn_s[:, out] += mm(du_s[...], wu_s[out, pl.ds(start, D)], NT)
        return 0

    lax.fori_loop(0, 4, group, 0)
    for n, z, r, at in spots:
        vp_s[z, r : r + 1, at : at + 256] = gbu_s[n, 0:1, :]
    puts = []

    def put(src, dst):
        copy = pltpu.make_async_copy(src, dst, out_sem.at[len(puts)])
        copy.start()
        puts.append(copy)

    put(gd_s, gd_out)
    put(gu_s, gu_out)
    bias_down = vec_s[2, 1:2, :].astype(f32)

    def back(j, carry):
        gains, shifts, bias_o, bias_d = carry
        rows = pl.ds(pl.multiple_of(j * SP, 16), SP)
        h = h_s[j]
        y_s[j] = (h + (mlp_s[rows, :] + bias_down)).astype(bf)
        unit, scale = norm_parts(h)
        dn = dn_s[rows, :]
        gains = gains + jnp.sum(dn * unit, axis=0, keepdims=True)
        shifts = shifts + jnp.sum(dn, axis=0, keepdims=True)
        dy = dy_s[j].astype(f32)
        dh = dy + norm_grad(dn * gain, unit, scale)
        h_s[j] = dh
        db = dh.astype(bf)
        db_s[j] = db
        bias_o = bias_o + jnp.sum(db.astype(f32), axis=0, keepdims=True)
        return gains, shifts, bias_o, bias_d + jnp.sum(dy, axis=0, keepdims=True)
    gains, shifts, bias_o, bias_d = lax.fori_loop(0, 4, back, (zero,) * 4)
    put(y_s, y_out)
    put(h_s, dh_out)
    vp_s[1, 1:2, :] = bias_o
    vp_s[1, 2:3, :] = gains
    vp_s[2, 0:1, :] = shifts
    vp_s[2, 1:2, :] = bias_d
    put(vp_s, vp_out)

    def attended(t, _):
        cols = pl.ds(pl.multiple_of(t * 256, 256), 256)
        do_s[:, :, cols] = mm(flat(db_s), wo_s[cols, :], NT).astype(bf).reshape(4, SP, 256)
        return 0
    lax.fori_loop(0, 3, attended, 0)
    put(do_s, do_out)

    def out_grad(t, _):
        cols = pl.ds(pl.multiple_of(t * 256, 256), 256)
        turned = jnp.transpose(o_s[:, :, cols].reshape(4 * SP, 256))
        go_s[cols, :] = mm(turned, flat(db_s)).astype(bf)
        return 0
    lax.fori_loop(0, 3, out_grad, 0)
    put(go_s, go_out)
    for copy in puts:
        copy.wait()


def mid(o, x, dy, vec, wo, wu, wd):
    bf, f32 = jnp.bfloat16, jnp.float32
    S = jax.ShapeDtypeStruct
    hb = pl.BlockSpec(memory_space=pltpu.HBM)
    dma = pltpu.SemaphoreType.DMA
    v = lambda shape, dtype=bf: pltpu.VMEM(shape, dtype)
    rows = (4, SP, D)
    return pl.pallas_call(
        mid_kernel,
        out_shape=(S(rows, bf), S(rows, f32), S(rows, bf), S((4 * D, D), bf), S((D, 4 * D), bf), S((D, D), bf),
                   S((4, 8, D), f32)),
        in_specs=[hb] * 7,
        out_specs=(hb,) * 7,
        scratch_shapes=[
            v(rows), v(rows, f32), v(rows), v((4, VEC_ROWS, D)), v((D, D)), v((D, 4 * D)), v((4 * D, D)),
            v(rows), v((D, 4 * SP)), v((4 * SP, D)), v((4 * SP, D)), v((4 * SP, D), f32), v((4 * SP, D), f32),
            v((4 * D, D)), v((D, 4 * D)), v((D, D)), v(rows), v(rows), v(rows), v((4, 8, D), f32),
            v((12, 8, 256), f32), v((12, 8, 256), f32), dma((7,)), dma((7,)),
        ],
        compiler_params=pltpu.CompilerParams(vmem_limit_bytes=62 * 2**20),
        cost_estimate=pl.CostEstimate(flops=2 * 27 * 832 * 768 * 768, bytes_accessed=40 * 2**20, transcendentals=832 * 3072 * 2),
        name="mid",
    )(o, x, dy, vec, wo, wu, wd)


class Sums:
    AX, AY, AC0, ADA, ADB, AC1, AC2, AC3 = range(31, 39)

    def __init__(self, n_items, grads, outs, bufs, sems, gathers=True):
        self.gathers = gathers
        self.grads, self.outs = grads, outs
        self.sums, self.crecv, self.r1, self.r2, self.r3, self.fin, self.ext = bufs
        self.g_send, self.g_recv, self.e_send, self.e_recv, self.half_sem, self.put_sem = sems
        i, f, core, stay, mine, other, far, flip = place()
        self.i, self.f, self.core, self.flip = i, f, core, flip
        xy = (i // 2) % 4
        self.xy, self.diag = xy, flip(flip(xy, 1), 2)
        self.xy_x, self.xy_y = halves(core, flip(xy, 1), flip(xy, 2)), halves(core, flip(xy, 2), flip(xy, 1))
        self.c_dev = (flip(i, 1), f)
        self.x_dev = (halves(core, flip(i, 2), flip(i, 4)), f)
        self.y_dev = (halves(core, flip(i, 4), flip(i, 2)), f)
        self.e_dev = (i, other)
        self.zs = [flip(f, 1), flip(f, 2), flip(flip(f, 1), 2)]
        self.extra = []
        bit = 8
        while bit < n_items:
            self.extra.append(bit)
            bit *= 2

    def greet(self, *more):
        barrier = pltpu.get_barrier_semaphore()
        partners = [self.c_dev, self.x_dev, self.y_dev] + [(self.i, z) for z in self.zs]
        partners += [(self.flip(self.i, b), self.f) for b in self.extra] + list(more)
        for dev in partners:
            pl.semaphore_signal(barrier, inc=1, device_id=dev, device_id_type=MESH)
        return lambda: pl.semaphore_wait(barrier, len(partners))

    @staticmethod
    def remote(src, dst, ssem, rsem, dev):
        return pltpu.make_async_remote_copy(
            src_ref=src, dst_ref=dst, send_sem=ssem, recv_sem=rsem, device_id=dev, device_id_type=MESH)

    def cols_of(self, w, half):
        width = self.sums[w].shape[-1]
        return pl.ds(pl.multiple_of(half * width, 128), width)

    def half_load(self, w):
        return pltpu.make_async_copy(
            self.grads[w].at[:, :, :, self.cols_of(w, self.core)], self.sums[w], self.half_sem.at[w])

    def rows_of(self, w):
        unit = self.sums[w].shape[2] // 3
        return (pl.ds(0, 2 * unit), pl.ds(2 * unit, unit))

    def copies(self, w, stage):
        s, base = self.sums[w], (0, 4, 20, 28)[stage]
        ra, rb = self.rows_of(w)
        found = []
        if stage == 0:
            for z in range(4):
                found.append((self.grads[w].at[z, :, :, self.cols_of(w, 1 - self.core)], self.crecv[w].at[z], self.c_dev))
        elif stage == 1:
            for z in range(4):
                found.append((s.at[z, self.xy_x, ra], self.r1[w].at[z, 0, ra], self.x_dev))
                found.append((s.at[z, self.diag, ra], self.r1[w].at[z, 1, ra], self.x_dev))
                found.append((s.at[z, self.xy_y, rb], self.r1[w].at[z, 0, rb], self.y_dev))
                found.append((s.at[z, self.diag, rb], self.r1[w].at[z, 1, rb], self.y_dev))
        elif stage == 2:
            for z in range(4):
                found.append((s.at[z, self.xy_y, ra], self.r2[w].at[z, ra], self.y_dev))
                found.append((s.at[z, self.xy_x, rb], self.r2[w].at[z, rb], self.x_dev))
        else:
            for d in range(3):
                found.append((s.at[self.zs[d], self.xy], self.r3[w].at[d], (self.i, self.zs[d])))
        return [self.remote(src, dst, self.g_send.at[w, base + n], self.g_recv.at[w, base + n], dev)
                for n, (src, dst, dev) in enumerate(found)]

    def region(self, w, at, half, piece):
        rows = self.sums[w].shape[2]
        unit = rows // 3
        start, count = at * rows, rows
        if piece == 1:
            count = 2 * unit
        elif piece == 2:
            start, count = start + 2 * unit, unit
        return self.outs[w].at[pl.ds(pl.multiple_of(start, 16), count), self.cols_of(w, half)]

    def a_copy(self, w, kind):
        at = {self.AX: self.xy, self.AY: self.xy, self.AC0: self.xy, self.ADA: self.xy_x, self.ADB: self.xy_y,
              self.AC1: self.xy_x, self.AC2: self.xy_y, self.AC3: self.diag}[kind]
        piece = {self.ADA: 1, self.ADB: 2}.get(kind, 0)
        dev = {self.AX: self.x_dev, self.AY: self.y_dev, self.ADA: self.y_dev, self.ADB: self.x_dev}.get(kind, self.c_dev)
        dst = self.region(w, at, self.core, piece)
        src = self.fin[w] if kind in (self.AX, self.AY, self.AC0) else dst
        return self.remote(src, dst, self.g_send.at[w, kind], self.g_recv.at[w, kind], dev)

    def a_arrival(self, w, kind):
        at = {self.AX: self.xy_x, self.AY: self.xy_y, self.ADA: self.diag, self.ADB: self.diag, self.AC0: self.xy,
              self.AC1: self.xy_y, self.AC2: self.xy_x, self.AC3: self.diag}[kind]
        piece = {self.ADA: 1, self.ADB: 2}.get(kind, 0)
        half = (1 - self.core) if kind in (self.AC0, self.AC1, self.AC2, self.AC3) else self.core
        ref = self.region(w, at, half, piece)
        return self.remote(ref, ref, self.g_send.at[w, kind], self.g_recv.at[w, kind], self.c_dev)

    def begin(self, w):
        self.half_load(w).start()
        self.send_halves(w)

    def send_halves(self, w):
        for copy in self.copies(w, 0):
            copy.start()

    @staticmethod
    def plus(ref, where, other_ref, other_where):
        ref[where] = ref[where] + other_ref[other_where]

    def step(self, w, stage):
        f32 = jnp.float32
        ra, rb = self.rows_of(w)
        plus, s, xy, xy_x, xy_y = self.plus, self.sums[w], self.xy, self.xy_x, self.xy_y
        for copy in self.copies(w, stage):
            copy.wait_recv()
        if stage == 0:
            self.half_load(w).wait()

            def one(n, _):
                plus(s, (n // 4, n % 4), self.crecv[w], (n // 4, n % 4))
                return 0
            lax.fori_loop(0, 16, one, 0)
        elif stage == 1:
            def one(z, _):
                plus(s, (z, xy, ra), self.r1[w], (z, 0, ra))
                plus(s, (z, xy_y, ra), self.r1[w], (z, 1, ra))
                plus(s, (z, xy, rb), self.r1[w], (z, 0, rb))
                plus(s, (z, xy_x, rb), self.r1[w], (z, 1, rb))
                return 0
            lax.fori_loop(0, 4, one, 0)
        elif stage == 2:
            def one(z, _):
                plus(s, (z, xy), self.r2[w], (z,))
                return 0
            lax.fori_loop(0, 4, one, 0)
        else:
            fin = self.fin[w]
            total = s[self.f, xy].astype(f32)
            for d in range(3):
                total = total + self.r3[w][d].astype(f32)
            fin[...] = total.astype(jnp.bfloat16)
            for n, b in enumerate(self.extra):
                copy = self.remote(fin, self.ext[w].at[n], self.e_send.at[w, n], self.e_recv.at[w, n],
                                   (self.flip(self.i, b), self.f))
                copy.start()
                copy.wait()
                fin[...] = (fin[...].astype(f32) + self.ext[w][n].astype(f32)).astype(jnp.bfloat16)
            if self.gathers:
                self.gather_begin(w)
            else:
                self.fin_put(w).start()
        if stage < 3:
            for copy in self.copies(w, stage + 1):
                copy.start()

    def fin_put(self, w):
        dst = self.region(w, self.xy, self.core, 0) if self.gathers else self.outs[w]
        return pltpu.make_async_copy(self.fin[w], dst, self.put_sem.at[w])

    def gather_begin(self, w):
        self.fin_put(w).start()
        for kind in (self.AX, self.AY, self.AC0):
            self.a_copy(w, kind).start()

    def gather_one(self, w):
        self.a_arrival(w, self.AX).wait_recv()
        self.a_copy(w, self.ADA).start()
        self.a_copy(w, self.AC1).start()
        self.a_arrival(w, self.AY).wait_recv()
        self.a_copy(w, self.ADB).start()
        self.a_copy(w, self.AC2).start()

    def gather_two(self, w):
        self.a_arrival(w, self.ADA).wait_recv()
        self.a_arrival(w, self.ADB).wait_recv()
        self.a_copy(w, self.AC3).start()

    def gather_three(self, w):
        for kind in (self.AC0, self.AC1, self.AC2, self.AC3):
            self.a_arrival(w, kind).wait_recv()
        self.fin_put(w).wait()

    def finish(self, w, sums=True):
        if sums:
            for stage in range(4):
                for copy in self.copies(w, stage):
                    copy.wait_send()
        if self.gathers:
            for kind in range(self.AX, self.AC3 + 1):
                self.a_copy(w, kind).wait_send()
        else:
            self.fin_put(w).wait()


def sums_scratch(n_items, shapes):
    v = lambda shape: pltpu.VMEM(shape, jnp.bfloat16)
    dma = pltpu.SemaphoreType.DMA
    n_extra, n = 0, len(shapes)
    while 8 * 2**n_extra < n_items:
        n_extra += 1
    bufs = []
    for lead in ((4, 4), (4, 4), (4, 2), (4,), (3,), ()):
        bufs += [v(lead + s) for s in shapes]
    bufs += [v((n_extra,) + s) if n_extra else v((1, 16, 128)) for s in shapes]
    sems = [dma((n, 39)), dma((n, 39)), dma((n, max(n_extra, 1))), dma((n, max(n_extra, 1))), dma((n,)), dma((n,))]
    return bufs, sems


def split_refs(refs, n):
    return [refs[k * n : (k + 1) * n] for k in range(7)]


def back_kernel(
    n_items, tab_ref, q_in, k_in, v_in, o_in, do_in, lse_in, nt_in, wq_in, y_in, gd, gu, go,
    y_out, dq_out, part_out, gq_out, bias_out, gd_out, gu_out, go_out,
    q_s, k_s, v_s, o_s, do_s, lse_s, nt_s, wq_s, pk_s, pv_s, gq_s, bias_s, load_sem, out_sem, y_send, y_recv, *rest,
):
    bf, f32 = jnp.bfloat16, jnp.float32
    net = Sums(n_items, (gd, gu, go), (gd_out, gu_out, go_out), split_refs(rest[:21], 3), rest[21:], False)
    i, f, core, stay, mine, other, far, flip = place()
    m_dev = (flip(i, 1), 3 - f)
    ready = net.greet(m_dev)
    loads = [pltpu.make_async_copy(a, b, load_sem.at[n]) for n, (a, b) in enumerate(
        [(q_in, q_s), (k_in, k_s), (v_in, v_s), (o_in, o_s), (do_in, do_s), (lse_in, lse_s), (nt_in, nt_s), (wq_in, wq_s)])]
    for copy in loads[:6]:
        copy.start()
    ready()
    for w in range(3):
        net.send_halves(w)
    y_stay = pltpu.make_async_copy(y_in, y_out, y_send.at[0])

    def y_copy(j):
        return net.remote(y_in.at[j], y_out.at[j], y_send.at[j], y_recv.at[j], m_dev)

    @pl.when(stay)
    def _():
        y_stay.start()

    @pl.when(jnp.logical_not(stay))
    def _():
        for j in range(4):
            y_copy(j).start()

    for n in range(6):
        loads[n].wait()
    for w in range(3):
        net.half_load(w).start()
    for copy in loads[6:]:
        copy.start()
    lane = lax.broadcasted_iota(jnp.int32, (SP, 128), 1)
    plan = ((1, 0, 0), (2, 1, 0), (3, 2, 0), (5, 0, 1), (7, 1, 1), (8, 2, 1), (9, 0, 2), (11, 1, 2))

    def attend_back(step):
        j, b = step // 6, step % 6
        cols = pl.ds(pl.multiple_of(b * 128, 128), 128)
        parts = [k_s[tab_ref[0, j * NK + t], :, cols] for t in range(NK)]
        valid = [jnp.where(tab_ref[0, (4 + j) * NK + t] > 0, 0.0, NEG) for t in range(NK)]
        kg = jnp.concatenate(parts, axis=0)
        vg = jnp.concatenate([v_s[tab_ref[0, j * NK + t], :, cols] for t in range(NK)], axis=0)
        kg_t = jnp.transpose(kg)
        q, do, o = q_s[j, :, cols], do_s[j, :, cols], o_s[j, :, cols]
        prod_t = jnp.transpose(do.astype(f32) * o.astype(f32))
        logs = lse_s[j, b]
        dk_h, dv_h, dq_t = [], [], []
        for h in range(2):
            mine = (lane < 64) if h == 0 else (lane >= 64)
            spare = 64 if h == 0 else 0
            ka = augmented_keys(parts, valid, spare, mine)
            qm = jnp.where(mine, q, jnp.zeros_like(q))
            qa = jnp.where(lane == spare, jnp.ones_like(q), qm)
            dom = jnp.where(mine, do, jnp.zeros_like(do))
            centre = jnp.sum(prod_t[h * 64 : (h + 1) * 64], axis=0, keepdims=True)
            s_t = mm(ka, qa, NT)
            da_t = mm(vg, dom, NT)
            p = jnp.exp(s_t - logs[h : h + 1])
            ds = (p * (da_t - centre)).astype(bf)
            dv_h.append(mm(p.astype(bf), dom))
            dk_h.append(mm(ds, qm))
            dq_t.append(mm(kg_t, ds))
        dq = jnp.transpose(jnp.concatenate([dq_t[0][:64], dq_t[1][64:]], axis=0))
        dk, dv = dk_h[0] + dk_h[1], dv_h[0] + dv_h[1]
        q_s[j, :, cols] = (dq * 0.125).astype(bf)
        for t in range(NK):
            pk_s[j * NK + t, :, cols] = dk[t * SP : (t + 1) * SP].astype(bf)
            pv_s[j * NK + t, :, cols] = dv[t * SP : (t + 1) * SP].astype(bf)

    def one(step, _):
        for at, w, stage in plan:
            @pl.when(step == at)
            def _():
                net.step(w, stage)
        for half in range(2):
            attend_back(2 * step + half)
        return 0

    lax.fori_loop(0, 12, one, 0)
    puts = []

    def put(src, dst):
        copy = pltpu.make_async_copy(src, dst, out_sem.at[len(puts)])
        copy.start()
        puts.append(copy)

    put(q_s, dq_out)
    net.step(2, 2)

    def combine(slot, _):
        first, second = tab_ref[0, 8 * NK + slot], tab_ref[0, 8 * NK + 16 + slot]
        keep_a, keep_b = tab_ref[0, 8 * NK + 32 + slot] > 0, tab_ref[0, 8 * NK + 48 + slot] > 0
        none = jnp.zeros((SP, D), bf)
        for out, part in ((k_s, pk_s), (v_s, pv_s)):
            out[slot] = jnp.where(keep_a, part[first], none) + jnp.where(keep_b, part[second], none)
        return 0

    lax.fori_loop(0, 16, combine, 0)
    net.step(0, 3)
    for n in (6, 7):
        loads[n].wait()

    def slots(ref, shard):
        return ref[pl.ds(4 * shard, 4)].reshape(4 * SP, D)

    def partial_rows(shard, _):
        def tile(t, _):
            at = pl.multiple_of(t * 256, 256)
            keys = mm(slots(k_s, shard), wq_s[pl.ds(at, 256), D : 2 * D], NT)
            values = mm(slots(v_s, shard), wq_s[pl.ds(at, 256), 2 * D :], NT)
            pk_s[pl.ds(4 * shard, 4), :, pl.ds(at, 256)] = (keys + values).astype(bf).reshape(4, SP, 256)
            return 0
        lax.fori_loop(0, 3, tile, 0)
        return 0

    lax.fori_loop(0, 2, partial_rows, 0)
    net.step(1, 3)
    net.step(2, 3)
    lax.fori_loop(2, 4, partial_rows, 0)
    put(pk_s.at[pl.ds(0, 16)], part_out)

    def grad_q(t, _):
        cols = pl.ds(pl.multiple_of(t * 256, 256), 256)
        g = mm(nt_s[mine], q_s[:, :, cols].reshape(4 * SP, 256))
        gq_s[:, :, :, cols] = g.astype(bf).reshape(4, 4, D // 16, 256)
        return 0
    lax.fori_loop(0, 3, grad_q, 0)

    def grad_kv(t, _):
        cols = pl.ds(pl.multiple_of((t % 3) * 256, 256), 256)
        for at, ref in ((0, k_s), (1, v_s)):
            @pl.when(t // 3 == at)
            def _():
                g = jnp.zeros((D, 256), f32)
                for s in range(4):
                    g = g + mm(nt_s[s], ref[4 * s : 4 * s + 4, :, cols].reshape(4 * SP, 256))
                gq_s[:, :, :, pl.ds(pl.multiple_of(D + t * 256, 256), 256)] = g.astype(bf).reshape(4, 4, D // 16, 256)
        return 0
    lax.fori_loop(0, 3, grad_kv, 0)
    lax.fori_loop(3, 6, grad_kv, 0)
    put(gq_s, gq_out)

    def bias_sums(slot, carry):
        bias_q, bias_v = carry
        bias_v = bias_v + jnp.sum(v_s[slot].astype(f32), axis=0, keepdims=True)
        return bias_q, bias_v
    zero = jnp.zeros((1, D), f32)
    bias_q, bias_v = lax.fori_loop(0, 16, bias_sums, (zero, zero))
    for j in range(4):
        bias_q = bias_q + jnp.sum(q_s[j].astype(f32), axis=0, keepdims=True)
    bias_s[0:1, :] = bias_q
    bias_s[1:2, :] = bias_v
    bias_s[2:8, :] = jnp.zeros((6, D), f32)
    put(bias_s, bias_out)
    for w in range(3):
        net.finish(w)

    @pl.when(stay)
    def _():
        y_stay.wait()

    @pl.when(jnp.logical_not(stay))
    def _():
        for j in range(4):
            y_copy(j).wait()

    for copy in puts:
        copy.wait()


def back(n_items, tab, q, k, v_, o, do, lse, nt, wq, y, gd, gu, go):
    bf, f32 = jnp.bfloat16, jnp.float32
    S = jax.ShapeDtypeStruct
    hb = pl.BlockSpec(memory_space=pltpu.HBM)
    dma = pltpu.SemaphoreType.DMA
    v = lambda shape, dtype=bf: pltpu.VMEM(shape, dtype)
    rows = (4, SP, D)
    bufs, sems = sums_scratch(n_items, [(g.shape[2], g.shape[3] // 2) for g in (gd, gu, go)])
    return pl.pallas_call(
        functools.partial(back_kernel, n_items),
        out_shape=(S(rows, bf), S(rows, bf), S((16, SP, D), bf), S((4, 4, D // 16, 3 * D), bf), S((8, D), f32))
        + tuple(S((g.shape[2], g.shape[3] // 2), bf) for g in (gd, gu, go)),
        in_specs=[SM] + [hb] * 12,
        out_specs=(hb,) * 8,
        scratch_shapes=[
            v(rows), v((16, SP, D)), v((16, SP, D)), v(rows), v(rows), v((4, 6, 8, SP), f32), v((4, D, 4 * SP)),
            v((D, 3 * D)), v((24, SP, D)), v((24, SP, D)), v((4, 4, D // 16, 3 * D)), v((8, D), f32), dma((8,)), dma((4,)), dma((4,)), dma((4,)),
        ] + bufs + sems,
        compiler_params=pltpu.CompilerParams(
            collective_id=3, has_side_effects=True, vmem_limit_bytes=63 * 2**20),
        cost_estimate=pl.CostEstimate(
            flops=2 * 5 * 24 * 12 * SP * SP * 256, bytes_accessed=60 * 2**20, transcendentals=24 * 12 * SP * SP),
        name="back",
    )(tab, q, k, v_, o, do, lse, nt, wq, y, gd, gu, go)


def tail_kernel(
    n_items, gq, part, dq, x_in, dh, wq, vec, vp, bias, fd, fu, fo,
    tg_out, tb_out, vec_out, gq_out, gd_out, gu_out, go_out,
    dq_s, x_s, dh_s, wq_s, vec_s, vp_s, bias_s, mine_s, far_mine_s, far_s, near_s, far_e, cut_s, vb_s,
    load_sem, out_sem, low_sem, late_send, late_recv, late_put, p_send, p_recv, vb_send, vb_recv, *rest,
):
    bf, f32 = jnp.bfloat16, jnp.float32
    net = Sums(n_items, (gq,), (gq_out,), split_refs(rest[:7], 1), rest[7:])
    i, f, core, stay, mine, other, far, flip = place()
    shapes = [jax.ShapeDtypeStruct((4, 4) + r.shape, bf) for r in (fd, fu, fo)]
    late = Sums(n_items, (None,) * 3, (gd_out, gu_out, go_out), (shapes,) + (None,) * 4 + ((fd, fu, fo), None),
                (late_send, late_recv, None, None, None, late_put))
    late.AX, late.AY, late.AC0, late.ADA, late.ADB, late.AC1, late.AC2, late.AC3 = range(8)
    ready = net.greet()
    loads = [pltpu.make_async_copy(a, b, load_sem.at[n]) for n, (a, b) in enumerate(
        [(part.at[far], far_mine_s), (dq, dq_s), (wq.at[:, pl.ds(0, D)], wq_s), (part.at[mine], mine_s), (vec, vec_s),
         (vp, vp_s), (bias, bias_s), (x_in, x_s), (dh, dh_s)])]
    for copy in loads:
        copy.start()
    ready()

    def far_copy(j):
        return net.remote(part.at[3 - far, j], far_s.at[j], p_send.at[0, j], p_recv.at[0, j], net.c_dev)

    def near_copy(j):
        return net.remote(part.at[3 - mine, j], near_s.at[j], p_send.at[1, j], p_recv.at[1, j], net.c_dev)

    def chip_copy(j):
        return net.remote(far_mine_s.at[j], far_e.at[j], p_send.at[2, j], p_recv.at[2, j], net.e_dev)

    for j in range(4):
        far_copy(j).start()
    net.begin(0)
    for w in range(3):
        late.gather_begin(w)
    for j in range(4):
        near_copy(j).start()
    loads[0].wait()
    for j in range(4):
        far_copy(j).wait_recv()
        net.plus(far_mine_s, (j,), far_s, (j,))
        chip_copy(j).start()
    net.step(0, 0)
    late.gather_one(2)
    for n in range(1, 9):
        loads[n].wait()
    zero = jnp.zeros((1, D), f32)
    gain = vec_s[0, 0:1, :].astype(f32)
    vp_s[0, 2:3, :] = bias_s[0:1, :]
    vp_s[1, 0:1, :] = bias_s[1:2, :]

    def norm_back(j, carry):
        gains, shifts = carry
        near_copy(j).wait_recv()
        dn = mm(dq_s[j], wq_s[...], NT) + mine_s[j].astype(f32) + near_s[j].astype(f32)
        unit, scale = norm_parts(x_s[j])
        chip_copy(j).wait_recv()
        dn = dn + far_e[j].astype(f32)
        gains = gains + jnp.sum(dn * unit, axis=0, keepdims=True)
        shifts = shifts + jnp.sum(dn, axis=0, keepdims=True)
        grad = dh_s[j] + norm_grad(dn * gain, unit, scale)
        cut_s[j] = grad[:FRAME_TOK]
        dq_s[j] = grad.astype(bf)
        return gains, shifts

    def slot_out(j):
        return pltpu.make_async_copy(cut_s.at[j], tg_out.at[j], out_sem.at[j])

    def low_out(j):
        return pltpu.make_async_copy(dq_s.at[j], tb_out.at[j], low_sem.at[j])

    carry = (zero, zero)
    for j in range(4):
        if j == 1:
            net.step(0, 1)
            late.gather_one(0)
            late.gather_one(1)
        if j == 3:
            net.step(0, 2)
            for w in range(3):
                late.gather_two(w)
        carry = norm_back(j, carry)
        slot_out(j).start()
        low_out(j).start()
    vp_s[0, 0:1, :] = carry[0]
    vp_s[0, 1:2, :] = carry[1]
    ring = [net.c_dev, net.x_dev, net.y_dev, (i, net.zs[0]), (i, net.zs[1])] + [(flip(i, b), f) for b in net.extra]

    def v_copy(n):
        return net.remote(vp_s, vb_s.at[n], vb_send.at[n], vb_recv.at[n], ring[n])

    def v_step(n):
        v_copy(n).wait()
        vp_s[...] = vp_s[...] + vb_s[n]
        if n + 1 < len(ring):
            v_copy(n + 1).start()

    v_copy(0).start()
    v_step(0)
    v_step(1)
    net.step(0, 3)
    v_step(2)
    net.gather_one(0)
    v_step(3)
    net.gather_two(0)
    for n in range(4, len(ring)):
        v_step(n)
    vec_put = pltpu.make_async_copy(vp_s.at[f], vec_out, out_sem.at[4])
    vec_put.start()
    net.gather_three(0)
    net.finish(0)
    for w in range(3):
        late.gather_three(w)
        late.finish(w, False)
    for j in range(4):
        far_copy(j).wait_send()
        near_copy(j).wait_send()
        chip_copy(j).wait_send()
        slot_out(j).wait()
        low_out(j).wait()
    vec_put.wait()


def tail(n_items, gq, part, dq, x_in, dh, wq, vec, vp, bias, fd, fu, fo):
    bf, f32 = jnp.bfloat16, jnp.float32
    S = jax.ShapeDtypeStruct
    hb = pl.BlockSpec(memory_space=pltpu.HBM)
    dma = pltpu.SemaphoreType.DMA
    v = lambda shape, dtype=bf: pltpu.VMEM(shape, dtype)
    rows = (4, SP, D)
    bufs, sems = sums_scratch(n_items, [(gq.shape[2], gq.shape[3] // 2)])
    steps = 5
    while 2 ** (steps - 2) < n_items:
        steps += 1
    return pl.pallas_call(
        functools.partial(tail_kernel, n_items),
        out_shape=(S((4, FRAME_TOK, D), f32), S(rows, bf), S((8, D), f32), S((D // 4, 3 * D), bf))
        + tuple(S((4 * r.shape[0], 2 * r.shape[1]), bf) for r in (fd, fu, fo)),
        in_specs=[hb] * 12,
        out_specs=(hb,) * 7,
        scratch_shapes=[
            v(rows), v(rows, f32), v(rows, f32), v((D, D)), v((4, VEC_ROWS, D)), v((4, 8, D), f32), v((8, D), f32),
            v(rows), v(rows), v(rows), v(rows), v(rows), v((4, FRAME_TOK, D), f32), v((steps, 4, 8, D), f32),
            dma((9,)), dma((5,)), dma((4,)), dma((3, 8)), dma((3, 8)), dma((3,)), dma((3, 4)), dma((3, 4)), dma((steps,)), dma((steps,)),
        ] + bufs + sems,
        compiler_params=pltpu.CompilerParams(
            collective_id=2, has_side_effects=True, vmem_limit_bytes=60 * 2**20),
        cost_estimate=pl.CostEstimate(flops=2 * 14 * 784 * 768 * 768, bytes_accessed=60 * 2**20, transcendentals=0),
        name="tail",
    )(gq, part, dq, x_in, dh, wq, vec, vp, bias, fd, fu, fo)


def on_device(
    tokens,
    cotangent,
    date_year,
    date_day,
    item_dates,
    slot_frame,
    frame_mask,
    qkv_weight,
    qkv_first,
    qkv_second,
    out_weight,
    out_first,
    out_second,
    up_weight,
    up_first,
    up_second,
    down_weight,
    down_first,
    down_second,
    vectors,
    vector_first,
    vector_second,
):
    bf, f32 = jnp.bfloat16, jnp.float32
    n_items = lax.axis_size("items")
    i, f, core, stay, mine, other, far, flip = place()
    swap = []
    for k in range(n_items):
        for z in range(4):
            if k % 2 != z // 2:
                swap.append((k * 4 + z, (k ^ 1) * 4 + 3 - z))

    pad = lambda a: jnp.pad(a[0], ((0, 0), (0, SP - FRAME_TOK), (0, 0)))
    item_index, is_valid = slot_items(item_dates[0], slot_frame[0], frame_mask[0])
    own_items = lax.dynamic_slice_in_dim(item_index, f * 4, 4)
    tables = key_tables(item_index, is_valid, own_items)
    tab = jnp.pad(tables[None], ((0, 7), (0, 128 - tables.shape[0])))
    tmp = jnp.pad(temporal_rows(date_year[0], date_day[0]), ((0, 4), (0, 0)))
    vec = jnp.pad(vectors.astype(bf).reshape(3, D), ((0, VEC_ROWS - 3), (0, 0)))
    q3, k3, v3, o3, lse, nt, x3, dy, vec_all, tab_own, wq, wo, wu, wd = front(
        pad(tokens), pad(cotangent), tmp, tab, vec, jnp.asarray(spatial_rows()),
        qkv_weight, out_weight, up_weight, down_weight)
    block_out, hidden_grad, do3, down_grad, up_grad, out_grad, vector_part = mid(
        o3, x3, dy, vec_all, wo, wu, wd)
    blocks = lambda g: g.reshape(4, 4, g.shape[0] // 16, g.shape[1])
    block_out, dq3, part, gq, bias_part, *regions = back(
        n_items, tab_own, q3, k3, v3, o3, do3, lse, nt, wq, block_out, blocks(down_grad), blocks(up_grad), blocks(out_grad))
    token_grad, token_low, vector_sum, qkv_sum, down_sum, up_sum, out_sum = tail(
        n_items, gq, part.reshape(4, 4, SP, D), dq3, x3, hidden_grad, wq, vec_all, vector_part, bias_part, *regions)
    home = lax.ppermute(token_low, ("items", "frames"), swap)
    token_grad = jnp.where(stay, token_grad, home[:, :FRAME_TOK].astype(f32))
    qkv_new = adamw(qkv_weight, qkv_first, qkv_second, qkv_sum.astype(f32), 0.05, 0.05)
    out_new = adamw(out_weight, out_first, out_second, out_sum.astype(f32), 0.5, 0.05)
    up_new = adamw(up_weight, up_first, up_second, up_sum.astype(f32), 0.05, 0.05)
    down_new = adamw(down_weight, down_first, down_second, down_sum.astype(f32), 0.03, 0.05)
    vector_new = adamw(vectors, vector_first, vector_second, vector_sum[:3].reshape(3 * D), 0.3, 0.0)
    cut = lambda a: a.reshape(1, 4, SP, D)[:, :, :FRAME_TOK]
    return (cut(block_out), token_grad[None]) + qkv_new + out_new + up_new + down_new + vector_new


def solution(mesh):
    placed = (
        P("items", "frames", None, None),
        P("items", "frames", None, None),
        P("items", "frames"),
        P("items", "frames"),
        P("items", None),
        P("items", None),
        P("items", None),
        P("frames", None),
        P("frames", None),
        P("frames", None),
        P("frames", None),
        P("frames", None),
        P("frames", None),
        P("frames", None),
        P("frames", None),
        P("frames", None),
        P("frames", None),
        P("frames", None),
        P("frames", None),
        P("frames"),
        P("frames"),
        P("frames"),
    )
    return jax.shard_map(
        on_device,
        mesh=mesh,
        in_specs=placed,
        out_specs=(
            P("items", "frames", None, None),
            P("items", "frames", None, None),
            P("frames", None),
            P("frames", None),
            P("frames", None),
            P("frames", None),
            P("frames", None),
            P("frames", None),
            P("frames", None),
            P("frames", None),
            P("frames", None),
            P("frames", None),
            P("frames", None),
            P("frames", None),
            P("frames"),
            P("frames"),
            P("frames"),
        ),
        check_vma=False,
    )
```
